32 devices in a mesh: groups: 2 (over y), tp: 4 (over z), rep: 2 (over x), sub: 2 (over core).
Axes of the slice: x: 2, y: 2, z: 4, core: 2. Of those that a mesh axis runs over, the one named last changes fastest.
Arguments:
- hidden: bfloat16 [4, 512, 28672], P(None, ('groups', 'rep', 'sub'), 'tp'), parts along dimension 1, may hold values from -6 to 6
- base_weight: bfloat16 [28672, 8192], P('tp', ('rep', 'sub')), may hold values from -0.03125 to 0.03125
- down_a: bfloat16 [4, 28672, 64], P(('rep', 'sub'), 'tp'), may hold values from -0.03125 to 0.03125
- up_b: bfloat16 [4, 64, 8192], P('tp', None, ('rep', 'sub')), may hold values from -0.75 to 0.75
- adapter_ids: int32 [512, 1], P('groups'), parts along dimension 0, may hold values from 0 to 3; in each aligned block of 256 rows (0 to 255, 256 to 511, ...) at most 128 rows name the same one
- owner_map: int32 [4], replicated, may hold values from 0 to 3, each once
Outputs:
- projected: bfloat16 [4, 512, 8192], P(None, ('groups', 'tp'), ('rep', 'sub')), parts along dimension 1
The draws below stay inside these ranges and needn't reach their ends.
There are 2 independent parts, one for each index of `groups`. The reference program is written for one: setup_inputs(seed, part) draws one part's arguments, and reference() takes and returns one part's arrays. A program takes and returns all parts, laid end to end along the dimension named above; an argument that names none is the same for every part. Nothing has to cross between parts.
Inputs may be any that keep to these rules, and one draw needn't show every extreme that they name: `adapter_ids`: no adapter is named by more than 128 requests, a bound that some block reaches. `owner_map`: each slot holds exactly one adapter.
All inputs are finite; a program needn't handle non-finite values.
Results may differ from the reference program's by a relative error of at most 0.0036.
Values may be sent and summed in bfloat16 or wider, within the bound.
No kernel may reach another device: no remote copies, remote signals or barrier semaphores. Data moves between devices by JAX's collectives and lax.ppermute only.
A program may use at most 192 MiB of HBM per device.

```python
import math
import jax
import jax.numpy as jnp
import numpy as np
from jax import lax

D = 8192
FF = 28672
RANK = 64
STEPS = 4
REQ = 256
SLOTS = 4
CAP = 128


def steps_of(key, extent, pieces, least, top_value):
    loudness, own = 1.0, jax.random.fold_in(key, 6)
    for axis_at, parts in pieces:
        steps = jnp.exp(jax.random.uniform(jax.random.fold_in(own, axis_at), (parts,), jnp.float32, least / len(pieces), top_value / len(pieces)))
        loudness = loudness * jnp.repeat(steps, extent[axis_at] // parts).reshape([-1 if axis == axis_at else 1 for axis in range(len(extent))])
    return loudness


def routed_block(rng, own, number, rows, number_of, top, most, lean):
    order = jax.random.permutation(rng, number_of)
    heavy_load, common = shares(number_of, rows * top, most, lean, True), shares(number_of, rows * top, most, lean, False)
    places = jnp.arange(number_of)

    def named(sizes, offset_by):
        used = int((sizes > 0).sum())
        fixed = max(1, used // 4)
        moved = fixed + (places - fixed + offset_by * (used - fixed)) % max(1, number_of - fixed)
        return jnp.zeros((number_of,), jnp.int32).at[order[jnp.where(places < fixed, places, moved)]].set(jnp.asarray(sizes, jnp.int32))

    sizes = jnp.where(number % 4 == 0, named(heavy_load, number // 4), named(common, number - number // 4 - 1))
    mixed = jax.random.permutation(jax.random.fold_in(own, 3), number_of)
    source_of, receiver = mixed[0:number_of // 2 * 2:2], mixed[1:number_of // 2 * 2:2]
    margin = jnp.minimum(sizes[source_of] - 1, most - sizes[receiver]) // 2
    margin = jnp.where((source_of == order[0]) | (receiver == order[0]) | (sizes[receiver] == 0), 0, jnp.maximum(margin, 0))
    moved = jax.random.randint(jax.random.fold_in(own, 4), (number_of // 2,), 0, 1 << 20) % (margin + 1)
    sizes = sizes.at[source_of].add(-moved).at[receiver].add(moved)
    items = jnp.searchsorted(jnp.cumsum(sizes), jnp.arange(rows * top), side="right").astype(jnp.int32)
    grid = items.reshape(top, rows).T
    grid = grid[jax.random.permutation(jax.random.fold_in(own, 1), rows)]
    offset_by = jax.random.randint(jax.random.fold_in(own, 2), (rows, 1), 0, top)
    return jnp.take_along_axis(grid, (jnp.arange(top)[None, :] + offset_by) % top, axis=1)


def shares(count, total, reach, skew, full):
    weights = [(1 << 20) // math.isqrt(grade ** skew) + 1 for grade in range(1, count + 1)]
    largest = reach if full else min(reach, max(-(-total // count), total * weights[0] // sum(weights)))
    least = 1 if total - largest >= count - 1 else 0
    holding, surplus = [largest] + [least] * (count - 1), total - largest - least * (count - 1)
    while surplus > 0:
        movable = [i for i in range(1, count) if holding[i] < largest] or [i for i in range(1, count) if holding[i] < reach]
        pool, remaining = sum([weights[i] for i in movable]), surplus
        for i in movable:
            addition = min(reach - holding[i], max(1, remaining * weights[i] // pool), surplus)
            holding[i] = holding[i] + addition
            surplus = surplus - addition
    return np.array(holding)


def centred(stream_key, dims, scale, bound, shards=(), kind=jnp.bfloat16):
    values = scale * jax.random.normal(stream_key, dims, jnp.float32)
    if shards:
        values = values * steps_of(stream_key, dims, shards, -0.22, 0.18)
    return jnp.clip(values, -bound, bound).astype(kind)


def setup_inputs(seed: int = 0, part: int = 0) -> dict:
    keys = jax.random.split(jax.random.key(seed), 7)
    own_keys = jax.random.split(jax.random.fold_in(keys[6], part), 7)
    hidden = centred(own_keys[0], (STEPS, REQ, FF), 1.0, 6.0, ((1, 4), (2, 4)))
    base_weight = centred(keys[1], (FF, D), FF ** -0.5, 0.03125, ((0, 4), (1, 4)))
    down_a = centred(keys[2], (SLOTS, FF, RANK), FF ** -0.5, 0.03125, ((0, 4), (1, 4)))
    up_b = centred(keys[3], (SLOTS, RANK, D), RANK ** -0.5, 0.75, ((0, 4), (2, 4)))
    adapter_ids_keys = jax.random.split(jax.random.fold_in(own_keys[4], 1), REQ // REQ)
    adapter_ids_turns = jax.random.permutation(jax.random.fold_in(own_keys[4], 3), REQ // REQ)
    adapter_ids = jax.vmap(lambda own, number: routed_block(jax.random.fold_in(own_keys[4], 2), own, number, REQ, SLOTS, 1, CAP, 2))(adapter_ids_keys, adapter_ids_turns).reshape((REQ, 1))
    owner_map = jax.random.permutation(keys[5], SLOTS).astype(jnp.int32)
    return {"hidden": hidden, "base_weight": base_weight, "down_a": down_a, "up_b": up_b, "adapter_ids": adapter_ids, "owner_map": owner_map}


def reference(hidden, base_weight, down_a, up_b, adapter_ids, owner_map):
    step_count = hidden.shape[0]
    requests = hidden.shape[1]
    row_slots = owner_map[adapter_ids[:, 0]].astype(jnp.int32)
    flat_rows = hidden.reshape(step_count * requests, hidden.shape[2])
    base_output = jnp.dot(flat_rows, base_weight, preferred_element_type=jnp.float32)
    base_output = base_output.reshape(step_count, requests, base_weight.shape[1])

    def one_request(operands):
        decode_step_rows, row_slot = operands
        panel_a = lax.dynamic_index_in_dim(down_a, row_slot, 0, keepdims=False)
        rank_part = jnp.dot(decode_step_rows, panel_a, preferred_element_type=jnp.float32).astype(jnp.bfloat16)
        panel_b = lax.dynamic_index_in_dim(up_b, row_slot, 0, keepdims=False)
        return jnp.dot(rank_part, panel_b, preferred_element_type=jnp.float32).astype(jnp.bfloat16)

    expanded_rows = lax.map(one_request, (jnp.swapaxes(hidden, 0, 1), row_slots))
    expanded_rows = jnp.swapaxes(expanded_rows, 0, 1)
    return (base_output + 0.5 * expanded_rows.astype(jnp.float32)).astype(jnp.bfloat16)
```

```python
import functools

import jax
import jax.numpy as jnp
from jax import lax
from jax.experimental import pallas as pl
from jax.experimental.pallas import tpu as pltpu
from jax.sharding import PartitionSpec as P

ADAPTER_SCALE = 0.5
BLOCK_N = 256
VMEM_BYTES = 40 * 1024 * 1024


def matmul_body(first, steps, pos_ref, own_ref, sib_ref, w_ref, a_ref,
                send_ref, keep_ref, rank_send_ref, rank_keep_ref, x_ref, sems):
    rows = send_ref.shape[0]
    depth = w_ref.shape[0]
    slots, _, rank = a_ref.shape
    place = pl.program_id(0)

    @pl.when(place == 0)
    def _():
        own_at = pos_ref[0]
        own_copy = pltpu.make_async_copy(own_ref.at[pl.ds(first, steps)], x_ref.at[own_at], sems.at[0])
        sib_copy = pltpu.make_async_copy(sib_ref.at[pl.ds(first, steps)], x_ref.at[1 - own_at], sems.at[1])
        own_copy.start()
        sib_copy.start()
        own_copy.wait()
        sib_copy.wait()
        x = x_ref[...].reshape(2 * rows, depth)
        for slot in range(slots):
            part = jnp.dot(x, a_ref[slot], preferred_element_type=jnp.float32)
            rank_send_ref[:, slot * rank:(slot + 1) * rank] = part[:rows]
            rank_keep_ref[:, slot * rank:(slot + 1) * rank] = part[rows:]

    x = x_ref[...].reshape(2 * rows, depth)
    term = jnp.dot(x, w_ref[...], preferred_element_type=jnp.float32)
    send_ref[...] = term[:rows].astype(send_ref.dtype)
    keep_ref[...] = term[rows:]


def partial_products(pos, own, sib, first, steps, weight, down_a):
    _, per_block, depth = own.shape
    width = weight.shape[1]
    slots, _, rank = down_a.shape
    rows = steps * per_block
    block_n = min(BLOCK_N, width)
    any_spec = pl.BlockSpec(memory_space=pl.ANY)
    flops = 2 * 2 * rows * depth * (width + slots * rank)
    moved = 2 * depth * (2 * rows + width + slots * rank) + 6 * rows * width
    return pl.pallas_call(
        functools.partial(matmul_body, first, steps),
        grid=(width // block_n,),
        in_specs=[
            pl.BlockSpec(memory_space=pltpu.SMEM),
            any_spec,
            any_spec,
            pl.BlockSpec((depth, block_n), lambda i: (0, i)),
            pl.BlockSpec((slots, depth, rank), lambda i: (0, 0, 0)),
        ],
        out_specs=[
            pl.BlockSpec((rows, block_n), lambda i: (0, i)),
            pl.BlockSpec((rows, block_n), lambda i: (0, i)),
            pl.BlockSpec((rows, slots * rank), lambda i: (0, 0)),
            pl.BlockSpec((rows, slots * rank), lambda i: (0, 0)),
        ],
        out_shape=[
            jax.ShapeDtypeStruct((rows, width), jnp.bfloat16),
            jax.ShapeDtypeStruct((rows, width), jnp.float32),
            jax.ShapeDtypeStruct((rows, slots * rank), jnp.float32),
            jax.ShapeDtypeStruct((rows, slots * rank), jnp.float32),
        ],
        scratch_shapes=[
            pltpu.VMEM((2, steps, per_block, depth), jnp.bfloat16),
            pltpu.SemaphoreType.DMA((2,)),
        ],
        compiler_params=pltpu.CompilerParams(
            dimension_semantics=("arbitrary",), vmem_limit_bytes=VMEM_BYTES
        ),
        cost_estimate=pl.CostEstimate(flops=flops, bytes_accessed=moved, transcendentals=0),
        name="partial_products",
    )(pos, own, sib, weight, down_a)


def per_device(hidden, base_weight, down_a, up_b, adapter_ids, owner_map):
    step_count, per_block, _ = hidden.shape
    n_tensor = lax.axis_size("tp")
    n_rep = lax.axis_size("rep")
    n_sub = lax.axis_size("sub")
    n_owners = n_rep * n_sub
    tensor_index = lax.axis_index("tp")
    rep_index = lax.axis_index("rep")
    sub_index = lax.axis_index("sub")
    owner_index = lax.axis_index(("rep", "sub"))
    requests = per_block * n_owners
    rows_mine = requests // n_tensor
    group = n_tensor // n_rep
    group_index = tensor_index // group
    owned_slots, _, rank_size = down_a.shape
    slot_count = owned_slots * n_owners
    width = base_weight.shape[1]

    def swap_cores(value):
        return lax.ppermute(value, "sub", [(i, i ^ 1) for i in range(n_sub)])

    def from_rep(value, shift):
        return lax.ppermute(value, "rep", [((i + shift) % n_rep, i) for i in range(n_rep)])

    def swap_tensor(value, bit):
        return lax.ppermute(value, "tp", [(i, i ^ bit) for i in range(n_tensor)])

    def to_group(value, shift, hop):
        pairs = []
        for rep in range(n_rep):
            target = (rep + shift) % n_rep
            source = (target + hop) % n_rep
            for low in range(group):
                pairs.append(((source * group + low) * n_rep + rep, (target * group + low) * n_rep + rep))
        return lax.ppermute(value, ("tp", "rep"), pairs)

    def reduce_rows(send, keep, steps, shift, kind):
        columns = keep.shape[1]
        total = keep + swap_tensor(send, group // 2).astype(jnp.float32)
        extent, bit = per_block, group // 4
        while bit:
            extent //= 2
            halves = total.reshape(steps, 2, extent, columns)
            mine = (tensor_index // bit) % 2
            kept = lax.dynamic_index_in_dim(halves, mine, 1, keepdims=False)
            sent = lax.dynamic_index_in_dim(halves, 1 - mine, 1, keepdims=False)
            total = kept + swap_tensor(sent.astype(kind), bit).astype(jnp.float32)
            bit //= 2
        total = total.reshape(steps, rows_mine, columns)
        rounded = total.astype(kind)
        for hop in range(1, n_rep):
            total = total + to_group(rounded, shift, hop).astype(jnp.float32)
        return total

    keeps = (tensor_index // (group // 2)) % 2
    pos = (sub_index == keeps).astype(jnp.int32).reshape(1)

    panels = lax.all_gather(up_b, "tp", axis=0, tiled=True).reshape(slot_count * rank_size, width)

    remote = {}
    for step in range(step_count):
        for shift in range(1, n_rep):
            remote[step, shift] = from_rep(hidden[step:step + 1], shift)

    my_ids = lax.dynamic_slice_in_dim(adapter_ids, tensor_index * rows_mine, rows_mine)
    iota = lax.broadcasted_iota(jnp.int32, (rows_mine, slot_count), 1)
    my_slot = jnp.sum((my_ids == iota).astype(jnp.int32) * owner_map[None, :], axis=1)
    slot_hot = my_slot[:, None] == iota

    base_sum = [None] * step_count
    rank_sum = [None] * step_count
    half = step_count // 2
    for first in (0, half):
        sib = swap_cores(hidden[first:first + half])
        own = hidden[first:first + half]
        send, keep, rank_send, rank_keep = partial_products(
            pos, own, sib, 0, half, base_weight, down_a
        )
        ranks = reduce_rows(rank_send, rank_keep, half, 0, jnp.float32)
        sums = reduce_rows(send, keep, half, 0, jnp.bfloat16)
        for step in range(half):
            base_sum[first + step] = sums[step]
            rank_sum[first + step] = ranks[step]

    outputs = []
    for step in range(step_count):
        for shift in range(1, n_rep):
            own = remote[step, shift]
            sib = swap_cores(own)
            send, keep, rank_send, rank_keep = partial_products(
                pos, own, sib, 0, 1, base_weight, down_a
            )
            here = group_index == (rep_index + shift) % n_rep
            ranks = reduce_rows(rank_send, rank_keep, 1, shift, jnp.float32)[0]
            rank_sum[step] = jnp.where(here, ranks, rank_sum[step])
            sums = reduce_rows(send, keep, 1, shift, jnp.bfloat16)[0]
            base_sum[step] = jnp.where(here, sums, base_sum[step])
        finished = rank_sum[step].astype(jnp.bfloat16).reshape(rows_mine, owned_slots, rank_size)
        owned_hot = lax.dynamic_slice_in_dim(slot_hot, owner_index * owned_slots, owned_slots, axis=1)
        masked = jnp.sum(
            jnp.where(owned_hot[:, :, None], finished, 0), axis=1, dtype=jnp.float32
        ).astype(jnp.bfloat16)
        chosen = masked
        for turn in range(1, n_owners):
            chosen = chosen + lax.ppermute(
                masked, ("rep", "sub"), [(i, (i + turn) % n_owners) for i in range(n_owners)]
            )
        spread = jnp.where(slot_hot[:, :, None], chosen[:, None, :], 0).reshape(
            rows_mine, slot_count * rank_size
        )
        lifted = jnp.dot(spread, panels, preferred_element_type=jnp.float32).astype(jnp.bfloat16)
        outputs.append(
            (base_sum[step] + ADAPTER_SCALE * lifted.astype(jnp.float32)).astype(jnp.bfloat16)
        )
    return jnp.stack(outputs, axis=0)


def solution(mesh):
    return jax.shard_map(
        per_device,
        mesh=mesh,
        in_specs=(
            P(None, ("groups", "rep", "sub"), "tp"),
            P("tp", ("rep", "sub")),
            P(("rep", "sub"), "tp", None),
            P("tp", None, ("rep", "sub")),
            P("groups", None),
            P(),
        ),
        out_specs=P(None, ("groups", "tp"), ("rep", "sub")),
        check_vma=False,
    )
```

```python
import functools

import jax
import jax.numpy as jnp
from jax import lax
from jax.experimental import pallas as pl
from jax.experimental.pallas import tpu as pltpu
from jax.sharding import PartitionSpec as P

ADAPTER_SCALE = 0.5
BLOCK_N = 256
VMEM_BYTES = 6 * 1024 * 1024


def matmul_body(first, steps, pos_ref, own_ref, sib_ref, w_ref, a_ref,
                send_ref, keep_ref, rank_send_ref, rank_keep_ref, x_ref, sems):
    rows, width = send_ref.shape
    depth = w_ref.shape[0]
    slots, _, rank = a_ref.shape
    block_n = min(BLOCK_N, width)
    own_at = pos_ref[0]
    own_copy = pltpu.make_async_copy(own_ref.at[pl.ds(first, steps)], x_ref.at[own_at], sems.at[0])
    sib_copy = pltpu.make_async_copy(sib_ref.at[pl.ds(first, steps)], x_ref.at[1 - own_at], sems.at[1])
    own_copy.start()
    sib_copy.start()
    own_copy.wait()
    sib_copy.wait()
    for slot in range(slots):
        x = x_ref[...].reshape(2 * rows, depth)
        part = jnp.dot(x, a_ref[slot], preferred_element_type=jnp.float32)
        rank_send_ref[:, slot * rank:(slot + 1) * rank] = part[:rows]
        rank_keep_ref[:, slot * rank:(slot + 1) * rank] = part[rows:]

    @pl.loop(0, width // block_n)
    def _(place):
        columns = pl.ds(pl.multiple_of(place * block_n, block_n), block_n)
        x = x_ref[...].reshape(2 * rows, depth)
        term = jnp.dot(x, w_ref[:, columns], preferred_element_type=jnp.float32)
        send_ref[:, columns] = term[:rows].astype(send_ref.dtype)
        keep_ref[:, columns] = term[rows:]


def load_body(weight_ref, out_ref, sem):
    copy = pltpu.make_async_copy(weight_ref, out_ref, sem)
    copy.start()
    copy.wait()


def load_weight(weight):
    return pl.pallas_call(
        load_body,
        in_specs=[pl.BlockSpec(memory_space=pl.ANY)],
        out_specs=pl.BlockSpec(memory_space=pltpu.VMEM),
        out_shape=pltpu.VMEM(weight.shape, weight.dtype),
        scratch_shapes=[pltpu.SemaphoreType.DMA],
        compiler_params=pltpu.CompilerParams(vmem_limit_bytes=1024 * 1024),
        name="load_weight",
    )(weight)


def partial_products(pos, own, sib, first, steps, weight, down_a):
    _, per_block, depth = own.shape
    width = weight.shape[1]
    slots, _, rank = down_a.shape
    rows = steps * per_block
    any_spec = pl.BlockSpec(memory_space=pl.ANY)
    vmem_spec = pl.BlockSpec(memory_space=pltpu.VMEM)
    return pl.pallas_call(
        functools.partial(matmul_body, first, steps),
        in_specs=[pl.BlockSpec(memory_space=pltpu.SMEM), any_spec, any_spec, vmem_spec, vmem_spec],
        out_specs=[vmem_spec] * 4,
        out_shape=[
            jax.ShapeDtypeStruct((rows, width), jnp.bfloat16),
            jax.ShapeDtypeStruct((rows, width), jnp.float32),
            jax.ShapeDtypeStruct((rows, slots * rank), jnp.float32),
            jax.ShapeDtypeStruct((rows, slots * rank), jnp.float32),
        ],
        scratch_shapes=[
            pltpu.VMEM((2, steps, per_block, depth), jnp.bfloat16),
            pltpu.SemaphoreType.DMA((2,)),
        ],
        compiler_params=pltpu.CompilerParams(vmem_limit_bytes=VMEM_BYTES),
        cost_estimate=pl.CostEstimate(flops=0, bytes_accessed=0, transcendentals=0),
        name="partial_products",
    )(pos, own, sib, weight, down_a)


def per_device(hidden, base_weight, down_a, up_b, adapter_ids, owner_map):
    step_count, per_block, _ = hidden.shape
    n_tensor = lax.axis_size("tp")
    n_rep = lax.axis_size("rep")
    n_sub = lax.axis_size("sub")
    n_owners = n_rep * n_sub
    tensor_index = lax.axis_index("tp")
    rep_index = lax.axis_index("rep")
    sub_index = lax.axis_index("sub")
    owner_index = lax.axis_index(("rep", "sub"))
    requests = per_block * n_owners
    rows_mine = requests // n_tensor
    group = n_tensor // n_rep
    group_index = tensor_index // group
    owned_slots, _, rank_size = down_a.shape
    slot_count = owned_slots * n_owners
    width = base_weight.shape[1]

    def swap_cores(value):
        return lax.ppermute(value, "sub", [(i, i ^ 1) for i in range(n_sub)])

    def from_rep(value, shift):
        return lax.ppermute(value, "rep", [((i + shift) % n_rep, i) for i in range(n_rep)])

    def swap_tensor(value, bit):
        return lax.ppermute(value, "tp", [(i, i ^ bit) for i in range(n_tensor)])

    def to_group(value, shift, hop):
        pairs = []
        for rep in range(n_rep):
            target = (rep + shift) % n_rep
            source = (target + hop) % n_rep
            for low in range(group):
                pairs.append(((source * group + low) * n_rep + rep, (target * group + low) * n_rep + rep))
        return lax.ppermute(value, ("tp", "rep"), pairs)

    keeps = (tensor_index // (group // 2)) % 2
    pos = (sub_index == keeps).astype(jnp.int32).reshape(1)

    def after(value, *done):
        return lax.optimization_barrier((value, *done))[0]

    half = step_count // 2
    siblings = swap_cores(hidden)

    remote = {}
    for shift in range(1, n_rep):
        for step in range(step_count):
            piece = hidden[step:step + 1]
            if step >= 2:
                piece = after(piece, remote[step - 2, shift])
            remote[step, shift] = from_rep(piece, shift)

    panels, bit = up_b, 1
    while bit < n_tensor:
        panels = jnp.concatenate([panels, swap_tensor(panels, bit)], axis=0)
        bit *= 2
    panels = panels.reshape(slot_count * rank_size, width)
    panel_slots = (
        (tensor_index ^ lax.broadcasted_iota(jnp.int32, (n_tensor, up_b.shape[0]), 0)) * up_b.shape[0]
        + lax.broadcasted_iota(jnp.int32, (n_tensor, up_b.shape[0]), 1)
    ).reshape(slot_count)

    my_ids = lax.dynamic_slice_in_dim(adapter_ids, tensor_index * rows_mine, rows_mine)
    iota = lax.broadcasted_iota(jnp.int32, (rows_mine, slot_count), 1)
    my_slot = jnp.sum((my_ids == iota).astype(jnp.int32) * owner_map[None, :], axis=1)
    panel_hot = my_slot[:, None] == panel_slots[None, :]
    owned_hot = my_slot[:, None] == (
        owner_index * owned_slots + lax.broadcasted_iota(jnp.int32, (rows_mine, owned_slots), 1)
    )

    weight = pltpu.with_memory_space_constraint(load_weight(base_weight), pltpu.VMEM)
    factor = pltpu.with_memory_space_constraint(down_a, pltpu.VMEM)

    def multiply(own, sib, first, steps):
        return partial_products(pos, own, sib, first, steps, weight, factor)

    def halve(send, keep, steps, kind):
        columns = keep.shape[1]
        total = keep + swap_tensor(send, group // 2).astype(jnp.float32)
        extent, bit = per_block, group // 4
        while bit:
            extent //= 2
            halves = total.reshape(steps, 2, extent, columns)
            mine = (tensor_index // bit) % 2
            kept = lax.dynamic_index_in_dim(halves, mine, 1, keepdims=False)
            sent = lax.dynamic_index_in_dim(halves, 1 - mine, 1, keepdims=False)
            total = kept + swap_tensor(sent.astype(kind), bit).astype(jnp.float32)
            bit //= 2
        total = total.reshape(steps, rows_mine, columns)
        return total, total.astype(kind)

    def collect(total, rounded, shift):
        for hop in range(1, n_rep):
            total = total + to_group(rounded, shift, hop).astype(jnp.float32)
        return total

    def choose(local, others):
        value = local
        for shift, other in others:
            value = jnp.where(group_index == (rep_index + shift) % n_rep, other, value)
        return value

    def exchange(ranks):
        steps = ranks.shape[0]
        finished = ranks.astype(jnp.bfloat16).reshape(steps, rows_mine, owned_slots, rank_size)
        masked = jnp.sum(
            jnp.where(owned_hot[None, :, :, None], finished, 0), axis=2, dtype=jnp.float32
        ).astype(jnp.bfloat16)
        chosen = masked
        for turn in range(1, n_owners):
            chosen = chosen + lax.ppermute(
                masked, ("rep", "sub"), [(i, (i + turn) % n_owners) for i in range(n_owners)]
            )
        spread = jnp.where(panel_hot[None, :, :, None], chosen[:, :, None, :], 0)
        return spread.reshape(steps, rows_mine, slot_count * rank_size)

    def finish(sums, spread):
        lifted = jnp.dot(spread, panels, preferred_element_type=jnp.float32).astype(jnp.bfloat16)
        return (sums + ADAPTER_SCALE * lifted.astype(jnp.float32)).astype(jnp.bfloat16)

    local_parts, local_halved, local_sums = {}, {}, {}
    remote_parts, remote_halved, remote_sums = {}, {}, {}

    def local_rows(index, *done):
        first = index * half
        send, keep, rank_send, rank_keep = multiply(
            hidden, after(siblings, *done), first, half
        )
        local_parts[index] = (rank_send, rank_keep)
        local_halved[index] = halve(send, keep, half, jnp.bfloat16)
        local_sums[index] = collect(*local_halved[index], 0)
        return rank_keep

    def remote_rows(index, *done):
        for shift in range(1, n_rep):
            own = remote[index, shift]
            sib = after(swap_cores(own), *done)
            send, keep, rank_send, rank_keep = multiply(own, sib, 0, 1)
            remote_parts[index, shift] = (rank_send, rank_keep)
            remote_halved[index, shift] = halve(send, keep, 1, jnp.bfloat16)
            remote_sums[index, shift] = collect(*remote_halved[index, shift], shift)
            done = (rank_keep,)
        return done[0]

    def arrived(index):
        return tuple(remote[index, shift] for shift in range(1, n_rep))

    def halved(index):
        return tuple(remote_halved[index, shift][1] for shift in range(1, n_rep))

    token = local_rows(0, *arrived(0))
    token = remote_rows(0, token)
    token = local_rows(1, token, local_halved[0][1], *arrived(1))
    token = remote_rows(1, token, *halved(0))
    token = remote_rows(2, token, local_halved[1][1], *halved(1))
    token = remote_rows(3, token, *halved(2))

    local_ranks = collect(*halve(
        jnp.concatenate([local_parts[0][0], local_parts[1][0]]),
        jnp.concatenate([local_parts[0][1], local_parts[1][1]]),
        step_count, jnp.float32), 0)
    outputs = []
    for begin, end in ((0, step_count - 1), (step_count - 1, step_count)):
        others = []
        for shift in range(1, n_rep):
            parts = [remote_parts[step, shift] for step in range(begin, end)]
            rank = collect(*halve(
                jnp.concatenate([part[0] for part in parts]),
                jnp.concatenate([part[1] for part in parts]),
                end - begin, jnp.float32), shift)
            others.append((shift, rank))
        spread = exchange(choose(local_ranks[begin:end], others))
        for step in range(begin, end):
            sums = choose(
                local_sums[step // half][step % half],
                [(shift, remote_sums[step, shift][0]) for shift in range(1, n_rep)],
            )
            outputs.append(finish(sums, spread[step - begin]))
    return jnp.stack(outputs, axis=0)


def solution(mesh):
    return jax.shard_map(
        per_device,
        mesh=mesh,
        in_specs=(
            P(None, ("groups", "rep", "sub"), "tp"),
            P("tp", ("rep", "sub")),
            P(("rep", "sub"), "tp", None),
            P("tp", None, ("rep", "sub")),
            P("groups", None),
            P(),
        ),
        out_specs=P(None, ("groups", "tp"), ("rep", "sub")),
        check_vma=False,
    )
```

```python
import functools

import jax
import jax.numpy as jnp
from jax import lax
from jax.experimental import pallas as pl
from jax.experimental.pallas import tpu as pltpu
from jax.sharding import PartitionSpec as P

ADAPTER_SCALE = 0.5
BLOCK_N = 256
WEIGHT_PARTS = 7
VMEM_BYTES = 6 * 1024 * 1024


def load_body(weight_ref, *refs):
    parts, sems = refs[:-1], refs[-1]
    size = parts[0].shape[0]
    copies = [
        pltpu.make_async_copy(weight_ref.at[pl.ds(index * size, size)], part, sems.at[index])
        for index, part in enumerate(parts)
    ]
    for copy in copies:
        copy.start()
    for copy in copies:
        copy.wait()


def load_weight(weight):
    depth, width = weight.shape
    parts = WEIGHT_PARTS if depth % (128 * WEIGHT_PARTS) == 0 else 1
    loaded = pl.pallas_call(
        load_body,
        in_specs=[pl.BlockSpec(memory_space=pl.ANY)],
        out_specs=[pl.BlockSpec(memory_space=pltpu.VMEM)] * parts,
        out_shape=[pltpu.VMEM((depth // parts, width), weight.dtype)] * parts,
        scratch_shapes=[pltpu.SemaphoreType.DMA((parts,))],
        compiler_params=pltpu.CompilerParams(vmem_limit_bytes=1024 * 1024),
        name="load_weight",
    )(weight)
    return [pltpu.with_memory_space_constraint(part, pltpu.VMEM) for part in loaded]


def matmul_body(first, parts, pos_ref, own_ref, sib_ref, a_ref, *refs):
    w_refs = refs[:parts]
    send_ref, keep_ref, rank_send_ref, rank_keep_ref, x_ref, x_sems = refs[parts:]
    rows, width = send_ref.shape
    size = w_refs[0].shape[0]
    depth = parts * size
    _, steps, per_block, _ = x_ref.shape
    slots, _, rank = a_ref.shape
    block_n = min(BLOCK_N, width)

    own_at = pos_ref[0]
    own_copy = pltpu.make_async_copy(own_ref.at[pl.ds(first, steps)], x_ref.at[own_at], x_sems.at[0])
    sib_copy = pltpu.make_async_copy(sib_ref.at[pl.ds(first, steps)], x_ref.at[1 - own_at], x_sems.at[1])
    own_copy.start()
    sib_copy.start()
    own_copy.wait()
    sib_copy.wait()
    for slot in range(slots):
        x = x_ref[...].reshape(2 * rows, depth)
        part = jnp.dot(x, a_ref[slot], preferred_element_type=jnp.float32)
        rank_send_ref[:, slot * rank:(slot + 1) * rank] = part[:rows]
        rank_keep_ref[:, slot * rank:(slot + 1) * rank] = part[rows:]

    @pl.loop(0, width // block_n)
    def _(place):
        columns = pl.ds(pl.multiple_of(place * block_n, block_n), block_n)
        term = None
        for index in range(parts):
            x = x_ref[:, :, :, index * size:(index + 1) * size].reshape(2 * rows, size)
            value = jnp.dot(x, w_refs[index][:, columns], preferred_element_type=jnp.float32)
            term = value if term is None else term + value
        send_ref[:, columns] = term[:rows].astype(send_ref.dtype)
        keep_ref[:, columns] = term[rows:]


def partial_products(pos, own, sib, first, steps, weight, down_a):
    _, per_block, depth = own.shape
    width = weight[0].shape[1]
    slots, _, rank = down_a.shape
    rows = steps * per_block
    any_spec = pl.BlockSpec(memory_space=pl.ANY)
    vmem_spec = pl.BlockSpec(memory_space=pltpu.VMEM)
    return pl.pallas_call(
        functools.partial(matmul_body, first, len(weight)),
        in_specs=[pl.BlockSpec(memory_space=pltpu.SMEM), any_spec, any_spec, vmem_spec] + [vmem_spec] * len(weight),
        out_specs=[vmem_spec] * 4,
        out_shape=[
            jax.ShapeDtypeStruct((rows, width), jnp.bfloat16),
            jax.ShapeDtypeStruct((rows, width), jnp.float32),
            jax.ShapeDtypeStruct((rows, slots * rank), jnp.float32),
            jax.ShapeDtypeStruct((rows, slots * rank), jnp.float32),
        ],
        scratch_shapes=[
            pltpu.VMEM((2, steps, per_block, depth), jnp.bfloat16),
            pltpu.SemaphoreType.DMA((2,)),
        ],
        compiler_params=pltpu.CompilerParams(vmem_limit_bytes=VMEM_BYTES),
        cost_estimate=pl.CostEstimate(flops=0, bytes_accessed=0, transcendentals=0),
        name="partial_products",
    )(pos, own, sib, down_a, *weight)


def per_device(hidden, base_weight, down_a, up_b, adapter_ids, owner_map):
    step_count, per_block, depth = hidden.shape
    n_tensor = lax.axis_size("tp")
    n_rep = lax.axis_size("rep")
    n_sub = lax.axis_size("sub")
    n_owners = n_rep * n_sub
    tensor_index = lax.axis_index("tp")
    rep_index = lax.axis_index("rep")
    sub_index = lax.axis_index("sub")
    owner_index = lax.axis_index(("rep", "sub"))
    requests = per_block * n_owners
    rows_mine = requests // n_tensor
    targets = per_block // rows_mine
    group = n_tensor // n_rep
    group_index = tensor_index // group
    owned_slots, _, rank_size = down_a.shape
    slot_count = owned_slots * n_owners
    width = base_weight.shape[1]

    def after(value, *done):
        return lax.optimization_barrier((value, *done))[0]

    def swap_cores(value):
        return lax.ppermute(value, "sub", [(i, i ^ 1) for i in range(n_sub)])

    def from_rep(value, shift):
        return lax.ppermute(value, "rep", [((i + shift) % n_rep, i) for i in range(n_rep)])

    def swap_tensor(value, bit):
        return lax.ppermute(value, "tp", [(i, i ^ bit) for i in range(n_tensor)])

    def to_group(value, shift, hop):
        pairs = []
        for rep in range(n_rep):
            target = (rep + shift) % n_rep
            source = (target + hop) % n_rep
            for low in range(group):
                pairs.append(((source * group + low) * n_rep + rep, (target * group + low) * n_rep + rep))
        return lax.ppermute(value, ("tp", "rep"), pairs)

    def halve(send, keep, steps, kind):
        rows, columns = keep.shape
        total = keep + swap_tensor(send, group // 2).astype(jnp.float32)
        extent, bit = rows // steps, group // 4
        while bit:
            extent //= 2
            halves = total.reshape(steps, 2, extent, columns)
            mine = (tensor_index // bit) % 2
            kept = lax.dynamic_index_in_dim(halves, mine, 1, keepdims=False)
            sent = lax.dynamic_index_in_dim(halves, 1 - mine, 1, keepdims=False)
            total = kept + swap_tensor(sent.astype(kind), bit).astype(jnp.float32)
            bit //= 2
        total = total.reshape(steps, extent, columns)
        return total, total.astype(kind)

    def collect(total, rounded, shift, *done):
        if done:
            total = after(total, *done)
        for hop in range(1, n_rep):
            total = total + to_group(rounded, shift, hop).astype(jnp.float32)
        return total

    def choose(local, others):
        value = local
        for shift, other in others:
            value = jnp.where(group_index == (rep_index + shift) % n_rep, other, value)
        return value

    keeps = (tensor_index // (group // 2)) % 2
    pos = (sub_index == keeps).astype(jnp.int32).reshape(1)

    pieces = [(step, 0, 2) for step in range(step_count - 1)] + [(step_count - 1, 0, 1), (step_count - 1, 1, 1)]
    share = rows_mine // 2
    remote = {}
    for index, (step, begin, parts) in enumerate(pieces):
        piece = hidden[step].reshape(targets, rows_mine, depth)[:, begin * share:(begin + parts) * share]
        piece = piece.reshape(1, targets * parts * share, depth)
        for shift in range(1, n_rep):
            remote[index, shift] = from_rep(piece, shift)

    siblings = swap_cores(hidden)
    half = step_count // 2

    panels, bit = up_b, 1
    while bit < n_tensor:
        panels = jnp.concatenate([panels, swap_tensor(panels, bit)], axis=0)
        bit *= 2
    panels = panels.reshape(slot_count * rank_size, width)
    panel_slots = (
        (tensor_index ^ lax.broadcasted_iota(jnp.int32, (n_tensor, up_b.shape[0]), 0)) * up_b.shape[0]
        + lax.broadcasted_iota(jnp.int32, (n_tensor, up_b.shape[0]), 1)
    ).reshape(slot_count)

    my_ids = lax.dynamic_slice_in_dim(adapter_ids, tensor_index * rows_mine, rows_mine)
    iota = lax.broadcasted_iota(jnp.int32, (rows_mine, slot_count), 1)
    my_slot = jnp.sum((my_ids == iota).astype(jnp.int32) * owner_map[None, :], axis=1)
    panel_hot = my_slot[:, None] == panel_slots[None, :]
    owned_hot = my_slot[:, None] == (
        owner_index * owned_slots + lax.broadcasted_iota(jnp.int32, (rows_mine, owned_slots), 1)
    )

    weight = load_weight(base_weight)
    factor = pltpu.with_memory_space_constraint(down_a, pltpu.VMEM)
    local_parts, local_halved, local_sums = {}, {}, {}
    remote_parts, remote_halved, remote_sums = {}, {}, {}

    def local_rows(index, *done):
        send, keep, rank_send, rank_keep = partial_products(
            pos, hidden, after(siblings, *done), index * half, half, weight, factor
        )
        local_parts[index] = (rank_send, rank_keep)
        local_halved[index] = halve(send, keep, half, jnp.bfloat16)
        return rank_keep

    def remote_rows(index, *done):
        for shift in range(1, n_rep):
            own = after(remote[index, shift], *done)
            sib = swap_cores(own)
            send, keep, rank_send, rank_keep = partial_products(pos, own, sib, 0, 1, weight, factor)
            remote_parts[index, shift] = (rank_send, rank_keep)
            remote_halved[index, shift] = halve(send, keep, 1, jnp.bfloat16)
            done = (rank_keep,)
        return done[0]

    def arrived(index):
        return tuple(remote[index, shift] for shift in range(1, n_rep))

    def halved(index):
        return tuple(remote_halved[index, shift][1] for shift in range(1, n_rep))

    def local_collect(index, *done):
        local_sums[index] = collect(*local_halved[index], 0, *done)

    def remote_collect(index, *done):
        for shift in range(1, n_rep):
            remote_sums[index, shift] = collect(*remote_halved[index, shift], shift, *done)

    def summed(index):
        return tuple(remote_sums[index, shift] for shift in range(1, n_rep))

    token = local_rows(0)
    token = local_rows(1, token)
    token = remote_rows(0, token, local_halved[0][1])
    token = remote_rows(1, token, local_halved[1][1])
    local_collect(0, token)
    token = remote_rows(2, token, *halved(0))
    local_collect(1, token)
    remote_collect(0, token)
    token = remote_rows(3, token, *halved(1), local_sums[0])
    remote_collect(1, token)
    token = remote_rows(4, token, *halved(2), local_sums[1], *summed(0))
    remote_collect(2, token)
    remote_collect(3, token)
    remote_collect(4, token)

    def joined(parts, at):
        last = [part[at].reshape(targets, -1, owned_slots * rank_size) for part in parts[-2:]]
        last = jnp.concatenate(last, axis=1).reshape(per_block, owned_slots * rank_size)
        return jnp.concatenate([part[at] for part in parts[:-2]] + [last])

    local_ranks = collect(*halve(
        jnp.concatenate([local_parts[0][0], local_parts[1][0]]),
        jnp.concatenate([local_parts[0][1], local_parts[1][1]]),
        step_count, jnp.float32), 0)
    others = []
    for shift in range(1, n_rep):
        parts = [remote_parts[index, shift] for index in range(len(pieces))]
        others.append((shift, collect(
            *halve(joined(parts, 0), joined(parts, 1), step_count, jnp.float32), shift)))
    finished = choose(local_ranks, others).astype(jnp.bfloat16)
    finished = finished.reshape(step_count, rows_mine, owned_slots, rank_size)
    masked = jnp.sum(
        jnp.where(owned_hot[None, :, :, None], finished, 0), axis=2, dtype=jnp.float32
    ).astype(jnp.bfloat16)
    chosen = masked
    for turn in range(1, n_owners):
        chosen = chosen + lax.ppermute(
            masked, ("rep", "sub"), [(i, (i + turn) % n_owners) for i in range(n_owners)]
        )
    spread = jnp.where(panel_hot[None, :, :, None], chosen[:, :, None, :], 0)
    spread = spread.reshape(step_count, rows_mine, slot_count * rank_size)

    outputs = []
    for index, (step, begin, parts) in enumerate(pieces):
        span = slice(begin * share, (begin + parts) * share)
        sums = choose(
            local_sums[step // half][step % half, span],
            [(shift, remote_sums[index, shift][0]) for shift in range(1, n_rep)],
        )
        lifted = jnp.dot(spread[step, span], panels, preferred_element_type=jnp.float32)
        lifted = lifted.astype(jnp.bfloat16).astype(jnp.float32)
        outputs.append((sums + ADAPTER_SCALE * lifted).astype(jnp.bfloat16))
    return jnp.concatenate(outputs).reshape(step_count, rows_mine, width)


def solution(mesh):
    return jax.shard_map(
        per_device,
        mesh=mesh,
        in_specs=(
            P(None, ("groups", "rep", "sub"), "tp"),
            P("tp", ("rep", "sub")),
            P(("rep", "sub"), "tp", None),
            P("tp", None, ("rep", "sub")),
            P("groups", None),
            P(),
        ),
        out_specs=P(None, ("groups", "tp"), ("rep", "sub")),
        check_vma=False,
    )
```

```python
import functools

import jax
import jax.numpy as jnp
from jax import lax
from jax.experimental import pallas as pl
from jax.experimental.pallas import tpu as pltpu
from jax.sharding import PartitionSpec as P

ADAPTER_SCALE = 0.5
BLOCK_N = 256
BLOCK_VALUES = 1024 * 1024
BUFFERS = 4
VMEM_BYTES = 24 * 1024 * 1024


def block_depth(depth, width):
    for size in (1024, 512, 256):
        if depth % size == 0 and size * width <= BLOCK_VALUES:
            return size
    return depth


def matmul_body(first, left, pos_ref, own_ref, sib_ref, w_ref, a_ref, send_ref, keep_ref, *refs):
    rank_refs = refs[:-5]
    x_ref, w_buf, total_ref, x_sems, w_sems = refs[-5:]
    rows, width = send_ref.shape
    depth = w_ref.shape[0]
    _, steps, per_block, _ = x_ref.shape
    slots, _, rank = a_ref.shape
    buffers, block_k, _ = w_buf.shape
    block_n = min(BLOCK_N, width)
    count = depth // block_k

    def fetch(block, slot):
        return pltpu.make_async_copy(
            w_ref.at[pl.ds(block * block_k, block_k), pl.ds(left, width)], w_buf.at[slot], w_sems.at[slot]
        )

    own_at = pos_ref[0]
    own_copy = pltpu.make_async_copy(own_ref.at[pl.ds(first, steps)], x_ref.at[own_at], x_sems.at[0])
    sib_copy = pltpu.make_async_copy(sib_ref.at[pl.ds(first, steps)], x_ref.at[1 - own_at], x_sems.at[1])
    own_copy.start()
    sib_copy.start()
    for block in range(buffers):
        fetch(block, block).start()
    keep_ref[...] = jnp.zeros_like(keep_ref)
    total_ref[...] = jnp.zeros_like(total_ref)
    own_copy.wait()
    sib_copy.wait()
    if rank_refs:
        for slot in range(slots):
            x = x_ref[...].reshape(2 * rows, depth)
            part = jnp.dot(x, a_ref[slot], preferred_element_type=jnp.float32)
            rank_refs[0][:, slot * rank:(slot + 1) * rank] = part[:rows]
            rank_refs[1][:, slot * rank:(slot + 1) * rank] = part[rows:]

    @pl.loop(0, count)
    def _(block):
        slot = lax.rem(block, buffers)
        fetch(block, slot).wait()
        inner = pl.ds(pl.multiple_of(block * block_k, block_k), block_k)
        x = x_ref[:, :, :, inner].reshape(2 * rows, block_k)
        for place in range(width // block_n):
            columns = slice(place * block_n, (place + 1) * block_n)
            term = jnp.dot(x, w_buf[slot, :, columns], preferred_element_type=jnp.float32)
            total_ref[:, columns] += term[:rows]
            keep_ref[:, columns] += term[rows:]

        @pl.when(block + buffers < count)
        def _():
            fetch(block + buffers, slot).start()

    send_ref[...] = total_ref[...].astype(send_ref.dtype)


def partial_products(pos, own, sib, first, steps, weight, left, width, down_a, with_rank):
    _, per_block, depth = own.shape
    slots, _, rank = down_a.shape
    rows = steps * per_block
    block_k = block_depth(depth, width)
    buffers = min(BUFFERS, depth // block_k)
    any_spec = pl.BlockSpec(memory_space=pl.ANY)
    vmem_spec = pl.BlockSpec(memory_space=pltpu.VMEM)
    ranks = [jax.ShapeDtypeStruct((rows, slots * rank), jnp.float32)] * (2 if with_rank else 0)
    return pl.pallas_call(
        functools.partial(matmul_body, first, left),
        in_specs=[pl.BlockSpec(memory_space=pltpu.SMEM), any_spec, any_spec, any_spec, vmem_spec],
        out_specs=[vmem_spec] * (2 + len(ranks)),
        out_shape=[
            jax.ShapeDtypeStruct((rows, width), jnp.bfloat16),
            jax.ShapeDtypeStruct((rows, width), jnp.float32),
        ] + ranks,
        scratch_shapes=[
            pltpu.VMEM((2, steps, per_block, depth), jnp.bfloat16),
            pltpu.VMEM((buffers, block_k, width), jnp.bfloat16),
            pltpu.VMEM((rows, width), jnp.float32),
            pltpu.SemaphoreType.DMA((2,)),
            pltpu.SemaphoreType.DMA((buffers,)),
        ],
        compiler_params=pltpu.CompilerParams(vmem_limit_bytes=VMEM_BYTES),
        cost_estimate=pl.CostEstimate(flops=0, bytes_accessed=0, transcendentals=0),
        name="partial_products",
    )(pos, own, sib, weight, down_a)


def lift_body(chosen_ref, slot_ref, order_ref, panel_ref, out_ref):
    rank = chosen_ref.shape[1]
    chosen = chosen_ref[...]
    slot = slot_ref[...]
    spread = jnp.concatenate(
        [
            jnp.where(slot == order_ref[place], chosen, jnp.zeros_like(chosen))
            for place in range(panel_ref.shape[0] // rank)
        ],
        axis=1,
    )
    lifted = jnp.dot(spread, panel_ref[...], preferred_element_type=jnp.float32)
    out_ref[...] = lifted.astype(out_ref.dtype)


def lift(chosen, slots, order, panels):
    vmem_spec = pl.BlockSpec(memory_space=pltpu.VMEM)
    return pl.pallas_call(
        lift_body,
        in_specs=[vmem_spec, vmem_spec, pl.BlockSpec(memory_space=pltpu.SMEM), vmem_spec],
        out_specs=vmem_spec,
        out_shape=jax.ShapeDtypeStruct((chosen.shape[0], panels.shape[1]), jnp.bfloat16),
        compiler_params=pltpu.CompilerParams(vmem_limit_bytes=VMEM_BYTES),
        cost_estimate=pl.CostEstimate(flops=0, bytes_accessed=0, transcendentals=0),
        name="lift",
    )(chosen, slots, order, panels)


def per_device(hidden, base_weight, down_a, up_b, adapter_ids, owner_map):
    step_count, per_block, _ = hidden.shape
    n_tensor = lax.axis_size("tp")
    n_rep = lax.axis_size("rep")
    n_sub = lax.axis_size("sub")
    n_owners = n_rep * n_sub
    tensor_index = lax.axis_index("tp")
    rep_index = lax.axis_index("rep")
    sub_index = lax.axis_index("sub")
    owner_index = lax.axis_index(("rep", "sub"))
    requests = per_block * n_owners
    rows_mine = requests // n_tensor
    group = n_tensor // n_rep
    group_index = tensor_index // group
    owned_slots, _, rank_size = down_a.shape
    slot_count = owned_slots * n_owners
    width = base_weight.shape[1]

    def after(value, *done):
        return lax.optimization_barrier((value, *done))[0]

    def swap_cores(value):
        return lax.ppermute(value, "sub", [(i, i ^ 1) for i in range(n_sub)])

    def from_rep(value, shift):
        return lax.ppermute(value, "rep", [((i + shift) % n_rep, i) for i in range(n_rep)])

    def swap_tensor(value, bit):
        return lax.ppermute(value, "tp", [(i, i ^ bit) for i in range(n_tensor)])

    def to_group(value, shift, hop):
        pairs = []
        for rep in range(n_rep):
            target = (rep + shift) % n_rep
            source = (target + hop) % n_rep
            for low in range(group):
                pairs.append(((source * group + low) * n_rep + rep, (target * group + low) * n_rep + rep))
        return lax.ppermute(value, ("tp", "rep"), pairs)

    def halve(send, keep, steps, kind, *done):
        rows, columns = keep.shape
        total = (after(keep, *done) if done else keep) + swap_tensor(send, group // 2).astype(jnp.float32)
        extent, bit = rows // steps, group // 4
        while bit:
            extent //= 2
            halves = total.reshape(steps, 2, extent, columns)
            mine = (tensor_index // bit) % 2
            kept = lax.dynamic_index_in_dim(halves, mine, 1, keepdims=False)
            sent = lax.dynamic_index_in_dim(halves, 1 - mine, 1, keepdims=False)
            total = kept + swap_tensor(sent.astype(kind), bit).astype(jnp.float32)
            bit //= 2
        total = total.reshape(steps, extent, columns)
        return total, total.astype(kind)

    def collect(total, rounded, shift, *done):
        if done:
            total = after(total, *done)
        for hop in range(1, n_rep):
            total = total + to_group(rounded, shift, hop).astype(jnp.float32)
        return total

    def choose(local, others):
        value = local
        for shift, other in others:
            value = jnp.where(group_index == (rep_index + shift) % n_rep, other, value)
        return value

    keeps = (tensor_index // (group // 2)) % 2
    pos = (sub_index == keeps).astype(jnp.int32).reshape(1)

    remote = {}
    for step in range(step_count):
        for shift in range(1, n_rep):
            remote[step, shift] = from_rep(hidden[step:step + 1], shift)

    siblings = swap_cores(hidden)
    half = step_count // 2

    panels, bit = up_b, 1
    while bit < n_tensor:
        panels = jnp.concatenate([panels, swap_tensor(panels, bit)], axis=0)
        bit *= 2
    panels = panels.reshape(slot_count * rank_size, width)
    panel_slots = (
        (tensor_index ^ lax.broadcasted_iota(jnp.int32, (n_tensor, up_b.shape[0]), 0)) * up_b.shape[0]
        + lax.broadcasted_iota(jnp.int32, (n_tensor, up_b.shape[0]), 1)
    ).reshape(slot_count)

    my_ids = lax.dynamic_slice_in_dim(adapter_ids, tensor_index * rows_mine, rows_mine)
    iota = lax.broadcasted_iota(jnp.int32, (rows_mine, slot_count), 1)
    my_slot = jnp.sum((my_ids == iota).astype(jnp.int32) * owner_map[None, :], axis=1)
    owned_hot = my_slot[:, None] == (
        owner_index * owned_slots + lax.broadcasted_iota(jnp.int32, (rows_mine, owned_slots), 1)
    )

    local_halved, local_sums, local_ranks = {}, {}, {}
    remote_halved, remote_sums, remote_ranks = {}, {}, {}
    cuts = {step: [(0, width)] for step in range(step_count)}
    cuts[step_count - 1] = [(0, width // 2), (width // 2, width // 2)]

    def local_rows(index, *done):
        send, keep, *local_ranks[index] = partial_products(
            pos, hidden, after(siblings, *done), index * half, half, base_weight, 0, width, down_a, True
        )
        local_halved[index] = halve(send, keep, half, jnp.bfloat16)
        return local_ranks[index][1]

    def local_collect(index, *done):
        local_sums[index] = collect(*local_halved[index], 0, *done)

    def remote_rows(step, before, done):
        for shift in range(1, n_rep):
            own = after(remote[step, shift], *before)
            sib = after(swap_cores(own), *done)
            products = []
            for cut, (left, size) in enumerate(cuts[step]):
                send, keep, *ranks = partial_products(
                    pos, own, sib, 0, 1, base_weight, left, size, down_a, cut == 0
                )
                products.append((send, keep))
                if cut == 0:
                    remote_ranks[step, shift] = ranks
                    token = ranks[1]
                    before = (token,)
                    if len(cuts[step]) > 1:
                        remote_collect(step - 2, 0, token)
                        sib = after(sib, token, *summed(step - 2))
            held = ()
            if len(products) > 1:
                remote_collect(step - 1, 0, products[1][0])
                held = summed(step - 1)
            for cut, (send, keep) in enumerate(products):
                if cut > 0:
                    send = after(send, *held)
                remote_halved[step, cut, shift] = halve(send, keep, 1, jnp.bfloat16)
                held = (*held, remote_halved[step, cut, shift][1])
        return token, tuple(send for send, _ in products)

    def remote_collect(step, cut, *done):
        for shift in range(1, n_rep):
            remote_sums[step, cut, shift] = collect(*remote_halved[step, cut, shift], shift, *done)

    def halved(step, cut=0):
        return tuple(remote_halved[step, cut, shift][1] for shift in range(1, n_rep))

    def summed(step, cut=0):
        return tuple(remote_sums[step, cut, shift] for shift in range(1, n_rep))

    def rank_sums(ranks, shift):
        return collect(*halve(
            jnp.concatenate([rank[0] for rank in ranks]),
            jnp.concatenate([rank[1] for rank in ranks]),
            step_count, jnp.float32), shift)

    token = local_rows(0)
    token = local_rows(1, token, *(remote[0, shift] for shift in range(1, n_rep)))
    token, _ = remote_rows(0, (token, local_halved[0][1]), ())
    token, _ = remote_rows(1, (token, local_halved[1][1]), (panels,))
    local_rank_sum = rank_sums([local_ranks[index] for index in (0, 1)], 0)
    local_collect(0, token)
    token, _ = remote_rows(2, (token,), (*halved(0), local_sums[0], local_rank_sum))
    local_collect(1, token)
    remote_collect(0, 0, token)
    token, raw = remote_rows(3, (token, *halved(1)), (*halved(2), local_sums[1], *summed(0)))
    remote_collect(3, 0)
    remote_collect(3, 1)
    last = (*halved(3, 0), *raw)

    finished = choose(
        local_rank_sum,
        [
            (shift, rank_sums([[after(rank, *last) for rank in remote_ranks[step, shift]] for step in range(step_count)], shift))
            for shift in range(1, n_rep)
        ],
    ).astype(jnp.bfloat16)
    finished = after(finished, *halved(3, 1), *summed(3, 0))
    finished = finished.reshape(step_count, rows_mine, owned_slots, rank_size)
    masked = jnp.sum(
        jnp.where(owned_hot[None, :, :, None], finished, 0), axis=2, dtype=jnp.float32
    ).astype(jnp.bfloat16)
    chosen = masked
    for turn in range(1, n_owners):
        chosen = chosen + lax.ppermute(
            masked, ("rep", "sub"), [(i, (i + turn) % n_owners) for i in range(n_owners)]
        )
    lifted = lift(
        chosen.reshape(step_count * rows_mine, rank_size),
        jnp.broadcast_to(my_slot, (step_count, rows_mine)).reshape(step_count * rows_mine, 1),
        panel_slots,
        panels,
    ).reshape(step_count, rows_mine, width)

    output = jnp.zeros((step_count, rows_mine, width), jnp.bfloat16)
    for step in range(step_count):
        for cut, (left, size) in enumerate(cuts[step]):
            columns = slice(left, left + size)
            sums = choose(
                local_sums[step // half][step % half, :, columns],
                [(shift, remote_sums[step, cut, shift][0]) for shift in range(1, n_rep)],
            )
            value = sums + ADAPTER_SCALE * lifted[step, :, columns].astype(jnp.float32)
            output = output.at[step, :, columns].set(value.astype(jnp.bfloat16))
    return output


def solution(mesh):
    return jax.shard_map(
        per_device,
        mesh=mesh,
        in_specs=(
            P(None, ("groups", "rep", "sub"), "tp"),
            P("tp", ("rep", "sub")),
            P(("rep", "sub"), "tp", None),
            P("tp", None, ("rep", "sub")),
            P("groups", None),
            P(),
        ),
        out_specs=P(None, ("groups", "tp"), ("rep", "sub")),
        check_vma=False,
    )
```

```python
import functools

import jax
import jax.numpy as jnp
from jax import lax
from jax.experimental import pallas as pl
from jax.experimental.pallas import tpu as pltpu
from jax.sharding import PartitionSpec as P

ADAPTER_SCALE = 0.5
BLOCK_N = 256
BLOCK_VALUES = 1024 * 1024
BUFFERS = 3
WIDE_ROWS = 128
VMEM_BYTES = 24 * 1024 * 1024


def block_depth(depth, width, rows):
    values = BLOCK_VALUES * (2 if rows >= WIDE_ROWS else 1)
    for size in (1024, 512, 256):
        if depth % size == 0 and size * width <= values:
            return size
    return depth


def matmul_body(spans, left, pos_ref, *refs):
    sources = refs[:2 * len(spans)]
    w_ref, a_ref, send_ref, keep_ref = refs[2 * len(spans):2 * len(spans) + 4]
    rank_refs = refs[2 * len(spans) + 4:-5]
    x_ref, w_buf, total_ref, x_sems, w_sems = refs[-5:]
    rows, width = send_ref.shape
    depth = w_ref.shape[0]
    slots, rank, _ = a_ref.shape
    buffers, block_k, _ = w_buf.shape
    block_n = min(BLOCK_N, width)
    count = depth // block_k

    def fetch(block, slot):
        return pltpu.make_async_copy(
            w_ref.at[pl.ds(block * block_k, block_k), pl.ds(left, width)], w_buf.at[slot], w_sems.at[slot]
        )

    own_at = pos_ref[0]
    copies, begin = [], 0
    for index, (first, steps) in enumerate(spans):
        for core, at in enumerate((own_at, 1 - own_at)):
            source = sources[2 * index + core]
            copies.append(pltpu.make_async_copy(
                source.at[pl.ds(first, steps)], x_ref.at[at, pl.ds(begin, steps)], x_sems.at[2 * index + core]
            ))
        begin += steps
    for copy in copies:
        copy.start()
    for block in range(buffers):
        fetch(block, block).start()
    keep_ref[...] = jnp.zeros_like(keep_ref)
    total_ref[...] = jnp.zeros_like(total_ref)
    for copy in copies:
        copy.wait()
    if rank_refs:
        for slot in range(slots):
            x = x_ref[...].reshape(2 * rows, depth)
            part = lax.dot_general(
                x, a_ref[slot], (((1,), (1,)), ((), ())), preferred_element_type=jnp.float32
            )
            rank_refs[0][:, slot * rank:(slot + 1) * rank] = part[:rows]
            rank_refs[1][:, slot * rank:(slot + 1) * rank] = part[rows:]

    @pl.loop(0, count)
    def _(block):
        slot = lax.rem(block, buffers)
        fetch(block, slot).wait()
        inner = pl.ds(pl.multiple_of(block * block_k, block_k), block_k)
        x = x_ref[:, :, :, inner].reshape(2 * rows, block_k)
        for place in range(width // block_n):
            columns = slice(place * block_n, (place + 1) * block_n)
            term = jnp.dot(x, w_buf[slot, :, columns], preferred_element_type=jnp.float32)
            total_ref[:, columns] += term[:rows]
            keep_ref[:, columns] += term[rows:]

        @pl.when(block + buffers < count)
        def _():
            fetch(block + buffers, slot).start()

    send_ref[...] = total_ref[...].astype(send_ref.dtype)


def partial_products(pos, chunks, weight, left, width, factors, with_rank):
    _, per_block, depth = chunks[0][0].shape
    slots, rank, _ = factors.shape
    spans = tuple((first, steps) for _, _, first, steps in chunks)
    steps = sum(length for _, length in spans)
    rows = steps * per_block
    block_k = block_depth(depth, width, rows)
    buffers = min(BUFFERS, depth // block_k)
    any_spec = pl.BlockSpec(memory_space=pl.ANY)
    vmem_spec = pl.BlockSpec(memory_space=pltpu.VMEM)
    ranks = [jax.ShapeDtypeStruct((rows, slots * rank), jnp.float32)] * (2 if with_rank else 0)
    return pl.pallas_call(
        functools.partial(matmul_body, spans, left),
        in_specs=[pl.BlockSpec(memory_space=pltpu.SMEM)] + [any_spec] * (2 * len(chunks) + 1) + [vmem_spec],
        out_specs=[vmem_spec] * (2 + len(ranks)),
        out_shape=[
            jax.ShapeDtypeStruct((rows, width), jnp.bfloat16),
            jax.ShapeDtypeStruct((rows, width), jnp.float32),
        ] + ranks,
        scratch_shapes=[
            pltpu.VMEM((2, steps, per_block, depth), jnp.bfloat16),
            pltpu.VMEM((buffers, block_k, width), jnp.bfloat16),
            pltpu.VMEM((rows, width), jnp.float32),
            pltpu.SemaphoreType.DMA((2 * len(chunks),)),
            pltpu.SemaphoreType.DMA((buffers,)),
        ],
        compiler_params=pltpu.CompilerParams(vmem_limit_bytes=VMEM_BYTES),
        cost_estimate=pl.CostEstimate(flops=0, bytes_accessed=0, transcendentals=0),
        name="partial_products",
    )(pos, *[source for own, sib, _, _ in chunks for source in (own, sib)], weight, factors)


def lift_body(chosen_ref, slot_ref, order_ref, panel_ref, out_ref):
    rank = chosen_ref.shape[1]
    chosen = chosen_ref[...]
    slot = slot_ref[...]
    spread = jnp.concatenate(
        [
            jnp.where(slot == order_ref[place], chosen, jnp.zeros_like(chosen))
            for place in range(panel_ref.shape[0] // rank)
        ],
        axis=1,
    )
    lifted = jnp.dot(spread, panel_ref[...], preferred_element_type=jnp.float32)
    out_ref[...] = lifted.astype(out_ref.dtype)


def lift(chosen, slots, order, panels):
    vmem_spec = pl.BlockSpec(memory_space=pltpu.VMEM)
    return pl.pallas_call(
        lift_body,
        in_specs=[vmem_spec, vmem_spec, pl.BlockSpec(memory_space=pltpu.SMEM), vmem_spec],
        out_specs=vmem_spec,
        out_shape=jax.ShapeDtypeStruct((chosen.shape[0], panels.shape[1]), jnp.bfloat16),
        compiler_params=pltpu.CompilerParams(vmem_limit_bytes=VMEM_BYTES),
        cost_estimate=pl.CostEstimate(flops=0, bytes_accessed=0, transcendentals=0),
        name="lift",
    )(chosen, slots, order, panels)


def per_device(hidden, base_weight, down_a, up_b, adapter_ids, owner_map):
    step_count, per_block, _ = hidden.shape
    n_tensor = lax.axis_size("tp")
    n_rep = lax.axis_size("rep")
    n_sub = lax.axis_size("sub")
    n_owners = n_rep * n_sub
    tensor_index = lax.axis_index("tp")
    rep_index = lax.axis_index("rep")
    sub_index = lax.axis_index("sub")
    owner_index = lax.axis_index(("rep", "sub"))
    requests = per_block * n_owners
    rows_mine = requests // n_tensor
    group = n_tensor // n_rep
    group_index = tensor_index // group
    owned_slots, _, rank_size = down_a.shape
    slot_count = owned_slots * n_owners
    width = base_weight.shape[1]

    def after(value, *done):
        return lax.optimization_barrier((value, *done))[0]

    def swap_cores(value):
        return lax.ppermute(value, "sub", [(i, i ^ 1) for i in range(n_sub)])

    def from_rep(value, shift):
        return lax.ppermute(value, "rep", [((i + shift) % n_rep, i) for i in range(n_rep)])

    def swap_tensor(value, bit):
        return lax.ppermute(value, "tp", [(i, i ^ bit) for i in range(n_tensor)])

    def to_group(value, shift, hop):
        pairs = []
        for rep in range(n_rep):
            target = (rep + shift) % n_rep
            source = (target + hop) % n_rep
            for low in range(group):
                pairs.append(((source * group + low) * n_rep + rep, (target * group + low) * n_rep + rep))
        return lax.ppermute(value, ("tp", "rep"), pairs)

    def choose(local, others):
        value = local
        for shift, other in others:
            value = jnp.where(group_index == (rep_index + shift) % n_rep, other, value)
        return value

    keeps = (tensor_index // (group // 2)) % 2
    pos = (sub_index == keeps).astype(jnp.int32).reshape(1)

    siblings = swap_cores(hidden)
    pieces = [(step, shift) for step in range(step_count) for shift in range(1, n_rep)]
    remote = {}
    for step, shift in pieces:
        source = hidden if step == 0 else after(hidden, siblings)
        remote[step, shift] = from_rep(source[step:step + 1], shift)

    panels, bit = up_b, 1
    while bit < n_tensor:
        panels = jnp.concatenate([panels, swap_tensor(panels, bit)], axis=0)
        bit *= 2
    panels = panels.reshape(slot_count * rank_size, width)
    panel_slots = (
        (tensor_index ^ lax.broadcasted_iota(jnp.int32, (n_tensor, up_b.shape[0]), 0)) * up_b.shape[0]
        + lax.broadcasted_iota(jnp.int32, (n_tensor, up_b.shape[0]), 1)
    ).reshape(slot_count)

    my_ids = lax.dynamic_slice_in_dim(adapter_ids, tensor_index * rows_mine, rows_mine)
    iota = lax.broadcasted_iota(jnp.int32, (rows_mine, slot_count), 1)
    my_slot = jnp.sum((my_ids == iota).astype(jnp.int32) * owner_map[None, :], axis=1)
    owned_hot = my_slot[:, None] == (
        owner_index * owned_slots + lax.broadcasted_iota(jnp.int32, (rows_mine, owned_slots), 1)
    )

    first_leg, second_leg, sums = [], [], {}

    def second_half(total, received, steps, kind):
        total = total + received.astype(jnp.float32)
        rows, columns = total.shape
        extent, bit = rows // steps, group // 4
        while bit:
            extent //= 2
            halves = total.reshape(steps, 2, extent, columns)
            mine = (tensor_index // bit) % 2
            kept = lax.dynamic_index_in_dim(halves, mine, 1, keepdims=False)
            sent = lax.dynamic_index_in_dim(halves, 1 - mine, 1, keepdims=False)
            total = kept + swap_tensor(sent.astype(kind), bit).astype(jnp.float32)
            bit //= 2
        return total.reshape(steps, extent, columns)

    def gap(token, jobs, *extra, short=False):
        nonlocal first_leg, second_leg
        halved = []
        for parts, received, keep, kind in first_leg:
            steps = sum(length for _, length, _ in parts)
            total, begin = second_half(after(keep, token), received, steps, kind), 0
            for key, length, shift in parts:
                part = total[begin:begin + length]
                halved.append((key, part, part.astype(kind), shift))
                begin += length
        waiting, ended = [], {}
        for key, received, total, lag in second_leg:
            if short or lag > 1:
                waiting.append((key, received, total, lag if short else lag - 1))
                continue
            total = after(total, token)
            for value in received:
                total = total + value.astype(jnp.float32)
            ended[key] = total
        sends = [job[1] for job in jobs]
        rounded = [value for _, _, value, _ in halved]
        sends, rounded, extra, totals = lax.optimization_barrier((sends, rounded, extra, list(ended.values())))
        sums.update(zip(ended, totals))
        first_leg = [
            (parts, swap_tensor(send, group // 2), keep, kind) for (parts, _, keep, kind), send in zip(jobs, sends)
        ]
        second_leg = waiting + [
            (key, [to_group(value, shift, hop) for hop in range(1, n_rep)], total, 2 if short else 1)
            for (key, total, _, shift), value in zip(halved, rounded)
        ]
        return extra

    factors = jnp.swapaxes(down_a, 1, 2)

    def multiply(chunks, left=0, columns=width, with_rank=True):
        return partial_products(pos, chunks, base_weight, left, columns, factors, with_rank)

    half = step_count // 2
    send, keep, *ranks = multiply([(hidden, siblings, 0, half)])
    rank_rows = {("local", 0): ranks}
    jobs = [([(("local", 0), half, 0)], send, keep, jnp.bfloat16)]
    token, next_local, rank_jobs = ranks[1], half, []
    for piece, (step, shift) in enumerate(pieces):
        own, siblings, panels = gap(token, jobs + rank_jobs, remote[step, shift], siblings, panels)
        rank_jobs = []
        sib = swap_cores(own)
        if piece == len(pieces) - 1:
            own, sib = gap(token, [], own, sib, short=True)
            cuts = [(0, width // 2), (width // 2, width // 2)]
            send, keep, *rank_rows[step, shift] = multiply([(own, sib, 0, 1)], *cuts[0])
            token = rank_rows[step, shift][1]
            jobs = [([((step, shift, 0), 1, shift)], send, keep, jnp.bfloat16)]
            for along in range(1, n_rep):
                both = [jnp.concatenate([rank_rows[at, along][side] for at in range(step_count)]) for side in (0, 1)]
                jobs.append(([(("ranks", along), step_count, along)], *both, jnp.float32))
            own, sib = gap(token, jobs, own, sib)
            send, keep = multiply([(own, sib, 0, 1)], *cuts[1], with_rank=False)
            token = send
            jobs = [([((step, shift, 1), 1, shift)], send, keep, jnp.bfloat16)]
            break
        chunks, parts = [(own, sib, 0, 1)], [((step, shift, 0), 1, shift)]
        if next_local < step_count:
            chunks.insert(0, (hidden, siblings, next_local, 1))
            parts.insert(0, (("local", next_local), 1, 0))
        send, keep, *ranks = multiply(chunks)
        token = ranks[1]
        rank_rows[step, shift] = [rank[-per_block:] for rank in ranks]
        if next_local < step_count:
            rank_rows["local", next_local] = [rank[:per_block] for rank in ranks]
            next_local += 1
            if next_local == step_count:
                whole = [rank_rows["local", at] for at in (0, *range(half, step_count))]
                both = [jnp.concatenate([rank[side] for rank in whole]) for side in (0, 1)]
                rank_jobs = [([("ranks", step_count, 0)], *both, jnp.float32)]
        jobs = [(parts, send, keep, jnp.bfloat16)]
    gap(token, jobs)
    gap(token, [])

    def local_sum(step):
        return sums["local", 0][step] if step < half else sums["local", step][0]

    finished = choose(
        sums["ranks"], [(shift, sums["ranks", shift]) for shift in range(1, n_rep)]
    ).astype(jnp.bfloat16)
    finished = finished.reshape(step_count, rows_mine, owned_slots, rank_size)
    masked = jnp.sum(
        jnp.where(owned_hot[None, :, :, None], finished, 0), axis=2, dtype=jnp.float32
    ).astype(jnp.bfloat16)
    chosen = masked
    for turn in range(1, n_owners):
        chosen = chosen + lax.ppermute(
            masked, ("rep", "sub"), [(i, (i + turn) % n_owners) for i in range(n_owners)]
        )
    lifted = lift(
        chosen.reshape(step_count * rows_mine, rank_size),
        jnp.broadcast_to(my_slot, (step_count, rows_mine)).reshape(step_count * rows_mine, 1),
        panel_slots,
        panels,
    ).reshape(step_count, rows_mine, width)

    gap(lifted, [])
    output = jnp.zeros((step_count, rows_mine, width), jnp.bfloat16)
    for step in range(step_count):
        for cut, (left, size) in enumerate([(0, width)] if step < step_count - 1 else cuts):
            columns = slice(left, left + size)
            others = []
            for along in range(1, n_rep):
                if (step, along, 1) in sums:
                    others.append((along, sums[step, along, cut][0]))
                else:
                    others.append((along, sums[step, along, 0][0, :, columns]))
            total = choose(local_sum(step)[:, columns], others)
            value = total + ADAPTER_SCALE * lifted[step, :, columns].astype(jnp.float32)
            output = output.at[step, :, columns].set(value.astype(jnp.bfloat16))
    return output


def solution(mesh):
    return jax.shard_map(
        per_device,
        mesh=mesh,
        in_specs=(
            P(None, ("groups", "rep", "sub"), "tp"),
            P("tp", ("rep", "sub")),
            P(("rep", "sub"), "tp", None),
            P("tp", None, ("rep", "sub")),
            P("groups", None),
            P(),
        ),
        out_specs=P(None, ("groups", "tp"), ("rep", "sub")),
        check_vma=False,
    )
```

```python
import functools

import jax
import jax.numpy as jnp
from jax import lax
from jax.experimental import pallas as pl
from jax.experimental.pallas import tpu as pltpu
from jax.sharding import PartitionSpec as P

ADAPTER_SCALE = 0.5
BLOCK_N = 256
BLOCK_VALUES = 1024 * 1024
BUFFERS = 3
WIDE_ROWS = 128
RANK_NAME = 1000
VMEM_BYTES = 24 * 1024 * 1024


def block_depth(depth, width, rows):
    values = BLOCK_VALUES * (2 if rows >= WIDE_ROWS else 1)
    for size in (1024, 512, 256):
        if depth % size == 0 and size * width <= values:
            return size
    return depth


def matmul_body(spans, pos_ref, *refs):
    sources = refs[:2 * len(spans)]
    w_ref, a_ref, send_ref, keep_ref = refs[2 * len(spans):2 * len(spans) + 4]
    rank_refs = refs[2 * len(spans) + 4:-5]
    x_ref, w_buf, total_ref, x_sems, w_sems = refs[-5:]
    rows = send_ref.shape[0]
    depth, width = w_ref.shape
    slots, rank, _ = a_ref.shape
    buffers, block_k, _ = w_buf.shape
    block_n = min(BLOCK_N, width)
    count = depth // block_k

    def fetch(block, slot):
        return pltpu.make_async_copy(
            w_ref.at[pl.ds(block * block_k, block_k)], w_buf.at[slot], w_sems.at[slot]
        )

    own_at = pos_ref[0]
    copies, begin = [], 0
    for index, (first, steps) in enumerate(spans):
        for core, at in enumerate((own_at, 1 - own_at)):
            source = sources[2 * index + core]
            copies.append(pltpu.make_async_copy(
                source.at[pl.ds(first, steps)], x_ref.at[at, pl.ds(begin, steps)], x_sems.at[2 * index + core]
            ))
        begin += steps
    for copy in copies:
        copy.start()
    for block in range(buffers):
        fetch(block, block).start()
    keep_ref[...] = jnp.zeros_like(keep_ref)
    total_ref[...] = jnp.zeros_like(total_ref)
    for rank_ref in rank_refs:
        rank_ref[...] = jnp.zeros_like(rank_ref)
    for copy in copies:
        copy.wait()
    send_rank, keep_rank = rank_refs or (total_ref, keep_ref)
    for slot in range(slots):
        x = x_ref[...].reshape(2 * rows, depth)
        part = lax.dot_general(
            x, a_ref[slot], (((1,), (1,)), ((), ())), preferred_element_type=jnp.float32
        )
        begin = slot * rank + (0 if rank_refs else width)
        send_rank[:, begin:begin + rank] = part[:rows]
        keep_rank[:, begin:begin + rank] = part[rows:]

    @pl.loop(0, count)
    def _(block):
        slot = lax.rem(block, buffers)
        fetch(block, slot).wait()
        inner = pl.ds(pl.multiple_of(block * block_k, block_k), block_k)
        x = x_ref[:, :, :, inner].reshape(2 * rows, block_k)
        for place in range(width // block_n):
            columns = slice(place * block_n, (place + 1) * block_n)
            term = jnp.dot(x, w_buf[slot, :, columns], preferred_element_type=jnp.float32)
            total_ref[:, columns] += term[:rows]
            keep_ref[:, columns] += term[rows:]

        @pl.when(block + buffers < count)
        def _():
            fetch(block + buffers, slot).start()

    send_ref[...] = total_ref[...].astype(send_ref.dtype)


def rank_columns(factors):
    slots, rank, _ = factors.shape
    return -(-slots * rank // 128) * 128


def partial_products(pos, chunks, weight, factors, apart):
    _, per_block, depth = chunks[0][0].shape
    width = weight.shape[1]
    spans = tuple((first, steps) for _, _, first, steps in chunks)
    steps = sum(length for _, length in spans)
    rows = steps * per_block
    block_k = block_depth(depth, width, rows)
    buffers = min(BUFFERS, depth // block_k)
    any_spec = pl.BlockSpec(memory_space=pl.ANY)
    vmem_spec = pl.BlockSpec(memory_space=pltpu.VMEM)
    extra = rank_columns(factors)
    columns = width + (0 if apart else extra)
    ranks = [jax.ShapeDtypeStruct((rows, extra), jnp.float32)] * (2 if apart else 0)
    return pl.pallas_call(
        functools.partial(matmul_body, spans),
        in_specs=[pl.BlockSpec(memory_space=pltpu.SMEM)] + [any_spec] * (2 * len(chunks) + 1) + [vmem_spec],
        out_specs=[vmem_spec] * (2 + len(ranks)),
        out_shape=[
            jax.ShapeDtypeStruct((rows, columns), jnp.bfloat16),
            jax.ShapeDtypeStruct((rows, columns), jnp.float32),
        ] + ranks,
        scratch_shapes=[
            pltpu.VMEM((2, steps, per_block, depth), jnp.bfloat16),
            pltpu.VMEM((buffers, block_k, width), jnp.bfloat16),
            pltpu.VMEM((rows, columns), jnp.float32),
            pltpu.SemaphoreType.DMA((2 * len(chunks),)),
            pltpu.SemaphoreType.DMA((buffers,)),
        ],
        compiler_params=pltpu.CompilerParams(vmem_limit_bytes=VMEM_BYTES),
        cost_estimate=pl.CostEstimate(flops=0, bytes_accessed=0, transcendentals=0),
        name="partial_products",
    )(pos, *[source for own, sib, _, _ in chunks for source in (own, sib)], weight, factors)


def finish_body(received, chosen_ref, slot_ref, order_ref, panel_ref, *refs):
    out_ref, lifted_ref, done_ref, sem = refs[-4:]
    steps, rows, width = done_ref.shape
    rank = chosen_ref.shape[1]
    chosen = chosen_ref[...]
    slot = slot_ref[...]
    spread = jnp.concatenate(
        [
            jnp.where(slot == order_ref[place], chosen, jnp.zeros_like(chosen))
            for place in range(panel_ref.shape[0] // rank)
        ],
        axis=1,
    )
    block_n = min(BLOCK_N, width)
    for place in range(width // block_n):
        columns = slice(place * block_n, (place + 1) * block_n)
        lifted = jnp.dot(spread, panel_ref[:, columns], preferred_element_type=jnp.float32).astype(jnp.bfloat16)
        for step in range(steps):
            total = refs[step * (received + 1)][:, columns]
            for value_ref in refs[step * (received + 1) + 1:(step + 1) * (received + 1)]:
                total = total + value_ref[:, columns].astype(jnp.float32)
            value = total + ADAPTER_SCALE * lifted[step * rows:(step + 1) * rows].astype(jnp.float32)
            done_ref[step, :, columns] = value.astype(done_ref.dtype)
        lifted_ref[:, columns] = lifted[steps * rows:]
    copy = pltpu.make_async_copy(done_ref, out_ref.at[pl.ds(0, steps)], sem)
    copy.start()
    copy.wait()


def finish_steps(totals, chosen, slots, order, panels):
    steps, width = len(totals), panels.shape[1]
    rows = chosen.shape[0] // (steps + 1)
    vmem_spec = pl.BlockSpec(memory_space=pltpu.VMEM)
    arrays = [value for total in totals for value in total]
    return pl.pallas_call(
        functools.partial(finish_body, len(totals[0]) - 1),
        in_specs=[vmem_spec, vmem_spec, pl.BlockSpec(memory_space=pltpu.SMEM)] + [vmem_spec] * (1 + len(arrays)),
        out_specs=[pl.BlockSpec(memory_space=pl.ANY), vmem_spec],
        out_shape=[
            jax.ShapeDtypeStruct((steps + 1, rows, width), jnp.bfloat16),
            jax.ShapeDtypeStruct((rows, width), jnp.bfloat16),
        ],
        scratch_shapes=[pltpu.VMEM((steps, rows, width), jnp.bfloat16), pltpu.SemaphoreType.DMA],
        compiler_params=pltpu.CompilerParams(vmem_limit_bytes=VMEM_BYTES),
        cost_estimate=pl.CostEstimate(flops=0, bytes_accessed=0, transcendentals=0),
        name="finish_steps",
    )(chosen, slots, order, panels, *arrays)


def last_body(partial_ref, lifted_ref, *refs):
    out_ref, done_ref, sem = refs[-3:]
    total = refs[0][...]
    for value_ref in refs[1:-3]:
        total = total + value_ref[...].astype(jnp.float32)
    value = total + ADAPTER_SCALE * lifted_ref[...].astype(jnp.float32)
    done_ref[0] = value.astype(done_ref.dtype)
    copy = pltpu.make_async_copy(done_ref, out_ref.at[pl.ds(out_ref.shape[0] - 1, 1)], sem)
    copy.start()
    copy.wait()


def finish_last(partial, lifted, arrays):
    vmem_spec = pl.BlockSpec(memory_space=pltpu.VMEM)
    any_spec = pl.BlockSpec(memory_space=pl.ANY)
    return pl.pallas_call(
        last_body,
        in_specs=[any_spec] + [vmem_spec] * (1 + len(arrays)),
        out_specs=any_spec,
        out_shape=jax.ShapeDtypeStruct(partial.shape, partial.dtype),
        input_output_aliases={0: 0},
        scratch_shapes=[pltpu.VMEM((1,) + partial.shape[1:], partial.dtype), pltpu.SemaphoreType.DMA],
        compiler_params=pltpu.CompilerParams(vmem_limit_bytes=VMEM_BYTES),
        cost_estimate=pl.CostEstimate(flops=0, bytes_accessed=0, transcendentals=0),
        name="finish_last",
    )(partial, lifted, *arrays)


def per_device(hidden, base_weight, down_a, up_b, adapter_ids, owner_map):
    step_count, per_block, _ = hidden.shape
    n_tensor = lax.axis_size("tp")
    n_rep = lax.axis_size("rep")
    n_sub = lax.axis_size("sub")
    n_owners = n_rep * n_sub
    tensor_index = lax.axis_index("tp")
    rep_index = lax.axis_index("rep")
    sub_index = lax.axis_index("sub")
    owner_index = lax.axis_index(("rep", "sub"))
    requests = per_block * n_owners
    rows_mine = requests // n_tensor
    group = n_tensor // n_rep
    group_index = tensor_index // group
    owned_slots, _, rank_size = down_a.shape
    slot_count = owned_slots * n_owners
    width = base_weight.shape[1]

    def after(value, *done):
        return lax.optimization_barrier((value, *done))[0]

    def swap_cores(value):
        return lax.ppermute(value, "sub", [(i, i ^ 1) for i in range(n_sub)])

    def from_rep(value, shift):
        return lax.ppermute(value, "rep", [((i + shift) % n_rep, i) for i in range(n_rep)])

    def swap_tensor(value, bit):
        return lax.ppermute(value, "tp", [(i, i ^ bit) for i in range(n_tensor)])

    def to_group(value, hop):
        moved = group * hop
        return lax.ppermute(value, "tp", [(i, (i + moved) % n_tensor) for i in range(n_tensor)])

    def pick(values, index):
        value = values[0]
        for at in range(1, len(values)):
            value = jnp.where(index == at, values[at], value)
        return value

    keeps = (tensor_index // (group // 2)) % 2
    pos = (sub_index == keeps).astype(jnp.int32).reshape(1)

    siblings = swap_cores(hidden)
    pieces = [(step, shift) for step in range(step_count) for shift in range(1, n_rep)]
    remote = {}
    for step, shift in pieces:
        source = hidden if step == 0 else after(hidden, siblings)
        remote[step, shift] = from_rep(source[step:step + 1], shift)

    panels, order, bit = up_b, [0], n_tensor // 2
    while bit:
        panels = jnp.concatenate([panels, swap_tensor(panels, bit)], axis=0)
        order = order + [at ^ bit for at in order]
        bit //= 2
    panels = panels.reshape(slot_count * rank_size, width)
    panel_slots = jnp.stack([
        (tensor_index ^ at) * up_b.shape[0] + each for at in order for each in range(up_b.shape[0])
    ]).astype(jnp.int32)

    my_ids = lax.dynamic_slice_in_dim(adapter_ids, tensor_index * rows_mine, rows_mine)
    iota = lax.broadcasted_iota(jnp.int32, (rows_mine, slot_count), 1)
    my_slot = jnp.sum((my_ids == iota).astype(jnp.int32) * owner_map[None, :], axis=1)
    owned_hot = my_slot[:, None] == (
        owner_index * owned_slots + lax.broadcasted_iota(jnp.int32, (rows_mine, owned_slots), 1)
    )

    first_leg, halved, begun, second_leg, ended = [], {}, set(), [], {}

    def second_half(total, received, steps, kind):
        total = total + received.astype(jnp.float32)
        rows, columns = total.shape
        extent, bit = rows // steps, group // 4
        while bit:
            extent //= 2
            halves = total.reshape(steps, 2, extent, columns)
            mine = (tensor_index // bit) % 2
            kept = lax.dynamic_index_in_dim(halves, mine, 1, keepdims=False)
            sent = lax.dynamic_index_in_dim(halves, 1 - mine, 1, keepdims=False)
            total = kept + swap_tensor(sent.astype(kind), bit).astype(jnp.float32)
            bit //= 2
        return total.reshape(steps, extent, columns)

    def gap(token, jobs, *extra):
        nonlocal first_leg, second_leg
        for parts, received, keep, kind in first_leg:
            steps = sum(length for _, length in parts)
            total, begin = second_half(after(keep, token), received, steps, kind), 0
            for key, length in parts:
                for at in range(begin, begin + length):
                    halved[key[0] + at - begin, key[1]] = total[at]
                    if key == (step_count - 1, 0):
                        halved[RANK_NAME, 0] = total[at][:, width:]
                begin += length
        closed = {}
        for name, kept, received in second_leg:
            closed[name] = (kept, *received)
        started, sends = [], []
        for name in sorted({name for name, _ in halved}):
            if name in begun or any((name, at) not in halved for at in range(n_rep)):
                continue
            begun.add(name)
            values = [halved[name, at] for at in range(n_rep)]
            columns = min(value.shape[1] for value in values)
            values = [value[:, :columns] for value in values]
            kind = jnp.float32 if name >= RANK_NAME else jnp.bfloat16
            kept = pick(values, (group_index - rep_index) % n_rep)
            sent = [pick(values, (group_index + hop - rep_index) % n_rep).astype(kind) for hop in range(1, n_rep)]
            started.append((name, kept))
            sends.append(sent)
        first_sends = [job[1] for job in jobs]
        first_sends, sends, extra, closed = lax.optimization_barrier((first_sends, sends, extra, closed))
        ended.update(closed)
        first_leg = [
            (parts, swap_tensor(send, group // 2), keep, kind) for (parts, _, keep, kind), send in zip(jobs, first_sends)
        ]
        second_leg = [
            (name, kept, [to_group(value, hop + 1) for hop, value in enumerate(sent)])
            for (name, kept), sent in zip(started, sends)
        ]
        return extra

    factors = jnp.swapaxes(down_a, 1, 2)

    def multiply(chunks, apart=False):
        return partial_products(pos, chunks, base_weight, factors, apart)

    half = step_count // 2
    send, keep = multiply([(hidden, siblings, 0, half)])
    jobs = [([((0, 0), half)], send, keep, jnp.bfloat16)]
    next_local = half
    for piece, (step, shift) in enumerate(pieces):
        own, siblings = gap(send, jobs, remote[step, shift], siblings)
        if piece == 1:
            siblings, panels = lax.optimization_barrier((siblings, panels))
        sib = swap_cores(own)
        chunks, parts = [(own, sib, 0, 1)], [((step, shift), 1)]
        if next_local < step_count:
            chunks.insert(0, (hidden, siblings, next_local, 1))
            parts.insert(0, ((next_local, 0), 1))
            next_local += 1
        send, keep, *ranks = multiply(chunks, step == step_count - 1)
        jobs = [(parts, send, keep, jnp.bfloat16)]
        if ranks:
            jobs.insert(0, ([((RANK_NAME, shift), 1)], *ranks, jnp.float32))
    gap(send, jobs)
    gap(send, [])
    ended.update((name, (kept, *received)) for name, kept, received in second_leg)

    def rank_sum(name):
        kept, *received = [value[:, -rank_columns(factors):] for value in ended[name]]
        for value in received:
            kept = kept + value.astype(jnp.float32)
        return kept[:, :owned_slots * rank_size]

    finished = jnp.stack([rank_sum(step) for step in range(step_count - 1)] + [rank_sum(RANK_NAME)])
    finished = finished.astype(jnp.bfloat16).reshape(step_count, rows_mine, owned_slots, rank_size)
    masked = jnp.sum(
        jnp.where(owned_hot[None, :, :, None], finished, 0), axis=2, dtype=jnp.float32
    ).astype(jnp.bfloat16)
    chosen = masked
    for turn in range(1, n_owners):
        chosen = chosen + lax.ppermute(
            masked, ("rep", "sub"), [(i, (i + turn) % n_owners) for i in range(n_owners)]
        )
    partial, lifted = finish_steps(
        [ended[step] for step in range(step_count - 1)],
        chosen.reshape(step_count * rows_mine, rank_size),
        jnp.broadcast_to(my_slot, (step_count, rows_mine)).reshape(step_count * rows_mine, 1),
        panel_slots,
        panels,
    )
    return finish_last(partial, lifted, ended[step_count - 1])


def solution(mesh):
    return jax.shard_map(
        per_device,
        mesh=mesh,
        in_specs=(
            P(None, ("groups", "rep", "sub"), "tp"),
            P("tp", ("rep", "sub")),
            P(("rep", "sub"), "tp", None),
            P("tp", None, ("rep", "sub")),
            P("groups", None),
            P(),
        ),
        out_specs=P(None, ("groups", "tp"), ("rep", "sub")),
        check_vma=False,
    )
```

```python
import functools

import jax
import jax.numpy as jnp
from jax import lax
from jax.experimental import pallas as pl
from jax.experimental.pallas import tpu as pltpu
from jax.sharding import PartitionSpec as P

ADAPTER_SCALE = 0.5
BLOCK_N = 256
BLOCK_VALUES = 1024 * 1024
BUFFERS = 3
WIDE_ROWS = 128
RANK_NAME = 1000
VMEM_BYTES = 24 * 1024 * 1024


def block_depth(depth, width, rows):
    values = BLOCK_VALUES * (2 if rows >= WIDE_ROWS else 1)
    for size in (1024, 512, 256):
        if depth % size == 0 and size * width <= values:
            return size
    return depth


def rank_columns(factors):
    slots, rank, _ = factors.shape
    return -(-slots * rank // 128) * 128


def matmul_body(spans, begin, mixed, kind, pos_ref, *refs):
    sources = refs[:len(spans)]
    mine_ref = refs[len(spans)] if mixed else None
    refs = refs[len(spans) + mixed:]
    w_ref, a_ref = refs[:2]
    outs = refs[2:-5]
    x_ref, w_buf, total_ref, x_sems, w_sems = refs[-5:]
    blocks, per_block, depth = x_ref.shape
    rows = blocks * per_block
    width = w_ref.shape[1]
    slots, rank, _ = a_ref.shape
    buffers, block_k, _ = w_buf.shape
    block_n = min(BLOCK_N, width)
    count = depth // block_k
    own_at = pos_ref[0]

    def fetch(block, slot):
        return pltpu.make_async_copy(
            w_ref.at[pl.ds(block * block_k, block_k)], w_buf.at[slot], w_sems.at[slot]
        )

    copies = []
    for index, (first, steps, place, core) in enumerate(spans):
        at = place if core is None else place + (own_at if core == 0 else 1 - own_at)
        copies.append(pltpu.make_async_copy(
            sources[index].at[pl.ds(first, steps)], x_ref.at[pl.ds(at, steps)], x_sems.at[index]
        ))
    for copy in copies:
        copy.start()
    for block in range(buffers):
        fetch(block, block).start()
    pieces = []
    if kind == "own":
        for index, out_ref in enumerate(outs[1:]):
            pieces.append(pltpu.make_async_copy(
                sources[0].at[pl.ds(index + 1, 1)], out_ref, x_sems.at[len(spans) + index]
            ))
            pieces[-1].start()
    total_ref[...] = jnp.zeros_like(total_ref)
    for copy in copies:
        copy.wait()
    for slot in range(slots):
        total_ref[:, width + slot * rank:width + (slot + 1) * rank] = lax.dot_general(
            x_ref[...].reshape(rows, depth), a_ref[slot], (((1,), (1,)), ((), ())),
            preferred_element_type=jnp.float32,
        )

    @pl.loop(0, count)
    def _(block):
        slot = lax.rem(block, buffers)
        fetch(block, slot).wait()
        inner = pl.ds(pl.multiple_of(block * block_k, block_k), block_k)
        x = x_ref[:, :, inner].reshape(rows, block_k)
        for place in range(width // block_n):
            columns = slice(place * block_n, (place + 1) * block_n)
            total_ref[:, columns] += jnp.dot(x, w_buf[slot, :, columns], preferred_element_type=jnp.float32)

        @pl.when(block + buffers < count)
        def _():
            fetch(block + buffers, slot).start()

    if kind == "own":
        outs[0][...] = total_ref[...]
        for copy in pieces:
            copy.wait()
        return
    send_ref, keep_ref = outs[:2]
    columns = slice(0, send_ref.shape[1])
    split = rows - 2 * per_block
    if mixed:
        own_sent = own_at == 0
        mine, other = mine_ref[begin * per_block:begin * per_block + split], total_ref[:split]
        send_ref[:split] = jnp.where(own_sent, mine, other).astype(send_ref.dtype)
        keep_ref[:split] = jnp.where(own_sent, other, mine)
    send_ref[split:] = total_ref[split:split + per_block, columns].astype(send_ref.dtype)
    keep_ref[split:] = total_ref[split + per_block:, columns]
    if kind == "apart":
        outs[2][...] = total_ref[split:split + per_block, width:]
        outs[3][...] = total_ref[split + per_block:, width:]


def call_matmul(name, body, pos, sources, mine, weight, factors, blocks, out_shape, out_specs, copies):
    _, per_block, depth = sources[0].shape
    width = weight.shape[1]
    block_k = block_depth(depth, width, blocks * per_block // 2)
    buffers = min(BUFFERS if blocks * per_block >= 2 * WIDE_ROWS else 2 * BUFFERS, depth // block_k)
    any_spec = pl.BlockSpec(memory_space=pl.ANY)
    vmem_spec = pl.BlockSpec(memory_space=pltpu.VMEM)
    return pl.pallas_call(
        body,
        in_specs=[pl.BlockSpec(memory_space=pltpu.SMEM)] + [any_spec] * len(sources)
        + [vmem_spec] * len(mine) + [any_spec, vmem_spec],
        out_specs=out_specs,
        out_shape=out_shape,
        scratch_shapes=[
            pltpu.VMEM((blocks, per_block, depth), jnp.bfloat16),
            pltpu.VMEM((buffers, block_k, width), jnp.bfloat16),
            pltpu.VMEM((blocks * per_block, width + rank_columns(factors)), jnp.float32),
            pltpu.SemaphoreType.DMA((copies,)),
            pltpu.SemaphoreType.DMA((buffers,)),
        ],
        compiler_params=pltpu.CompilerParams(vmem_limit_bytes=VMEM_BYTES),
        cost_estimate=pl.CostEstimate(flops=0, bytes_accessed=0, transcendentals=0),
        name=name,
    )(pos, *sources, *mine, weight, factors)


def own_products(pos, hidden, weight, factors):
    steps, per_block, depth = hidden.shape
    columns = weight.shape[1] + rank_columns(factors)
    spans = ((0, steps, 0, None),)
    any_spec = pl.BlockSpec(memory_space=pl.ANY)
    return call_matmul(
        "own_products", functools.partial(matmul_body, spans, 0, 0, "own"), pos, [hidden], [], weight, factors, steps,
        [jax.ShapeDtypeStruct((steps * per_block, columns), jnp.float32)]
        + [jax.ShapeDtypeStruct((1, per_block, depth), hidden.dtype)] * (steps - 1),
        [pl.BlockSpec(memory_space=pltpu.VMEM)] + [any_spec] * (steps - 1),
        steps,
    )


def pair_products(pos, own, sib, weight, factors, apart, siblings=None, mine=None, first=0, steps=0):
    _, per_block, _ = own.shape
    width, extra = weight.shape[1], rank_columns(factors)
    spans = ((first, steps, 0, None),) if steps else ()
    spans += ((0, 1, steps, 0), (0, 1, steps, 1))
    rows = (steps + 1) * per_block
    columns = width + (0 if apart else extra)
    out_shape = [
        jax.ShapeDtypeStruct((rows, columns), jnp.bfloat16),
        jax.ShapeDtypeStruct((rows, columns), jnp.float32),
    ] + [jax.ShapeDtypeStruct((rows, extra), jnp.float32)] * (2 if apart else 0)
    body = functools.partial(matmul_body, spans, first, 1 if steps else 0, "apart" if apart else "joined")
    return call_matmul(
        "pair_products", body, pos, ([siblings] if steps else []) + [own, sib], [mine] if steps else [], weight,
        factors, steps + 2, out_shape, [pl.BlockSpec(memory_space=pltpu.VMEM)] * len(out_shape), len(spans),
    )


def finish_body(received, panels, chosen_ref, slot_ref, order_ref, *refs):
    panel_refs, refs = refs[:panels], refs[panels:]
    per_panel = panel_refs[0].shape[0]
    out_ref, lifted_ref, done_ref, sem = refs[-4:]
    steps, rows, width = done_ref.shape
    rank = chosen_ref.shape[1]
    chosen = chosen_ref[...]
    slot = slot_ref[...]
    spread = jnp.concatenate(
        [
            jnp.where(slot == order_ref[place], chosen, jnp.zeros_like(chosen))
            for place in range(panels * per_panel // rank)
        ],
        axis=1,
    )
    block_n = min(BLOCK_N, width)
    for place in range(width // block_n):
        columns = slice(place * block_n, (place + 1) * block_n)
        panel = jnp.concatenate([panel_ref[:, columns] for panel_ref in panel_refs], axis=0)
        lifted = jnp.dot(spread, panel, preferred_element_type=jnp.float32).astype(jnp.bfloat16)
        for step in range(steps):
            total = refs[step * (received + 1)][:, columns]
            for value_ref in refs[step * (received + 1) + 1:(step + 1) * (received + 1)]:
                total = total + value_ref[:, columns].astype(jnp.float32)
            value = total + ADAPTER_SCALE * lifted[step * rows:(step + 1) * rows].astype(jnp.float32)
            done_ref[step, :, columns] = value.astype(done_ref.dtype)
        lifted_ref[:, columns] = lifted[steps * rows:]
    copy = pltpu.make_async_copy(done_ref, out_ref.at[pl.ds(0, steps)], sem)
    copy.start()
    copy.wait()


def finish_steps(totals, chosen, slots, order, panels):
    steps, width = len(totals), panels[0].shape[1]
    rows = chosen.shape[0] // (steps + 1)
    vmem_spec = pl.BlockSpec(memory_space=pltpu.VMEM)
    arrays = [value for total in totals for value in total]
    return pl.pallas_call(
        functools.partial(finish_body, len(totals[0]) - 1, len(panels)),
        in_specs=[vmem_spec, vmem_spec, pl.BlockSpec(memory_space=pltpu.SMEM)] + [vmem_spec] * (len(panels) + len(arrays)),
        out_specs=[pl.BlockSpec(memory_space=pl.ANY), vmem_spec],
        out_shape=[
            jax.ShapeDtypeStruct((steps + 1, rows, width), jnp.bfloat16),
            jax.ShapeDtypeStruct((rows, width), jnp.bfloat16),
        ],
        scratch_shapes=[pltpu.VMEM((steps, rows, width), jnp.bfloat16), pltpu.SemaphoreType.DMA],
        compiler_params=pltpu.CompilerParams(vmem_limit_bytes=VMEM_BYTES),
        cost_estimate=pl.CostEstimate(flops=0, bytes_accessed=0, transcendentals=0),
        name="finish_steps",
    )(chosen, slots, order, *panels, *arrays)


def last_body(partial_ref, lifted_ref, *refs):
    out_ref, done_ref, sem = refs[-3:]
    total = refs[0][...]
    for value_ref in refs[1:-3]:
        total = total + value_ref[...].astype(jnp.float32)
    value = total + ADAPTER_SCALE * lifted_ref[...].astype(jnp.float32)
    done_ref[0] = value.astype(done_ref.dtype)
    copy = pltpu.make_async_copy(done_ref, out_ref.at[pl.ds(out_ref.shape[0] - 1, 1)], sem)
    copy.start()
    copy.wait()


def finish_last(partial, lifted, arrays):
    vmem_spec = pl.BlockSpec(memory_space=pltpu.VMEM)
    any_spec = pl.BlockSpec(memory_space=pl.ANY)
    return pl.pallas_call(
        last_body,
        in_specs=[any_spec] + [vmem_spec] * (1 + len(arrays)),
        out_specs=any_spec,
        out_shape=jax.ShapeDtypeStruct(partial.shape, partial.dtype),
        input_output_aliases={0: 0},
        scratch_shapes=[pltpu.VMEM((1,) + partial.shape[1:], partial.dtype), pltpu.SemaphoreType.DMA],
        compiler_params=pltpu.CompilerParams(vmem_limit_bytes=VMEM_BYTES),
        cost_estimate=pl.CostEstimate(flops=0, bytes_accessed=0, transcendentals=0),
        name="finish_last",
    )(partial, lifted, *arrays)


def per_device(hidden, base_weight, down_a, up_b, adapter_ids, owner_map):
    step_count, per_block, _ = hidden.shape
    n_tensor = lax.axis_size("tp")
    n_rep = lax.axis_size("rep")
    n_sub = lax.axis_size("sub")
    n_owners = n_rep * n_sub
    tensor_index = lax.axis_index("tp")
    rep_index = lax.axis_index("rep")
    sub_index = lax.axis_index("sub")
    owner_index = lax.axis_index(("rep", "sub"))
    requests = per_block * n_owners
    rows_mine = requests // n_tensor
    group = n_tensor // n_rep
    group_index = tensor_index // group
    owned_slots, _, rank_size = down_a.shape
    slot_count = owned_slots * n_owners
    width = base_weight.shape[1]

    def after(value, *done):
        return lax.optimization_barrier((value, *done))[0]

    def swap_cores(value):
        return lax.ppermute(value, "sub", [(i, i ^ 1) for i in range(n_sub)])

    def from_rep(value, shift):
        return lax.ppermute(value, "rep", [((i + shift) % n_rep, i) for i in range(n_rep)])

    def swap_tensor(value, bit):
        return lax.ppermute(value, "tp", [(i, i ^ bit) for i in range(n_tensor)])

    def to_group(value, hop):
        moved = group * hop
        return lax.ppermute(value, "tp", [(i, (i + moved) % n_tensor) for i in range(n_tensor)])

    def pick(values, index):
        value = values[0]
        for at in range(1, len(values)):
            value = jnp.where(index == at, values[at], value)
        return value

    keeps = (tensor_index // (group // 2)) % 2
    pos = (sub_index == keeps).astype(jnp.int32).reshape(1)

    siblings = swap_cores(hidden)
    pieces = [(step, shift) for step in range(step_count) for shift in range(1, n_rep)]
    remote = {(0, shift): from_rep(hidden[:1], shift) for shift in range(1, n_rep)}

    def spread_panels(panels, order, bits):
        for bit in bits:
            panels = panels + [swap_tensor(panel, bit) for panel in panels]
            order = order + [at ^ bit for at in order]
        return panels, order

    bits = [n_tensor >> at for at in range(1, n_tensor.bit_length())]
    panels, order = spread_panels([up_b], [0], bits[:1])
    my_ids = lax.dynamic_slice_in_dim(adapter_ids, tensor_index * rows_mine, rows_mine)
    iota = lax.broadcasted_iota(jnp.int32, (rows_mine, slot_count), 1)
    my_slot = jnp.sum((my_ids == iota).astype(jnp.int32) * owner_map[None, :], axis=1)
    owned_hot = my_slot[:, None] == (
        owner_index * owned_slots + lax.broadcasted_iota(jnp.int32, (rows_mine, owned_slots), 1)
    )

    first_leg, halved, begun, second_leg, ended = [], {}, set(), [], {}

    def second_half(total, received, steps, kind):
        total = total + received.astype(jnp.float32)
        rows, columns = total.shape
        extent, bit = rows // steps, group // 4
        while bit:
            extent //= 2
            halves = total.reshape(steps, 2, extent, columns)
            mine = (tensor_index // bit) % 2
            kept = lax.dynamic_index_in_dim(halves, mine, 1, keepdims=False)
            sent = lax.dynamic_index_in_dim(halves, 1 - mine, 1, keepdims=False)
            total = kept + swap_tensor(sent.astype(kind), bit).astype(jnp.float32)
            bit //= 2
        return total.reshape(steps, extent, columns)

    def gap(token, jobs, *extra, short=False):
        nonlocal first_leg, second_leg
        for parts, received, keep, kind in first_leg:
            steps = sum(length for _, length in parts)
            total, begin = second_half(after(keep, token), received, steps, kind), 0
            for key, length in parts:
                for at in range(begin, begin + length):
                    halved[key[0] + at - begin, key[1]] = total[at]
                    if (key[0] + at - begin, key[1]) == (step_count - 1, 0):
                        halved[RANK_NAME, 0] = total[at][:, width:]
                begin += length
        closed, waiting = {}, second_leg if short else []
        for name, kept, received in [] if short else second_leg:
            closed[name] = (after(kept, token), *received)
        started, sends = [], []
        for name in sorted({name for name, _ in halved}):
            if name in begun or name == RANK_NAME or any((name, at) not in halved for at in range(n_rep)):
                continue
            begun.add(name)
            values = [halved[name, at] for at in range(n_rep)]
            columns = min(value.shape[1] for value in values)
            values = [value[:, :columns] for value in values]
            kept = pick(values, (group_index - rep_index) % n_rep)
            sent = [pick(values, (group_index + hop - rep_index) % n_rep).astype(jnp.bfloat16) for hop in range(1, n_rep)]
            started.append((name, kept))
            sends.append(sent)
        first_sends = [job[1] for job in jobs]
        first_sends, sends, extra, closed, _ = lax.optimization_barrier((first_sends, sends, extra, closed, token))
        ended.update(closed)
        first_leg = [
            (parts, swap_tensor(send, group // 2), keep, kind) for (parts, _, keep, kind), send in zip(jobs, first_sends)
        ]
        second_leg = waiting + [
            (name, kept, [to_group(value, hop + 1) for hop, value in enumerate(sent)])
            for (name, kept), sent in zip(started, sends)
        ]
        return extra

    factors = jnp.swapaxes(down_a, 1, 2)

    half = step_count // 2
    source = pltpu.with_memory_space_constraint(hidden, pltpu.HBM)
    mine, *slices = own_products(pos, source, base_weight, factors)
    for step in range(1, step_count):
        for shift in range(1, n_rep):
            remote[step, shift] = from_rep(slices[step - 1], shift)
    send, jobs, joined, last_ranks = mine, [], 0, {}
    for piece, (step, shift) in enumerate(pieces):
        own, siblings, panels = gap(send, jobs, remote[step, shift], siblings, panels)
        if piece == 0:
            panels, order = spread_panels(panels, order, bits[1:])
        sib = swap_cores(own)
        if piece == len(pieces) - 1:
            own, sib = gap(send, [], own, sib, short=True)
        last, parts, extra = step == step_count - 1, [((step, shift), 1)], {}
        if joined < step_count:
            parts.insert(0, ((joined, 0), half))
            extra = dict(
                siblings=siblings, mine=mine, first=joined, steps=half
            )
            joined += half
        send, keep, *ranks = pair_products(pos, own, sib, base_weight, factors, last, **extra)
        jobs = [(parts, send, keep, jnp.bfloat16)]
        if last:
            last_ranks[shift] = ranks
    last_ranks, = gap(send, jobs, last_ranks)
    for shift, ranks in last_ranks.items():
        halved[RANK_NAME, shift] = second_half(ranks[1], swap_tensor(ranks[0], group // 2), 1, jnp.float32)[0]
    values = [halved[RANK_NAME, at] for at in range(n_rep)]
    ended[RANK_NAME] = (pick(values, (group_index - rep_index) % n_rep), *[
        to_group(pick(values, (group_index + hop - rep_index) % n_rep), hop) for hop in range(1, n_rep)
    ])
    def rank_sum(name):
        kept, *received = [value[:, -rank_columns(factors):] for value in ended[name]]
        for value in received:
            kept = kept + value.astype(jnp.float32)
        return kept[:, :owned_slots * rank_size]

    finished = jnp.stack([rank_sum(step) for step in range(step_count - 1)] + [rank_sum(RANK_NAME)])
    finished = finished.astype(jnp.bfloat16).reshape(step_count, rows_mine, owned_slots, rank_size)
    finished, = gap(send, [], finished)
    ended.update((name, (kept, *received)) for name, kept, received in second_leg)
    masked = jnp.sum(
        jnp.where(owned_hot[None, :, :, None], finished, 0), axis=2, dtype=jnp.float32
    ).astype(jnp.bfloat16)
    chosen = masked
    for turn in range(1, n_owners):
        chosen = chosen + lax.ppermute(
            masked, ("rep", "sub"), [(i, (i + turn) % n_owners) for i in range(n_owners)]
        )
    panel_slots = jnp.stack([
        (tensor_index ^ at) * up_b.shape[0] + each for at in order for each in range(up_b.shape[0])
    ]).astype(jnp.int32)

    panels = [panel.reshape(-1, width) for panel in panels]
    partial, lifted = finish_steps(
        [ended[step] for step in range(step_count - 1)],
        chosen.reshape(step_count * rows_mine, rank_size),
        jnp.broadcast_to(my_slot, (step_count, rows_mine)).reshape(step_count * rows_mine, 1),
        panel_slots,
        panels,
    )
    return finish_last(partial, lifted, ended[step_count - 1])


def solution(mesh):
    return jax.shard_map(
        per_device,
        mesh=mesh,
        in_specs=(
            P(None, ("groups", "rep", "sub"), "tp"),
            P("tp", ("rep", "sub")),
            P(("rep", "sub"), "tp", None),
            P("tp", None, ("rep", "sub")),
            P("groups", None),
            P(),
        ),
        out_specs=P(None, ("groups", "tp"), ("rep", "sub")),
        check_vma=False,
    )
```

```python
import functools

import jax
import jax.numpy as jnp
from jax import lax
from jax.experimental import pallas as pl
from jax.experimental.pallas import tpu as pltpu
from jax.sharding import PartitionSpec as P

ADAPTER_SCALE = 0.5
BLOCK_N = 256
BLOCK_VALUES = 1024 * 1024
BUFFERS = 3
WIDE_ROWS = 128
RANK_NAME = 1000
VMEM_BYTES = 24 * 1024 * 1024


def block_depth(depth, width, rows):
    values = BLOCK_VALUES * (2 if rows >= WIDE_ROWS else 1)
    for size in (1024, 512, 256):
        if depth % size == 0 and size * width <= values:
            return size
    return depth


def rank_columns(factors):
    slots, rank, _ = factors.shape
    return -(-slots * rank // 128) * 128


def matmul_body(spans, emitted, apart, pos_ref, *refs):
    sources = refs[:2 * len(spans)]
    w_ref, a_ref, send_ref, keep_ref = refs[2 * len(spans):2 * len(spans) + 4]
    outs = refs[2 * len(spans) + 4:-5]
    x_ref, w_buf, total_ref, x_sems, w_sems = refs[-5:]
    rows = send_ref.shape[0]
    depth, width = w_ref.shape
    slots, rank, _ = a_ref.shape
    buffers, block_k, _ = w_buf.shape
    block_n = min(BLOCK_N, width)
    count = depth // block_k

    def fetch(block, slot):
        return pltpu.make_async_copy(
            w_ref.at[pl.ds(block * block_k, block_k)], w_buf.at[slot], w_sems.at[slot]
        )

    own_at = pos_ref[0]
    copies, begin = [], 0
    for index, (first, steps) in enumerate(spans):
        for core, at in enumerate((own_at, 1 - own_at)):
            source = sources[2 * index + core]
            copies.append(pltpu.make_async_copy(
                source.at[pl.ds(first, steps)], x_ref.at[at, pl.ds(begin, steps)], x_sems.at[2 * index + core]
            ))
        begin += steps
    for copy in copies:
        copy.start()
    for block in range(buffers):
        fetch(block, block).start()
    keep_ref[...] = jnp.zeros_like(keep_ref)
    total_ref[...] = jnp.zeros_like(total_ref)
    send_rank, keep_rank = outs[:2] if apart else (total_ref, keep_ref)
    if apart:
        send_rank[...] = jnp.zeros_like(send_rank)
        keep_rank[...] = jnp.zeros_like(keep_rank)
    for copy in copies:
        copy.wait()
    emit = None
    if emitted is not None:
        emit = pltpu.make_async_copy(
            x_ref.at[own_at, pl.ds(emitted, 1)], outs[-1], x_sems.at[2 * len(spans)]
        )
        emit.start()
    for slot in range(slots):
        x = x_ref[...].reshape(2 * rows, depth)
        part = lax.dot_general(
            x, a_ref[slot], (((1,), (1,)), ((), ())), preferred_element_type=jnp.float32
        )
        begin = slot * rank + (0 if apart else width)
        send_rank[:, begin:begin + rank] = part[:rows]
        keep_rank[:, begin:begin + rank] = part[rows:]

    @pl.loop(0, count)
    def _(block):
        slot = lax.rem(block, buffers)
        fetch(block, slot).wait()
        inner = pl.ds(pl.multiple_of(block * block_k, block_k), block_k)
        x = x_ref[:, :, :, inner].reshape(2 * rows, block_k)
        for place in range(width // block_n):
            columns = slice(place * block_n, (place + 1) * block_n)
            term = jnp.dot(x, w_buf[slot, :, columns], preferred_element_type=jnp.float32)
            total_ref[:, columns] += term[:rows]
            keep_ref[:, columns] += term[rows:]

        @pl.when(block + buffers < count)
        def _():
            fetch(block + buffers, slot).start()

    send_ref[...] = total_ref[...].astype(send_ref.dtype)
    if emit is not None:
        emit.wait()


def partial_products(pos, chunks, weight, factors, apart=False, emitted=None):
    _, per_block, depth = chunks[0][0].shape
    width = weight.shape[1]
    spans = tuple((first, steps) for _, _, first, steps in chunks)
    steps = sum(length for _, length in spans)
    rows = steps * per_block
    block_k = block_depth(depth, width, rows)
    buffers = min(BUFFERS if rows >= WIDE_ROWS else 2 * BUFFERS, depth // block_k)
    any_spec = pl.BlockSpec(memory_space=pl.ANY)
    vmem_spec = pl.BlockSpec(memory_space=pltpu.VMEM)
    extra = rank_columns(factors)
    columns = width + (0 if apart else extra)
    out_shape = [
        jax.ShapeDtypeStruct((rows, columns), jnp.bfloat16),
        jax.ShapeDtypeStruct((rows, columns), jnp.float32),
    ] + [jax.ShapeDtypeStruct((rows, extra), jnp.float32)] * (2 if apart else 0)
    out_specs = [vmem_spec] * len(out_shape)
    if emitted is not None:
        out_shape.append(jax.ShapeDtypeStruct((1, per_block, depth), jnp.bfloat16))
        out_specs.append(any_spec)
    return pl.pallas_call(
        functools.partial(matmul_body, spans, emitted, apart),
        in_specs=[pl.BlockSpec(memory_space=pltpu.SMEM)] + [any_spec] * (2 * len(chunks) + 1) + [vmem_spec],
        out_specs=out_specs,
        out_shape=out_shape,
        scratch_shapes=[
            pltpu.VMEM((2, steps, per_block, depth), jnp.bfloat16),
            pltpu.VMEM((buffers, block_k, width), jnp.bfloat16),
            pltpu.VMEM((rows, columns), jnp.float32),
            pltpu.SemaphoreType.DMA((2 * len(chunks) + 1,)),
            pltpu.SemaphoreType.DMA((buffers,)),
        ],
        compiler_params=pltpu.CompilerParams(vmem_limit_bytes=VMEM_BYTES),
        cost_estimate=pl.CostEstimate(flops=0, bytes_accessed=0, transcendentals=0),
        name="partial_products",
    )(pos, *[source for own, sib, _, _ in chunks for source in (own, sib)], weight, factors)


def finish_body(received, panels, chosen_ref, slot_ref, order_ref, *refs):
    panel_refs, refs = refs[:panels], refs[panels:]
    per_panel = panel_refs[0].shape[0]
    out_ref, lifted_ref, done_ref, sem = refs[-4:]
    steps, rows, width = done_ref.shape
    rank = chosen_ref.shape[1]
    chosen = chosen_ref[...]
    slot = slot_ref[...]
    spread = jnp.concatenate(
        [
            jnp.where(slot == order_ref[place], chosen, jnp.zeros_like(chosen))
            for place in range(panels * per_panel // rank)
        ],
        axis=1,
    )
    block_n = min(BLOCK_N, width)
    for place in range(width // block_n):
        columns = slice(place * block_n, (place + 1) * block_n)
        panel = jnp.concatenate([panel_ref[:, columns] for panel_ref in panel_refs], axis=0)
        lifted = jnp.dot(spread, panel, preferred_element_type=jnp.float32).astype(jnp.bfloat16)
        for step in range(steps):
            total = refs[step * (received + 1)][:, columns]
            for value_ref in refs[step * (received + 1) + 1:(step + 1) * (received + 1)]:
                total = total + value_ref[:, columns].astype(jnp.float32)
            value = total + ADAPTER_SCALE * lifted[step * rows:(step + 1) * rows].astype(jnp.float32)
            done_ref[step, :, columns] = value.astype(done_ref.dtype)
        lifted_ref[:, columns] = lifted[steps * rows:]
    copy = pltpu.make_async_copy(done_ref, out_ref.at[pl.ds(0, steps)], sem)
    copy.start()
    copy.wait()


def finish_steps(totals, chosen, slots, order, panels):
    steps, width = len(totals), panels[0].shape[1]
    rows = chosen.shape[0] // (steps + 1)
    vmem_spec = pl.BlockSpec(memory_space=pltpu.VMEM)
    arrays = [value for total in totals for value in total]
    return pl.pallas_call(
        functools.partial(finish_body, len(totals[0]) - 1, len(panels)),
        in_specs=[vmem_spec, vmem_spec, pl.BlockSpec(memory_space=pltpu.SMEM)] + [vmem_spec] * (len(panels) + len(arrays)),
        out_specs=[pl.BlockSpec(memory_space=pl.ANY), vmem_spec],
        out_shape=[
            jax.ShapeDtypeStruct((steps + 1, rows, width), jnp.bfloat16),
            jax.ShapeDtypeStruct((rows, width), jnp.bfloat16),
        ],
        scratch_shapes=[pltpu.VMEM((steps, rows, width), jnp.bfloat16), pltpu.SemaphoreType.DMA],
        compiler_params=pltpu.CompilerParams(vmem_limit_bytes=VMEM_BYTES),
        cost_estimate=pl.CostEstimate(flops=0, bytes_accessed=0, transcendentals=0),
        name="finish_steps",
    )(chosen, slots, order, *panels, *arrays)


def last_body(partial_ref, lifted_ref, *refs):
    out_ref, done_ref, sem = refs[-3:]
    total = refs[0][...]
    for value_ref in refs[1:-3]:
        total = total + value_ref[...].astype(jnp.float32)
    value = total + ADAPTER_SCALE * lifted_ref[...].astype(jnp.float32)
    done_ref[0] = value.astype(done_ref.dtype)
    copy = pltpu.make_async_copy(done_ref, out_ref.at[pl.ds(out_ref.shape[0] - 1, 1)], sem)
    copy.start()
    copy.wait()


def finish_last(partial, lifted, arrays):
    vmem_spec = pl.BlockSpec(memory_space=pltpu.VMEM)
    any_spec = pl.BlockSpec(memory_space=pl.ANY)
    return pl.pallas_call(
        last_body,
        in_specs=[any_spec] + [vmem_spec] * (1 + len(arrays)),
        out_specs=any_spec,
        out_shape=jax.ShapeDtypeStruct(partial.shape, partial.dtype),
        input_output_aliases={0: 0},
        scratch_shapes=[pltpu.VMEM((1,) + partial.shape[1:], partial.dtype), pltpu.SemaphoreType.DMA],
        compiler_params=pltpu.CompilerParams(vmem_limit_bytes=VMEM_BYTES),
        cost_estimate=pl.CostEstimate(flops=0, bytes_accessed=0, transcendentals=0),
        name="finish_last",
    )(partial, lifted, *arrays)


def per_device(hidden, base_weight, down_a, up_b, adapter_ids, owner_map):
    step_count, per_block, _ = hidden.shape
    n_tensor = lax.axis_size("tp")
    n_rep = lax.axis_size("rep")
    n_sub = lax.axis_size("sub")
    n_owners = n_rep * n_sub
    tensor_index = lax.axis_index("tp")
    rep_index = lax.axis_index("rep")
    sub_index = lax.axis_index("sub")
    owner_index = lax.axis_index(("rep", "sub"))
    requests = per_block * n_owners
    rows_mine = requests // n_tensor
    group = n_tensor // n_rep
    group_index = tensor_index // group
    owned_slots, _, rank_size = down_a.shape
    slot_count = owned_slots * n_owners
    width = base_weight.shape[1]

    def after(value, *done):
        return lax.optimization_barrier((value, *done))[0]

    def swap_cores(value):
        return lax.ppermute(value, "sub", [(i, i ^ 1) for i in range(n_sub)])

    def from_rep(value, shift):
        return lax.ppermute(value, "rep", [((i + shift) % n_rep, i) for i in range(n_rep)])

    def swap_tensor(value, bit):
        return lax.ppermute(value, "tp", [(i, i ^ bit) for i in range(n_tensor)])

    def to_group(value, hop):
        moved = group * hop
        return lax.ppermute(value, "tp", [(i, (i + moved) % n_tensor) for i in range(n_tensor)])

    def pick(values, index):
        value = values[0]
        for at in range(1, len(values)):
            value = jnp.where(index == at, values[at], value)
        return value

    keeps = (tensor_index // (group // 2)) % 2
    pos = (sub_index == keeps).astype(jnp.int32).reshape(1)

    siblings = swap_cores(hidden)
    pieces = [(step, shift) for step in range(step_count) for shift in range(1, n_rep)]
    remote = {(0, shift): from_rep(hidden[:1], shift) for shift in range(1, n_rep)}

    def spread_panels(panels, order, bits):
        for bit in bits:
            panels = panels + [swap_tensor(panel, bit) for panel in panels]
            order = order + [at ^ bit for at in order]
        return panels, order

    bits = [n_tensor >> at for at in range(1, n_tensor.bit_length())]
    panels, order = spread_panels([up_b], [0], bits[:1])
    my_ids = lax.dynamic_slice_in_dim(adapter_ids, tensor_index * rows_mine, rows_mine)
    iota = lax.broadcasted_iota(jnp.int32, (rows_mine, slot_count), 1)
    my_slot = jnp.sum((my_ids == iota).astype(jnp.int32) * owner_map[None, :], axis=1)
    owned_hot = my_slot[:, None] == (
        owner_index * owned_slots + lax.broadcasted_iota(jnp.int32, (rows_mine, owned_slots), 1)
    )

    first_leg, halved, begun, second_leg, ended = [], {}, set(), [], {}

    def second_half(total, received, steps, kind):
        total = total + received.astype(jnp.float32)
        rows, columns = total.shape
        extent, bit = rows // steps, group // 4
        while bit:
            extent //= 2
            halves = total.reshape(steps, 2, extent, columns)
            mine = (tensor_index // bit) % 2
            kept = lax.dynamic_index_in_dim(halves, mine, 1, keepdims=False)
            sent = lax.dynamic_index_in_dim(halves, 1 - mine, 1, keepdims=False)
            total = kept + swap_tensor(sent.astype(kind), bit).astype(jnp.float32)
            bit //= 2
        return total.reshape(steps, extent, columns)

    def gap(token, jobs, *extra, short=False):
        nonlocal first_leg, second_leg
        for parts, received, keep, kind in first_leg:
            steps = sum(length for _, length in parts)
            total, begin = second_half(after(keep, token), received, steps, kind), 0
            for key, length in parts:
                for at in range(begin, begin + length):
                    halved[key[0] + at - begin, key[1]] = total[at]
                    if (key[0] + at - begin, key[1]) == (step_count - 1, 0):
                        halved[RANK_NAME, 0] = total[at][:, width:]
                begin += length
        closed, waiting = {}, second_leg if short else []
        for name, kept, received in [] if short else second_leg:
            closed[name] = (after(kept, token), *received)
        started, sends = [], []
        for name in sorted({name for name, _ in halved}):
            if name in begun or name == RANK_NAME or any((name, at) not in halved for at in range(n_rep)):
                continue
            begun.add(name)
            values = [halved[name, at] for at in range(n_rep)]
            columns = min(value.shape[1] for value in values)
            values = [value[:, :columns] for value in values]
            kept = pick(values, (group_index - rep_index) % n_rep)
            sent = [pick(values, (group_index + hop - rep_index) % n_rep).astype(jnp.bfloat16) for hop in range(1, n_rep)]
            started.append((name, kept))
            sends.append(sent)
        first_sends = [job[1] for job in jobs]
        first_sends, sends, extra, closed, _ = lax.optimization_barrier((first_sends, sends, extra, closed, token))
        ended.update(closed)
        first_leg = [
            (parts, swap_tensor(send, group // 2), keep, kind) for (parts, _, keep, kind), send in zip(jobs, first_sends)
        ]
        second_leg = waiting + [
            (name, kept, [to_group(value, hop + 1) for hop, value in enumerate(sent)])
            for (name, kept), sent in zip(started, sends)
        ]
        return extra

    factors = jnp.swapaxes(down_a, 1, 2)

    half = step_count // 2
    source = pltpu.with_memory_space_constraint(hidden, pltpu.HBM)
    jobs, next_local, last_ranks = [([((0, 0), half)], *partial_products(
        pos, [(source, siblings, 0, half)], base_weight, factors, emitted=half - 1
    ))], half, {}
    for piece, (step, shift) in enumerate(pieces):
        (parts, send, keep, *emitted), *others = jobs
        jobs = [(parts, send, keep, jnp.bfloat16)]
        if emitted:
            for along in range(1, n_rep):
                remote[next_local - 1, along] = from_rep(emitted[0], along)
        own, siblings, panels = gap(send, jobs, remote[step, shift], siblings, panels)
        if piece == 0:
            panels, order = spread_panels(panels, order, bits[1:])
        sib = swap_cores(own)
        if piece == len(pieces) - 1:
            own, sib = gap(send, [], own, sib, short=True)
        last, chunks, parts, place = step == step_count - 1, [(own, sib, 0, 1)], [((step, shift), 1)], None
        if next_local < step_count:
            chunks.insert(0, (source, siblings, next_local, 1))
            parts.insert(0, ((next_local, 0), 1))
            next_local, place = next_local + 1, 0
        send, keep, *outs = partial_products(pos, chunks, base_weight, factors, last, place)
        if last:
            last_ranks[shift] = outs
            outs = []
        jobs = [(parts, send, keep, *outs)]
    jobs = [(parts, send, keep, jnp.bfloat16)]
    last_ranks, = gap(send, jobs, last_ranks)
    for shift, ranks in last_ranks.items():
        halved[RANK_NAME, shift] = second_half(ranks[1], swap_tensor(ranks[0], group // 2), 1, jnp.float32)[0]
    values = [halved[RANK_NAME, at] for at in range(n_rep)]
    ended[RANK_NAME] = (pick(values, (group_index - rep_index) % n_rep), *[
        to_group(pick(values, (group_index + hop - rep_index) % n_rep), hop) for hop in range(1, n_rep)
    ])
    def rank_sum(name):
        kept, *received = [value[:, -rank_columns(factors):] for value in ended[name]]
        for value in received:
            kept = kept + value.astype(jnp.float32)
        return kept[:, :owned_slots * rank_size]

    finished = jnp.stack([rank_sum(step) for step in range(step_count - 1)] + [rank_sum(RANK_NAME)])
    finished = finished.astype(jnp.bfloat16).reshape(step_count, rows_mine, owned_slots, rank_size)
    finished, = gap(send, [], finished)
    ended.update((name, (kept, *received)) for name, kept, received in second_leg)
    masked = jnp.sum(
        jnp.where(owned_hot[None, :, :, None], finished, 0), axis=2, dtype=jnp.float32
    ).astype(jnp.bfloat16)
    chosen = masked
    for turn in range(1, n_owners):
        chosen = chosen + lax.ppermute(
            masked, ("rep", "sub"), [(i, (i + turn) % n_owners) for i in range(n_owners)]
        )
    panel_slots = jnp.stack([
        (tensor_index ^ at) * up_b.shape[0] + each for at in order for each in range(up_b.shape[0])
    ]).astype(jnp.int32)

    panels = [panel.reshape(-1, width) for panel in panels]
    partial, lifted = finish_steps(
        [ended[step] for step in range(step_count - 1)],
        chosen.reshape(step_count * rows_mine, rank_size),
        jnp.broadcast_to(my_slot, (step_count, rows_mine)).reshape(step_count * rows_mine, 1),
        panel_slots,
        panels,
    )
    return finish_last(partial, lifted, ended[step_count - 1])


def solution(mesh):
    return jax.shard_map(
        per_device,
        mesh=mesh,
        in_specs=(
            P(None, ("groups", "rep", "sub"), "tp"),
            P("tp", ("rep", "sub")),
            P(("rep", "sub"), "tp", None),
            P("tp", None, ("rep", "sub")),
            P("groups", None),
            P(),
        ),
        out_specs=P(None, ("groups", "tp"), ("rep", "sub")),
        check_vma=False,
    )
```

```python
import functools

import jax
import jax.numpy as jnp
from jax import lax
from jax.experimental import pallas as pl
from jax.experimental.pallas import tpu as pltpu
from jax.sharding import PartitionSpec as P

ADAPTER_SCALE = 0.5
BLOCK_N = 256
BLOCK = 1024
BUFFERS = 4
RANK_NAME = 1000
VMEM_BYTES = 17 * 1024 * 1024


def block_shape(depth, width):
    columns = BLOCK if width % BLOCK == 0 else width
    for size in (BLOCK, BLOCK // 2, BLOCK // 4):
        if depth % size == 0:
            return size, columns
    return depth, columns


def rank_columns(factors):
    slots, rank, _ = factors.shape
    return -(-slots * rank // 128) * 128


def matmul_body(spans, emitted, apart, pos_ref, *refs):
    sources = refs[:2 * len(spans)]
    w_ref, a_ref, send_ref, keep_ref = refs[2 * len(spans):2 * len(spans) + 4]
    outs = refs[2 * len(spans) + 4:-5]
    x_ref, w_buf, total_ref, x_sems, w_sems = refs[-5:]
    rows = send_ref.shape[0]
    depth, width = w_ref.shape
    slots, rank, _ = a_ref.shape
    buffers, block_k, block_w = w_buf.shape
    block_n = min(BLOCK_N, block_w)
    depths, count = depth // block_k, (depth // block_k) * (width // block_w)

    def fetch(block, slot):
        begin = pl.multiple_of(lax.rem(block, depths) * block_k, block_k)
        left = pl.multiple_of(lax.div(block, depths) * block_w, block_w)
        return pltpu.make_async_copy(
            w_ref.at[pl.ds(begin, block_k), pl.ds(left, block_w)], w_buf.at[slot], w_sems.at[slot]
        )

    own_at = pos_ref[0]
    copies, begin = [], 0
    for index, (first, steps) in enumerate(spans):
        for core, at in enumerate((own_at, 1 - own_at)):
            source = sources[2 * index + core]
            copies.append(pltpu.make_async_copy(
                source.at[pl.ds(first, steps)], x_ref.at[at, pl.ds(begin, steps)], x_sems.at[2 * index + core]
            ))
        begin += steps
    for copy in copies:
        copy.start()
    for block in range(buffers):
        fetch(jnp.int32(block), block).start()
    keep_ref[...] = jnp.zeros_like(keep_ref)
    total_ref[...] = jnp.zeros_like(total_ref)
    send_rank, keep_rank = outs[:2] if apart else (total_ref, keep_ref)
    if apart:
        send_rank[...] = jnp.zeros_like(send_rank)
        keep_rank[...] = jnp.zeros_like(keep_rank)
    for copy in copies:
        copy.wait()
    emit = None
    if emitted is not None:
        emit = pltpu.make_async_copy(
            x_ref.at[own_at, pl.ds(emitted, 1)], outs[-1], x_sems.at[2 * len(spans)]
        )
        emit.start()
    for slot in range(slots):
        x = x_ref[...].reshape(2 * rows, depth)
        part = lax.dot_general(
            x, a_ref[slot], (((1,), (1,)), ((), ())), preferred_element_type=jnp.float32
        )
        begin = slot * rank + (0 if apart else width)
        send_rank[:, begin:begin + rank] = part[:rows]
        keep_rank[:, begin:begin + rank] = part[rows:]

    @pl.loop(0, count)
    def _(block):
        slot = lax.rem(block, buffers)
        fetch(block, slot).wait()
        inner = pl.ds(pl.multiple_of(lax.rem(block, depths) * block_k, block_k), block_k)
        left = pl.multiple_of(lax.div(block, depths) * block_w, block_w)
        x = x_ref[:, :, :, inner].reshape(2 * rows, block_k)
        for place in range(block_w // block_n):
            columns = pl.ds(left + place * block_n, block_n)
            term = jnp.dot(
                x, w_buf[slot, :, place * block_n:(place + 1) * block_n], preferred_element_type=jnp.float32
            )
            total_ref[:, columns] += term[:rows]
            keep_ref[:, columns] += term[rows:]

        @pl.when(block + buffers < count)
        def _():
            fetch(block + buffers, slot).start()

    send_ref[...] = total_ref[...].astype(send_ref.dtype)
    if emit is not None:
        emit.wait()


def partial_products(pos, chunks, weight, factors, apart=False, emitted=None):
    _, per_block, depth = chunks[0][0].shape
    width = weight.shape[1]
    spans = tuple((first, steps) for _, _, first, steps in chunks)
    steps = sum(length for _, length in spans)
    rows = steps * per_block
    block_k, block_w = block_shape(depth, width)
    buffers = min(BUFFERS, (depth // block_k) * (width // block_w))
    any_spec = pl.BlockSpec(memory_space=pl.ANY)
    vmem_spec = pl.BlockSpec(memory_space=pltpu.VMEM)
    extra = rank_columns(factors)
    columns = width + (0 if apart else extra)
    out_shape = [
        jax.ShapeDtypeStruct((rows, columns), jnp.bfloat16),
        jax.ShapeDtypeStruct((rows, columns), jnp.float32),
    ] + [jax.ShapeDtypeStruct((rows, extra), jnp.float32)] * (2 if apart else 0)
    out_specs = [vmem_spec] * len(out_shape)
    if emitted is not None:
        out_shape.append(jax.ShapeDtypeStruct((1, per_block, depth), jnp.bfloat16))
        out_specs.append(any_spec)
    return pl.pallas_call(
        functools.partial(matmul_body, spans, emitted, apart),
        in_specs=[pl.BlockSpec(memory_space=pltpu.SMEM)] + [any_spec] * (2 * len(chunks) + 1) + [vmem_spec],
        out_specs=out_specs,
        out_shape=out_shape,
        scratch_shapes=[
            pltpu.VMEM((2, steps, per_block, depth), jnp.bfloat16),
            pltpu.VMEM((buffers, block_k, block_w), jnp.bfloat16),
            pltpu.VMEM((rows, columns), jnp.float32),
            pltpu.SemaphoreType.DMA((2 * len(chunks) + 1,)),
            pltpu.SemaphoreType.DMA((buffers,)),
        ],
        compiler_params=pltpu.CompilerParams(vmem_limit_bytes=VMEM_BYTES),
        cost_estimate=pl.CostEstimate(flops=0, bytes_accessed=0, transcendentals=0),
        name="partial_products",
    )(pos, *[source for own, sib, _, _ in chunks for source in (own, sib)], weight, factors)


def cut_body(source_ref, out_ref, sem):
    copy = pltpu.make_async_copy(source_ref.at[pl.ds(0, 1)], out_ref, sem)
    copy.start()
    copy.wait()


def cut_first(hidden):
    return pl.pallas_call(
        cut_body,
        in_specs=[pl.BlockSpec(memory_space=pl.ANY)],
        out_specs=pl.BlockSpec(memory_space=pltpu.VMEM),
        out_shape=jax.ShapeDtypeStruct((1,) + hidden.shape[1:], hidden.dtype),
        scratch_shapes=[pltpu.SemaphoreType.DMA],
        cost_estimate=pl.CostEstimate(flops=0, bytes_accessed=0, transcendentals=0),
        name="cut_first",
    )(hidden)


def finish_body(received, panels, chosen_ref, slot_ref, order_ref, *refs):
    panel_refs, refs = refs[:panels], refs[panels:]
    per_panel = panel_refs[0].shape[0]
    out_ref, lifted_ref, done_ref, sem = refs[-4:]
    steps, rows, width = done_ref.shape
    rank = chosen_ref.shape[1]
    chosen = chosen_ref[...]
    slot = slot_ref[...]
    spread = jnp.concatenate(
        [
            jnp.where(slot == order_ref[place], chosen, jnp.zeros_like(chosen))
            for place in range(panels * per_panel // rank)
        ],
        axis=1,
    )
    block_n = min(BLOCK_N, width)
    for place in range(width // block_n):
        columns = slice(place * block_n, (place + 1) * block_n)
        panel = jnp.concatenate([panel_ref[:, columns] for panel_ref in panel_refs], axis=0)
        lifted = jnp.dot(spread, panel, preferred_element_type=jnp.float32).astype(jnp.bfloat16)
        for step in range(steps):
            total = refs[step * (received + 1)][:, columns]
            for value_ref in refs[step * (received + 1) + 1:(step + 1) * (received + 1)]:
                total = total + value_ref[:, columns].astype(jnp.float32)
            value = total + ADAPTER_SCALE * lifted[step * rows:(step + 1) * rows].astype(jnp.float32)
            done_ref[step, :, columns] = value.astype(done_ref.dtype)
        lifted_ref[:, columns] = lifted[steps * rows:]
    copy = pltpu.make_async_copy(done_ref, out_ref.at[pl.ds(0, steps)], sem)
    copy.start()
    copy.wait()


def finish_steps(totals, chosen, slots, order, panels):
    steps, width = len(totals), panels[0].shape[1]
    rows = chosen.shape[0] // (steps + 1)
    vmem_spec = pl.BlockSpec(memory_space=pltpu.VMEM)
    arrays = [value for total in totals for value in total]
    return pl.pallas_call(
        functools.partial(finish_body, len(totals[0]) - 1, len(panels)),
        in_specs=[vmem_spec, vmem_spec, pl.BlockSpec(memory_space=pltpu.SMEM)] + [vmem_spec] * (len(panels) + len(arrays)),
        out_specs=[pl.BlockSpec(memory_space=pl.ANY), vmem_spec],
        out_shape=[
            jax.ShapeDtypeStruct((steps + 1, rows, width), jnp.bfloat16),
            jax.ShapeDtypeStruct((rows, width), jnp.bfloat16),
        ],
        scratch_shapes=[pltpu.VMEM((steps, rows, width), jnp.bfloat16), pltpu.SemaphoreType.DMA],
        compiler_params=pltpu.CompilerParams(vmem_limit_bytes=VMEM_BYTES),
        cost_estimate=pl.CostEstimate(flops=0, bytes_accessed=0, transcendentals=0),
        name="finish_steps",
    )(chosen, slots, order, *panels, *arrays)


def last_body(partial_ref, lifted_ref, *refs):
    out_ref, done_ref, sem = refs[-3:]
    total = refs[0][...]
    for value_ref in refs[1:-3]:
        total = total + value_ref[...].astype(jnp.float32)
    value = total + ADAPTER_SCALE * lifted_ref[...].astype(jnp.float32)
    done_ref[0] = value.astype(done_ref.dtype)
    copy = pltpu.make_async_copy(done_ref, out_ref.at[pl.ds(out_ref.shape[0] - 1, 1)], sem)
    copy.start()
    copy.wait()


def finish_last(partial, lifted, arrays):
    vmem_spec = pl.BlockSpec(memory_space=pltpu.VMEM)
    any_spec = pl.BlockSpec(memory_space=pl.ANY)
    return pl.pallas_call(
        last_body,
        in_specs=[any_spec] + [vmem_spec] * (1 + len(arrays)),
        out_specs=any_spec,
        out_shape=jax.ShapeDtypeStruct(partial.shape, partial.dtype),
        input_output_aliases={0: 0},
        scratch_shapes=[pltpu.VMEM((1,) + partial.shape[1:], partial.dtype), pltpu.SemaphoreType.DMA],
        compiler_params=pltpu.CompilerParams(vmem_limit_bytes=VMEM_BYTES),
        cost_estimate=pl.CostEstimate(flops=0, bytes_accessed=0, transcendentals=0),
        name="finish_last",
    )(partial, lifted, *arrays)


def per_device(hidden, base_weight, down_a, up_b, adapter_ids, owner_map):
    step_count, per_block, _ = hidden.shape
    n_tensor = lax.axis_size("tp")
    n_rep = lax.axis_size("rep")
    n_sub = lax.axis_size("sub")
    n_owners = n_rep * n_sub
    tensor_index = lax.axis_index("tp")
    rep_index = lax.axis_index("rep")
    sub_index = lax.axis_index("sub")
    owner_index = lax.axis_index(("rep", "sub"))
    requests = per_block * n_owners
    rows_mine = requests // n_tensor
    group = n_tensor // n_rep
    group_index = tensor_index // group
    owned_slots, _, rank_size = down_a.shape
    slot_count = owned_slots * n_owners
    width = base_weight.shape[1]

    def after(value, *done):
        return lax.optimization_barrier((value, *done))[0]

    def swap_cores(value):
        return lax.ppermute(value, "sub", [(i, i ^ 1) for i in range(n_sub)])

    def from_rep(value, shift):
        return lax.ppermute(value, "rep", [((i + shift) % n_rep, i) for i in range(n_rep)])

    def swap_tensor(value, bit):
        return lax.ppermute(value, "tp", [(i, i ^ bit) for i in range(n_tensor)])

    def to_group(value, hop):
        moved = group * hop
        return lax.ppermute(value, "tp", [(i, (i + moved) % n_tensor) for i in range(n_tensor)])

    def pick(values, index):
        value = values[0]
        for at in range(1, len(values)):
            value = jnp.where(index == at, values[at], value)
        return value

    keeps = (tensor_index // (group // 2)) % 2
    pos = (sub_index == keeps).astype(jnp.int32).reshape(1)

    siblings = swap_cores(hidden)
    pieces = [(step, shift) for step in range(step_count) for shift in range(1, n_rep)]
    source = pltpu.with_memory_space_constraint(hidden, pltpu.HBM)
    first_rows = cut_first(source)
    remote = {(0, shift): from_rep(first_rows, shift) for shift in range(1, n_rep)}

    def spread_panels(panels, order, bits):
        for bit in bits:
            panels = panels + [swap_tensor(panel, bit) for panel in panels]
            order = order + [at ^ bit for at in order]
        return panels, order

    bits = [n_tensor >> at for at in range(1, n_tensor.bit_length())]
    order = [0] + [at for at in range(1, n_tensor) if at % (n_tensor // 4) == 0]
    panels = [up_b] + [swap_tensor(up_b, at) for at in order[1:]]
    my_ids = lax.dynamic_slice_in_dim(adapter_ids, tensor_index * rows_mine, rows_mine)
    iota = lax.broadcasted_iota(jnp.int32, (rows_mine, slot_count), 1)
    my_slot = jnp.sum((my_ids == iota).astype(jnp.int32) * owner_map[None, :], axis=1)
    owned_hot = my_slot[:, None] == (
        owner_index * owned_slots + lax.broadcasted_iota(jnp.int32, (rows_mine, owned_slots), 1)
    )

    first_leg, halved, begun, second_leg, ended = [], {}, set(), [], {}

    def second_half(total, received, steps, kind):
        total = total + received.astype(jnp.float32)
        rows, columns = total.shape
        extent, bit = rows // steps, group // 4
        while bit:
            extent //= 2
            halves = total.reshape(steps, 2, extent, columns)
            mine = (tensor_index // bit) % 2
            kept = lax.dynamic_index_in_dim(halves, mine, 1, keepdims=False)
            sent = lax.dynamic_index_in_dim(halves, 1 - mine, 1, keepdims=False)
            total = kept + swap_tensor(sent.astype(kind), bit).astype(jnp.float32)
            bit //= 2
        return total.reshape(steps, extent, columns)

    def gap(token, jobs, *extra):
        nonlocal first_leg, second_leg
        for parts, received, keep, kind in first_leg:
            steps = sum(length for _, length in parts)
            total, begin = second_half(after(keep, token), received, steps, kind), 0
            for key, length in parts:
                for at in range(begin, begin + length):
                    halved[key[0] + at - begin, key[1]] = total[at]
                    if (key[0] + at - begin, key[1]) == (step_count - 1, 0):
                        halved[RANK_NAME, 0] = total[at][:, width:]
                begin += length
        closed = {}
        for name, kept, received in second_leg:
            closed[name] = (after(kept, token), *received)
        started, sends = [], []
        for name in sorted({name for name, _ in halved}):
            if name in begun or name == RANK_NAME or any((name, at) not in halved for at in range(n_rep)):
                continue
            begun.add(name)
            values = [halved[name, at] for at in range(n_rep)]
            columns = min(value.shape[1] for value in values)
            values = [value[:, :columns] for value in values]
            kept = pick(values, (group_index - rep_index) % n_rep)
            sent = [pick(values, (group_index + hop - rep_index) % n_rep).astype(jnp.bfloat16) for hop in range(1, n_rep)]
            started.append((name, kept))
            sends.append(sent)
        first_sends = [job[1] for job in jobs]
        first_sends, sends, extra, closed, _ = lax.optimization_barrier((first_sends, sends, extra, closed, token))
        ended.update(closed)
        first_leg = [
            (parts, swap_tensor(send, group // 2), keep, kind) for (parts, _, keep, kind), send in zip(jobs, first_sends)
        ]
        second_leg = [
            (name, kept, [to_group(value, hop + 1) for hop, value in enumerate(sent)])
            for (name, kept), sent in zip(started, sends)
        ]
        return extra if extra else [sent for sent in sends]

    factors = jnp.swapaxes(down_a, 1, 2)

    half = step_count // 2
    jobs, next_local, last_ranks = [([((0, 0), half)], *partial_products(
        pos, [(source, siblings, 0, half)], base_weight, factors, emitted=half - 1
    ))], half, {}
    for piece, (step, shift) in enumerate(pieces):
        (parts, send, keep, *emitted), *others = jobs
        jobs = [(parts, send, keep, jnp.bfloat16)]
        if emitted:
            for along in range(1, n_rep):
                remote[next_local - 1, along] = from_rep(emitted[0], along)
        own, siblings, panels = gap(send, jobs, remote[step, shift], siblings, panels)
        if piece == 0:
            panels, order = spread_panels(panels, order, bits[2:])
        sib = swap_cores(own)
        last, chunks, parts, place = step == step_count - 1, [(own, sib, 0, 1)], [((step, shift), 1)], None
        if next_local < step_count:
            chunks.insert(0, (source, siblings, next_local, 1))
            parts.insert(0, ((next_local, 0), 1))
            next_local, place = next_local + 1, 0
        send, keep, *outs = partial_products(pos, chunks, base_weight, factors, last, place)
        if last:
            last_ranks[shift] = outs
            outs = []
        jobs = [(parts, send, keep, *outs)]
    jobs = [(parts, send, keep, jnp.bfloat16)]
    last_ranks, = gap(send, jobs, last_ranks)
    for shift, ranks in last_ranks.items():
        halved[RANK_NAME, shift] = second_half(ranks[1], swap_tensor(ranks[0], group // 2), 1, jnp.float32)[0]
    values = [halved[RANK_NAME, at] for at in range(n_rep)]
    ended[RANK_NAME] = (pick(values, (group_index - rep_index) % n_rep), *[
        to_group(pick(values, (group_index + hop - rep_index) % n_rep), hop) for hop in range(1, n_rep)
    ])
    rounded = gap(send, [])

    def rank_sum(name):
        kept, *received = [value[:, -rank_columns(factors):] for value in ended[name]]
        for value in received:
            kept = kept + value.astype(jnp.float32)
        return kept[:, :owned_slots * rank_size]

    finished = jnp.stack([rank_sum(step) for step in range(step_count - 1)] + [rank_sum(RANK_NAME)])
    finished = finished.astype(jnp.bfloat16).reshape(step_count, rows_mine, owned_slots, rank_size)
    finished = lax.optimization_barrier((finished, rounded))[0]
    ended.update((name, (kept, *received)) for name, kept, received in second_leg)
    masked = jnp.sum(
        jnp.where(owned_hot[None, :, :, None], finished, 0), axis=2, dtype=jnp.float32
    ).astype(jnp.bfloat16)
    chosen = masked
    for turn in range(1, n_owners):
        chosen = chosen + lax.ppermute(
            masked, ("rep", "sub"), [(i, (i + turn) % n_owners) for i in range(n_owners)]
        )
    panel_slots = jnp.stack([
        (tensor_index ^ at) * up_b.shape[0] + each for at in order for each in range(up_b.shape[0])
    ]).astype(jnp.int32)

    panels = [panel.reshape(-1, width) for panel in panels]
    partial, lifted = finish_steps(
        [ended[step] for step in range(step_count - 1)],
        chosen.reshape(step_count * rows_mine, rank_size),
        jnp.broadcast_to(my_slot, (step_count, rows_mine)).reshape(step_count * rows_mine, 1),
        panel_slots,
        panels,
    )
    return finish_last(partial, lifted, ended[step_count - 1])


def solution(mesh):
    return jax.shard_map(
        per_device,
        mesh=mesh,
        in_specs=(
            P(None, ("groups", "rep", "sub"), "tp"),
            P("tp", ("rep", "sub")),
            P(("rep", "sub"), "tp", None),
            P("tp", None, ("rep", "sub")),
            P("groups", None),
            P(),
        ),
        out_specs=P(None, ("groups", "tp"), ("rep", "sub")),
        check_vma=False,
    )
```

```python
import functools

import jax
import jax.numpy as jnp
from jax import lax
from jax.experimental import pallas as pl
from jax.experimental.pallas import tpu as pltpu
from jax.sharding import PartitionSpec as P

ADAPTER_SCALE = 0.5
BLOCK_N = 256
BLOCK = 1024
BUFFERS = 4
RANK_NAME = 1000
VMEM_BYTES = 17 * 1024 * 1024


def block_shape(depth, width):
    columns = BLOCK if width % BLOCK == 0 else width
    for size in (BLOCK, BLOCK // 2, BLOCK // 4):
        if depth % size == 0:
            return size, columns
    return depth, columns


def rank_columns(factors):
    slots, rank, _ = factors.shape
    return -(-slots * rank // 128) * 128


def matmul_body(spans, emitted, apart, pos_ref, *refs):
    sources = refs[:2 * len(spans)]
    w_ref, a_ref, send_ref, keep_ref = refs[2 * len(spans):2 * len(spans) + 4]
    outs = refs[2 * len(spans) + 4:-5]
    x_ref, w_buf, total_ref, x_sems, w_sems = refs[-5:]
    rows = send_ref.shape[0]
    depth, width = w_ref.shape
    slots, rank, _ = a_ref.shape
    buffers, block_k, block_w = w_buf.shape
    block_n = min(BLOCK_N, block_w)
    depths, count = depth // block_k, (depth // block_k) * (width // block_w)

    def fetch(block, slot):
        begin = pl.multiple_of(lax.rem(block, depths) * block_k, block_k)
        left = pl.multiple_of(lax.div(block, depths) * block_w, block_w)
        return pltpu.make_async_copy(
            w_ref.at[pl.ds(begin, block_k), pl.ds(left, block_w)], w_buf.at[slot], w_sems.at[slot]
        )

    own_at = pos_ref[0]
    copies, begin = [], 0
    for index, (first, steps) in enumerate(spans):
        for core, at in enumerate((own_at, 1 - own_at)):
            source = sources[2 * index + core]
            copies.append(pltpu.make_async_copy(
                source.at[pl.ds(first, steps)], x_ref.at[at, pl.ds(begin, steps)], x_sems.at[2 * index + core]
            ))
        begin += steps
    for copy in copies:
        copy.start()
    for block in range(buffers):
        fetch(jnp.int32(block), block).start()
    keep_ref[...] = jnp.zeros_like(keep_ref)
    total_ref[...] = jnp.zeros_like(total_ref)
    send_rank, keep_rank = outs[:2] if apart else (total_ref, keep_ref)
    if apart:
        send_rank[...] = jnp.zeros_like(send_rank)
        keep_rank[...] = jnp.zeros_like(keep_rank)
    for copy in copies:
        copy.wait()
    emit = None
    if emitted is not None:
        emit = pltpu.make_async_copy(
            x_ref.at[own_at, pl.ds(emitted, 1)], outs[-1], x_sems.at[2 * len(spans)]
        )
        emit.start()
    for slot in range(slots):
        x = x_ref[...].reshape(2 * rows, depth)
        part = lax.dot_general(
            x, a_ref[slot], (((1,), (1,)), ((), ())), preferred_element_type=jnp.float32
        )
        begin = slot * rank + (0 if apart else width)
        send_rank[:, begin:begin + rank] = part[:rows]
        keep_rank[:, begin:begin + rank] = part[rows:]

    @pl.loop(0, count)
    def _(block):
        slot = lax.rem(block, buffers)
        fetch(block, slot).wait()
        inner = pl.ds(pl.multiple_of(lax.rem(block, depths) * block_k, block_k), block_k)
        left = pl.multiple_of(lax.div(block, depths) * block_w, block_w)
        x = x_ref[:, :, :, inner].reshape(2 * rows, block_k)
        for place in range(block_w // block_n):
            columns = pl.ds(left + place * block_n, block_n)
            term = jnp.dot(
                x, w_buf[slot, :, place * block_n:(place + 1) * block_n], preferred_element_type=jnp.float32
            )
            total_ref[:, columns] += term[:rows]
            keep_ref[:, columns] += term[rows:]

        @pl.when(block + buffers < count)
        def _():
            fetch(block + buffers, slot).start()

    send_ref[...] = total_ref[...].astype(send_ref.dtype)
    if emit is not None:
        emit.wait()


def partial_products(pos, chunks, weight, factors, apart=False, emitted=None):
    _, per_block, depth = chunks[0][0].shape
    width = weight.shape[1]
    spans = tuple((first, steps) for _, _, first, steps in chunks)
    steps = sum(length for _, length in spans)
    rows = steps * per_block
    block_k, block_w = block_shape(depth, width)
    buffers = min(BUFFERS, (depth // block_k) * (width // block_w))
    any_spec = pl.BlockSpec(memory_space=pl.ANY)
    vmem_spec = pl.BlockSpec(memory_space=pltpu.VMEM)
    extra = rank_columns(factors)
    columns = width + (0 if apart else extra)
    out_shape = [
        jax.ShapeDtypeStruct((rows, columns), jnp.bfloat16),
        jax.ShapeDtypeStruct((rows, columns), jnp.float32),
    ] + [jax.ShapeDtypeStruct((rows, extra), jnp.float32)] * (2 if apart else 0)
    out_specs = [vmem_spec] * len(out_shape)
    if emitted is not None:
        out_shape.append(jax.ShapeDtypeStruct((1, per_block, depth), jnp.bfloat16))
        out_specs.append(any_spec)
    return pl.pallas_call(
        functools.partial(matmul_body, spans, emitted, apart),
        in_specs=[pl.BlockSpec(memory_space=pltpu.SMEM)] + [any_spec] * (2 * len(chunks) + 1) + [vmem_spec],
        out_specs=out_specs,
        out_shape=out_shape,
        scratch_shapes=[
            pltpu.VMEM((2, steps, per_block, depth), jnp.bfloat16),
            pltpu.VMEM((buffers, block_k, block_w), jnp.bfloat16),
            pltpu.VMEM((rows, columns), jnp.float32),
            pltpu.SemaphoreType.DMA((2 * len(chunks) + 1,)),
            pltpu.SemaphoreType.DMA((buffers,)),
        ],
        compiler_params=pltpu.CompilerParams(vmem_limit_bytes=VMEM_BYTES),
        cost_estimate=pl.CostEstimate(flops=0, bytes_accessed=0, transcendentals=0),
        name="partial_products",
    )(pos, *[source for own, sib, _, _ in chunks for source in (own, sib)], weight, factors)


def finish_body(received, panels, chosen_ref, slot_ref, order_ref, *refs):
    panel_refs, refs = refs[:panels], refs[panels:]
    per_panel = panel_refs[0].shape[0]
    out_ref, lifted_ref, done_ref, sem = refs[-4:]
    steps, rows, width = done_ref.shape
    rank = chosen_ref.shape[1]
    chosen = chosen_ref[...]
    slot = slot_ref[...]
    spread = jnp.concatenate(
        [
            jnp.where(slot == order_ref[place], chosen, jnp.zeros_like(chosen))
            for place in range(panels * per_panel // rank)
        ],
        axis=1,
    )
    block_n = min(BLOCK_N, width)
    for place in range(width // block_n):
        columns = slice(place * block_n, (place + 1) * block_n)
        panel = jnp.concatenate([panel_ref[:, columns] for panel_ref in panel_refs], axis=0)
        lifted = jnp.dot(spread, panel, preferred_element_type=jnp.float32).astype(jnp.bfloat16)
        for step in range(steps):
            total = refs[step * (received + 1)][:, columns]
            for value_ref in refs[step * (received + 1) + 1:(step + 1) * (received + 1)]:
                total = total + value_ref[:, columns].astype(jnp.float32)
            value = total + ADAPTER_SCALE * lifted[step * rows:(step + 1) * rows].astype(jnp.float32)
            done_ref[step, :, columns] = value.astype(done_ref.dtype)
        lifted_ref[:, columns] = lifted[steps * rows:]
    copy = pltpu.make_async_copy(done_ref, out_ref.at[pl.ds(0, steps)], sem)
    copy.start()
    copy.wait()


def finish_steps(totals, chosen, slots, order, panels):
    steps, width = len(totals), panels[0].shape[1]
    rows = chosen.shape[0] // (steps + 1)
    vmem_spec = pl.BlockSpec(memory_space=pltpu.VMEM)
    arrays = [value for total in totals for value in total]
    return pl.pallas_call(
        functools.partial(finish_body, len(totals[0]) - 1, len(panels)),
        in_specs=[vmem_spec, vmem_spec, pl.BlockSpec(memory_space=pltpu.SMEM)] + [vmem_spec] * (len(panels) + len(arrays)),
        out_specs=[pl.BlockSpec(memory_space=pl.ANY), vmem_spec],
        out_shape=[
            jax.ShapeDtypeStruct((steps + 1, rows, width), jnp.bfloat16),
            jax.ShapeDtypeStruct((rows, width), jnp.bfloat16),
        ],
        scratch_shapes=[pltpu.VMEM((steps, rows, width), jnp.bfloat16), pltpu.SemaphoreType.DMA],
        compiler_params=pltpu.CompilerParams(vmem_limit_bytes=VMEM_BYTES),
        cost_estimate=pl.CostEstimate(flops=0, bytes_accessed=0, transcendentals=0),
        name="finish_steps",
    )(chosen, slots, order, *panels, *arrays)


def last_body(partial_ref, lifted_ref, *refs):
    out_ref, done_ref, sem = refs[-3:]
    total = refs[0][...]
    for value_ref in refs[1:-3]:
        total = total + value_ref[...].astype(jnp.float32)
    value = total + ADAPTER_SCALE * lifted_ref[...].astype(jnp.float32)
    done_ref[0] = value.astype(done_ref.dtype)
    copy = pltpu.make_async_copy(done_ref, out_ref.at[pl.ds(out_ref.shape[0] - 1, 1)], sem)
    copy.start()
    copy.wait()


def finish_last(partial, lifted, arrays):
    vmem_spec = pl.BlockSpec(memory_space=pltpu.VMEM)
    any_spec = pl.BlockSpec(memory_space=pl.ANY)
    return pl.pallas_call(
        last_body,
        in_specs=[any_spec] + [vmem_spec] * (1 + len(arrays)),
        out_specs=any_spec,
        out_shape=jax.ShapeDtypeStruct(partial.shape, partial.dtype),
        input_output_aliases={0: 0},
        scratch_shapes=[pltpu.VMEM((1,) + partial.shape[1:], partial.dtype), pltpu.SemaphoreType.DMA],
        compiler_params=pltpu.CompilerParams(vmem_limit_bytes=VMEM_BYTES),
        cost_estimate=pl.CostEstimate(flops=0, bytes_accessed=0, transcendentals=0),
        name="finish_last",
    )(partial, lifted, *arrays)


def per_device(hidden, base_weight, down_a, up_b, adapter_ids, owner_map):
    step_count, per_block, _ = hidden.shape
    n_tensor = lax.axis_size("tp")
    n_rep = lax.axis_size("rep")
    n_sub = lax.axis_size("sub")
    n_owners = n_rep * n_sub
    tensor_index = lax.axis_index("tp")
    rep_index = lax.axis_index("rep")
    sub_index = lax.axis_index("sub")
    owner_index = lax.axis_index(("rep", "sub"))
    requests = per_block * n_owners
    rows_mine = requests // n_tensor
    group = n_tensor // n_rep
    group_index = tensor_index // group
    owned_slots, _, rank_size = down_a.shape
    slot_count = owned_slots * n_owners
    width = base_weight.shape[1]

    def after(value, *done):
        return lax.optimization_barrier((value, *done))[0]

    def swap_cores(value):
        return lax.ppermute(value, "sub", [(i, i ^ 1) for i in range(n_sub)])

    def from_rep(value, shift):
        return lax.ppermute(value, "rep", [((i + shift) % n_rep, i) for i in range(n_rep)])

    def swap_tensor(value, bit):
        return lax.ppermute(value, "tp", [(i, i ^ bit) for i in range(n_tensor)])

    def to_group(value, hop):
        moved = group * hop
        return lax.ppermute(value, "tp", [(i, (i + moved) % n_tensor) for i in range(n_tensor)])

    def pick(values, index):
        value = values[0]
        for at in range(1, len(values)):
            value = jnp.where(index == at, values[at], value)
        return value

    keeps = (tensor_index // (group // 2)) % 2
    pos = (sub_index == keeps).astype(jnp.int32).reshape(1)

    siblings = swap_cores(hidden)
    pieces = [(step, shift) for step in range(step_count) for shift in range(1, n_rep)]
    source = pltpu.with_memory_space_constraint(hidden, pltpu.HBM)
    weight = pltpu.with_memory_space_constraint(base_weight, pltpu.HBM)
    remote = {(0, shift): from_rep(hidden[:1], shift) for shift in range(1, n_rep)}

    def spread_panels(panels, order, bits):
        for bit in bits:
            panels = panels + [swap_tensor(panel, bit) for panel in panels]
            order = order + [at ^ bit for at in order]
        return panels, order

    bits = [n_tensor >> at for at in range(1, n_tensor.bit_length())]
    order = [0] + [at for at in range(1, n_tensor) if at % (n_tensor // 4) == 0]
    panels = [up_b] + [swap_tensor(up_b, at) for at in order[1:]]
    my_ids = lax.dynamic_slice_in_dim(adapter_ids, tensor_index * rows_mine, rows_mine)
    iota = lax.broadcasted_iota(jnp.int32, (rows_mine, slot_count), 1)
    my_slot = jnp.sum((my_ids == iota).astype(jnp.int32) * owner_map[None, :], axis=1)
    owned_hot = my_slot[:, None] == (
        owner_index * owned_slots + lax.broadcasted_iota(jnp.int32, (rows_mine, owned_slots), 1)
    )

    first_leg, halved, begun, second_leg, ended = [], {}, set(), [], {}

    def second_half(total, received, steps, kind):
        total = total + received.astype(jnp.float32)
        rows, columns = total.shape
        extent, bit = rows // steps, group // 4
        while bit:
            extent //= 2
            halves = total.reshape(steps, 2, extent, columns)
            mine = (tensor_index // bit) % 2
            kept = lax.dynamic_index_in_dim(halves, mine, 1, keepdims=False)
            sent = lax.dynamic_index_in_dim(halves, 1 - mine, 1, keepdims=False)
            total = kept + swap_tensor(sent.astype(kind), bit).astype(jnp.float32)
            bit //= 2
        return total.reshape(steps, extent, columns)

    def gap(token, jobs, *extra):
        nonlocal first_leg, second_leg
        for parts, received, keep, kind in first_leg:
            steps = sum(length for _, length in parts)
            total, begin = second_half(after(keep, token), received, steps, kind), 0
            for key, length in parts:
                for at in range(begin, begin + length):
                    halved[key[0] + at - begin, key[1]] = total[at]
                    if (key[0] + at - begin, key[1]) == (step_count - 1, 0):
                        halved[RANK_NAME, 0] = total[at][:, width:]
                begin += length
        closed = {}
        for name, kept, received in second_leg:
            closed[name] = (after(kept, token), *received)
        started, sends = [], []
        for name in sorted({name for name, _ in halved}):
            if name in begun or name == RANK_NAME or any((name, at) not in halved for at in range(n_rep)):
                continue
            begun.add(name)
            values = [halved[name, at] for at in range(n_rep)]
            columns = min(value.shape[1] for value in values)
            values = [value[:, :columns] for value in values]
            kept = pick(values, (group_index - rep_index) % n_rep)
            sent = [pick(values, (group_index + hop - rep_index) % n_rep).astype(jnp.bfloat16) for hop in range(1, n_rep)]
            started.append((name, kept))
            sends.append(sent)
        first_sends = [job[1] for job in jobs]
        first_sends, sends, extra, closed, _ = lax.optimization_barrier((first_sends, sends, extra, closed, token))
        ended.update(closed)
        first_leg = [
            (parts, swap_tensor(send, group // 2), keep, kind) for (parts, _, keep, kind), send in zip(jobs, first_sends)
        ]
        second_leg = [
            (name, kept, [to_group(value, hop + 1) for hop, value in enumerate(sent)])
            for (name, kept), sent in zip(started, sends)
        ]
        return extra if extra else [sent for sent in sends]

    factors = jnp.swapaxes(down_a, 1, 2)

    half = step_count // 2
    jobs, next_local, last_ranks = [([((0, 0), half)], *partial_products(
        pos, [(source, siblings, 0, half)], weight, factors, emitted=half - 1
    ))], half, {}
    for piece, (step, shift) in enumerate(pieces):
        (parts, send, keep, *emitted), *others = jobs
        jobs = [(parts, send, keep, jnp.bfloat16)]
        if emitted:
            for along in range(1, n_rep):
                remote[next_local - 1, along] = from_rep(emitted[0], along)
        own, siblings, panels = gap(send, jobs, remote[step, shift], siblings, panels)
        if piece == 0:
            panels, order = spread_panels(panels, order, bits[2:])
        sib = swap_cores(own)
        last, chunks, parts, place = step == step_count - 1, [(own, sib, 0, 1)], [((step, shift), 1)], None
        if next_local < step_count:
            chunks.insert(0, (source, siblings, next_local, 1))
            parts.insert(0, ((next_local, 0), 1))
            next_local, place = next_local + 1, 0
        send, keep, *outs = partial_products(pos, chunks, weight, factors, last, place)
        if last:
            last_ranks[shift] = outs
            outs = []
        jobs = [(parts, send, keep, *outs)]
    jobs = [(parts, send, keep, jnp.bfloat16)]
    last_ranks, = gap(send, jobs, last_ranks)
    for shift, ranks in last_ranks.items():
        halved[RANK_NAME, shift] = second_half(ranks[1], swap_tensor(ranks[0], group // 2), 1, jnp.float32)[0]
    values = [halved[RANK_NAME, at] for at in range(n_rep)]
    ended[RANK_NAME] = (pick(values, (group_index - rep_index) % n_rep), *[
        to_group(pick(values, (group_index + hop - rep_index) % n_rep), hop) for hop in range(1, n_rep)
    ])
    rounded = gap(send, [])

    def rank_sum(name):
        kept, *received = [value[:, -rank_columns(factors):] for value in ended[name]]
        for value in received:
            kept = kept + value.astype(jnp.float32)
        return kept[:, :owned_slots * rank_size]

    finished = jnp.stack([rank_sum(step) for step in range(step_count - 1)] + [rank_sum(RANK_NAME)])
    finished = finished.astype(jnp.bfloat16).reshape(step_count, rows_mine, owned_slots, rank_size)
    finished = lax.optimization_barrier((finished, rounded))[0]
    ended.update((name, (kept, *received)) for name, kept, received in second_leg)
    masked = jnp.sum(
        jnp.where(owned_hot[None, :, :, None], finished, 0), axis=2, dtype=jnp.float32
    ).astype(jnp.bfloat16)
    chosen = masked
    for turn in range(1, n_owners):
        chosen = chosen + lax.ppermute(
            masked, ("rep", "sub"), [(i, (i + turn) % n_owners) for i in range(n_owners)]
        )
    panel_slots = jnp.stack([
        (tensor_index ^ at) * up_b.shape[0] + each for at in order for each in range(up_b.shape[0])
    ]).astype(jnp.int32)

    panels = [panel.reshape(-1, width) for panel in panels]
    partial, lifted = finish_steps(
        [ended[step] for step in range(step_count - 1)],
        chosen.reshape(step_count * rows_mine, rank_size),
        jnp.broadcast_to(my_slot, (step_count, rows_mine)).reshape(step_count * rows_mine, 1),
        panel_slots,
        panels,
    )
    return finish_last(partial, lifted, ended[step_count - 1])


def solution(mesh):
    return jax.shard_map(
        per_device,
        mesh=mesh,
        in_specs=(
            P(None, ("groups", "rep", "sub"), "tp"),
            P("tp", ("rep", "sub")),
            P(("rep", "sub"), "tp", None),
            P("tp", None, ("rep", "sub")),
            P("groups", None),
            P(),
        ),
        out_specs=P(None, ("groups", "tp"), ("rep", "sub")),
        check_vma=False,
    )
```

```python
import functools

import jax
import jax.numpy as jnp
from jax import lax
from jax.experimental import pallas as pl
from jax.experimental.pallas import tpu as pltpu
from jax.sharding import PartitionSpec as P

ADAPTER_SCALE = 0.5
BLOCK_N = 256
BLOCK = 1024
BUFFERS = 4
RANK_NAME = 1000
VMEM_BYTES = 22 * 1024 * 1024


def block_shape(depth, width):
    columns = BLOCK if width % BLOCK == 0 else width
    for size in (BLOCK, BLOCK // 2, BLOCK // 4):
        if depth % size == 0:
            return size, columns
    return depth, columns


def rank_columns(factors):
    slots, rank, _ = factors.shape
    return -(-slots * rank // 128) * 128


def matmul_body(spans, emitted, apart, pos_ref, *refs):
    sources = refs[:2 * len(spans)]
    w_ref, a_ref, send_ref, keep_ref = refs[2 * len(spans):2 * len(spans) + 4]
    outs = refs[2 * len(spans) + 4:-5]
    x_ref, w_buf, total_ref, x_sems, w_sems = refs[-5:]
    rows = send_ref.shape[0]
    depth, width = w_ref.shape
    slots, rank, _ = a_ref.shape
    buffers, block_k, block_w = w_buf.shape
    block_n = min(BLOCK_N, block_w)
    depths, count = depth // block_k, (depth // block_k) * (width // block_w)

    def fetch(block, slot):
        begin = pl.multiple_of(lax.rem(block, depths) * block_k, block_k)
        left = pl.multiple_of(lax.div(block, depths) * block_w, block_w)
        return pltpu.make_async_copy(
            w_ref.at[pl.ds(begin, block_k), pl.ds(left, block_w)], w_buf.at[slot], w_sems.at[slot]
        )

    own_at = pos_ref[0]
    copies, begin = [], 0
    for index, (first, steps) in enumerate(spans):
        for core, at in enumerate((own_at, 1 - own_at)):
            source = sources[2 * index + core]
            copies.append(pltpu.make_async_copy(
                source.at[pl.ds(first, steps)], x_ref.at[at, pl.ds(begin, steps)], x_sems.at[2 * index + core]
            ))
        begin += steps
    for copy in copies:
        copy.start()
    for block in range(buffers):
        fetch(jnp.int32(block), block).start()
    keep_ref[...] = jnp.zeros_like(keep_ref)
    total_ref[...] = jnp.zeros_like(total_ref)
    send_rank, keep_rank = outs[:2] if apart else (total_ref, keep_ref)
    if apart:
        send_rank[...] = jnp.zeros_like(send_rank)
        keep_rank[...] = jnp.zeros_like(keep_rank)
    for copy in copies:
        copy.wait()
    emits = [
        pltpu.make_async_copy(x_ref.at[own_at, pl.ds(block, 1)], out_ref, x_sems.at[2 * len(spans) + index])
        for index, (block, out_ref) in enumerate(zip(emitted, outs[2 if apart else 0:]))
    ]
    for emit in emits:
        emit.start()
    for slot in range(slots):
        x = x_ref[...].reshape(2 * rows, depth)
        part = lax.dot_general(
            x, a_ref[slot], (((1,), (1,)), ((), ())), preferred_element_type=jnp.float32
        )
        begin = slot * rank + (0 if apart else width)
        send_rank[:, begin:begin + rank] = part[:rows]
        keep_rank[:, begin:begin + rank] = part[rows:]

    @pl.loop(0, count)
    def _(block):
        slot = lax.rem(block, buffers)
        fetch(block, slot).wait()
        inner = pl.ds(pl.multiple_of(lax.rem(block, depths) * block_k, block_k), block_k)
        left = pl.multiple_of(lax.div(block, depths) * block_w, block_w)
        x = x_ref[:, :, :, inner].reshape(2 * rows, block_k)
        for place in range(block_w // block_n):
            columns = pl.ds(left + place * block_n, block_n)
            term = jnp.dot(
                x, w_buf[slot, :, place * block_n:(place + 1) * block_n], preferred_element_type=jnp.float32
            )
            total_ref[:, columns] += term[:rows]
            keep_ref[:, columns] += term[rows:]

        @pl.when(block + buffers < count)
        def _():
            fetch(block + buffers, slot).start()

    send_ref[...] = total_ref[...].astype(send_ref.dtype)
    for emit in emits:
        emit.wait()


def partial_products(pos, chunks, weight, factors, apart=False, emitted=()):
    _, per_block, depth = chunks[0][0].shape
    width = weight.shape[1]
    spans = tuple((first, steps) for _, _, first, steps in chunks)
    steps = sum(length for _, length in spans)
    rows = steps * per_block
    block_k, block_w = block_shape(depth, width)
    buffers = min(BUFFERS, (depth // block_k) * (width // block_w))
    any_spec = pl.BlockSpec(memory_space=pl.ANY)
    vmem_spec = pl.BlockSpec(memory_space=pltpu.VMEM)
    extra = rank_columns(factors)
    columns = width + (0 if apart else extra)
    out_shape = [
        jax.ShapeDtypeStruct((rows, columns), jnp.bfloat16),
        jax.ShapeDtypeStruct((rows, columns), jnp.float32),
    ] + [jax.ShapeDtypeStruct((rows, extra), jnp.float32)] * (2 if apart else 0)
    out_specs = [vmem_spec] * len(out_shape)
    out_shape += [jax.ShapeDtypeStruct((1, per_block, depth), jnp.bfloat16)] * len(emitted)
    out_specs += [any_spec] * len(emitted)
    return pl.pallas_call(
        functools.partial(matmul_body, spans, emitted, apart),
        in_specs=[pl.BlockSpec(memory_space=pltpu.SMEM)] + [any_spec] * (2 * len(chunks) + 1) + [vmem_spec],
        out_specs=out_specs,
        out_shape=out_shape,
        scratch_shapes=[
            pltpu.VMEM((2, steps, per_block, depth), jnp.bfloat16),
            pltpu.VMEM((buffers, block_k, block_w), jnp.bfloat16),
            pltpu.VMEM((rows, columns), jnp.float32),
            pltpu.SemaphoreType.DMA((2 * len(chunks) + len(emitted),)),
            pltpu.SemaphoreType.DMA((buffers,)),
        ],
        compiler_params=pltpu.CompilerParams(vmem_limit_bytes=VMEM_BYTES),
        cost_estimate=pl.CostEstimate(flops=0, bytes_accessed=0, transcendentals=0),
        name="partial_products",
    )(pos, *[source for own, sib, _, _ in chunks for source in (own, sib)], weight, factors)


def finish_body(received, panels, chosen_ref, slot_ref, order_ref, *refs):
    panel_refs, refs = refs[:panels], refs[panels:]
    per_panel = panel_refs[0].shape[0]
    out_ref, lifted_ref, done_ref, sem = refs[-4:]
    steps, rows, width = done_ref.shape
    rank = chosen_ref.shape[1]
    chosen = chosen_ref[...]
    slot = slot_ref[...]
    spread = jnp.concatenate(
        [
            jnp.where(slot == order_ref[place], chosen, jnp.zeros_like(chosen))
            for place in range(panels * per_panel // rank)
        ],
        axis=1,
    )
    block_n = min(BLOCK_N, width)
    for place in range(width // block_n):
        columns = slice(place * block_n, (place + 1) * block_n)
        panel = jnp.concatenate([panel_ref[:, columns] for panel_ref in panel_refs], axis=0)
        lifted = jnp.dot(spread, panel, preferred_element_type=jnp.float32).astype(jnp.bfloat16)
        for step in range(steps):
            total = refs[step * (received + 1)][:, columns]
            for value_ref in refs[step * (received + 1) + 1:(step + 1) * (received + 1)]:
                total = total + value_ref[:, columns].astype(jnp.float32)
            value = total + ADAPTER_SCALE * lifted[step * rows:(step + 1) * rows].astype(jnp.float32)
            done_ref[step, :, columns] = value.astype(done_ref.dtype)
        lifted_ref[:, columns] = lifted[steps * rows:]
    copy = pltpu.make_async_copy(done_ref, out_ref.at[pl.ds(0, steps)], sem)
    copy.start()
    copy.wait()


def finish_steps(totals, chosen, slots, order, panels):
    steps, width = len(totals), panels[0].shape[1]
    rows = chosen.shape[0] // (steps + 1)
    vmem_spec = pl.BlockSpec(memory_space=pltpu.VMEM)
    arrays = [value for total in totals for value in total]
    return pl.pallas_call(
        functools.partial(finish_body, len(totals[0]) - 1, len(panels)),
        in_specs=[vmem_spec, vmem_spec, pl.BlockSpec(memory_space=pltpu.SMEM)] + [vmem_spec] * (len(panels) + len(arrays)),
        out_specs=[pl.BlockSpec(memory_space=pl.ANY), vmem_spec],
        out_shape=[
            jax.ShapeDtypeStruct((steps + 1, rows, width), jnp.bfloat16),
            jax.ShapeDtypeStruct((rows, width), jnp.bfloat16),
        ],
        scratch_shapes=[pltpu.VMEM((steps, rows, width), jnp.bfloat16), pltpu.SemaphoreType.DMA],
        compiler_params=pltpu.CompilerParams(vmem_limit_bytes=VMEM_BYTES),
        cost_estimate=pl.CostEstimate(flops=0, bytes_accessed=0, transcendentals=0),
        name="finish_steps",
    )(chosen, slots, order, *panels, *arrays)


def last_body(partial_ref, lifted_ref, *refs):
    out_ref, done_ref, sem = refs[-3:]
    total = refs[0][...]
    for value_ref in refs[1:-3]:
        total = total + value_ref[...].astype(jnp.float32)
    value = total + ADAPTER_SCALE * lifted_ref[...].astype(jnp.float32)
    done_ref[0] = value.astype(done_ref.dtype)
    copy = pltpu.make_async_copy(done_ref, out_ref.at[pl.ds(out_ref.shape[0] - 1, 1)], sem)
    copy.start()
    copy.wait()


def finish_last(partial, lifted, arrays):
    vmem_spec = pl.BlockSpec(memory_space=pltpu.VMEM)
    any_spec = pl.BlockSpec(memory_space=pl.ANY)
    return pl.pallas_call(
        last_body,
        in_specs=[any_spec] + [vmem_spec] * (1 + len(arrays)),
        out_specs=any_spec,
        out_shape=jax.ShapeDtypeStruct(partial.shape, partial.dtype),
        input_output_aliases={0: 0},
        scratch_shapes=[pltpu.VMEM((1,) + partial.shape[1:], partial.dtype), pltpu.SemaphoreType.DMA],
        compiler_params=pltpu.CompilerParams(vmem_limit_bytes=VMEM_BYTES),
        cost_estimate=pl.CostEstimate(flops=0, bytes_accessed=0, transcendentals=0),
        name="finish_last",
    )(partial, lifted, *arrays)


def per_device(hidden, base_weight, down_a, up_b, adapter_ids, owner_map):
    step_count, per_block, _ = hidden.shape
    n_tensor = lax.axis_size("tp")
    n_rep = lax.axis_size("rep")
    n_sub = lax.axis_size("sub")
    n_owners = n_rep * n_sub
    tensor_index = lax.axis_index("tp")
    rep_index = lax.axis_index("rep")
    sub_index = lax.axis_index("sub")
    owner_index = lax.axis_index(("rep", "sub"))
    requests = per_block * n_owners
    rows_mine = requests // n_tensor
    group = n_tensor // n_rep
    group_index = tensor_index // group
    owned_slots, _, rank_size = down_a.shape
    slot_count = owned_slots * n_owners
    width = base_weight.shape[1]

    def after(value, *done):
        return lax.optimization_barrier((value, *done))[0]

    def swap_cores(value):
        return lax.ppermute(value, "sub", [(i, i ^ 1) for i in range(n_sub)])

    def from_rep(value, shift):
        return lax.ppermute(value, "rep", [((i + shift) % n_rep, i) for i in range(n_rep)])

    def swap_tensor(value, bit):
        return lax.ppermute(value, "tp", [(i, i ^ bit) for i in range(n_tensor)])

    def to_group(value, hop):
        moved = group * hop
        return lax.ppermute(value, "tp", [(i, (i + moved) % n_tensor) for i in range(n_tensor)])

    def pick(values, index):
        value = values[0]
        for at in range(1, len(values)):
            value = jnp.where(index == at, values[at], value)
        return value

    keeps = (tensor_index // (group // 2)) % 2
    pos = (sub_index == keeps).astype(jnp.int32).reshape(1)

    siblings = swap_cores(hidden)
    pieces = [(step, shift) for step in range(step_count) for shift in range(1, n_rep)]
    source = pltpu.with_memory_space_constraint(hidden, pltpu.HBM)
    weight = pltpu.with_memory_space_constraint(base_weight, pltpu.HBM)
    remote = {(0, shift): from_rep(hidden[:1], shift) for shift in range(1, n_rep)}

    def spread_panels(panels, order, bits):
        for bit in bits:
            panels = panels + [swap_tensor(panel, bit) for panel in panels]
            order = order + [at ^ bit for at in order]
        return panels, order

    bits = [n_tensor >> at for at in range(1, n_tensor.bit_length())]
    order = [0] + [at for at in range(1, n_tensor) if at % (n_tensor // 4) == 0]
    panels = [up_b] + [swap_tensor(up_b, at) for at in order[1:]]
    my_ids = lax.dynamic_slice_in_dim(adapter_ids, tensor_index * rows_mine, rows_mine)
    iota = lax.broadcasted_iota(jnp.int32, (rows_mine, slot_count), 1)
    my_slot = jnp.sum((my_ids == iota).astype(jnp.int32) * owner_map[None, :], axis=1)
    owned_hot = my_slot[:, None] == (
        owner_index * owned_slots + lax.broadcasted_iota(jnp.int32, (rows_mine, owned_slots), 1)
    )

    first_leg, halved, begun, second_leg, ended = [], {}, set(), [], {}

    def second_half(total, received, steps, kind):
        total = total + received.astype(jnp.float32)
        rows, columns = total.shape
        extent, bit = rows // steps, group // 4
        while bit:
            extent //= 2
            halves = total.reshape(steps, 2, extent, columns)
            mine = (tensor_index // bit) % 2
            kept = lax.dynamic_index_in_dim(halves, mine, 1, keepdims=False)
            sent = lax.dynamic_index_in_dim(halves, 1 - mine, 1, keepdims=False)
            total = kept + swap_tensor(sent.astype(kind), bit).astype(jnp.float32)
            bit //= 2
        return total.reshape(steps, extent, columns)

    def gap(token, jobs, short=False):
        nonlocal first_leg, second_leg
        for parts, received, keep, kind in first_leg:
            steps = sum(length for _, length in parts)
            total, begin = second_half(after(keep, token), received, steps, kind), 0
            for key, length in parts:
                for at in range(begin, begin + length):
                    halved[key[0] + at - begin, key[1]] = total[at]
                    if (key[0] + at - begin, key[1]) == (step_count - 1, 0):
                        halved[RANK_NAME, 0] = total[at][:, width:]
                begin += length
        closed, waiting = {}, []
        for name, kept, received, lag in second_leg:
            if short or lag > 1:
                waiting.append((name, kept, received, lag if short else lag - 1))
            else:
                closed[name] = (after(kept, token), *received)
        started, sends = [], []
        for name in sorted({name for name, _ in halved}):
            if name in begun or name == RANK_NAME or any((name, at) not in halved for at in range(n_rep)):
                continue
            begun.add(name)
            values = [halved[name, at] for at in range(n_rep)]
            columns = min(value.shape[1] for value in values)
            values = [value[:, :columns] for value in values]
            kept = pick(values, (group_index - rep_index) % n_rep)
            sends.append([
                pick(values, (group_index + hop - rep_index) % n_rep).astype(jnp.bfloat16) for hop in range(1, n_rep)
            ])
            started.append((name, kept))
        sends, token = lax.optimization_barrier((sends, token))
        first_sends, closed = lax.optimization_barrier(([job[1] for job in jobs], closed))
        ended.update(closed)
        first_leg = [
            (parts, swap_tensor(send, group // 2), keep, kind) for (parts, _, keep, kind), send in zip(jobs, first_sends)
        ]
        second_leg = waiting + [
            (name, kept, [to_group(value, hop + 1) for hop, value in enumerate(sent)], 2 if short else 1)
            for (name, kept), sent in zip(started, sends)
        ]
        return sends

    factors = jnp.swapaxes(down_a, 1, 2)

    lead = step_count - 1
    parts, last_ranks = [((0, 0), lead)], {}
    send, keep, *emitted = partial_products(
        pos, [(source, siblings, 0, lead)], weight, factors, emitted=tuple(range(1, lead))
    )
    for step, rows in enumerate(emitted, 1):
        remote.update({(step, shift): from_rep(rows, shift) for shift in range(1, n_rep)})
    for piece, (step, shift) in enumerate(pieces):
        sends = gap(send, [(parts, send, keep, jnp.bfloat16)])
        own, panels, _ = lax.optimization_barrier((remote[step, shift], panels, send))
        if piece == 0:
            panels, order = spread_panels(panels, order, bits[2:])
        sib = swap_cores(own)
        held = [sends, siblings] if piece == 0 else [sends]
        if piece == len(pieces) - 1:
            held += gap(lax.optimization_barrier((send, sends))[0], [], short=True)
        own, sib, held = lax.optimization_barrier((own, sib, held))
        last, chunks, parts, places = step == step_count - 1, [(own, sib, 0, 1)], [((step, shift), 1)], ()
        if piece == 0:
            chunks.insert(0, (source, held[1], lead, 1))
            parts.insert(0, ((lead, 0), 1))
            places = (0,)
        send, keep, *outs = partial_products(pos, chunks, weight, factors, last, places)
        if last:
            last_ranks[shift] = outs
        elif outs:
            remote.update({(lead, along): from_rep(outs[0], along) for along in range(1, n_rep)})
    gap(send, [(parts, send, keep, jnp.bfloat16)])
    for shift, ranks in last_ranks.items():
        halved[RANK_NAME, shift] = second_half(ranks[1], swap_tensor(ranks[0], group // 2), 1, jnp.float32)[0]
    values = [halved[RANK_NAME, at] for at in range(n_rep)]
    ended[RANK_NAME] = (pick(values, (group_index - rep_index) % n_rep), *[
        to_group(pick(values, (group_index + hop - rep_index) % n_rep), hop) for hop in range(1, n_rep)
    ])
    rounded = gap(send, [])

    def rank_sum(name):
        kept, *received = [value[:, -rank_columns(factors):] for value in ended[name]]
        for value in received:
            kept = kept + value.astype(jnp.float32)
        return kept[:, :owned_slots * rank_size]

    finished = jnp.stack([rank_sum(step) for step in range(step_count - 1)] + [rank_sum(RANK_NAME)])
    finished = finished.astype(jnp.bfloat16).reshape(step_count, rows_mine, owned_slots, rank_size)
    finished = lax.optimization_barrier((finished, rounded))[0]
    ended.update((name, (kept, *received)) for name, kept, received, _ in second_leg)
    masked = jnp.sum(
        jnp.where(owned_hot[None, :, :, None], finished, 0), axis=2, dtype=jnp.float32
    ).astype(jnp.bfloat16)
    chosen = masked
    for turn in range(1, n_owners):
        chosen = chosen + lax.ppermute(
            masked, ("rep", "sub"), [(i, (i + turn) % n_owners) for i in range(n_owners)]
        )
    panel_slots = jnp.stack([
        (tensor_index ^ at) * up_b.shape[0] + each for at in order for each in range(up_b.shape[0])
    ]).astype(jnp.int32)

    panels = [panel.reshape(-1, width) for panel in panels]
    partial, lifted = finish_steps(
        [ended[step] for step in range(step_count - 1)],
        chosen.reshape(step_count * rows_mine, rank_size),
        jnp.broadcast_to(my_slot, (step_count, rows_mine)).reshape(step_count * rows_mine, 1),
        panel_slots,
        panels,
    )
    return finish_last(partial, lifted, ended[step_count - 1])


def solution(mesh):
    return jax.shard_map(
        per_device,
        mesh=mesh,
        in_specs=(
            P(None, ("groups", "rep", "sub"), "tp"),
            P("tp", ("rep", "sub")),
            P(("rep", "sub"), "tp", None),
            P("tp", None, ("rep", "sub")),
            P("groups", None),
            P(),
        ),
        out_specs=P(None, ("groups", "tp"), ("rep", "sub")),
        check_vma=False,
    )
```

```python
import functools

import jax
import jax.numpy as jnp
from jax import lax
from jax.experimental import pallas as pl
from jax.experimental.pallas import tpu as pltpu
from jax.sharding import PartitionSpec as P

ADAPTER_SCALE = 0.5
BLOCK_N = 256
BLOCK = 1024
BUFFERS = 4
RANK_NAME = 1000
VMEM_BYTES = 17 * 1024 * 1024


def block_shape(depth, width):
    columns = BLOCK if width % BLOCK == 0 else width
    for size in (BLOCK, BLOCK // 2, BLOCK // 4):
        if depth % size == 0:
            return size, columns
    return depth, columns


def rank_columns(factors):
    slots, rank, _ = factors.shape
    return -(-slots * rank // 128) * 128


def matmul_body(spans, emitted, apart, pos_ref, *refs):
    sources = refs[:2 * len(spans)]
    w_ref, a_ref, send_ref, keep_ref = refs[2 * len(spans):2 * len(spans) + 4]
    outs = refs[2 * len(spans) + 4:-5]
    x_ref, w_buf, total_ref, x_sems, w_sems = refs[-5:]
    rows = send_ref.shape[0]
    depth, width = w_ref.shape
    slots, rank, _ = a_ref.shape
    buffers, block_k, block_w = w_buf.shape
    block_n = min(BLOCK_N, block_w)
    depths, count = depth // block_k, (depth // block_k) * (width // block_w)

    def fetch(block, slot):
        begin = pl.multiple_of(lax.rem(block, depths) * block_k, block_k)
        left = pl.multiple_of(lax.div(block, depths) * block_w, block_w)
        return pltpu.make_async_copy(
            w_ref.at[pl.ds(begin, block_k), pl.ds(left, block_w)], w_buf.at[slot], w_sems.at[slot]
        )

    own_at = pos_ref[0]
    copies, begin = [], 0
    for index, (first, steps) in enumerate(spans):
        for core, at in enumerate((own_at, 1 - own_at)):
            source = sources[2 * index + core]
            copies.append(pltpu.make_async_copy(
                source.at[pl.ds(first, steps)], x_ref.at[at, pl.ds(begin, steps)], x_sems.at[2 * index + core]
            ))
        begin += steps
    for copy in copies:
        copy.start()
    for block in range(buffers):
        fetch(jnp.int32(block), block).start()
    keep_ref[...] = jnp.zeros_like(keep_ref)
    total_ref[...] = jnp.zeros_like(total_ref)
    send_rank, keep_rank = outs[:2] if apart else (total_ref, keep_ref)
    if apart:
        send_rank[...] = jnp.zeros_like(send_rank)
        keep_rank[...] = jnp.zeros_like(keep_rank)
    for copy in copies:
        copy.wait()
    emits = [
        pltpu.make_async_copy(x_ref.at[own_at, pl.ds(block, 1)], out_ref, x_sems.at[2 * len(spans) + index])
        for index, (block, out_ref) in enumerate(zip(emitted, outs[2 if apart else 0:]))
    ]
    for emit in emits:
        emit.start()
    for slot in range(slots):
        x = x_ref[...].reshape(2 * rows, depth)
        part = lax.dot_general(
            x, a_ref[slot], (((1,), (1,)), ((), ())), preferred_element_type=jnp.float32
        )
        begin = slot * rank + (0 if apart else width)
        send_rank[:, begin:begin + rank] = part[:rows]
        keep_rank[:, begin:begin + rank] = part[rows:]

    @pl.loop(0, count)
    def _(block):
        slot = lax.rem(block, buffers)
        fetch(block, slot).wait()
        inner = pl.ds(pl.multiple_of(lax.rem(block, depths) * block_k, block_k), block_k)
        left = pl.multiple_of(lax.div(block, depths) * block_w, block_w)
        x = x_ref[:, :, :, inner].reshape(2 * rows, block_k)
        for place in range(block_w // block_n):
            columns = pl.ds(left + place * block_n, block_n)
            term = jnp.dot(
                x, w_buf[slot, :, place * block_n:(place + 1) * block_n], preferred_element_type=jnp.float32
            )
            total_ref[:, columns] += term[:rows]
            keep_ref[:, columns] += term[rows:]

        @pl.when(block + buffers < count)
        def _():
            fetch(block + buffers, slot).start()

    send_ref[...] = total_ref[...].astype(send_ref.dtype)
    for emit in emits:
        emit.wait()


def partial_products(pos, chunks, weight, factors, apart=False, emitted=()):
    _, per_block, depth = chunks[0][0].shape
    width = weight.shape[1]
    spans = tuple((first, steps) for _, _, first, steps in chunks)
    steps = sum(length for _, length in spans)
    rows = steps * per_block
    block_k, block_w = block_shape(depth, width)
    buffers = min(BUFFERS, (depth // block_k) * (width // block_w))
    any_spec = pl.BlockSpec(memory_space=pl.ANY)
    vmem_spec = pl.BlockSpec(memory_space=pltpu.VMEM)
    extra = rank_columns(factors)
    columns = width + (0 if apart else extra)
    out_shape = [
        jax.ShapeDtypeStruct((rows, columns), jnp.bfloat16),
        jax.ShapeDtypeStruct((rows, columns), jnp.float32),
    ] + [jax.ShapeDtypeStruct((rows, extra), jnp.float32)] * (2 if apart else 0)
    out_specs = [vmem_spec] * len(out_shape)
    out_shape += [jax.ShapeDtypeStruct((1, per_block, depth), jnp.bfloat16)] * len(emitted)
    out_specs += [any_spec] * len(emitted)
    return pl.pallas_call(
        functools.partial(matmul_body, spans, emitted, apart),
        in_specs=[pl.BlockSpec(memory_space=pltpu.SMEM)] + [any_spec] * (2 * len(chunks) + 1) + [vmem_spec],
        out_specs=out_specs,
        out_shape=out_shape,
        scratch_shapes=[
            pltpu.VMEM((2, steps, per_block, depth), jnp.bfloat16),
            pltpu.VMEM((buffers, block_k, block_w), jnp.bfloat16),
            pltpu.VMEM((rows, columns), jnp.float32),
            pltpu.SemaphoreType.DMA((2 * len(chunks) + len(emitted),)),
            pltpu.SemaphoreType.DMA((buffers,)),
        ],
        compiler_params=pltpu.CompilerParams(vmem_limit_bytes=VMEM_BYTES),
        cost_estimate=pl.CostEstimate(flops=0, bytes_accessed=0, transcendentals=0),
        name="partial_products",
    )(pos, *[source for own, sib, _, _ in chunks for source in (own, sib)], weight, factors)


def finish_body(received, panels, chosen_ref, slot_ref, order_ref, *refs):
    panel_refs, refs = refs[:panels], refs[panels:]
    per_panel = panel_refs[0].shape[0]
    out_ref, lifted_ref, done_ref, sem = refs[-4:]
    steps, rows, width = done_ref.shape
    rank = chosen_ref.shape[1]
    chosen = chosen_ref[...]
    slot = slot_ref[...]
    spread = jnp.concatenate(
        [
            jnp.where(slot == order_ref[place], chosen, jnp.zeros_like(chosen))
            for place in range(panels * per_panel // rank)
        ],
        axis=1,
    )
    block_n = min(BLOCK_N, width)
    for place in range(width // block_n):
        columns = slice(place * block_n, (place + 1) * block_n)
        panel = jnp.concatenate([panel_ref[:, columns] for panel_ref in panel_refs], axis=0)
        lifted = jnp.dot(spread, panel, preferred_element_type=jnp.float32).astype(jnp.bfloat16)
        for step in range(steps):
            total = refs[step * (received + 1)][:, columns]
            for value_ref in refs[step * (received + 1) + 1:(step + 1) * (received + 1)]:
                total = total + value_ref[:, columns].astype(jnp.float32)
            value = total + ADAPTER_SCALE * lifted[step * rows:(step + 1) * rows].astype(jnp.float32)
            done_ref[step, :, columns] = value.astype(done_ref.dtype)
        lifted_ref[:, columns] = lifted[steps * rows:]
    copy = pltpu.make_async_copy(done_ref, out_ref.at[pl.ds(0, steps)], sem)
    copy.start()
    copy.wait()


def finish_steps(totals, chosen, slots, order, panels):
    steps, width = len(totals), panels[0].shape[1]
    rows = chosen.shape[0] // (steps + 1)
    vmem_spec = pl.BlockSpec(memory_space=pltpu.VMEM)
    arrays = [value for total in totals for value in total]
    return pl.pallas_call(
        functools.partial(finish_body, len(totals[0]) - 1, len(panels)),
        in_specs=[vmem_spec, vmem_spec, pl.BlockSpec(memory_space=pltpu.SMEM)] + [vmem_spec] * (len(panels) + len(arrays)),
        out_specs=[pl.BlockSpec(memory_space=pl.ANY), vmem_spec],
        out_shape=[
            jax.ShapeDtypeStruct((steps + 1, rows, width), jnp.bfloat16),
            jax.ShapeDtypeStruct((rows, width), jnp.bfloat16),
        ],
        scratch_shapes=[pltpu.VMEM((steps, rows, width), jnp.bfloat16), pltpu.SemaphoreType.DMA],
        compiler_params=pltpu.CompilerParams(vmem_limit_bytes=VMEM_BYTES),
        cost_estimate=pl.CostEstimate(flops=0, bytes_accessed=0, transcendentals=0),
        name="finish_steps",
    )(chosen, slots, order, *panels, *arrays)


def last_body(partial_ref, lifted_ref, *refs):
    out_ref, done_ref, sem = refs[-3:]
    total = refs[0][...]
    for value_ref in refs[1:-3]:
        total = total + value_ref[...].astype(jnp.float32)
    value = total + ADAPTER_SCALE * lifted_ref[...].astype(jnp.float32)
    done_ref[0] = value.astype(done_ref.dtype)
    copy = pltpu.make_async_copy(done_ref, out_ref.at[pl.ds(out_ref.shape[0] - 1, 1)], sem)
    copy.start()
    copy.wait()


def finish_last(partial, lifted, arrays):
    vmem_spec = pl.BlockSpec(memory_space=pltpu.VMEM)
    any_spec = pl.BlockSpec(memory_space=pl.ANY)
    return pl.pallas_call(
        last_body,
        in_specs=[any_spec] + [vmem_spec] * (1 + len(arrays)),
        out_specs=any_spec,
        out_shape=jax.ShapeDtypeStruct(partial.shape, partial.dtype),
        input_output_aliases={0: 0},
        scratch_shapes=[pltpu.VMEM((1,) + partial.shape[1:], partial.dtype), pltpu.SemaphoreType.DMA],
        compiler_params=pltpu.CompilerParams(vmem_limit_bytes=VMEM_BYTES),
        cost_estimate=pl.CostEstimate(flops=0, bytes_accessed=0, transcendentals=0),
        name="finish_last",
    )(partial, lifted, *arrays)


def per_device(hidden, base_weight, down_a, up_b, adapter_ids, owner_map):
    step_count, per_block, _ = hidden.shape
    n_tensor = lax.axis_size("tp")
    n_rep = lax.axis_size("rep")
    n_sub = lax.axis_size("sub")
    n_owners = n_rep * n_sub
    tensor_index = lax.axis_index("tp")
    rep_index = lax.axis_index("rep")
    sub_index = lax.axis_index("sub")
    owner_index = lax.axis_index(("rep", "sub"))
    requests = per_block * n_owners
    rows_mine = requests // n_tensor
    group = n_tensor // n_rep
    group_index = tensor_index // group
    owned_slots, _, rank_size = down_a.shape
    slot_count = owned_slots * n_owners
    width = base_weight.shape[1]

    def after(value, *done):
        return lax.optimization_barrier((value, *done))[0]

    def swap_cores(value):
        return lax.ppermute(value, "sub", [(i, i ^ 1) for i in range(n_sub)])

    def from_rep(value, shift):
        return lax.ppermute(value, "rep", [((i + shift) % n_rep, i) for i in range(n_rep)])

    def swap_tensor(value, bit):
        return lax.ppermute(value, "tp", [(i, i ^ bit) for i in range(n_tensor)])

    def to_group(value, hop):
        moved = group * hop
        return lax.ppermute(value, "tp", [(i, (i + moved) % n_tensor) for i in range(n_tensor)])

    def pick(values, index):
        value = values[0]
        for at in range(1, len(values)):
            value = jnp.where(index == at, values[at], value)
        return value

    keeps = (tensor_index // (group // 2)) % 2
    pos = (sub_index == keeps).astype(jnp.int32).reshape(1)

    siblings = swap_cores(hidden)
    pieces = [(step, shift) for step in range(step_count) for shift in range(1, n_rep)]
    source = pltpu.with_memory_space_constraint(hidden, pltpu.HBM)
    weight = pltpu.with_memory_space_constraint(base_weight, pltpu.HBM)
    remote = {(0, shift): from_rep(hidden[:1], shift) for shift in range(1, n_rep)}

    def spread_panels(panels, order, bits):
        for bit in bits:
            panels = panels + [swap_tensor(panel, bit) for panel in panels]
            order = order + [at ^ bit for at in order]
        return panels, order

    bits = [n_tensor >> at for at in range(1, n_tensor.bit_length())]
    order = [0] + [at for at in range(1, n_tensor) if at % (n_tensor // 4) == 0]
    panels = [up_b] + [swap_tensor(up_b, at) for at in order[1:]]
    my_ids = lax.dynamic_slice_in_dim(adapter_ids, tensor_index * rows_mine, rows_mine)
    iota = lax.broadcasted_iota(jnp.int32, (rows_mine, slot_count), 1)
    my_slot = jnp.sum((my_ids == iota).astype(jnp.int32) * owner_map[None, :], axis=1)
    owned_hot = my_slot[:, None] == (
        owner_index * owned_slots + lax.broadcasted_iota(jnp.int32, (rows_mine, owned_slots), 1)
    )

    first_leg, halved, begun, second_leg, ended = [], {}, set(), [], {}

    def second_half(total, received, steps, kind):
        total = total + received.astype(jnp.float32)
        rows, columns = total.shape
        extent, bit = rows // steps, group // 4
        while bit:
            extent //= 2
            halves = total.reshape(steps, 2, extent, columns)
            mine = (tensor_index // bit) % 2
            kept = lax.dynamic_index_in_dim(halves, mine, 1, keepdims=False)
            sent = lax.dynamic_index_in_dim(halves, 1 - mine, 1, keepdims=False)
            total = kept + swap_tensor(sent.astype(kind), bit).astype(jnp.float32)
            bit //= 2
        return total.reshape(steps, extent, columns)

    def gap(token, jobs, held_back=False):
        nonlocal first_leg, second_leg
        for parts, received, keep, kind in first_leg:
            steps = sum(length for _, length in parts)
            total, begin = second_half(after(keep, token), received, steps, kind), 0
            for key, length in parts:
                for at in range(begin, begin + length):
                    halved[key[0] + at - begin, key[1]] = total[at]
                    if (key[0] + at - begin, key[1]) == (step_count - 1, 0):
                        halved[RANK_NAME, 0] = total[at][:, width:]
                begin += length
        closed = {name: (after(kept, token), *received) for name, kept, received in second_leg}
        started, sends = [], []
        for name in sorted({name for name, _ in halved}):
            if name in begun or name == RANK_NAME or any((name, at) not in halved for at in range(n_rep)):
                continue
            begun.add(name)
            values = [halved[name, at] for at in range(n_rep)]
            columns = min(value.shape[1] for value in values)
            values = [value[:, :columns] for value in values]
            kept = pick(values, (group_index - rep_index) % n_rep)
            sends.append([
                pick(values, (group_index + hop - rep_index) % n_rep).astype(jnp.bfloat16) for hop in range(1, n_rep)
            ])
            started.append((name, kept))
        sends, token = lax.optimization_barrier((sends, token))
        first_sends = [job[1] for job in jobs]
        if held_back:
            first_sends, closed = lax.optimization_barrier((first_sends, closed))
        ended.update(closed)
        first_leg = [
            (parts, swap_tensor(send, group // 2), keep, kind) for (parts, _, keep, kind), send in zip(jobs, first_sends)
        ]
        second_leg = [
            (name, kept, [to_group(value, hop + 1) for hop, value in enumerate(sent)])
            for (name, kept), sent in zip(started, sends)
        ]
        return sends, closed

    factors = jnp.swapaxes(down_a, 1, 2)

    lead = step_count // 2
    parts, last_ranks, next_local = [((0, 0), lead)], {}, lead
    send, keep, *emitted = partial_products(
        pos, [(source, siblings, 0, lead)], weight, factors, emitted=tuple(range(1, lead))
    )
    for step, rows in enumerate(emitted, 1):
        remote.update({(step, shift): from_rep(rows, shift) for shift in range(1, n_rep)})
    for piece, (step, shift) in enumerate(pieces):
        sends, closed = gap(send, [(parts, send, keep, jnp.bfloat16)])
        own, panels, closed, _ = lax.optimization_barrier((remote[step, shift], panels, closed, send))
        ended.update(closed)
        if piece == 0:
            panels, order = spread_panels(panels, order, bits[2:])
        sib = swap_cores(own)
        own, sib, siblings, _ = lax.optimization_barrier((own, sib, siblings, sends))
        last, chunks, parts, places = step == step_count - 1, [(own, sib, 0, 1)], [((step, shift), 1)], ()
        if next_local < step_count:
            chunks.insert(0, (source, siblings, next_local, 1))
            parts.insert(0, ((next_local, 0), 1))
            places = (0,)
        send, keep, *outs = partial_products(pos, chunks, weight, factors, last, places)
        if last:
            last_ranks[shift] = outs
        elif outs:
            remote.update({(next_local, along): from_rep(outs[0], along) for along in range(1, n_rep)})
            next_local += 1
    gap(send, [(parts, send, keep, jnp.bfloat16)], held_back=True)
    for shift, ranks in last_ranks.items():
        halved[RANK_NAME, shift] = second_half(ranks[1], swap_tensor(ranks[0], group // 2), 1, jnp.float32)[0]
    values = [halved[RANK_NAME, at] for at in range(n_rep)]
    ended[RANK_NAME] = (pick(values, (group_index - rep_index) % n_rep), *[
        to_group(pick(values, (group_index + hop - rep_index) % n_rep), hop) for hop in range(1, n_rep)
    ])
    rounded, _ = gap(send, [])
    kept, *received = ended[RANK_NAME]
    ended[RANK_NAME] = (after(kept, rounded), *received)

    def rank_sum(name):
        kept, *received = [value[:, -rank_columns(factors):] for value in ended[name]]
        for value in received:
            kept = kept + value.astype(jnp.float32)
        return kept[:, :owned_slots * rank_size]

    finished = jnp.stack([rank_sum(step) for step in range(step_count - 1)] + [rank_sum(RANK_NAME)])
    finished = finished.astype(jnp.bfloat16).reshape(step_count, rows_mine, owned_slots, rank_size)
    finished = lax.optimization_barrier((finished, rounded))[0]
    ended.update((name, (kept, *received)) for name, kept, received in second_leg)
    masked = jnp.sum(
        jnp.where(owned_hot[None, :, :, None], finished, 0), axis=2, dtype=jnp.float32
    ).astype(jnp.bfloat16)
    chosen = masked
    for turn in range(1, n_owners):
        chosen = chosen + lax.ppermute(
            masked, ("rep", "sub"), [(i, (i + turn) % n_owners) for i in range(n_owners)]
        )
    panel_slots = jnp.stack([
        (tensor_index ^ at) * up_b.shape[0] + each for at in order for each in range(up_b.shape[0])
    ]).astype(jnp.int32)

    panels = [panel.reshape(-1, width) for panel in panels]
    partial, lifted = finish_steps(
        [ended[step] for step in range(step_count - 1)],
        chosen.reshape(step_count * rows_mine, rank_size),
        jnp.broadcast_to(my_slot, (step_count, rows_mine)).reshape(step_count * rows_mine, 1),
        panel_slots,
        panels,
    )
    return finish_last(partial, lifted, ended[step_count - 1])


def solution(mesh):
    return jax.shard_map(
        per_device,
        mesh=mesh,
        in_specs=(
            P(None, ("groups", "rep", "sub"), "tp"),
            P("tp", ("rep", "sub")),
            P(("rep", "sub"), "tp", None),
            P("tp", None, ("rep", "sub")),
            P("groups", None),
            P(),
        ),
        out_specs=P(None, ("groups", "tp"), ("rep", "sub")),
        check_vma=False,
    )
```

```python
import functools

import jax
import jax.numpy as jnp
from jax import lax
from jax.experimental import pallas as pl
from jax.experimental.pallas import tpu as pltpu
from jax.sharding import PartitionSpec as P

ADAPTER_SCALE = 0.5
BLOCK_N = 256
BLOCK = 1024
BUFFERS = 4
RANK_NAME = 1000
VMEM_BYTES = 20 * 1024 * 1024


def block_shape(depth, width):
    columns = BLOCK if width % BLOCK == 0 else width
    for size in (BLOCK, BLOCK // 2, BLOCK // 4):
        if depth % size == 0:
            return size, columns
    return depth, columns


def rank_columns(factors):
    slots, rank, _ = factors.shape
    return -(-slots * rank // 128) * 128


def matmul_body(spans, staged, apart, pos_ref, token_ref, *refs):
    sources = refs[:2 * len(spans)]
    w_ref, a_ref, send_ref, keep_ref = refs[2 * len(spans):2 * len(spans) + 4]
    outs, refs = refs[2 * len(spans) + 4:], ()
    outs, refs = (outs[:-7], outs[-7:]) if staged else (outs[:-5], outs[-5:])
    x_ref, w_buf, total_ref, x_sems, w_sems = refs[:5]
    rows = send_ref.shape[0]
    depth, width = w_ref.shape
    slots, rank, _ = a_ref.shape
    buffers, block_k, block_w = w_buf.shape
    block_n = min(BLOCK_N, block_w)
    depths, count = depth // block_k, (depth // block_k) * (width // block_w)

    def fetch(block, slot):
        begin = pl.multiple_of(lax.rem(block, depths) * block_k, block_k)
        left = pl.multiple_of(lax.div(block, depths) * block_w, block_w)
        return pltpu.make_async_copy(
            w_ref.at[pl.ds(begin, block_k), pl.ds(left, block_w)], w_buf.at[slot], w_sems.at[slot]
        )

    own_at = pos_ref[0]
    copies, begin = [], 0
    for index, (first, steps) in enumerate(spans):
        for core, at in enumerate((own_at, 1 - own_at)):
            source = sources[2 * index + core]
            copies.append(pltpu.make_async_copy(
                source.at[pl.ds(first, steps)], x_ref.at[at, pl.ds(begin, steps)], x_sems.at[2 * index + core]
            ))
        begin += steps
    for copy in copies:
        copy.start()
    if staged:
        stage_ref, stage_sems = refs[5:]
        stage_in = pltpu.make_async_copy(sources[0].at[pl.ds(1, staged)], stage_ref, stage_sems.at[staged])
        stage_in.start()
        stage_out = [
            pltpu.make_async_copy(stage_ref.at[pl.ds(index, 1)], out_ref, stage_sems.at[index])
            for index, out_ref in enumerate(outs)
        ]
    for block in range(buffers):
        fetch(jnp.int32(block), block).start()
    keep_ref[...] = jnp.zeros_like(keep_ref)
    total_ref[...] = jnp.zeros_like(total_ref)
    send_rank, keep_rank = outs[:2] if apart else (total_ref, keep_ref)
    if apart:
        send_rank[...] = jnp.zeros_like(send_rank)
        keep_rank[...] = jnp.zeros_like(keep_rank)
    for copy in copies:
        copy.wait()
    if staged:
        stage_in.wait()
        for copy in stage_out:
            copy.start()
    for slot in range(slots):
        x = x_ref[...].reshape(2 * rows, depth)
        part = lax.dot_general(
            x, a_ref[slot], (((1,), (1,)), ((), ())), preferred_element_type=jnp.float32
        )
        begin = slot * rank + (0 if apart else width)
        send_rank[:, begin:begin + rank] = part[:rows]
        keep_rank[:, begin:begin + rank] = part[rows:]

    @pl.loop(0, count)
    def _(block):
        slot = lax.rem(block, buffers)
        fetch(block, slot).wait()
        inner = pl.ds(pl.multiple_of(lax.rem(block, depths) * block_k, block_k), block_k)
        left = pl.multiple_of(lax.div(block, depths) * block_w, block_w)
        x = x_ref[:, :, :, inner].reshape(2 * rows, block_k)
        for place in range(block_w // block_n):
            columns = pl.ds(left + place * block_n, block_n)
            term = jnp.dot(
                x, w_buf[slot, :, place * block_n:(place + 1) * block_n], preferred_element_type=jnp.float32
            )
            total_ref[:, columns] += term[:rows]
            keep_ref[:, columns] += term[rows:]

        @pl.when(block + buffers < count)
        def _():
            fetch(block + buffers, slot).start()

    send_ref[...] = total_ref[...].astype(send_ref.dtype)
    if staged:
        for copy in stage_out:
            copy.wait()


def partial_products(pos, token, chunks, weight, factors, apart=False, staged=0):
    _, per_block, depth = chunks[0][0].shape
    width = weight.shape[1]
    spans = tuple((first, steps) for _, _, first, steps in chunks)
    steps = sum(length for _, length in spans)
    rows = steps * per_block
    block_k, block_w = block_shape(depth, width)
    buffers = min(BUFFERS, (depth // block_k) * (width // block_w))
    any_spec = pl.BlockSpec(memory_space=pl.ANY)
    vmem_spec = pl.BlockSpec(memory_space=pltpu.VMEM)
    extra = rank_columns(factors)
    columns = width + (0 if apart else extra)
    out_shape = [
        jax.ShapeDtypeStruct((rows, columns), jnp.bfloat16),
        jax.ShapeDtypeStruct((rows, columns), jnp.float32),
    ] + [jax.ShapeDtypeStruct((rows, extra), jnp.float32)] * (2 if apart else 0)
    out_specs = [vmem_spec] * len(out_shape)
    out_shape += [jax.ShapeDtypeStruct((1, per_block, depth), jnp.bfloat16)] * staged
    out_specs += [any_spec] * staged
    return pl.pallas_call(
        functools.partial(matmul_body, spans, staged, apart),
        in_specs=[pl.BlockSpec(memory_space=pltpu.SMEM)] + [any_spec] * (2 * len(chunks) + 2) + [vmem_spec],
        out_specs=out_specs,
        out_shape=out_shape,
        scratch_shapes=[
            pltpu.VMEM((2, steps, per_block, depth), jnp.bfloat16),
            pltpu.VMEM((buffers, block_k, block_w), jnp.bfloat16),
            pltpu.VMEM((rows, columns), jnp.float32),
            pltpu.SemaphoreType.DMA((2 * len(chunks),)),
            pltpu.SemaphoreType.DMA((buffers,)),
        ] + ([
            pltpu.VMEM((staged, per_block, depth), jnp.bfloat16),
            pltpu.SemaphoreType.DMA((staged + 1,)),
        ] if staged else []),
        compiler_params=pltpu.CompilerParams(vmem_limit_bytes=VMEM_BYTES),
        cost_estimate=pl.CostEstimate(flops=0, bytes_accessed=0, transcendentals=0),
        name="partial_products",
    )(pos, token, *[source for own, sib, _, _ in chunks for source in (own, sib)], weight, factors)


def finish_body(received, panels, token_ref, chosen_ref, slot_ref, order_ref, *refs):
    panel_refs, refs = refs[:panels], refs[panels:]
    per_panel = panel_refs[0].shape[0]
    out_ref, lifted_ref, done_ref, sem = refs[-4:]
    steps, rows, width = done_ref.shape
    rank = chosen_ref.shape[1]
    chosen = chosen_ref[...]
    slot = slot_ref[...]
    spread = jnp.concatenate(
        [
            jnp.where(slot == order_ref[place], chosen, jnp.zeros_like(chosen))
            for place in range(panels * per_panel // rank)
        ],
        axis=1,
    )
    block_n = min(BLOCK_N, width)
    for place in range(width // block_n):
        columns = slice(place * block_n, (place + 1) * block_n)
        panel = jnp.concatenate([panel_ref[:, columns] for panel_ref in panel_refs], axis=0)
        lifted = jnp.dot(spread, panel, preferred_element_type=jnp.float32).astype(jnp.bfloat16)
        for step in range(steps):
            total = refs[step * (received + 1)][:, columns]
            for value_ref in refs[step * (received + 1) + 1:(step + 1) * (received + 1)]:
                total = total + value_ref[:, columns].astype(jnp.float32)
            value = total + ADAPTER_SCALE * lifted[step * rows:(step + 1) * rows].astype(jnp.float32)
            done_ref[step, :, columns] = value.astype(done_ref.dtype)
        lifted_ref[:, columns] = lifted[steps * rows:]
    copy = pltpu.make_async_copy(done_ref, out_ref.at[pl.ds(0, steps)], sem)
    copy.start()
    copy.wait()


def finish_steps(totals, chosen, slots, order, panels, token):
    steps, width = len(totals), panels[0].shape[1]
    rows = chosen.shape[0] // (steps + 1)
    vmem_spec = pl.BlockSpec(memory_space=pltpu.VMEM)
    arrays = [value for total in totals for value in total]
    return pl.pallas_call(
        functools.partial(finish_body, len(totals[0]) - 1, len(panels)),
        in_specs=[pl.BlockSpec(memory_space=pl.ANY), vmem_spec, vmem_spec, pl.BlockSpec(memory_space=pltpu.SMEM)]
        + [vmem_spec] * (len(panels) + len(arrays)),
        out_specs=[pl.BlockSpec(memory_space=pl.ANY), vmem_spec],
        out_shape=[
            jax.ShapeDtypeStruct((steps + 1, rows, width), jnp.bfloat16),
            jax.ShapeDtypeStruct((rows, width), jnp.bfloat16),
        ],
        scratch_shapes=[pltpu.VMEM((steps, rows, width), jnp.bfloat16), pltpu.SemaphoreType.DMA],
        compiler_params=pltpu.CompilerParams(vmem_limit_bytes=VMEM_BYTES),
        cost_estimate=pl.CostEstimate(flops=0, bytes_accessed=0, transcendentals=0),
        name="finish_steps",
    )(token, chosen, slots, order, *panels, *arrays)


def last_body(partial_ref, lifted_ref, *refs):
    out_ref, done_ref, sem = refs[-3:]
    total = refs[0][...]
    for value_ref in refs[1:-3]:
        total = total + value_ref[...].astype(jnp.float32)
    value = total + ADAPTER_SCALE * lifted_ref[...].astype(jnp.float32)
    done_ref[0] = value.astype(done_ref.dtype)
    copy = pltpu.make_async_copy(done_ref, out_ref.at[pl.ds(out_ref.shape[0] - 1, 1)], sem)
    copy.start()
    copy.wait()


def finish_last(partial, lifted, arrays):
    vmem_spec = pl.BlockSpec(memory_space=pltpu.VMEM)
    any_spec = pl.BlockSpec(memory_space=pl.ANY)
    return pl.pallas_call(
        last_body,
        in_specs=[any_spec] + [vmem_spec] * (1 + len(arrays)),
        out_specs=any_spec,
        out_shape=jax.ShapeDtypeStruct(partial.shape, partial.dtype),
        input_output_aliases={0: 0},
        scratch_shapes=[pltpu.VMEM((1,) + partial.shape[1:], partial.dtype), pltpu.SemaphoreType.DMA],
        compiler_params=pltpu.CompilerParams(vmem_limit_bytes=VMEM_BYTES),
        cost_estimate=pl.CostEstimate(flops=0, bytes_accessed=0, transcendentals=0),
        name="finish_last",
    )(partial, lifted, *arrays)


def per_device(hidden, base_weight, down_a, up_b, adapter_ids, owner_map):
    step_count, per_block, _ = hidden.shape
    n_tensor = lax.axis_size("tp")
    n_rep = lax.axis_size("rep")
    n_sub = lax.axis_size("sub")
    n_owners = n_rep * n_sub
    tensor_index = lax.axis_index("tp")
    rep_index = lax.axis_index("rep")
    sub_index = lax.axis_index("sub")
    owner_index = lax.axis_index(("rep", "sub"))
    requests = per_block * n_owners
    rows_mine = requests // n_tensor
    group = n_tensor // n_rep
    group_index = tensor_index // group
    owned_slots, _, rank_size = down_a.shape
    slot_count = owned_slots * n_owners
    width = base_weight.shape[1]

    def after(value, *done):
        return lax.optimization_barrier((value, *done))[0]

    def swap_cores(value):
        return lax.ppermute(value, "sub", [(i, i ^ 1) for i in range(n_sub)])

    def from_rep(value, shift):
        return lax.ppermute(value, "rep", [((i + shift) % n_rep, i) for i in range(n_rep)])

    def swap_tensor(value, bit):
        return lax.ppermute(value, "tp", [(i, i ^ bit) for i in range(n_tensor)])

    def to_group(value, hop):
        moved = group * hop
        return lax.ppermute(value, "tp", [(i, (i + moved) % n_tensor) for i in range(n_tensor)])

    def pick(values, index):
        value = values[0]
        for at in range(1, len(values)):
            value = jnp.where(index == at, values[at], value)
        return value

    keeps = (tensor_index // (group // 2)) % 2
    pos = (sub_index == keeps).astype(jnp.int32).reshape(1)

    siblings = swap_cores(hidden)
    pieces = [(step, shift) for step in range(step_count) for shift in range(1, n_rep)]
    source = pltpu.with_memory_space_constraint(hidden, pltpu.HBM)
    weight = pltpu.with_memory_space_constraint(base_weight, pltpu.HBM)
    remote = {(0, shift): from_rep(hidden[:1], shift) for shift in range(1, n_rep)}

    def spread_panels(panels, order, bits):
        for bit in bits:
            panels = panels + [swap_tensor(panel, bit) for panel in panels]
            order = order + [at ^ bit for at in order]
        return panels, order

    bits = [n_tensor >> at for at in range(1, n_tensor.bit_length())]
    order = [0, bits[0], bits[1]]
    panels = [up_b] + [swap_tensor(up_b, at) for at in order[1:]]

    my_ids = lax.dynamic_slice_in_dim(adapter_ids, tensor_index * rows_mine, rows_mine)
    iota = lax.broadcasted_iota(jnp.int32, (rows_mine, slot_count), 1)
    my_slot = jnp.sum((my_ids == iota).astype(jnp.int32) * owner_map[None, :], axis=1)
    owned_hot = my_slot[:, None] == (
        owner_index * owned_slots + lax.broadcasted_iota(jnp.int32, (rows_mine, owned_slots), 1)
    )

    first_leg, halved, begun, second_leg, ended = [], {}, set(), [], {}

    def second_half(total, received, steps, kind):
        total = total + received.astype(jnp.float32)
        rows, columns = total.shape
        extent, bit = rows // steps, group // 4
        while bit:
            extent //= 2
            halves = total.reshape(steps, 2, extent, columns)
            mine = (tensor_index // bit) % 2
            kept = lax.dynamic_index_in_dim(halves, mine, 1, keepdims=False)
            sent = lax.dynamic_index_in_dim(halves, 1 - mine, 1, keepdims=False)
            total = kept + swap_tensor(sent.astype(kind), bit).astype(jnp.float32)
            bit //= 2
        return total.reshape(steps, extent, columns)

    def gap(token, jobs, short=False):
        nonlocal first_leg, second_leg
        for parts, received, keep, kind in first_leg:
            steps = sum(length for _, length in parts)
            total, begin = second_half(after(keep, token), received, steps, kind), 0
            for key, length in parts:
                for at in range(begin, begin + length):
                    halved[key[0] + at - begin, key[1]] = total[at]
                    if (key[0] + at - begin, key[1]) == (step_count - 1, 0):
                        halved[RANK_NAME, 0] = total[at][:, width:]
                begin += length
        started, sends = [], []
        for name in sorted({name for name, _ in halved}):
            if name in begun or name == RANK_NAME or any((name, at) not in halved for at in range(n_rep)):
                continue
            begun.add(name)
            values = [halved[name, at] for at in range(n_rep)]
            columns = min(value.shape[1] for value in values)
            values = [value[:, :columns] for value in values]
            kept = pick(values, (group_index - rep_index) % n_rep)
            sends.append([
                pick(values, (group_index + hop - rep_index) % n_rep).astype(jnp.bfloat16) for hop in range(1, n_rep)
            ])
            started.append((name, kept))
        sends, token = lax.optimization_barrier((sends, token))
        closed, waiting = {}, []
        for name, kept, received, lag in second_leg:
            if short or lag > 1:
                waiting.append((name, kept, received, lag if short else lag - 1))
            else:
                closed[name], token = lax.optimization_barrier(((kept, *received), token))
        first_sends = [job[1] for job in jobs]
        ended.update(closed)
        first_leg = [
            (parts, swap_tensor(send, group // 2), keep, kind) for (parts, _, keep, kind), send in zip(jobs, first_sends)
        ]
        second_leg = waiting + [
            (name, kept, [to_group(value, hop + 1) for hop, value in enumerate(sent)], 2 if short else 1)
            for (name, kept), sent in zip(started, sends)
        ]
        return sends, token

    factors = jnp.swapaxes(down_a, 1, 2)

    lead = step_count // 2
    parts, last_ranks, next_local = [((0, 0), lead)], {}, lead
    send, keep, *slices = partial_products(
        pos, up_b, [(source, siblings, 0, lead)], weight, factors, staged=step_count - 1
    )
    for step, rows in enumerate(slices, 1):
        remote.update({(step, shift): from_rep(rows, shift) for shift in range(1, n_rep)})
    send, panels = lax.optimization_barrier((send, panels))
    for piece, (step, shift) in enumerate(pieces):
        sends, token = gap(send, [(parts, send, keep, jnp.bfloat16)])
        own, panels, token = lax.optimization_barrier((remote[step, shift], panels, token))
        if piece == 0:
            panels, order = panels + [swap_tensor(panels[1], bits[1])], order + [bits[0] ^ bits[1]]
            panels, order = spread_panels(panels, order, bits[2:])
        sib = swap_cores(own)
        if piece == len(pieces) - 1:
            more, token = gap(token, [], short=True)
            sends = sends + more
        own, sib, siblings, sends, token = lax.optimization_barrier((own, sib, siblings, sends, token))
        last, chunks, parts = step == step_count - 1, [(own, sib, 0, 1)], [((step, shift), 1)]
        if next_local < step_count:
            chunks.insert(0, (source, siblings, next_local, 1))
            parts.insert(0, ((next_local, 0), 1))
            next_local += 1
        send, keep, *ranks = partial_products(pos, token, chunks, weight, factors, last)
        if last:
            last_ranks[shift] = ranks
    _, token = gap(send, [(parts, send, keep, jnp.bfloat16)])
    for shift, ranks in last_ranks.items():
        halved[RANK_NAME, shift] = second_half(ranks[1], swap_tensor(ranks[0], group // 2), 1, jnp.float32)[0]
    values = [halved[RANK_NAME, at] for at in range(n_rep)]
    ended[RANK_NAME] = (pick(values, (group_index - rep_index) % n_rep), *[
        to_group(pick(values, (group_index + hop - rep_index) % n_rep), hop) for hop in range(1, n_rep)
    ])
    _, token = gap(token, [])
    ended[RANK_NAME], token = lax.optimization_barrier((ended[RANK_NAME], token))

    def rank_sum(name):
        kept, *received = [value[:, -rank_columns(factors):] for value in ended[name]]
        for value in received:
            kept = kept + value.astype(jnp.float32)
        return kept[:, :owned_slots * rank_size]

    finished = jnp.stack([rank_sum(step) for step in range(step_count - 1)] + [rank_sum(RANK_NAME)])
    finished = finished.astype(jnp.bfloat16).reshape(step_count, rows_mine, owned_slots, rank_size)
    finished, token = lax.optimization_barrier((finished, token))
    ended.update((name, (kept, *received)) for name, kept, received, _ in second_leg)
    masked = jnp.sum(
        jnp.where(owned_hot[None, :, :, None], finished, 0), axis=2, dtype=jnp.float32
    ).astype(jnp.bfloat16)
    chosen = masked
    for turn in range(1, n_owners):
        chosen = chosen + lax.ppermute(
            masked, ("rep", "sub"), [(i, (i + turn) % n_owners) for i in range(n_owners)]
        )
    panel_slots = jnp.stack([
        (tensor_index ^ at) * up_b.shape[0] + each for at in order for each in range(up_b.shape[0])
    ]).astype(jnp.int32)

    panels = [panel.reshape(-1, width) for panel in panels]
    partial, lifted = finish_steps(
        [ended[step] for step in range(step_count - 1)],
        chosen.reshape(step_count * rows_mine, rank_size),
        jnp.broadcast_to(my_slot, (step_count, rows_mine)).reshape(step_count * rows_mine, 1),
        panel_slots,
        panels,
        token,
    )
    return finish_last(partial, lifted, ended[step_count - 1])


def solution(mesh):
    return jax.shard_map(
        per_device,
        mesh=mesh,
        in_specs=(
            P(None, ("groups", "rep", "sub"), "tp"),
            P("tp", ("rep", "sub")),
            P(("rep", "sub"), "tp", None),
            P("tp", None, ("rep", "sub")),
            P("groups", None),
            P(),
        ),
        out_specs=P(None, ("groups", "tp"), ("rep", "sub")),
        check_vma=False,
    )
```

```python
import functools

import jax
import jax.numpy as jnp
from jax import lax
from jax.experimental import pallas as pl
from jax.experimental.pallas import tpu as pltpu
from jax.sharding import PartitionSpec as P

ADAPTER_SCALE = 0.5
BLOCK_N = 256
BLOCK = 1024
BUFFERS = 4
RANK_NAME = 1000
VMEM_BYTES = 22 * 1024 * 1024


def block_shape(depth, width):
    columns = BLOCK if width % BLOCK == 0 else width
    for size in (BLOCK, BLOCK // 2, BLOCK // 4):
        if depth % size == 0:
            return size, columns
    return depth, columns


def rank_columns(factors):
    slots, rank, _ = factors.shape
    return -(-slots * rank // 128) * 128


def matmul_body(spans, staged, apart, pos_ref, *refs):
    sources = refs[:2 * len(spans)]
    w_ref, a_ref, send_ref, keep_ref = refs[2 * len(spans):2 * len(spans) + 4]
    outs, refs = refs[2 * len(spans) + 4:], ()
    outs, refs = (outs[:-7], outs[-7:]) if staged else (outs[:-5], outs[-5:])
    x_ref, w_buf, total_ref, x_sems, w_sems = refs[:5]
    rows = send_ref.shape[0]
    depth, width = w_ref.shape
    slots, rank, _ = a_ref.shape
    buffers, block_k, block_w = w_buf.shape
    block_n = min(BLOCK_N, block_w)
    depths, count = depth // block_k, (depth // block_k) * (width // block_w)

    def fetch(block, slot):
        begin = pl.multiple_of(lax.rem(block, depths) * block_k, block_k)
        left = pl.multiple_of(lax.div(block, depths) * block_w, block_w)
        return pltpu.make_async_copy(
            w_ref.at[pl.ds(begin, block_k), pl.ds(left, block_w)], w_buf.at[slot], w_sems.at[slot]
        )

    own_at = pos_ref[0]
    copies, begin = [], 0
    for index, (first, steps) in enumerate(spans):
        for core, at in enumerate((own_at, 1 - own_at)):
            source = sources[2 * index + core]
            copies.append(pltpu.make_async_copy(
                source.at[pl.ds(first, steps)], x_ref.at[at, pl.ds(begin, steps)], x_sems.at[2 * index + core]
            ))
        begin += steps
    for copy in copies:
        copy.start()
    if staged:
        stage_ref, stage_sems = refs[5:]
        stage_in = pltpu.make_async_copy(sources[0].at[pl.ds(1, staged)], stage_ref, stage_sems.at[staged])
        stage_in.start()
        stage_out = [
            pltpu.make_async_copy(stage_ref.at[pl.ds(index, 1)], out_ref, stage_sems.at[index])
            for index, out_ref in enumerate(outs)
        ]
    for block in range(buffers):
        fetch(jnp.int32(block), block).start()
    keep_ref[...] = jnp.zeros_like(keep_ref)
    total_ref[...] = jnp.zeros_like(total_ref)
    send_rank, keep_rank = outs[:2] if apart else (total_ref, keep_ref)
    if apart:
        send_rank[...] = jnp.zeros_like(send_rank)
        keep_rank[...] = jnp.zeros_like(keep_rank)
    for copy in copies:
        copy.wait()
    if staged:
        stage_in.wait()
        for copy in stage_out:
            copy.start()
    for slot in range(slots):
        x = x_ref[...].reshape(2 * rows, depth)
        part = lax.dot_general(
            x, a_ref[slot], (((1,), (1,)), ((), ())), preferred_element_type=jnp.float32
        )
        begin = slot * rank + (0 if apart else width)
        send_rank[:, begin:begin + rank] = part[:rows]
        keep_rank[:, begin:begin + rank] = part[rows:]

    @pl.loop(0, count)
    def _(block):
        slot = lax.rem(block, buffers)
        fetch(block, slot).wait()
        inner = pl.ds(pl.multiple_of(lax.rem(block, depths) * block_k, block_k), block_k)
        left = pl.multiple_of(lax.div(block, depths) * block_w, block_w)
        x = x_ref[:, :, :, inner].reshape(2 * rows, block_k)
        for place in range(block_w // block_n):
            columns = pl.ds(left + place * block_n, block_n)
            term = jnp.dot(
                x, w_buf[slot, :, place * block_n:(place + 1) * block_n], preferred_element_type=jnp.float32
            )
            total_ref[:, columns] += term[:rows]
            keep_ref[:, columns] += term[rows:]

        @pl.when(block + buffers < count)
        def _():
            fetch(block + buffers, slot).start()

    send_ref[...] = total_ref[...].astype(send_ref.dtype)
    if staged:
        for copy in stage_out:
            copy.wait()


def partial_products(pos, chunks, weight, factors, apart=False, staged=0):
    _, per_block, depth = chunks[0][0].shape
    width = weight.shape[1]
    spans = tuple((first, steps) for _, _, first, steps in chunks)
    steps = sum(length for _, length in spans)
    rows = steps * per_block
    block_k, block_w = block_shape(depth, width)
    buffers = min(BUFFERS, (depth // block_k) * (width // block_w))
    any_spec = pl.BlockSpec(memory_space=pl.ANY)
    vmem_spec = pl.BlockSpec(memory_space=pltpu.VMEM)
    extra = rank_columns(factors)
    columns = width + (0 if apart else extra)
    out_shape = [
        jax.ShapeDtypeStruct((rows, columns), jnp.bfloat16),
        jax.ShapeDtypeStruct((rows, columns), jnp.float32),
    ] + [jax.ShapeDtypeStruct((rows, extra), jnp.float32)] * (2 if apart else 0)
    out_specs = [vmem_spec] * len(out_shape)
    out_shape += [jax.ShapeDtypeStruct((1, per_block, depth), jnp.bfloat16)] * staged
    out_specs += [any_spec] * staged
    return pl.pallas_call(
        functools.partial(matmul_body, spans, staged, apart),
        in_specs=[pl.BlockSpec(memory_space=pltpu.SMEM)] + [any_spec] * (2 * len(chunks) + 1) + [vmem_spec],
        out_specs=out_specs,
        out_shape=out_shape,
        scratch_shapes=[
            pltpu.VMEM((2, steps, per_block, depth), jnp.bfloat16),
            pltpu.VMEM((buffers, block_k, block_w), jnp.bfloat16),
            pltpu.VMEM((rows, columns), jnp.float32),
            pltpu.SemaphoreType.DMA((2 * len(chunks),)),
            pltpu.SemaphoreType.DMA((buffers,)),
        ] + ([
            pltpu.VMEM((staged, per_block, depth), jnp.bfloat16),
            pltpu.SemaphoreType.DMA((staged + 1,)),
        ] if staged else []),
        compiler_params=pltpu.CompilerParams(vmem_limit_bytes=VMEM_BYTES),
        cost_estimate=pl.CostEstimate(flops=0, bytes_accessed=0, transcendentals=0),
        name="partial_products",
    )(pos, *[source for own, sib, _, _ in chunks for source in (own, sib)], weight, factors)


def finish_body(received, panels, chosen_ref, slot_ref, order_ref, *refs):
    panel_refs, refs = refs[:panels], refs[panels:]
    per_panel = panel_refs[0].shape[0]
    out_ref, lifted_ref, done_ref, sem = refs[-4:]
    steps, rows, width = done_ref.shape
    rank = chosen_ref.shape[1]
    chosen = chosen_ref[...]
    slot = slot_ref[...]
    spread = jnp.concatenate(
        [
            jnp.where(slot == order_ref[place], chosen, jnp.zeros_like(chosen))
            for place in range(panels * per_panel // rank)
        ],
        axis=1,
    )
    block_n = min(BLOCK_N, width)
    for place in range(width // block_n):
        columns = slice(place * block_n, (place + 1) * block_n)
        panel = jnp.concatenate([panel_ref[:, columns] for panel_ref in panel_refs], axis=0)
        lifted = jnp.dot(spread, panel, preferred_element_type=jnp.float32).astype(jnp.bfloat16)
        for step in range(steps):
            total = refs[step * (received + 1)][:, columns]
            for value_ref in refs[step * (received + 1) + 1:(step + 1) * (received + 1)]:
                total = total + value_ref[:, columns].astype(jnp.float32)
            value = total + ADAPTER_SCALE * lifted[step * rows:(step + 1) * rows].astype(jnp.float32)
            done_ref[step, :, columns] = value.astype(done_ref.dtype)
        lifted_ref[:, columns] = lifted[steps * rows:]
    copy = pltpu.make_async_copy(done_ref, out_ref.at[pl.ds(0, steps)], sem)
    copy.start()
    copy.wait()


def finish_steps(totals, chosen, slots, order, panels):
    steps, width = len(totals), panels[0].shape[1]
    rows = chosen.shape[0] // (steps + 1)
    vmem_spec = pl.BlockSpec(memory_space=pltpu.VMEM)
    arrays = [value for total in totals for value in total]
    return pl.pallas_call(
        functools.partial(finish_body, len(totals[0]) - 1, len(panels)),
        in_specs=[vmem_spec, vmem_spec, pl.BlockSpec(memory_space=pltpu.SMEM)] + [vmem_spec] * (len(panels) + len(arrays)),
        out_specs=[pl.BlockSpec(memory_space=pl.ANY), vmem_spec],
        out_shape=[
            jax.ShapeDtypeStruct((steps + 1, rows, width), jnp.bfloat16),
            jax.ShapeDtypeStruct((rows, width), jnp.bfloat16),
        ],
        scratch_shapes=[pltpu.VMEM((steps, rows, width), jnp.bfloat16), pltpu.SemaphoreType.DMA],
        compiler_params=pltpu.CompilerParams(vmem_limit_bytes=VMEM_BYTES),
        cost_estimate=pl.CostEstimate(flops=0, bytes_accessed=0, transcendentals=0),
        name="finish_steps",
    )(chosen, slots, order, *panels, *arrays)


def last_body(partial_ref, lifted_ref, *refs):
    out_ref, done_ref, sem = refs[-3:]
    total = refs[0][...]
    for value_ref in refs[1:-3]:
        total = total + value_ref[...].astype(jnp.float32)
    value = total + ADAPTER_SCALE * lifted_ref[...].astype(jnp.float32)
    done_ref[0] = value.astype(done_ref.dtype)
    copy = pltpu.make_async_copy(done_ref, out_ref.at[pl.ds(out_ref.shape[0] - 1, 1)], sem)
    copy.start()
    copy.wait()


def finish_last(partial, lifted, arrays):
    vmem_spec = pl.BlockSpec(memory_space=pltpu.VMEM)
    any_spec = pl.BlockSpec(memory_space=pl.ANY)
    return pl.pallas_call(
        last_body,
        in_specs=[any_spec] + [vmem_spec] * (1 + len(arrays)),
        out_specs=any_spec,
        out_shape=jax.ShapeDtypeStruct(partial.shape, partial.dtype),
        input_output_aliases={0: 0},
        scratch_shapes=[pltpu.VMEM((1,) + partial.shape[1:], partial.dtype), pltpu.SemaphoreType.DMA],
        compiler_params=pltpu.CompilerParams(vmem_limit_bytes=VMEM_BYTES),
        cost_estimate=pl.CostEstimate(flops=0, bytes_accessed=0, transcendentals=0),
        name="finish_last",
    )(partial, lifted, *arrays)


def per_device(hidden, base_weight, down_a, up_b, adapter_ids, owner_map):
    step_count, per_block, _ = hidden.shape
    n_tensor = lax.axis_size("tp")
    n_rep = lax.axis_size("rep")
    n_sub = lax.axis_size("sub")
    n_owners = n_rep * n_sub
    tensor_index = lax.axis_index("tp")
    rep_index = lax.axis_index("rep")
    sub_index = lax.axis_index("sub")
    owner_index = lax.axis_index(("rep", "sub"))
    requests = per_block * n_owners
    rows_mine = requests // n_tensor
    group = n_tensor // n_rep
    group_index = tensor_index // group
    owned_slots, _, rank_size = down_a.shape
    slot_count = owned_slots * n_owners
    width = base_weight.shape[1]

    def after(value, *done):
        return lax.optimization_barrier((value, *done))[0]

    def swap_cores(value):
        return lax.ppermute(value, "sub", [(i, i ^ 1) for i in range(n_sub)])

    def from_rep(value, shift):
        return lax.ppermute(value, "rep", [((i + shift) % n_rep, i) for i in range(n_rep)])

    def swap_tensor(value, bit):
        return lax.ppermute(value, "tp", [(i, i ^ bit) for i in range(n_tensor)])

    def to_group(value, hop):
        moved = group * hop
        return lax.ppermute(value, "tp", [(i, (i + moved) % n_tensor) for i in range(n_tensor)])

    def pick(values, index):
        value = values[0]
        for at in range(1, len(values)):
            value = jnp.where(index == at, values[at], value)
        return value

    keeps = (tensor_index // (group // 2)) % 2
    pos = (sub_index == keeps).astype(jnp.int32).reshape(1)

    siblings = swap_cores(hidden)
    pieces = [(step, shift) for step in range(step_count) for shift in range(1, n_rep)]
    source = pltpu.with_memory_space_constraint(hidden, pltpu.HBM)
    weight = pltpu.with_memory_space_constraint(base_weight, pltpu.HBM)
    remote = {(0, shift): from_rep(hidden[:1], shift) for shift in range(1, n_rep)}

    def spread_panels(panels, order, bits):
        for bit in bits:
            panels = panels + [swap_tensor(panel, bit) for panel in panels]
            order = order + [at ^ bit for at in order]
        return panels, order

    bits = [n_tensor >> at for at in range(1, n_tensor.bit_length())]
    order = [0] + [at for at in range(1, n_tensor) if at % (n_tensor // 4) == 0]
    panels = [up_b] + [swap_tensor(up_b, at) for at in order[1:]]
    my_ids = lax.dynamic_slice_in_dim(adapter_ids, tensor_index * rows_mine, rows_mine)
    iota = lax.broadcasted_iota(jnp.int32, (rows_mine, slot_count), 1)
    my_slot = jnp.sum((my_ids == iota).astype(jnp.int32) * owner_map[None, :], axis=1)
    owned_hot = my_slot[:, None] == (
        owner_index * owned_slots + lax.broadcasted_iota(jnp.int32, (rows_mine, owned_slots), 1)
    )

    first_leg, halved, begun, second_leg, ended = [], {}, set(), [], {}

    def second_half(total, received, steps, kind):
        total = total + received.astype(jnp.float32)
        rows, columns = total.shape
        extent, bit = rows // steps, group // 4
        while bit:
            extent //= 2
            halves = total.reshape(steps, 2, extent, columns)
            mine = (tensor_index // bit) % 2
            kept = lax.dynamic_index_in_dim(halves, mine, 1, keepdims=False)
            sent = lax.dynamic_index_in_dim(halves, 1 - mine, 1, keepdims=False)
            total = kept + swap_tensor(sent.astype(kind), bit).astype(jnp.float32)
            bit //= 2
        return total.reshape(steps, extent, columns)

    def gap(token, jobs, short=False):
        nonlocal first_leg, second_leg
        for parts, received, keep, kind in first_leg:
            steps = sum(length for _, length in parts)
            total, begin = second_half(after(keep, token), received, steps, kind), 0
            for key, length in parts:
                for at in range(begin, begin + length):
                    halved[key[0] + at - begin, key[1]] = total[at]
                    if (key[0] + at - begin, key[1]) == (step_count - 1, 0):
                        halved[RANK_NAME, 0] = total[at][:, width:]
                begin += length
        closed, waiting = {}, []
        for name, kept, received, lag in second_leg:
            if short or lag > 1:
                waiting.append((name, kept, received, lag if short else lag - 1))
            else:
                closed[name] = (after(kept, token), *received)
        started, sends = [], []
        for name in sorted({name for name, _ in halved}):
            if name in begun or name == RANK_NAME or any((name, at) not in halved for at in range(n_rep)):
                continue
            begun.add(name)
            values = [halved[name, at] for at in range(n_rep)]
            columns = min(value.shape[1] for value in values)
            values = [value[:, :columns] for value in values]
            kept = pick(values, (group_index - rep_index) % n_rep)
            sends.append([
                pick(values, (group_index + hop - rep_index) % n_rep).astype(jnp.bfloat16) for hop in range(1, n_rep)
            ])
            started.append((name, kept))
        sends, token = lax.optimization_barrier((sends, token))
        first_sends, closed = lax.optimization_barrier(([job[1] for job in jobs], closed))
        ended.update(closed)
        first_leg = [
            (parts, swap_tensor(send, group // 2), keep, kind) for (parts, _, keep, kind), send in zip(jobs, first_sends)
        ]
        second_leg = waiting + [
            (name, kept, [to_group(value, hop + 1) for hop, value in enumerate(sent)], 2 if short else 1)
            for (name, kept), sent in zip(started, sends)
        ]
        return sends

    factors = jnp.swapaxes(down_a, 1, 2)

    lead = step_count - 1
    parts, last_ranks = [((0, 0), lead)], {}
    send, keep, *slices = partial_products(
        pos, [(source, siblings, 0, lead)], weight, factors, staged=step_count - 1
    )
    for step, rows in enumerate(slices, 1):
        remote.update({(step, shift): from_rep(rows, shift) for shift in range(1, n_rep)})
    for piece, (step, shift) in enumerate(pieces):
        sends = gap(send, [(parts, send, keep, jnp.bfloat16)])
        own, panels, _ = lax.optimization_barrier((remote[step, shift], panels, send))
        if piece == 0:
            panels, order = spread_panels(panels, order, bits[2:])
        sib = swap_cores(own)
        held = [sends, siblings] if piece == 0 else [sends]
        own, sib, held = lax.optimization_barrier((own, sib, held))
        last, chunks, parts = step == step_count - 1, [(own, sib, 0, 1)], [((step, shift), 1)]
        if piece == 0:
            chunks.insert(0, (source, held[1], lead, 1))
            parts.insert(0, ((lead, 0), 1))
        send, keep, *ranks = partial_products(pos, chunks, weight, factors, last)
        if last:
            last_ranks[shift] = ranks
    gap(send, [(parts, send, keep, jnp.bfloat16)])
    for shift, ranks in last_ranks.items():
        halved[RANK_NAME, shift] = second_half(ranks[1], swap_tensor(ranks[0], group // 2), 1, jnp.float32)[0]
    values = [halved[RANK_NAME, at] for at in range(n_rep)]
    ended[RANK_NAME] = (pick(values, (group_index - rep_index) % n_rep), *[
        to_group(pick(values, (group_index + hop - rep_index) % n_rep), hop) for hop in range(1, n_rep)
    ])
    rounded = gap(send, [])

    def rank_sum(name):
        kept, *received = [value[:, -rank_columns(factors):] for value in ended[name]]
        for value in received:
            kept = kept + value.astype(jnp.float32)
        return kept[:, :owned_slots * rank_size]

    finished = jnp.stack([rank_sum(step) for step in range(step_count - 1)] + [rank_sum(RANK_NAME)])
    finished = finished.astype(jnp.bfloat16).reshape(step_count, rows_mine, owned_slots, rank_size)
    finished = lax.optimization_barrier((finished, rounded))[0]
    ended.update((name, (kept, *received)) for name, kept, received, _ in second_leg)
    masked = jnp.sum(
        jnp.where(owned_hot[None, :, :, None], finished, 0), axis=2, dtype=jnp.float32
    ).astype(jnp.bfloat16)
    chosen = masked
    for turn in range(1, n_owners):
        chosen = chosen + lax.ppermute(
            masked, ("rep", "sub"), [(i, (i + turn) % n_owners) for i in range(n_owners)]
        )
    panel_slots = jnp.stack([
        (tensor_index ^ at) * up_b.shape[0] + each for at in order for each in range(up_b.shape[0])
    ]).astype(jnp.int32)

    panels = [panel.reshape(-1, width) for panel in panels]
    partial, lifted = finish_steps(
        [ended[step] for step in range(step_count - 1)],
        chosen.reshape(step_count * rows_mine, rank_size),
        jnp.broadcast_to(my_slot, (step_count, rows_mine)).reshape(step_count * rows_mine, 1),
        panel_slots,
        panels,
    )
    return finish_last(partial, lifted, ended[step_count - 1])


def solution(mesh):
    return jax.shard_map(
        per_device,
        mesh=mesh,
        in_specs=(
            P(None, ("groups", "rep", "sub"), "tp"),
            P("tp", ("rep", "sub")),
            P(("rep", "sub"), "tp", None),
            P("tp", None, ("rep", "sub")),
            P("groups", None),
            P(),
        ),
        out_specs=P(None, ("groups", "tp"), ("rep", "sub")),
        check_vma=False,
    )
```

```python
import functools

import jax
import jax.numpy as jnp
from jax import lax
from jax.experimental import pallas as pl
from jax.experimental.pallas import tpu as pltpu
from jax.sharding import PartitionSpec as P

ADAPTER_SCALE = 0.5
BLOCK_N = 256
BLOCK = 1024
BUFFERS = 4
RANK_NAME = 1000
VMEM_BYTES = 20 * 1024 * 1024


def block_shape(depth, width):
    columns = BLOCK if width % BLOCK == 0 else width
    for size in (BLOCK, BLOCK // 2, BLOCK // 4):
        if depth % size == 0:
            return size, columns
    return depth, columns


def rank_columns(factors):
    slots, rank, _ = factors.shape
    return -(-slots * rank // 128) * 128


def matmul_body(spans, staged, apart, pos_ref, *refs):
    sources = refs[:2 * len(spans)]
    w_ref, a_ref, send_ref, keep_ref = refs[2 * len(spans):2 * len(spans) + 4]
    outs, refs = refs[2 * len(spans) + 4:], ()
    outs, refs = (outs[:-7], outs[-7:]) if staged else (outs[:-5], outs[-5:])
    x_ref, w_buf, total_ref, x_sems, w_sems = refs[:5]
    rows = send_ref.shape[0]
    depth, width = w_ref.shape
    slots, rank, _ = a_ref.shape
    buffers, block_k, block_w = w_buf.shape
    block_n = min(BLOCK_N, block_w)
    depths, count = depth // block_k, (depth // block_k) * (width // block_w)

    def fetch(block, slot):
        begin = pl.multiple_of(lax.rem(block, depths) * block_k, block_k)
        left = pl.multiple_of(lax.div(block, depths) * block_w, block_w)
        return pltpu.make_async_copy(
            w_ref.at[pl.ds(begin, block_k), pl.ds(left, block_w)], w_buf.at[slot], w_sems.at[slot]
        )

    own_at = pos_ref[0]
    copies, begin = [], 0
    for index, (first, steps) in enumerate(spans):
        for core, at in enumerate((own_at, 1 - own_at)):
            source = sources[2 * index + core]
            copies.append(pltpu.make_async_copy(
                source.at[pl.ds(first, steps)], x_ref.at[at, pl.ds(begin, steps)], x_sems.at[2 * index + core]
            ))
        begin += steps
    for copy in copies:
        copy.start()
    if staged:
        stage_ref, stage_sems = refs[5:]
        stage_in = pltpu.make_async_copy(sources[0].at[pl.ds(1, staged)], stage_ref, stage_sems.at[staged])
        stage_in.start()
        stage_out = [
            pltpu.make_async_copy(stage_ref.at[pl.ds(index, 1)], out_ref, stage_sems.at[index])
            for index, out_ref in enumerate(outs)
        ]
    for block in range(buffers):
        fetch(jnp.int32(block), block).start()
    keep_ref[...] = jnp.zeros_like(keep_ref)
    total_ref[...] = jnp.zeros_like(total_ref)
    send_rank, keep_rank = outs[:2] if apart else (total_ref, keep_ref)
    if apart:
        send_rank[...] = jnp.zeros_like(send_rank)
        keep_rank[...] = jnp.zeros_like(keep_rank)
    for copy in copies:
        copy.wait()
    if staged:
        stage_in.wait()
        for copy in stage_out:
            copy.start()
    for slot in range(slots):
        x = x_ref[...].reshape(2 * rows, depth)
        part = lax.dot_general(
            x, a_ref[slot], (((1,), (1,)), ((), ())), preferred_element_type=jnp.float32
        )
        begin = slot * rank + (0 if apart else width)
        send_rank[:, begin:begin + rank] = part[:rows]
        keep_rank[:, begin:begin + rank] = part[rows:]

    @pl.loop(0, count)
    def _(block):
        slot = lax.rem(block, buffers)
        fetch(block, slot).wait()
        inner = pl.ds(pl.multiple_of(lax.rem(block, depths) * block_k, block_k), block_k)
        left = pl.multiple_of(lax.div(block, depths) * block_w, block_w)
        x = x_ref[:, :, :, inner].reshape(2 * rows, block_k)
        for place in range(block_w // block_n):
            columns = pl.ds(left + place * block_n, block_n)
            term = jnp.dot(
                x, w_buf[slot, :, place * block_n:(place + 1) * block_n], preferred_element_type=jnp.float32
            )
            total_ref[:, columns] += term[:rows]
            keep_ref[:, columns] += term[rows:]

        @pl.when(block + buffers < count)
        def _():
            fetch(block + buffers, slot).start()

    send_ref[...] = total_ref[...].astype(send_ref.dtype)
    if staged:
        for copy in stage_out:
            copy.wait()


def partial_products(pos, chunks, weight, factors, apart=False, staged=0):
    _, per_block, depth = chunks[0][0].shape
    width = weight.shape[1]
    spans = tuple((first, steps) for _, _, first, steps in chunks)
    steps = sum(length for _, length in spans)
    rows = steps * per_block
    block_k, block_w = block_shape(depth, width)
    buffers = min(BUFFERS, (depth // block_k) * (width // block_w))
    any_spec = pl.BlockSpec(memory_space=pl.ANY)
    vmem_spec = pl.BlockSpec(memory_space=pltpu.VMEM)
    extra = rank_columns(factors)
    columns = width + (0 if apart else extra)
    out_shape = [
        jax.ShapeDtypeStruct((rows, columns), jnp.bfloat16),
        jax.ShapeDtypeStruct((rows, columns), jnp.float32),
    ] + [jax.ShapeDtypeStruct((rows, extra), jnp.float32)] * (2 if apart else 0)
    out_specs = [vmem_spec] * len(out_shape)
    out_shape += [pltpu.HBM((1, per_block, depth), jnp.bfloat16)] * staged
    out_specs += [any_spec] * staged
    return pl.pallas_call(
        functools.partial(matmul_body, spans, staged, apart),
        in_specs=[pl.BlockSpec(memory_space=pltpu.SMEM)] + [any_spec] * (2 * len(chunks) + 1) + [vmem_spec],
        out_specs=out_specs,
        out_shape=out_shape,
        scratch_shapes=[
            pltpu.VMEM((2, steps, per_block, depth), jnp.bfloat16),
            pltpu.VMEM((buffers, block_k, block_w), jnp.bfloat16),
            pltpu.VMEM((rows, columns), jnp.float32),
            pltpu.SemaphoreType.DMA((2 * len(chunks),)),
            pltpu.SemaphoreType.DMA((buffers,)),
        ] + ([
            pltpu.VMEM((staged, per_block, depth), jnp.bfloat16),
            pltpu.SemaphoreType.DMA((staged + 1,)),
        ] if staged else []),
        compiler_params=pltpu.CompilerParams(vmem_limit_bytes=VMEM_BYTES),
        cost_estimate=pl.CostEstimate(flops=0, bytes_accessed=0, transcendentals=0),
        name="partial_products",
    )(pos, *[source for own, sib, _, _ in chunks for source in (own, sib)], weight, factors)


def finish_body(received, panels, chosen_ref, slot_ref, order_ref, *refs):
    panel_refs, refs = refs[:panels], refs[panels:]
    per_panel = panel_refs[0].shape[0]
    out_ref, lifted_ref, done_ref, sem = refs[-4:]
    steps, rows, width = done_ref.shape
    rank = chosen_ref.shape[1]
    chosen = chosen_ref[...]
    slot = slot_ref[...]
    spread = jnp.concatenate(
        [
            jnp.where(slot == order_ref[place], chosen, jnp.zeros_like(chosen))
            for place in range(panels * per_panel // rank)
        ],
        axis=1,
    )
    block_n = min(BLOCK_N, width)
    for place in range(width // block_n):
        columns = slice(place * block_n, (place + 1) * block_n)
        panel = jnp.concatenate([panel_ref[:, columns] for panel_ref in panel_refs], axis=0)
        lifted = jnp.dot(spread, panel, preferred_element_type=jnp.float32).astype(jnp.bfloat16)
        for step in range(steps):
            total = refs[step * (received + 1)][:, columns]
            for value_ref in refs[step * (received + 1) + 1:(step + 1) * (received + 1)]:
                total = total + value_ref[:, columns].astype(jnp.float32)
            value = total + ADAPTER_SCALE * lifted[step * rows:(step + 1) * rows].astype(jnp.float32)
            done_ref[step, :, columns] = value.astype(done_ref.dtype)
        lifted_ref[:, columns] = lifted[steps * rows:]
    copy = pltpu.make_async_copy(done_ref, out_ref.at[pl.ds(0, steps)], sem)
    copy.start()
    copy.wait()


def finish_steps(totals, chosen, slots, order, panels):
    steps, width = len(totals), panels[0].shape[1]
    rows = chosen.shape[0] // (steps + 1)
    vmem_spec = pl.BlockSpec(memory_space=pltpu.VMEM)
    arrays = [value for total in totals for value in total]
    return pl.pallas_call(
        functools.partial(finish_body, len(totals[0]) - 1, len(panels)),
        in_specs=[vmem_spec, vmem_spec, pl.BlockSpec(memory_space=pltpu.SMEM)] + [vmem_spec] * (len(panels) + len(arrays)),
        out_specs=[pl.BlockSpec(memory_space=pl.ANY), vmem_spec],
        out_shape=[
            jax.ShapeDtypeStruct((steps + 1, rows, width), jnp.bfloat16),
            jax.ShapeDtypeStruct((rows, width), jnp.bfloat16),
        ],
        scratch_shapes=[pltpu.VMEM((steps, rows, width), jnp.bfloat16), pltpu.SemaphoreType.DMA],
        compiler_params=pltpu.CompilerParams(vmem_limit_bytes=VMEM_BYTES),
        cost_estimate=pl.CostEstimate(flops=0, bytes_accessed=0, transcendentals=0),
        name="finish_steps",
    )(chosen, slots, order, *panels, *arrays)


def last_body(partial_ref, lifted_ref, *refs):
    out_ref, done_ref, sem = refs[-3:]
    total = refs[0][...]
    for value_ref in refs[1:-3]:
        total = total + value_ref[...].astype(jnp.float32)
    value = total + ADAPTER_SCALE * lifted_ref[...].astype(jnp.float32)
    done_ref[0] = value.astype(done_ref.dtype)
    copy = pltpu.make_async_copy(done_ref, out_ref.at[pl.ds(out_ref.shape[0] - 1, 1)], sem)
    copy.start()
    copy.wait()


def finish_last(partial, lifted, arrays):
    vmem_spec = pl.BlockSpec(memory_space=pltpu.VMEM)
    any_spec = pl.BlockSpec(memory_space=pl.ANY)
    return pl.pallas_call(
        last_body,
        in_specs=[any_spec] + [vmem_spec] * (1 + len(arrays)),
        out_specs=any_spec,
        out_shape=jax.ShapeDtypeStruct(partial.shape, partial.dtype),
        input_output_aliases={0: 0},
        scratch_shapes=[pltpu.VMEM((1,) + partial.shape[1:], partial.dtype), pltpu.SemaphoreType.DMA],
        compiler_params=pltpu.CompilerParams(vmem_limit_bytes=VMEM_BYTES),
        cost_estimate=pl.CostEstimate(flops=0, bytes_accessed=0, transcendentals=0),
        name="finish_last",
    )(partial, lifted, *arrays)


def per_device(hidden, base_weight, down_a, up_b, adapter_ids, owner_map):
    step_count, per_block, _ = hidden.shape
    n_tensor = lax.axis_size("tp")
    n_rep = lax.axis_size("rep")
    n_sub = lax.axis_size("sub")
    n_owners = n_rep * n_sub
    tensor_index = lax.axis_index("tp")
    rep_index = lax.axis_index("rep")
    sub_index = lax.axis_index("sub")
    owner_index = lax.axis_index(("rep", "sub"))
    requests = per_block * n_owners
    rows_mine = requests // n_tensor
    group = n_tensor // n_rep
    group_index = tensor_index // group
    owned_slots, _, rank_size = down_a.shape
    slot_count = owned_slots * n_owners
    width = base_weight.shape[1]

    def after(value, *done):
        return lax.optimization_barrier((value, *done))[0]

    def swap_cores(value):
        return lax.ppermute(value, "sub", [(i, i ^ 1) for i in range(n_sub)])

    def from_rep(value, shift):
        return lax.ppermute(value, "rep", [((i + shift) % n_rep, i) for i in range(n_rep)])

    def swap_tensor(value, bit):
        return lax.ppermute(value, "tp", [(i, i ^ bit) for i in range(n_tensor)])

    def to_group(value, hop):
        moved = group * hop
        return lax.ppermute(value, "tp", [(i, (i + moved) % n_tensor) for i in range(n_tensor)])

    def pick(values, index):
        value = values[0]
        for at in range(1, len(values)):
            value = jnp.where(index == at, values[at], value)
        return value

    keeps = (tensor_index // (group // 2)) % 2
    pos = (sub_index == keeps).astype(jnp.int32).reshape(1)

    siblings = swap_cores(hidden)
    pieces = [(step, shift) for step in range(step_count) for shift in range(1, n_rep)]
    source = pltpu.with_memory_space_constraint(hidden, pltpu.HBM)
    weight = pltpu.with_memory_space_constraint(base_weight, pltpu.HBM)
    remote = {(0, shift): from_rep(hidden[:1], shift) for shift in range(1, n_rep)}

    def spread_panels(panels, order, bits):
        for bit in bits:
            panels = panels + [swap_tensor(panel, bit) for panel in panels]
            order = order + [at ^ bit for at in order]
        return panels, order

    bits = [n_tensor >> at for at in range(1, n_tensor.bit_length())]
    order = [0, bits[0], bits[1]]
    panels = [up_b] + [swap_tensor(up_b, at) for at in order[1:]]

    my_ids = lax.dynamic_slice_in_dim(adapter_ids, tensor_index * rows_mine, rows_mine)
    iota = lax.broadcasted_iota(jnp.int32, (rows_mine, slot_count), 1)
    my_slot = jnp.sum((my_ids == iota).astype(jnp.int32) * owner_map[None, :], axis=1)
    owned_hot = my_slot[:, None] == (
        owner_index * owned_slots + lax.broadcasted_iota(jnp.int32, (rows_mine, owned_slots), 1)
    )

    first_leg, halved, begun, second_leg, ended = [], {}, set(), [], {}

    def second_half(total, received, steps, kind):
        total = total + received.astype(jnp.float32)
        rows, columns = total.shape
        extent, bit = rows // steps, group // 4
        while bit:
            extent //= 2
            halves = total.reshape(steps, 2, extent, columns)
            mine = (tensor_index // bit) % 2
            kept = lax.dynamic_index_in_dim(halves, mine, 1, keepdims=False)
            sent = lax.dynamic_index_in_dim(halves, 1 - mine, 1, keepdims=False)
            total = kept + swap_tensor(sent.astype(kind), bit).astype(jnp.float32)
            bit //= 2
        return total.reshape(steps, extent, columns)

    def gap(token, jobs):
        nonlocal first_leg, second_leg
        for parts, received, keep, kind in first_leg:
            steps = sum(length for _, length in parts)
            total, begin = second_half(after(keep, token), received, steps, kind), 0
            for key, length in parts:
                for at in range(begin, begin + length):
                    halved[key[0] + at - begin, key[1]] = total[at]
                    if (key[0] + at - begin, key[1]) == (step_count - 1, 0):
                        halved[RANK_NAME, 0] = total[at][:, width:]
                begin += length
        closed = {name: (after(kept, token), *received) for name, kept, received in second_leg}
        started, sends = [], []
        for name in sorted({name for name, _ in halved}):
            if name in begun or name == RANK_NAME or any((name, at) not in halved for at in range(n_rep)):
                continue
            begun.add(name)
            values = [halved[name, at] for at in range(n_rep)]
            columns = min(value.shape[1] for value in values)
            values = [value[:, :columns] for value in values]
            kept = pick(values, (group_index - rep_index) % n_rep)
            sends.append([
                pick(values, (group_index + hop - rep_index) % n_rep).astype(jnp.bfloat16) for hop in range(1, n_rep)
            ])
            started.append((name, kept))
        sends, token = lax.optimization_barrier((sends, token))
        first_sends, closed = lax.optimization_barrier(([job[1] for job in jobs], closed))
        ended.update(closed)
        first_leg = [
            (parts, swap_tensor(send, group // 2), keep, kind) for (parts, _, keep, kind), send in zip(jobs, first_sends)
        ]
        second_leg = [
            (name, kept, [to_group(value, hop + 1) for hop, value in enumerate(sent)])
            for (name, kept), sent in zip(started, sends)
        ]
        return sends

    factors = jnp.swapaxes(down_a, 1, 2)

    lead = step_count // 2
    parts, last_ranks, next_local = [((0, 0), lead)], {}, lead
    send, keep, *slices = partial_products(
        pos, [(source, siblings, 0, lead)], weight, factors, staged=step_count - 1
    )
    for step, rows in enumerate(slices, 1):
        remote.update({(step, shift): from_rep(rows, shift) for shift in range(1, n_rep)})
    for piece, (step, shift) in enumerate(pieces):
        sends = gap(send, [(parts, send, keep, jnp.bfloat16)])
        own, panels, _ = lax.optimization_barrier((remote[step, shift], panels, send))
        if piece == 0:
            panels, order = panels + [swap_tensor(panels[1], bits[1])], order + [bits[0] ^ bits[1]]
            panels, order = spread_panels(panels, order, bits[2:])
        sib = swap_cores(own)
        own, sib, siblings, _ = lax.optimization_barrier((own, sib, siblings, sends))
        last, chunks, parts = step == step_count - 1, [(own, sib, 0, 1)], [((step, shift), 1)]
        if next_local < step_count:
            chunks.insert(0, (source, siblings, next_local, 1))
            parts.insert(0, ((next_local, 0), 1))
            next_local += 1
        send, keep, *ranks = partial_products(pos, chunks, weight, factors, last)
        if last:
            last_ranks[shift] = ranks
    gap(send, [(parts, send, keep, jnp.bfloat16)])
    for shift, ranks in last_ranks.items():
        halved[RANK_NAME, shift] = second_half(ranks[1], swap_tensor(ranks[0], group // 2), 1, jnp.float32)[0]
    values = [halved[RANK_NAME, at] for at in range(n_rep)]
    ended[RANK_NAME] = (pick(values, (group_index - rep_index) % n_rep), *[
        to_group(pick(values, (group_index + hop - rep_index) % n_rep), hop) for hop in range(1, n_rep)
    ])
    rounded = gap(send, [])

    def rank_sum(name):
        kept, *received = [value[:, -rank_columns(factors):] for value in ended[name]]
        for value in received:
            kept = kept + value.astype(jnp.float32)
        return kept[:, :owned_slots * rank_size]

    finished = jnp.stack([rank_sum(step) for step in range(step_count - 1)] + [rank_sum(RANK_NAME)])
    finished = finished.astype(jnp.bfloat16).reshape(step_count, rows_mine, owned_slots, rank_size)
    finished = lax.optimization_barrier((finished, rounded))[0]
    ended.update((name, (kept, *received)) for name, kept, received in second_leg)
    masked = jnp.sum(
        jnp.where(owned_hot[None, :, :, None], finished, 0), axis=2, dtype=jnp.float32
    ).astype(jnp.bfloat16)
    chosen = masked
    for turn in range(1, n_owners):
        chosen = chosen + lax.ppermute(
            masked, ("rep", "sub"), [(i, (i + turn) % n_owners) for i in range(n_owners)]
        )
    panel_slots = jnp.stack([
        (tensor_index ^ at) * up_b.shape[0] + each for at in order for each in range(up_b.shape[0])
    ]).astype(jnp.int32)

    panels = [panel.reshape(-1, width) for panel in panels]
    partial, lifted = finish_steps(
        [ended[step] for step in range(step_count - 1)],
        chosen.reshape(step_count * rows_mine, rank_size),
        jnp.broadcast_to(my_slot, (step_count, rows_mine)).reshape(step_count * rows_mine, 1),
        panel_slots,
        panels,
    )
    return finish_last(partial, lifted, ended[step_count - 1])


def solution(mesh):
    return jax.shard_map(
        per_device,
        mesh=mesh,
        in_specs=(
            P(None, ("groups", "rep", "sub"), "tp"),
            P("tp", ("rep", "sub")),
            P(("rep", "sub"), "tp", None),
            P("tp", None, ("rep", "sub")),
            P("groups", None),
            P(),
        ),
        out_specs=P(None, ("groups", "tp"), ("rep", "sub")),
        check_vma=False,
    )
```

```python
import functools

import jax
import jax.numpy as jnp
from jax import lax
from jax.experimental import pallas as pl
from jax.experimental.pallas import tpu as pltpu
from jax.sharding import PartitionSpec as P

ADAPTER_SCALE = 0.5
BLOCK_N = 256
BLOCK = 1024
BUFFERS = 4
RANK_NAME = 1000
VMEM_BYTES = 20 * 1024 * 1024


def block_shape(depth, width):
    columns = BLOCK if width % BLOCK == 0 else width
    for size in (BLOCK, BLOCK // 2, BLOCK // 4):
        if depth % size == 0:
            return size, columns
    return depth, columns


def rank_columns(factors):
    slots, rank, _ = factors.shape
    return -(-slots * rank // 128) * 128


def matmul_body(spans, staged, apart, pos_ref, *refs):
    sources = refs[:2 * len(spans)]
    w_ref, a_ref = refs[2 * len(spans):2 * len(spans) + 2]
    outs = refs[2 * len(spans) + 2:]
    send_refs, keep_refs, outs = outs[:len(spans)], outs[len(spans):2 * len(spans)], outs[2 * len(spans):]
    outs, refs = (outs[:-7], outs[-7:]) if staged else (outs[:-5], outs[-5:])
    x_ref, w_buf, total_ref, x_sems, w_sems = refs[:5]
    rows = total_ref.shape[0]
    edges = [0]
    for ref in send_refs:
        edges.append(edges[-1] + ref.shape[0])
    depth, width = w_ref.shape
    slots, rank, _ = a_ref.shape
    buffers, block_k, block_w = w_buf.shape
    block_n = min(BLOCK_N, block_w)
    depths, count = depth // block_k, (depth // block_k) * (width // block_w)

    def fetch(block, slot):
        begin = pl.multiple_of(lax.rem(block, depths) * block_k, block_k)
        left = pl.multiple_of(lax.div(block, depths) * block_w, block_w)
        return pltpu.make_async_copy(
            w_ref.at[pl.ds(begin, block_k), pl.ds(left, block_w)], w_buf.at[slot], w_sems.at[slot]
        )

    own_at = pos_ref[0]
    copies, begin = [], 0
    for index, (first, steps) in enumerate(spans):
        for core, at in enumerate((own_at, 1 - own_at)):
            source = sources[2 * index + core]
            copies.append(pltpu.make_async_copy(
                source.at[pl.ds(first, steps)], x_ref.at[at, pl.ds(begin, steps)], x_sems.at[2 * index + core]
            ))
        begin += steps
    for copy in copies:
        copy.start()
    if staged:
        stage_ref, stage_sems = refs[5:]
        stage_in = pltpu.make_async_copy(sources[0].at[pl.ds(1, staged)], stage_ref, stage_sems.at[staged])
        stage_in.start()
        stage_out = [
            pltpu.make_async_copy(stage_ref.at[pl.ds(index, 1)], out_ref, stage_sems.at[index])
            for index, out_ref in enumerate(outs)
        ]
    for block in range(buffers):
        fetch(jnp.int32(block), block).start()
    for ref in keep_refs:
        ref[...] = jnp.zeros_like(ref)
    total_ref[...] = jnp.zeros_like(total_ref)
    send_rank, keep_ranks = (outs[0], outs[1:2]) if apart else (total_ref, keep_refs)
    if apart:
        for ref in outs[:2]:
            ref[...] = jnp.zeros_like(ref)
    for copy in copies:
        copy.wait()
    if staged:
        stage_in.wait()
        for copy in stage_out:
            copy.start()
    for slot in range(slots):
        x = x_ref[...].reshape(2 * rows, depth)
        part = lax.dot_general(
            x, a_ref[slot], (((1,), (1,)), ((), ())), preferred_element_type=jnp.float32
        )
        begin = slot * rank + (0 if apart else width)
        send_rank[:, begin:begin + rank] = part[:rows]
        for index, ref in enumerate(keep_ranks):
            ref[:, begin:begin + rank] = part[rows + edges[index]:rows + edges[index + 1]]

    @pl.loop(0, count)
    def _(block):
        slot = lax.rem(block, buffers)
        fetch(block, slot).wait()
        inner = pl.ds(pl.multiple_of(lax.rem(block, depths) * block_k, block_k), block_k)
        left = pl.multiple_of(lax.div(block, depths) * block_w, block_w)
        x = x_ref[:, :, :, inner].reshape(2 * rows, block_k)
        for place in range(block_w // block_n):
            columns = pl.ds(left + place * block_n, block_n)
            term = jnp.dot(
                x, w_buf[slot, :, place * block_n:(place + 1) * block_n], preferred_element_type=jnp.float32
            )
            total_ref[:, columns] += term[:rows]
            for index, ref in enumerate(keep_refs):
                ref[:, columns] += term[rows + edges[index]:rows + edges[index + 1]]

        @pl.when(block + buffers < count)
        def _():
            fetch(block + buffers, slot).start()

    for index, ref in enumerate(send_refs):
        ref[...] = total_ref[edges[index]:edges[index + 1]].astype(ref.dtype)
    if staged:
        for copy in stage_out:
            copy.wait()


def partial_products(pos, chunks, weight, factors, apart=False, staged=0):
    _, per_block, depth = chunks[0][0].shape
    width = weight.shape[1]
    spans = tuple((first, steps) for _, _, first, steps in chunks)
    steps = sum(length for _, length in spans)
    rows = steps * per_block
    block_k, block_w = block_shape(depth, width)
    buffers = min(BUFFERS, (depth // block_k) * (width // block_w))
    any_spec = pl.BlockSpec(memory_space=pl.ANY)
    vmem_spec = pl.BlockSpec(memory_space=pltpu.VMEM)
    extra = rank_columns(factors)
    columns = width + (0 if apart else extra)
    out_shape = [
        jax.ShapeDtypeStruct((length * per_block, columns), kind)
        for kind in (jnp.bfloat16, jnp.float32) for _, length in spans
    ] + [jax.ShapeDtypeStruct((rows, extra), jnp.float32)] * (2 if apart else 0)
    out_specs = [vmem_spec] * len(out_shape)
    out_shape += [pltpu.HBM((1, per_block, depth), jnp.bfloat16)] * staged
    out_specs += [any_spec] * staged
    return pl.pallas_call(
        functools.partial(matmul_body, spans, staged, apart),
        in_specs=[pl.BlockSpec(memory_space=pltpu.SMEM)] + [any_spec] * (2 * len(chunks) + 1) + [vmem_spec],
        out_specs=out_specs,
        out_shape=out_shape,
        scratch_shapes=[
            pltpu.VMEM((2, steps, per_block, depth), jnp.bfloat16),
            pltpu.VMEM((buffers, block_k, block_w), jnp.bfloat16),
            pltpu.VMEM((rows, columns), jnp.float32),
            pltpu.SemaphoreType.DMA((2 * len(chunks),)),
            pltpu.SemaphoreType.DMA((buffers,)),
        ] + ([
            pltpu.VMEM((staged, per_block, depth), jnp.bfloat16),
            pltpu.SemaphoreType.DMA((staged + 1,)),
        ] if staged else []),
        compiler_params=pltpu.CompilerParams(vmem_limit_bytes=VMEM_BYTES),
        cost_estimate=pl.CostEstimate(flops=0, bytes_accessed=0, transcendentals=0),
        name="partial_products",
    )(pos, *[source for own, sib, _, _ in chunks for source in (own, sib)], weight, factors)


def finish_body(received, panels, chosen_ref, slot_ref, order_ref, *refs):
    panel_refs, refs = refs[:panels], refs[panels:]
    per_panel = panel_refs[0].shape[0]
    out_ref, lifted_ref, done_ref, sem = refs[-4:]
    steps, rows, width = done_ref.shape
    rank = chosen_ref.shape[1]
    chosen = chosen_ref[...]
    slot = slot_ref[...]
    spread = jnp.concatenate(
        [
            jnp.where(slot == order_ref[place], chosen, jnp.zeros_like(chosen))
            for place in range(panels * per_panel // rank)
        ],
        axis=1,
    )
    block_n = min(BLOCK_N, width)
    for place in range(width // block_n):
        columns = slice(place * block_n, (place + 1) * block_n)
        panel = jnp.concatenate([panel_ref[:, columns] for panel_ref in panel_refs], axis=0)
        lifted = jnp.dot(spread, panel, preferred_element_type=jnp.float32).astype(jnp.bfloat16)
        for step in range(steps):
            total = refs[step * (received + 1)][:, columns]
            for value_ref in refs[step * (received + 1) + 1:(step + 1) * (received + 1)]:
                total = total + value_ref[:, columns].astype(jnp.float32)
            value = total + ADAPTER_SCALE * lifted[step * rows:(step + 1) * rows].astype(jnp.float32)
            done_ref[step, :, columns] = value.astype(done_ref.dtype)
        lifted_ref[:, columns] = lifted[steps * rows:]
    copy = pltpu.make_async_copy(done_ref, out_ref.at[pl.ds(0, steps)], sem)
    copy.start()
    copy.wait()


def finish_steps(totals, chosen, slots, order, panels):
    steps, width = len(totals), panels[0].shape[1]
    rows = chosen.shape[0] // (steps + 1)
    vmem_spec = pl.BlockSpec(memory_space=pltpu.VMEM)
    arrays = [value for total in totals for value in total]
    return pl.pallas_call(
        functools.partial(finish_body, len(totals[0]) - 1, len(panels)),
        in_specs=[vmem_spec, vmem_spec, pl.BlockSpec(memory_space=pltpu.SMEM)] + [vmem_spec] * (len(panels) + len(arrays)),
        out_specs=[pl.BlockSpec(memory_space=pl.ANY), vmem_spec],
        out_shape=[
            jax.ShapeDtypeStruct((steps + 1, rows, width), jnp.bfloat16),
            jax.ShapeDtypeStruct((rows, width), jnp.bfloat16),
        ],
        scratch_shapes=[pltpu.VMEM((steps, rows, width), jnp.bfloat16), pltpu.SemaphoreType.DMA],
        compiler_params=pltpu.CompilerParams(vmem_limit_bytes=VMEM_BYTES),
        cost_estimate=pl.CostEstimate(flops=0, bytes_accessed=0, transcendentals=0),
        name="finish_steps",
    )(chosen, slots, order, *panels, *arrays)


def last_body(partial_ref, lifted_ref, *refs):
    out_ref, done_ref, sem = refs[-3:]
    total = refs[0][...]
    for value_ref in refs[1:-3]:
        total = total + value_ref[...].astype(jnp.float32)
    value = total + ADAPTER_SCALE * lifted_ref[...].astype(jnp.float32)
    done_ref[0] = value.astype(done_ref.dtype)
    copy = pltpu.make_async_copy(done_ref, out_ref.at[pl.ds(out_ref.shape[0] - 1, 1)], sem)
    copy.start()
    copy.wait()


def finish_last(partial, lifted, arrays):
    vmem_spec = pl.BlockSpec(memory_space=pltpu.VMEM)
    any_spec = pl.BlockSpec(memory_space=pl.ANY)
    return pl.pallas_call(
        last_body,
        in_specs=[any_spec] + [vmem_spec] * (1 + len(arrays)),
        out_specs=any_spec,
        out_shape=jax.ShapeDtypeStruct(partial.shape, partial.dtype),
        input_output_aliases={0: 0},
        scratch_shapes=[pltpu.VMEM((1,) + partial.shape[1:], partial.dtype), pltpu.SemaphoreType.DMA],
        compiler_params=pltpu.CompilerParams(vmem_limit_bytes=VMEM_BYTES),
        cost_estimate=pl.CostEstimate(flops=0, bytes_accessed=0, transcendentals=0),
        name="finish_last",
    )(partial, lifted, *arrays)


def per_device(hidden, base_weight, down_a, up_b, adapter_ids, owner_map):
    step_count, per_block, _ = hidden.shape
    n_tensor = lax.axis_size("tp")
    n_rep = lax.axis_size("rep")
    n_sub = lax.axis_size("sub")
    n_owners = n_rep * n_sub
    tensor_index = lax.axis_index("tp")
    rep_index = lax.axis_index("rep")
    sub_index = lax.axis_index("sub")
    owner_index = lax.axis_index(("rep", "sub"))
    requests = per_block * n_owners
    rows_mine = requests // n_tensor
    group = n_tensor // n_rep
    group_index = tensor_index // group
    owned_slots, _, rank_size = down_a.shape
    slot_count = owned_slots * n_owners
    width = base_weight.shape[1]

    def after(value, *done):
        return lax.optimization_barrier((value, *done))[0]

    def swap_cores(value):
        return lax.ppermute(value, "sub", [(i, i ^ 1) for i in range(n_sub)])

    def from_rep(value, shift):
        return lax.ppermute(value, "rep", [((i + shift) % n_rep, i) for i in range(n_rep)])

    def swap_tensor(value, bit):
        return lax.ppermute(value, "tp", [(i, i ^ bit) for i in range(n_tensor)])

    def to_group(value, hop):
        moved = group * hop
        return lax.ppermute(value, "tp", [(i, (i + moved) % n_tensor) for i in range(n_tensor)])

    def pick(values, index):
        value = values[0]
        for at in range(1, len(values)):
            value = jnp.where(index == at, values[at], value)
        return value

    keeps = (tensor_index // (group // 2)) % 2
    pos = (sub_index == keeps).astype(jnp.int32).reshape(1)

    siblings = swap_cores(hidden)
    pieces = [(step, shift) for step in range(step_count) for shift in range(1, n_rep)]
    source = pltpu.with_memory_space_constraint(hidden, pltpu.HBM)
    weight = pltpu.with_memory_space_constraint(base_weight, pltpu.HBM)
    remote = {(0, shift): from_rep(hidden[:1], shift) for shift in range(1, n_rep)}

    def spread_panels(panels, order, bits):
        for bit in bits:
            panels = panels + [swap_tensor(panel, bit) for panel in panels]
            order = order + [at ^ bit for at in order]
        return panels, order

    bits = [n_tensor >> at for at in range(1, n_tensor.bit_length())]
    order = [0, bits[0], bits[1]]
    panels = [up_b] + [swap_tensor(up_b, at) for at in order[1:]]

    my_ids = lax.dynamic_slice_in_dim(adapter_ids, tensor_index * rows_mine, rows_mine)
    iota = lax.broadcasted_iota(jnp.int32, (rows_mine, slot_count), 1)
    my_slot = jnp.sum((my_ids == iota).astype(jnp.int32) * owner_map[None, :], axis=1)
    owned_hot = my_slot[:, None] == (
        owner_index * owned_slots + lax.broadcasted_iota(jnp.int32, (rows_mine, owned_slots), 1)
    )

    first_leg, halved, begun, second_leg, ended = [], {}, set(), [], {}

    def second_half(total, received, steps, kind):
        total = total + received.astype(jnp.float32)
        rows, columns = total.shape
        extent, bit = rows // steps, group // 4
        while bit:
            extent //= 2
            halves = total.reshape(steps, 2, extent, columns)
            mine = (tensor_index // bit) % 2
            kept = lax.dynamic_index_in_dim(halves, mine, 1, keepdims=False)
            sent = lax.dynamic_index_in_dim(halves, 1 - mine, 1, keepdims=False)
            total = kept + swap_tensor(sent.astype(kind), bit).astype(jnp.float32)
            bit //= 2
        return total.reshape(steps, extent, columns)

    def gap(token, jobs):
        nonlocal first_leg, second_leg
        for parts, received, keep, kind in first_leg:
            steps = sum(length for _, length in parts)
            total, begin = second_half(after(keep, token), received, steps, kind), 0
            for key, length in parts:
                for at in range(begin, begin + length):
                    halved[key[0] + at - begin, key[1]] = total[at]
                    if (key[0] + at - begin, key[1]) == (step_count - 1, 0):
                        halved[RANK_NAME, 0] = total[at][:, width:]
                begin += length
        closed = {name: (after(kept, token), *received) for name, kept, received in second_leg}
        started, sends = [], []
        for name in sorted({name for name, _ in halved}):
            if name in begun or name == RANK_NAME or any((name, at) not in halved for at in range(n_rep)):
                continue
            begun.add(name)
            values = [halved[name, at] for at in range(n_rep)]
            columns = min(value.shape[1] for value in values)
            values = [value[:, :columns] for value in values]
            kept = pick(values, (group_index - rep_index) % n_rep)
            sends.append([
                pick(values, (group_index + hop - rep_index) % n_rep).astype(jnp.bfloat16) for hop in range(1, n_rep)
            ])
            started.append((name, kept))
        sends, token = lax.optimization_barrier((sends, token))
        first_sends, closed = lax.optimization_barrier(([job[1] for job in jobs], closed))
        ended.update(closed)
        first_leg = [
            (parts, swap_tensor(send, group // 2), keep, kind) for (parts, _, keep, kind), send in zip(jobs, first_sends)
        ]
        second_leg = [
            (name, kept, [to_group(value, hop + 1) for hop, value in enumerate(sent)])
            for (name, kept), sent in zip(started, sends)
        ]
        return sends

    factors = jnp.swapaxes(down_a, 1, 2)

    lead = step_count // 2
    last_ranks, next_local = {}, lead
    send, keep, *slices = partial_products(
        pos, [(source, siblings, 0, lead)], weight, factors, staged=step_count - 1
    )
    for step, rows in enumerate(slices, 1):
        remote.update({(step, shift): from_rep(rows, shift) for shift in range(1, n_rep)})
    jobs = [([((0, 0), lead)], send, keep, jnp.bfloat16)]
    for piece, (step, shift) in enumerate(pieces):
        sends = gap(send, jobs)
        own, panels, _ = lax.optimization_barrier((remote[step, shift], panels, send))
        if piece == 0:
            panels, order = panels + [swap_tensor(panels[1], bits[1])], order + [bits[0] ^ bits[1]]
            panels, order = spread_panels(panels, order, bits[2:])
        sib = swap_cores(own)
        own, sib, siblings, _ = lax.optimization_barrier((own, sib, siblings, sends))
        last, chunks, keys = step == step_count - 1, [(own, sib, 0, 1)], [(step, shift)]
        if next_local < step_count:
            chunks.append((source, siblings, next_local, 1))
            keys.append((next_local, 0))
            next_local += 1
        outs = partial_products(pos, chunks, weight, factors, last)
        send, count = outs[0], len(chunks)
        jobs = [([(key, 1)], outs[at], outs[count + at], jnp.bfloat16) for at, key in enumerate(keys)]
        if last:
            last_ranks[shift] = outs[2 * count:]
    gap(send, jobs)
    for shift, ranks in last_ranks.items():
        halved[RANK_NAME, shift] = second_half(ranks[1], swap_tensor(ranks[0], group // 2), 1, jnp.float32)[0]
    values = [halved[RANK_NAME, at] for at in range(n_rep)]
    ended[RANK_NAME] = (pick(values, (group_index - rep_index) % n_rep), *[
        to_group(pick(values, (group_index + hop - rep_index) % n_rep), hop) for hop in range(1, n_rep)
    ])
    rounded = gap(send, [])

    def rank_sum(name):
        kept, *received = [value[:, -rank_columns(factors):] for value in ended[name]]
        for value in received:
            kept = kept + value.astype(jnp.float32)
        return kept[:, :owned_slots * rank_size]

    finished = jnp.stack([rank_sum(step) for step in range(step_count - 1)] + [rank_sum(RANK_NAME)])
    finished = finished.astype(jnp.bfloat16).reshape(step_count, rows_mine, owned_slots, rank_size)
    finished = lax.optimization_barrier((finished, rounded))[0]
    ended.update((name, (kept, *received)) for name, kept, received in second_leg)
    masked = jnp.sum(
        jnp.where(owned_hot[None, :, :, None], finished, 0), axis=2, dtype=jnp.float32
    ).astype(jnp.bfloat16)
    chosen = masked
    for turn in range(1, n_owners):
        chosen = chosen + lax.ppermute(
            masked, ("rep", "sub"), [(i, (i + turn) % n_owners) for i in range(n_owners)]
        )
    panel_slots = jnp.stack([
        (tensor_index ^ at) * up_b.shape[0] + each for at in order for each in range(up_b.shape[0])
    ]).astype(jnp.int32)

    panels = [panel.reshape(-1, width) for panel in panels]
    partial, lifted = finish_steps(
        [ended[step] for step in range(step_count - 1)],
        chosen.reshape(step_count * rows_mine, rank_size),
        jnp.broadcast_to(my_slot, (step_count, rows_mine)).reshape(step_count * rows_mine, 1),
        panel_slots,
        panels,
    )
    return finish_last(partial, lifted, ended[step_count - 1])


def solution(mesh):
    return jax.shard_map(
        per_device,
        mesh=mesh,
        in_specs=(
            P(None, ("groups", "rep", "sub"), "tp"),
            P("tp", ("rep", "sub")),
            P(("rep", "sub"), "tp", None),
            P("tp", None, ("rep", "sub")),
            P("groups", None),
            P(),
        ),
        out_specs=P(None, ("groups", "tp"), ("rep", "sub")),
        check_vma=False,
    )
```

```python
import functools

import jax
import jax.numpy as jnp
from jax import lax
from jax.experimental import pallas as pl
from jax.experimental.pallas import tpu as pltpu
from jax.sharding import PartitionSpec as P

ADAPTER_SCALE = 0.5
BLOCK_N = 256
BLOCK = 1024
BUFFERS = 4
RANK_NAME = 1000
VMEM_BYTES = 20 * 1024 * 1024


def block_shape(depth, width):
    columns = BLOCK if width % BLOCK == 0 else width
    for size in (BLOCK, BLOCK // 2, BLOCK // 4):
        if depth % size == 0:
            return size, columns
    return depth, columns


def rank_columns(factors):
    slots, rank, _ = factors.shape
    return -(-slots * rank // 128) * 128


def matmul_body(spans, staged, apart, pos_ref, *refs):
    sources = refs[:2 * len(spans)]
    w_ref, a_ref = refs[2 * len(spans):2 * len(spans) + 2]
    outs = refs[2 * len(spans) + 2:]
    send_refs, keep_refs, outs = outs[:len(spans)], outs[len(spans):2 * len(spans)], outs[2 * len(spans):]
    outs, refs = (outs[:-7], outs[-7:]) if staged else (outs[:-5], outs[-5:])
    x_ref, w_buf, total_ref, x_sems, w_sems = refs[:5]
    rows = total_ref.shape[0]
    edges = [0]
    for ref in send_refs:
        edges.append(edges[-1] + ref.shape[0])
    depth, width = w_ref.shape
    slots, rank, _ = a_ref.shape
    buffers, block_k, block_w = w_buf.shape
    block_n = min(BLOCK_N, block_w)
    depths, count = depth // block_k, (depth // block_k) * (width // block_w)

    def fetch(block, slot):
        begin = pl.multiple_of(lax.rem(block, depths) * block_k, block_k)
        left = pl.multiple_of(lax.div(block, depths) * block_w, block_w)
        return pltpu.make_async_copy(
            w_ref.at[pl.ds(begin, block_k), pl.ds(left, block_w)], w_buf.at[slot], w_sems.at[slot]
        )

    own_at = pos_ref[0]
    copies, begin = [], 0
    for index, (first, steps) in enumerate(spans):
        for core, at in enumerate((own_at, 1 - own_at)):
            source = sources[2 * index + core]
            copies.append(pltpu.make_async_copy(
                source.at[pl.ds(first, steps)], x_ref.at[at, pl.ds(begin, steps)], x_sems.at[2 * index + core]
            ))
        begin += steps
    for copy in copies:
        copy.start()
    if staged:
        stage_ref, stage_sems = refs[5:]
        stage_in = pltpu.make_async_copy(sources[0].at[pl.ds(1, staged)], stage_ref, stage_sems.at[staged])
        stage_in.start()
        stage_out = [
            pltpu.make_async_copy(stage_ref.at[pl.ds(index, 1)], out_ref, stage_sems.at[index])
            for index, out_ref in enumerate(outs)
        ]
    for block in range(buffers):
        fetch(jnp.int32(block), block).start()
    for ref in keep_refs:
        ref[...] = jnp.zeros_like(ref)
    total_ref[...] = jnp.zeros_like(total_ref)
    send_rank, keep_ranks = (outs[0], outs[1:2]) if apart else (total_ref, keep_refs)
    if apart:
        for ref in outs[:2]:
            ref[...] = jnp.zeros_like(ref)
    for copy in copies:
        copy.wait()
    if staged:
        stage_in.wait()
        for copy in stage_out:
            copy.start()
    for slot in range(slots):
        x = x_ref[...].reshape(2 * rows, depth)
        part = lax.dot_general(
            x, a_ref[slot], (((1,), (1,)), ((), ())), preferred_element_type=jnp.float32
        )
        begin = slot * rank + (0 if apart else width)
        send_rank[:, begin:begin + rank] = part[:rows]
        for index, ref in enumerate(keep_ranks):
            ref[:, begin:begin + rank] = part[rows + edges[index]:rows + edges[index + 1]]

    @pl.loop(0, count)
    def _(block):
        slot = lax.rem(block, buffers)
        fetch(block, slot).wait()
        inner = pl.ds(pl.multiple_of(lax.rem(block, depths) * block_k, block_k), block_k)
        left = pl.multiple_of(lax.div(block, depths) * block_w, block_w)
        x = x_ref[:, :, :, inner].reshape(2 * rows, block_k)
        for place in range(block_w // block_n):
            columns = pl.ds(left + place * block_n, block_n)
            term = jnp.dot(
                x, w_buf[slot, :, place * block_n:(place + 1) * block_n], preferred_element_type=jnp.float32
            )
            total_ref[:, columns] += term[:rows]
            for index, ref in enumerate(keep_refs):
                ref[:, columns] += term[rows + edges[index]:rows + edges[index + 1]]

        @pl.when(block + buffers < count)
        def _():
            fetch(block + buffers, slot).start()

    for index, ref in enumerate(send_refs):
        ref[...] = total_ref[edges[index]:edges[index + 1]].astype(ref.dtype)
    if staged:
        for copy in stage_out:
            copy.wait()


def partial_products(pos, chunks, weight, factors, apart=False, staged=0):
    _, per_block, depth = chunks[0][0].shape
    width = weight.shape[1]
    spans = tuple((first, steps) for _, _, first, steps in chunks)
    steps = sum(length for _, length in spans)
    rows = steps * per_block
    block_k, block_w = block_shape(depth, width)
    buffers = min(BUFFERS, (depth // block_k) * (width // block_w))
    any_spec = pl.BlockSpec(memory_space=pl.ANY)
    vmem_spec = pl.BlockSpec(memory_space=pltpu.VMEM)
    extra = rank_columns(factors)
    columns = width + (0 if apart else extra)
    out_shape = [
        jax.ShapeDtypeStruct((length * per_block, columns), kind)
        for kind in (jnp.bfloat16, jnp.float32) for _, length in spans
    ] + [jax.ShapeDtypeStruct((rows, extra), jnp.float32)] * (2 if apart else 0)
    out_specs = [vmem_spec] * len(out_shape)
    out_shape += [pltpu.HBM((1, per_block, depth), jnp.bfloat16)] * staged
    out_specs += [any_spec] * staged
    return pl.pallas_call(
        functools.partial(matmul_body, spans, staged, apart),
        in_specs=[pl.BlockSpec(memory_space=pltpu.SMEM)] + [any_spec] * (2 * len(chunks) + 1) + [vmem_spec],
        out_specs=out_specs,
        out_shape=out_shape,
        scratch_shapes=[
            pltpu.VMEM((2, steps, per_block, depth), jnp.bfloat16),
            pltpu.VMEM((buffers, block_k, block_w), jnp.bfloat16),
            pltpu.VMEM((rows, columns), jnp.float32),
            pltpu.SemaphoreType.DMA((2 * len(chunks),)),
            pltpu.SemaphoreType.DMA((buffers,)),
        ] + ([
            pltpu.VMEM((staged, per_block, depth), jnp.bfloat16),
            pltpu.SemaphoreType.DMA((staged + 1,)),
        ] if staged else []),
        compiler_params=pltpu.CompilerParams(vmem_limit_bytes=VMEM_BYTES),
        cost_estimate=pl.CostEstimate(flops=0, bytes_accessed=0, transcendentals=0),
        name="partial_products",
    )(pos, *[source for own, sib, _, _ in chunks for source in (own, sib)], weight, factors)


def finish_body(received, panels, chosen_ref, slot_ref, order_ref, *refs):
    panel_refs, refs = refs[:panels], refs[panels:]
    per_panel = panel_refs[0].shape[0]
    out_ref, lifted_ref, done_ref, sem = refs[-4:]
    steps, rows, width = done_ref.shape
    rank = chosen_ref.shape[1]
    chosen = chosen_ref[...]
    slot = slot_ref[...]
    spread = jnp.concatenate(
        [
            jnp.where(slot == order_ref[place], chosen, jnp.zeros_like(chosen))
            for place in range(panels * per_panel // rank)
        ],
        axis=1,
    )
    block_n = min(BLOCK_N, width)
    for place in range(width // block_n):
        columns = slice(place * block_n, (place + 1) * block_n)
        panel = jnp.concatenate([panel_ref[:, columns] for panel_ref in panel_refs], axis=0)
        lifted = jnp.dot(spread, panel, preferred_element_type=jnp.float32).astype(jnp.bfloat16)
        for step in range(steps):
            total = refs[step * (received + 1)][:, columns]
            for value_ref in refs[step * (received + 1) + 1:(step + 1) * (received + 1)]:
                total = total + value_ref[:, columns].astype(jnp.float32)
            value = total + ADAPTER_SCALE * lifted[step * rows:(step + 1) * rows].astype(jnp.float32)
            done_ref[step, :, columns] = value.astype(done_ref.dtype)
        lifted_ref[:, columns] = lifted[steps * rows:]
    copy = pltpu.make_async_copy(done_ref, out_ref.at[pl.ds(0, steps)], sem)
    copy.start()
    copy.wait()


def finish_steps(totals, chosen, slots, order, panels):
    steps, width = len(totals), panels[0].shape[1]
    rows = chosen.shape[0] // (steps + 1)
    vmem_spec = pl.BlockSpec(memory_space=pltpu.VMEM)
    arrays = [value for total in totals for value in total]
    return pl.pallas_call(
        functools.partial(finish_body, len(totals[0]) - 1, len(panels)),
        in_specs=[vmem_spec, vmem_spec, pl.BlockSpec(memory_space=pltpu.SMEM)] + [vmem_spec] * (len(panels) + len(arrays)),
        out_specs=[pl.BlockSpec(memory_space=pl.ANY), vmem_spec],
        out_shape=[
            jax.ShapeDtypeStruct((steps + 1, rows, width), jnp.bfloat16),
            jax.ShapeDtypeStruct((rows, width), jnp.bfloat16),
        ],
        scratch_shapes=[pltpu.VMEM((steps, rows, width), jnp.bfloat16), pltpu.SemaphoreType.DMA],
        compiler_params=pltpu.CompilerParams(vmem_limit_bytes=VMEM_BYTES),
        cost_estimate=pl.CostEstimate(flops=0, bytes_accessed=0, transcendentals=0),
        name="finish_steps",
    )(chosen, slots, order, *panels, *arrays)


def last_body(partial_ref, lifted_ref, *refs):
    out_ref, done_ref, sem = refs[-3:]
    total = refs[0][...]
    for value_ref in refs[1:-3]:
        total = total + value_ref[...].astype(jnp.float32)
    value = total + ADAPTER_SCALE * lifted_ref[...].astype(jnp.float32)
    done_ref[0] = value.astype(done_ref.dtype)
    copy = pltpu.make_async_copy(done_ref, out_ref.at[pl.ds(out_ref.shape[0] - 1, 1)], sem)
    copy.start()
    copy.wait()


def finish_last(partial, lifted, arrays):
    vmem_spec = pl.BlockSpec(memory_space=pltpu.VMEM)
    any_spec = pl.BlockSpec(memory_space=pl.ANY)
    return pl.pallas_call(
        last_body,
        in_specs=[any_spec] + [vmem_spec] * (1 + len(arrays)),
        out_specs=any_spec,
        out_shape=jax.ShapeDtypeStruct(partial.shape, partial.dtype),
        input_output_aliases={0: 0},
        scratch_shapes=[pltpu.VMEM((1,) + partial.shape[1:], partial.dtype), pltpu.SemaphoreType.DMA],
        compiler_params=pltpu.CompilerParams(vmem_limit_bytes=VMEM_BYTES),
        cost_estimate=pl.CostEstimate(flops=0, bytes_accessed=0, transcendentals=0),
        name="finish_last",
    )(partial, lifted, *arrays)


def per_device(hidden, base_weight, down_a, up_b, adapter_ids, owner_map):
    step_count, per_block, _ = hidden.shape
    n_tensor = lax.axis_size("tp")
    n_rep = lax.axis_size("rep")
    n_sub = lax.axis_size("sub")
    n_owners = n_rep * n_sub
    tensor_index = lax.axis_index("tp")
    rep_index = lax.axis_index("rep")
    sub_index = lax.axis_index("sub")
    owner_index = lax.axis_index(("rep", "sub"))
    requests = per_block * n_owners
    rows_mine = requests // n_tensor
    group = n_tensor // n_rep
    group_index = tensor_index // group
    owned_slots, _, rank_size = down_a.shape
    slot_count = owned_slots * n_owners
    width = base_weight.shape[1]

    def after(value, *done):
        return lax.optimization_barrier((value, *done))[0]

    def swap_cores(value):
        return lax.ppermute(value, "sub", [(i, i ^ 1) for i in range(n_sub)])

    def from_rep(value, shift):
        return lax.ppermute(value, "rep", [((i + shift) % n_rep, i) for i in range(n_rep)])

    def swap_tensor(value, bit):
        return lax.ppermute(value, "tp", [(i, i ^ bit) for i in range(n_tensor)])

    def to_group(value, hop):
        moved = group * hop
        return lax.ppermute(value, "tp", [(i, (i + moved) % n_tensor) for i in range(n_tensor)])

    def pick(values, index):
        value = values[0]
        for at in range(1, len(values)):
            value = jnp.where(index == at, values[at], value)
        return value

    keeps = (tensor_index // (group // 2)) % 2
    pos = (sub_index == keeps).astype(jnp.int32).reshape(1)

    siblings = swap_cores(hidden)
    pieces = [(step, shift) for step in range(step_count) for shift in range(1, n_rep)]
    source = pltpu.with_memory_space_constraint(hidden, pltpu.HBM)
    weight = pltpu.with_memory_space_constraint(base_weight, pltpu.HBM)
    remote = {(0, shift): from_rep(hidden[:1], shift) for shift in range(1, n_rep)}

    def spread_panels(panels, order, bits):
        for bit in bits:
            panels = panels + [swap_tensor(panel, bit) for panel in panels]
            order = order + [at ^ bit for at in order]
        return panels, order

    bits = [n_tensor >> at for at in range(1, n_tensor.bit_length())]
    order = [0, bits[0], bits[1]]
    panels = [up_b] + [swap_tensor(up_b, at) for at in order[1:]]

    my_ids = lax.dynamic_slice_in_dim(adapter_ids, tensor_index * rows_mine, rows_mine)
    iota = lax.broadcasted_iota(jnp.int32, (rows_mine, slot_count), 1)
    my_slot = jnp.sum((my_ids == iota).astype(jnp.int32) * owner_map[None, :], axis=1)
    owned_hot = my_slot[:, None] == (
        owner_index * owned_slots + lax.broadcasted_iota(jnp.int32, (rows_mine, owned_slots), 1)
    )

    first_leg, halved, begun, second_leg, ended = [], {}, set(), [], {}

    def second_half(total, received, steps, kind):
        total = total + received.astype(jnp.float32)
        rows, columns = total.shape
        extent, bit = rows // steps, group // 4
        while bit:
            extent //= 2
            halves = total.reshape(steps, 2, extent, columns)
            mine = (tensor_index // bit) % 2
            kept = lax.dynamic_index_in_dim(halves, mine, 1, keepdims=False)
            sent = lax.dynamic_index_in_dim(halves, 1 - mine, 1, keepdims=False)
            total = kept + swap_tensor(sent.astype(kind), bit).astype(jnp.float32)
            bit //= 2
        return total.reshape(steps, extent, columns)

    def gap(token, jobs):
        nonlocal first_leg, second_leg
        for parts, received, keep, kind in first_leg:
            steps = sum(length for _, length in parts)
            total, begin = second_half(after(keep, token), received, steps, kind), 0
            for key, length in parts:
                for at in range(begin, begin + length):
                    halved[key[0] + at - begin, key[1]] = total[at]
                    if (key[0] + at - begin, key[1]) == (step_count - 1, 0):
                        halved[RANK_NAME, 0] = total[at][:, width:]
                begin += length
        closed = {name: (after(kept, token), *received) for name, kept, received in second_leg}
        started, sends = [], []
        for name in sorted({name for name, _ in halved}):
            if name in begun or name == RANK_NAME or any((name, at) not in halved for at in range(n_rep)):
                continue
            begun.add(name)
            values = [halved[name, at] for at in range(n_rep)]
            columns = min(value.shape[1] for value in values)
            values = [value[:, :columns] for value in values]
            kept = pick(values, (group_index - rep_index) % n_rep)
            sends.append([
                pick(values, (group_index + hop - rep_index) % n_rep).astype(jnp.bfloat16) for hop in range(1, n_rep)
            ])
            started.append((name, kept))
        sends, token = lax.optimization_barrier((sends, token))
        first_sends, closed = lax.optimization_barrier(([job[1] for job in jobs], closed))
        ended.update(closed)
        first_leg = [
            (parts, swap_tensor(send, group // 2), keep, kind) for (parts, _, keep, kind), send in zip(jobs, first_sends)
        ]
        second_leg = [
            (name, kept, [to_group(value, hop + 1) for hop, value in enumerate(sent)])
            for (name, kept), sent in zip(started, sends)
        ]
        return sends

    factors = jnp.swapaxes(down_a, 1, 2)

    lead = step_count // 2
    last_ranks, next_local = {}, lead
    send, keep, *slices = partial_products(
        pos, [(source, siblings, 0, lead)], weight, factors, staged=step_count - 1
    )
    for step, rows in enumerate(slices, 1):
        remote.update({(step, shift): from_rep(rows, shift) for shift in range(1, n_rep)})
    jobs = [([((0, 0), lead)], send, keep, jnp.bfloat16)]
    for piece, (step, shift) in enumerate(pieces):
        arrived = [received for _, received, _, _ in first_leg]
        sends = gap(send, jobs)
        own, panels, *_ = lax.optimization_barrier((remote[step, shift], panels, arrived, send))
        if piece == 0:
            panels, order = panels + [swap_tensor(panels[1], bits[1])], order + [bits[0] ^ bits[1]]
            panels, order = spread_panels(panels, order, bits[2:])
        sib = swap_cores(own)
        own, sib, siblings, _ = lax.optimization_barrier((own, sib, siblings, sends))
        last, chunks, keys = step == step_count - 1, [(own, sib, 0, 1)], [(step, shift)]
        if next_local < step_count:
            chunks.append((source, siblings, next_local, 1))
            keys.append((next_local, 0))
            next_local += 1
        outs = partial_products(pos, chunks, weight, factors, last)
        send, count = outs[0], len(chunks)
        jobs = [([(key, 1)], outs[at], outs[count + at], jnp.bfloat16) for at, key in enumerate(keys)]
        if last:
            last_ranks[shift] = outs[2 * count:]
    gap(send, jobs)
    for shift, ranks in last_ranks.items():
        halved[RANK_NAME, shift] = second_half(ranks[1], swap_tensor(ranks[0], group // 2), 1, jnp.float32)[0]
    values = [halved[RANK_NAME, at] for at in range(n_rep)]
    ended[RANK_NAME] = (pick(values, (group_index - rep_index) % n_rep), *[
        to_group(pick(values, (group_index + hop - rep_index) % n_rep), hop) for hop in range(1, n_rep)
    ])
    rounded = gap(send, [])
    kept, *received = ended[RANK_NAME]
    ended[RANK_NAME] = (after(kept, rounded), *received)

    def rank_sum(name):
        kept, *received = [value[:, -rank_columns(factors):] for value in ended[name]]
        for value in received:
            kept = kept + value.astype(jnp.float32)
        return kept[:, :owned_slots * rank_size]

    finished = jnp.stack([rank_sum(step) for step in range(step_count - 1)] + [rank_sum(RANK_NAME)])
    finished = finished.astype(jnp.bfloat16).reshape(step_count, rows_mine, owned_slots, rank_size)
    ended.update((name, (kept, *received)) for name, kept, received in second_leg)
    masked = jnp.sum(
        jnp.where(owned_hot[None, :, :, None], finished, 0), axis=2, dtype=jnp.float32
    ).astype(jnp.bfloat16)
    chosen = masked
    for turn in range(1, n_owners):
        chosen = chosen + lax.ppermute(
            masked, ("rep", "sub"), [(i, (i + turn) % n_owners) for i in range(n_owners)]
        )
    panel_slots = jnp.stack([
        (tensor_index ^ at) * up_b.shape[0] + each for at in order for each in range(up_b.shape[0])
    ]).astype(jnp.int32)

    panels = [panel.reshape(-1, width) for panel in panels]
    partial, lifted = finish_steps(
        [ended[step] for step in range(step_count - 1)],
        chosen.reshape(step_count * rows_mine, rank_size),
        jnp.broadcast_to(my_slot, (step_count, rows_mine)).reshape(step_count * rows_mine, 1),
        panel_slots,
        panels,
    )
    return finish_last(partial, lifted, ended[step_count - 1])


def solution(mesh):
    return jax.shard_map(
        per_device,
        mesh=mesh,
        in_specs=(
            P(None, ("groups", "rep", "sub"), "tp"),
            P("tp", ("rep", "sub")),
            P(("rep", "sub"), "tp", None),
            P("tp", None, ("rep", "sub")),
            P("groups", None),
            P(),
        ),
        out_specs=P(None, ("groups", "tp"), ("rep", "sub")),
        check_vma=False,
    )
```

```python
import functools

import jax
import jax.numpy as jnp
from jax import lax
from jax.experimental import pallas as pl
from jax.experimental.pallas import tpu as pltpu
from jax.sharding import PartitionSpec as P

ADAPTER_SCALE = 0.5
BLOCK_N = 256
BLOCK = 1024
BUFFERS = 4
RANK_NAME = 1000
VMEM_BYTES = 20 * 1024 * 1024


def block_shape(depth, width):
    columns = BLOCK if width % BLOCK == 0 else width
    for size in (BLOCK, BLOCK // 2, BLOCK // 4):
        if depth % size == 0:
            return size, columns
    return depth, columns


def rank_columns(factors):
    slots, rank, _ = factors.shape
    return -(-slots * rank // 128) * 128


def matmul_body(spans, staged, apart, pos_ref, *refs):
    sources = refs[:2 * len(spans)]
    w_ref, a_ref = refs[2 * len(spans):2 * len(spans) + 2]
    outs = refs[2 * len(spans) + 2:]
    send_refs, keep_refs, outs = outs[:len(spans)], outs[len(spans):2 * len(spans)], outs[2 * len(spans):]
    outs, refs = (outs[:-7], outs[-7:]) if staged else (outs[:-5], outs[-5:])
    x_ref, w_buf, total_ref, x_sems, w_sems = refs[:5]
    rows = total_ref.shape[0]
    edges = [0]
    for ref in send_refs:
        edges.append(edges[-1] + ref.shape[0])
    depth, width = w_ref.shape
    slots, rank, _ = a_ref.shape
    buffers, block_k, block_w = w_buf.shape
    block_n = min(BLOCK_N, block_w)
    depths, count = depth // block_k, (depth // block_k) * (width // block_w)

    def fetch(block, slot):
        begin = pl.multiple_of(lax.rem(block, depths) * block_k, block_k)
        left = pl.multiple_of(lax.div(block, depths) * block_w, block_w)
        return pltpu.make_async_copy(
            w_ref.at[pl.ds(begin, block_k), pl.ds(left, block_w)], w_buf.at[slot], w_sems.at[slot]
        )

    own_at = pos_ref[0]
    copies, begin = [], 0
    for index, (first, steps) in enumerate(spans):
        for core, at in enumerate((own_at, 1 - own_at)):
            source = sources[2 * index + core]
            copies.append(pltpu.make_async_copy(
                source.at[pl.ds(first, steps)], x_ref.at[at, pl.ds(begin, steps)], x_sems.at[2 * index + core]
            ))
        begin += steps
    for copy in copies:
        copy.start()
    if staged:
        stage_ref, stage_sems = refs[5:]
        stage_in = pltpu.make_async_copy(sources[0].at[pl.ds(1, staged)], stage_ref, stage_sems.at[staged])
        stage_in.start()
        stage_out = [
            pltpu.make_async_copy(stage_ref.at[pl.ds(index, 1)], out_ref, stage_sems.at[index])
            for index, out_ref in enumerate(outs)
        ]
    for block in range(buffers):
        fetch(jnp.int32(block), block).start()
    for ref in keep_refs:
        ref[...] = jnp.zeros_like(ref)
    total_ref[...] = jnp.zeros_like(total_ref)
    send_rank, keep_ranks = (outs[0], outs[1:2]) if apart else (total_ref, keep_refs)
    if apart:
        for ref in outs[:2]:
            ref[...] = jnp.zeros_like(ref)
    for copy in copies:
        copy.wait()
    if staged:
        stage_in.wait()
        for copy in stage_out:
            copy.start()
    for slot in range(slots):
        x = x_ref[...].reshape(2 * rows, depth)
        part = lax.dot_general(
            x, a_ref[slot], (((1,), (1,)), ((), ())), preferred_element_type=jnp.float32
        )
        begin = slot * rank + (0 if apart else width)
        send_rank[:, begin:begin + rank] = part[:rows]
        for index, ref in enumerate(keep_ranks):
            ref[:, begin:begin + rank] = part[rows + edges[index]:rows + edges[index + 1]]

    @pl.loop(0, count)
    def _(block):
        slot = lax.rem(block, buffers)
        fetch(block, slot).wait()
        inner = pl.ds(pl.multiple_of(lax.rem(block, depths) * block_k, block_k), block_k)
        left = pl.multiple_of(lax.div(block, depths) * block_w, block_w)
        x = x_ref[:, :, :, inner].reshape(2 * rows, block_k)
        for place in range(block_w // block_n):
            columns = pl.ds(left + place * block_n, block_n)
            term = jnp.dot(
                x, w_buf[slot, :, place * block_n:(place + 1) * block_n], preferred_element_type=jnp.float32
            )
            total_ref[:, columns] += term[:rows]
            for index, ref in enumerate(keep_refs):
                ref[:, columns] += term[rows + edges[index]:rows + edges[index + 1]]

        @pl.when(block + buffers < count)
        def _():
            fetch(block + buffers, slot).start()

    for index, ref in enumerate(send_refs):
        ref[...] = total_ref[edges[index]:edges[index + 1]].astype(ref.dtype)
    if staged:
        for copy in stage_out:
            copy.wait()


def partial_products(pos, chunks, weight, factors, apart=False, staged=0):
    _, per_block, depth = chunks[0][0].shape
    width = weight.shape[1]
    spans = tuple((first, steps) for _, _, first, steps in chunks)
    steps = sum(length for _, length in spans)
    rows = steps * per_block
    block_k, block_w = block_shape(depth, width)
    buffers = min(BUFFERS, (depth // block_k) * (width // block_w))
    any_spec = pl.BlockSpec(memory_space=pl.ANY)
    vmem_spec = pl.BlockSpec(memory_space=pltpu.VMEM)
    extra = rank_columns(factors)
    columns = width + (0 if apart else extra)
    out_shape = [
        jax.ShapeDtypeStruct((length * per_block, columns), kind)
        for kind in (jnp.bfloat16, jnp.float32) for _, length in spans
    ] + [jax.ShapeDtypeStruct((rows, extra), jnp.float32)] * (2 if apart else 0)
    out_specs = [vmem_spec] * len(out_shape)
    out_shape += [pltpu.HBM((1, per_block, depth), jnp.bfloat16)] * staged
    out_specs += [any_spec] * staged
    return pl.pallas_call(
        functools.partial(matmul_body, spans, staged, apart),
        in_specs=[pl.BlockSpec(memory_space=pltpu.SMEM)] + [any_spec] * (2 * len(chunks) + 1) + [vmem_spec],
        out_specs=out_specs,
        out_shape=out_shape,
        scratch_shapes=[
            pltpu.VMEM((2, steps, per_block, depth), jnp.bfloat16),
            pltpu.VMEM((buffers, block_k, block_w), jnp.bfloat16),
            pltpu.VMEM((rows, columns), jnp.float32),
            pltpu.SemaphoreType.DMA((2 * len(chunks),)),
            pltpu.SemaphoreType.DMA((buffers,)),
        ] + ([
            pltpu.VMEM((staged, per_block, depth), jnp.bfloat16),
            pltpu.SemaphoreType.DMA((staged + 1,)),
        ] if staged else []),
        compiler_params=pltpu.CompilerParams(vmem_limit_bytes=VMEM_BYTES),
        cost_estimate=pl.CostEstimate(flops=0, bytes_accessed=0, transcendentals=0),
        name="partial_products",
    )(pos, *[source for own, sib, _, _ in chunks for source in (own, sib)], weight, factors)


def finish_body(received, panels, chosen_ref, slot_ref, order_ref, *refs):
    panel_refs, refs = refs[:panels], refs[panels:]
    per_panel = panel_refs[0].shape[0]
    out_ref, lifted_ref, done_ref, sem = refs[-4:]
    steps, rows, width = done_ref.shape
    rank = chosen_ref.shape[1]
    chosen = chosen_ref[...]
    slot = slot_ref[...]
    spread = jnp.concatenate(
        [
            jnp.where(slot == order_ref[place], chosen, jnp.zeros_like(chosen))
            for place in range(panels * per_panel // rank)
        ],
        axis=1,
    )
    block_n = min(BLOCK_N, width)
    for place in range(width // block_n):
        columns = slice(place * block_n, (place + 1) * block_n)
        panel = jnp.concatenate([panel_ref[:, columns] for panel_ref in panel_refs], axis=0)
        lifted = jnp.dot(spread, panel, preferred_element_type=jnp.float32).astype(jnp.bfloat16)
        for step in range(steps):
            total = refs[step * (received + 1)][:, columns]
            for value_ref in refs[step * (received + 1) + 1:(step + 1) * (received + 1)]:
                total = total + value_ref[:, columns].astype(jnp.float32)
            value = total + ADAPTER_SCALE * lifted[step * rows:(step + 1) * rows].astype(jnp.float32)
            done_ref[step, :, columns] = value.astype(done_ref.dtype)
        lifted_ref[:, columns] = lifted[steps * rows:]
    copy = pltpu.make_async_copy(done_ref, out_ref.at[pl.ds(0, steps)], sem)
    copy.start()
    copy.wait()


def finish_steps(totals, chosen, slots, order, panels):
    steps, width = len(totals), panels[0].shape[1]
    rows = chosen.shape[0] // (steps + 1)
    vmem_spec = pl.BlockSpec(memory_space=pltpu.VMEM)
    arrays = [value for total in totals for value in total]
    return pl.pallas_call(
        functools.partial(finish_body, len(totals[0]) - 1, len(panels)),
        in_specs=[vmem_spec, vmem_spec, pl.BlockSpec(memory_space=pltpu.SMEM)] + [vmem_spec] * (len(panels) + len(arrays)),
        out_specs=[pl.BlockSpec(memory_space=pl.ANY), vmem_spec],
        out_shape=[
            jax.ShapeDtypeStruct((steps + 1, rows, width), jnp.bfloat16),
            jax.ShapeDtypeStruct((rows, width), jnp.bfloat16),
        ],
        scratch_shapes=[pltpu.VMEM((steps, rows, width), jnp.bfloat16), pltpu.SemaphoreType.DMA],
        compiler_params=pltpu.CompilerParams(vmem_limit_bytes=VMEM_BYTES),
        cost_estimate=pl.CostEstimate(flops=0, bytes_accessed=0, transcendentals=0),
        name="finish_steps",
    )(chosen, slots, order, *panels, *arrays)


def last_body(partial_ref, lifted_ref, *refs):
    out_ref, done_ref, sem = refs[-3:]
    total = refs[0][...]
    for value_ref in refs[1:-3]:
        total = total + value_ref[...].astype(jnp.float32)
    value = total + ADAPTER_SCALE * lifted_ref[...].astype(jnp.float32)
    done_ref[0] = value.astype(done_ref.dtype)
    copy = pltpu.make_async_copy(done_ref, out_ref.at[pl.ds(out_ref.shape[0] - 1, 1)], sem)
    copy.start()
    copy.wait()


def finish_last(partial, lifted, arrays):
    vmem_spec = pl.BlockSpec(memory_space=pltpu.VMEM)
    any_spec = pl.BlockSpec(memory_space=pl.ANY)
    return pl.pallas_call(
        last_body,
        in_specs=[any_spec] + [vmem_spec] * (1 + len(arrays)),
        out_specs=any_spec,
        out_shape=jax.ShapeDtypeStruct(partial.shape, partial.dtype),
        input_output_aliases={0: 0},
        scratch_shapes=[pltpu.VMEM((1,) + partial.shape[1:], partial.dtype), pltpu.SemaphoreType.DMA],
        compiler_params=pltpu.CompilerParams(vmem_limit_bytes=VMEM_BYTES),
        cost_estimate=pl.CostEstimate(flops=0, bytes_accessed=0, transcendentals=0),
        name="finish_last",
    )(partial, lifted, *arrays)


def per_device(hidden, base_weight, down_a, up_b, adapter_ids, owner_map):
    step_count, per_block, _ = hidden.shape
    n_tensor = lax.axis_size("tp")
    n_rep = lax.axis_size("rep")
    n_sub = lax.axis_size("sub")
    n_owners = n_rep * n_sub
    tensor_index = lax.axis_index("tp")
    rep_index = lax.axis_index("rep")
    sub_index = lax.axis_index("sub")
    owner_index = lax.axis_index(("rep", "sub"))
    requests = per_block * n_owners
    rows_mine = requests // n_tensor
    group = n_tensor // n_rep
    group_index = tensor_index // group
    owned_slots, _, rank_size = down_a.shape
    slot_count = owned_slots * n_owners
    width = base_weight.shape[1]

    def after(value, *done):
        return lax.optimization_barrier((value, *done))[0]

    def swap_cores(value):
        return lax.ppermute(value, "sub", [(i, i ^ 1) for i in range(n_sub)])

    def from_rep(value, shift):
        return lax.ppermute(value, "rep", [((i + shift) % n_rep, i) for i in range(n_rep)])

    def swap_tensor(value, bit):
        return lax.ppermute(value, "tp", [(i, i ^ bit) for i in range(n_tensor)])

    def to_group(value, hop):
        moved = group * hop
        return lax.ppermute(value, "tp", [(i, (i + moved) % n_tensor) for i in range(n_tensor)])

    def pick(values, index):
        value = values[0]
        for at in range(1, len(values)):
            value = jnp.where(index == at, values[at], value)
        return value

    keeps = (tensor_index // (group // 2)) % 2
    pos = (sub_index == keeps).astype(jnp.int32).reshape(1)

    siblings = swap_cores(hidden)
    pieces = [(step, shift) for step in range(step_count) for shift in range(1, n_rep)]
    source = pltpu.with_memory_space_constraint(hidden, pltpu.HBM)
    weight = pltpu.with_memory_space_constraint(base_weight, pltpu.HBM)
    remote = {(0, shift): from_rep(hidden[:1], shift) for shift in range(1, n_rep)}

    def spread_panels(panels, order, bits):
        for bit in bits:
            panels = panels + [swap_tensor(panel, bit) for panel in panels]
            order = order + [at ^ bit for at in order]
        return panels, order

    bits = [n_tensor >> at for at in range(1, n_tensor.bit_length())]
    order = [0, bits[0], bits[1]]
    panels = [up_b] + [swap_tensor(up_b, at) for at in order[1:]]

    my_ids = lax.dynamic_slice_in_dim(adapter_ids, tensor_index * rows_mine, rows_mine)
    iota = lax.broadcasted_iota(jnp.int32, (rows_mine, slot_count), 1)
    my_slot = jnp.sum((my_ids == iota).astype(jnp.int32) * owner_map[None, :], axis=1)
    owned_hot = my_slot[:, None] == (
        owner_index * owned_slots + lax.broadcasted_iota(jnp.int32, (rows_mine, owned_slots), 1)
    )

    first_leg, halved, begun, second_leg, ended = [], {}, set(), [], {}

    def second_half(total, received, steps, kind):
        total = total + received.astype(jnp.float32)
        rows, columns = total.shape
        extent, bit = rows // steps, group // 4
        while bit:
            extent //= 2
            halves = total.reshape(steps, 2, extent, columns)
            mine = (tensor_index // bit) % 2
            kept = lax.dynamic_index_in_dim(halves, mine, 1, keepdims=False)
            sent = lax.dynamic_index_in_dim(halves, 1 - mine, 1, keepdims=False)
            total = kept + swap_tensor(sent.astype(kind), bit).astype(jnp.float32)
            bit //= 2
        return total.reshape(steps, extent, columns)

    def gap(token, jobs, hold=False, lag=1):
        nonlocal first_leg, second_leg
        for parts, received, keep, kind in first_leg:
            steps = sum(length for _, length in parts)
            total, begin = second_half(after(keep, token), received, steps, kind), 0
            for key, length in parts:
                for at in range(begin, begin + length):
                    halved[key[0] + at - begin, key[1]] = total[at]
                    if (key[0] + at - begin, key[1]) == (step_count - 1, 0):
                        halved[RANK_NAME, 0] = total[at][:, width:]
                begin += length
        closed, waiting = {}, []
        for name, kept, received, turns in second_leg:
            if turns > 1:
                waiting.append((name, kept, received, turns - 1))
            else:
                closed[name] = (after(kept, token), *received)
        started, sends = [], []
        for name in [] if hold else sorted({name for name, _ in halved}):
            if name in begun or name == RANK_NAME or any((name, at) not in halved for at in range(n_rep)):
                continue
            begun.add(name)
            values = [halved[name, at] for at in range(n_rep)]
            columns = min(value.shape[1] for value in values)
            values = [value[:, :columns] for value in values]
            kept = pick(values, (group_index - rep_index) % n_rep)
            sends.append([
                pick(values, (group_index + hop - rep_index) % n_rep).astype(jnp.bfloat16) for hop in range(1, n_rep)
            ])
            started.append((name, kept))
        sends, token = lax.optimization_barrier((sends, token))
        first_sends, closed = lax.optimization_barrier(([job[1] for job in jobs], closed))
        ended.update(closed)
        first_leg = [
            (parts, swap_tensor(send, group // 2), keep, kind) for (parts, _, keep, kind), send in zip(jobs, first_sends)
        ]
        second_leg = waiting + [
            (name, kept, [to_group(value, hop + 1) for hop, value in enumerate(sent)], lag)
            for (name, kept), sent in zip(started, sends)
        ]
        return sends

    factors = jnp.swapaxes(down_a, 1, 2)

    lead = step_count // 2
    last_ranks, next_local = {}, lead
    send, keep, *slices = partial_products(
        pos, [(source, siblings, 0, lead)], weight, factors, staged=step_count - 1
    )
    for step, rows in enumerate(slices, 1):
        remote.update({(step, shift): from_rep(rows, shift) for shift in range(1, n_rep)})
    jobs = [([((0, 0), lead)], send, keep, jnp.bfloat16)]
    for piece, (step, shift) in enumerate(pieces):
        sends = gap(send, jobs, hold=piece == len(pieces) - 1)
        own, panels, _ = lax.optimization_barrier((remote[step, shift], panels, send))
        if piece == 0:
            panels, order = panels + [swap_tensor(panels[1], bits[1])], order + [bits[0] ^ bits[1]]
            panels, order = spread_panels(panels, order, bits[2:])
        sib = swap_cores(own)
        if piece == len(pieces) - 1:
            sends = gap(send, [], lag=2)
        own, sib, siblings, _ = lax.optimization_barrier((own, sib, siblings, sends))
        last, chunks, keys = step == step_count - 1, [(own, sib, 0, 1)], [(step, shift)]
        if next_local < step_count:
            chunks.append((source, siblings, next_local, 1))
            keys.append((next_local, 0))
            next_local += 1
        outs = partial_products(pos, chunks, weight, factors, last)
        send, count = outs[0], len(chunks)
        jobs = [([(key, 1)], outs[at], outs[count + at], jnp.bfloat16) for at, key in enumerate(keys)]
        if last:
            last_ranks[shift] = outs[2 * count:]
    gap(send, jobs)
    rank_received = {shift: swap_tensor(ranks[0], group // 2) for shift, ranks in last_ranks.items()}
    for shift, ranks in last_ranks.items():
        halved[RANK_NAME, shift] = second_half(ranks[1], rank_received[shift], 1, jnp.float32)[0]
    values = [halved[RANK_NAME, at] for at in range(n_rep)]
    rank_sends = [pick(values, (group_index + hop - rep_index) % n_rep) for hop in range(1, n_rep)]
    ended[RANK_NAME] = (
        pick(values, (group_index - rep_index) % n_rep),
        *[to_group(value, hop + 1) for hop, value in enumerate(rank_sends)],
    )
    second_leg = [
        (name, *after((kept, received), rank_sends), turns) for name, kept, received, turns in second_leg
    ]
    rounded = gap(send, [])

    def rank_sum(name):
        kept, *received = [value[:, -rank_columns(factors):] for value in ended[name]]
        for value in received:
            kept = kept + value.astype(jnp.float32)
        return kept[:, :owned_slots * rank_size]

    finished = jnp.stack([rank_sum(step) for step in range(step_count - 1)] + [rank_sum(RANK_NAME)])
    finished = finished.astype(jnp.bfloat16).reshape(step_count, rows_mine, owned_slots, rank_size)
    finished = after(finished, rounded)
    ended.update((name, (kept, *received)) for name, kept, received, _ in second_leg)
    masked = jnp.sum(
        jnp.where(owned_hot[None, :, :, None], finished, 0), axis=2, dtype=jnp.float32
    ).astype(jnp.bfloat16)
    chosen = masked
    for turn in range(1, n_owners):
        chosen = chosen + lax.ppermute(
            masked, ("rep", "sub"), [(i, (i + turn) % n_owners) for i in range(n_owners)]
        )
    panel_slots = jnp.stack([
        (tensor_index ^ at) * up_b.shape[0] + each for at in order for each in range(up_b.shape[0])
    ]).astype(jnp.int32)

    panels = [panel.reshape(-1, width) for panel in panels]
    partial, lifted = finish_steps(
        [ended[step] for step in range(step_count - 1)],
        chosen.reshape(step_count * rows_mine, rank_size),
        jnp.broadcast_to(my_slot, (step_count, rows_mine)).reshape(step_count * rows_mine, 1),
        panel_slots,
        panels,
    )
    return finish_last(partial, lifted, ended[step_count - 1])


def solution(mesh):
    return jax.shard_map(
        per_device,
        mesh=mesh,
        in_specs=(
            P(None, ("groups", "rep", "sub"), "tp"),
            P("tp", ("rep", "sub")),
            P(("rep", "sub"), "tp", None),
            P("tp", None, ("rep", "sub")),
            P("groups", None),
            P(),
        ),
        out_specs=P(None, ("groups", "tp"), ("rep", "sub")),
        check_vma=False,
    )
```

```python
import functools

import jax
import jax.numpy as jnp
from jax import lax
from jax.experimental import pallas as pl
from jax.experimental.pallas import tpu as pltpu
from jax.sharding import PartitionSpec as P

ADAPTER_SCALE = 0.5
BLOCK_N = 256
BLOCK = 1024
BUFFERS = 4
RANK_NAME = 1000
VMEM_BYTES = 20 * 1024 * 1024


def block_shape(depth, width):
    columns = BLOCK if width % BLOCK == 0 else width
    for size in (BLOCK, BLOCK // 2, BLOCK // 4):
        if depth % size == 0:
            return size, columns
    return depth, columns


def rank_columns(factors):
    slots, rank, _ = factors.shape
    return -(-slots * rank // 128) * 128


def matmul_body(spans, staged, apart, pos_ref, *refs):
    sources = refs[:2 * len(spans)]
    w_ref, a_ref = refs[2 * len(spans):2 * len(spans) + 2]
    outs = refs[2 * len(spans) + 2:]
    send_refs, keep_refs, outs = outs[:len(spans)], outs[len(spans):2 * len(spans)], outs[2 * len(spans):]
    outs, refs = (outs[:-7], outs[-7:]) if staged else (outs[:-5], outs[-5:])
    x_ref, w_buf, total_ref, x_sems, w_sems = refs[:5]
    rows = total_ref.shape[0]
    edges = [0]
    for ref in send_refs:
        edges.append(edges[-1] + ref.shape[0])
    depth, width = w_ref.shape
    slots, rank, _ = a_ref.shape
    buffers, block_k, block_w = w_buf.shape
    block_n = min(BLOCK_N, block_w)
    depths, count = depth // block_k, (depth // block_k) * (width // block_w)

    def fetch(block, slot):
        begin = pl.multiple_of(lax.rem(block, depths) * block_k, block_k)
        left = pl.multiple_of(lax.div(block, depths) * block_w, block_w)
        return pltpu.make_async_copy(
            w_ref.at[pl.ds(begin, block_k), pl.ds(left, block_w)], w_buf.at[slot], w_sems.at[slot]
        )

    own_at = pos_ref[0]
    copies, begin = [], 0
    for index, (first, steps) in enumerate(spans):
        for core, at in enumerate((own_at, 1 - own_at)):
            source = sources[2 * index + core]
            copies.append(pltpu.make_async_copy(
                source.at[pl.ds(first, steps)], x_ref.at[at, pl.ds(begin, steps)], x_sems.at[2 * index + core]
            ))
        begin += steps
    for copy in copies:
        copy.start()
    if staged:
        stage_ref, stage_sems = refs[5:]
        stage_in = pltpu.make_async_copy(sources[0].at[pl.ds(1, staged)], stage_ref, stage_sems.at[staged])
        stage_in.start()
        stage_out = [
            pltpu.make_async_copy(stage_ref.at[pl.ds(index, 1)], out_ref, stage_sems.at[index])
            for index, out_ref in enumerate(outs)
        ]
    for block in range(buffers):
        fetch(jnp.int32(block), block).start()
    for ref in keep_refs:
        ref[...] = jnp.zeros_like(ref)
    total_ref[...] = jnp.zeros_like(total_ref)
    send_rank, keep_ranks = (outs[0], outs[1:2]) if apart else (total_ref, keep_refs)
    if apart:
        for ref in outs[:2]:
            ref[...] = jnp.zeros_like(ref)
    for copy in copies:
        copy.wait()
    if staged:
        stage_in.wait()
        for copy in stage_out:
            copy.start()
    for slot in range(slots):
        x = x_ref[...].reshape(2 * rows, depth)
        part = lax.dot_general(
            x, a_ref[slot], (((1,), (1,)), ((), ())), preferred_element_type=jnp.float32
        )
        begin = slot * rank + (0 if apart else width)
        send_rank[:, begin:begin + rank] = part[:rows]
        for index, ref in enumerate(keep_ranks):
            ref[:, begin:begin + rank] = part[rows + edges[index]:rows + edges[index + 1]]

    @pl.loop(0, count)
    def _(block):
        slot = lax.rem(block, buffers)
        fetch(block, slot).wait()
        inner = pl.ds(pl.multiple_of(lax.rem(block, depths) * block_k, block_k), block_k)
        left = pl.multiple_of(lax.div(block, depths) * block_w, block_w)
        x = x_ref[:, :, :, inner].reshape(2 * rows, block_k)
        for place in range(block_w // block_n):
            columns = pl.ds(left + place * block_n, block_n)
            term = jnp.dot(
                x, w_buf[slot, :, place * block_n:(place + 1) * block_n], preferred_element_type=jnp.float32
            )
            total_ref[:, columns] += term[:rows]
            for index, ref in enumerate(keep_refs):
                ref[:, columns] += term[rows + edges[index]:rows + edges[index + 1]]

        @pl.when(block + buffers < count)
        def _():
            fetch(block + buffers, slot).start()

    for index, ref in enumerate(send_refs):
        ref[...] = total_ref[edges[index]:edges[index + 1]].astype(ref.dtype)
    if staged:
        for copy in stage_out:
            copy.wait()


def partial_products(pos, chunks, weight, factors, apart=False, staged=0):
    _, per_block, depth = chunks[0][0].shape
    width = weight.shape[1]
    spans = tuple((first, steps) for _, _, first, steps in chunks)
    steps = sum(length for _, length in spans)
    rows = steps * per_block
    block_k, block_w = block_shape(depth, width)
    buffers = min(BUFFERS, (depth // block_k) * (width // block_w))
    any_spec = pl.BlockSpec(memory_space=pl.ANY)
    vmem_spec = pl.BlockSpec(memory_space=pltpu.VMEM)
    extra = rank_columns(factors)
    columns = width + (0 if apart else extra)
    out_shape = [
        jax.ShapeDtypeStruct((length * per_block, columns), kind)
        for kind in (jnp.bfloat16, jnp.float32) for _, length in spans
    ] + [jax.ShapeDtypeStruct((rows, extra), jnp.float32)] * (2 if apart else 0)
    out_specs = [vmem_spec] * len(out_shape)
    out_shape += [pltpu.HBM((1, per_block, depth), jnp.bfloat16)] * staged
    out_specs += [any_spec] * staged
    return pl.pallas_call(
        functools.partial(matmul_body, spans, staged, apart),
        in_specs=[pl.BlockSpec(memory_space=pltpu.SMEM)] + [any_spec] * (2 * len(chunks) + 1) + [vmem_spec],
        out_specs=out_specs,
        out_shape=out_shape,
        scratch_shapes=[
            pltpu.VMEM((2, steps, per_block, depth), jnp.bfloat16),
            pltpu.VMEM((buffers, block_k, block_w), jnp.bfloat16),
            pltpu.VMEM((rows, columns), jnp.float32),
            pltpu.SemaphoreType.DMA((2 * len(chunks),)),
            pltpu.SemaphoreType.DMA((buffers,)),
        ] + ([
            pltpu.VMEM((staged, per_block, depth), jnp.bfloat16),
            pltpu.SemaphoreType.DMA((staged + 1,)),
        ] if staged else []),
        compiler_params=pltpu.CompilerParams(vmem_limit_bytes=VMEM_BYTES),
        cost_estimate=pl.CostEstimate(flops=0, bytes_accessed=0, transcendentals=0),
        name="partial_products",
    )(pos, *[source for own, sib, _, _ in chunks for source in (own, sib)], weight, factors)


def finish_body(received, panels, chosen_ref, slot_ref, order_ref, *refs):
    panel_refs, refs = refs[:panels], refs[panels:]
    per_panel = panel_refs[0].shape[0]
    out_ref, lifted_ref, done_ref, sem = refs[-4:]
    steps, rows, width = done_ref.shape
    rank = chosen_ref.shape[1]
    chosen = chosen_ref[...]
    slot = slot_ref[...]
    spread = jnp.concatenate(
        [
            jnp.where(slot == order_ref[place], chosen, jnp.zeros_like(chosen))
            for place in range(panels * per_panel // rank)
        ],
        axis=1,
    )
    block_n = min(BLOCK_N, width)
    for place in range(width // block_n):
        columns = slice(place * block_n, (place + 1) * block_n)
        panel = jnp.concatenate([panel_ref[:, columns] for panel_ref in panel_refs], axis=0)
        lifted = jnp.dot(spread, panel, preferred_element_type=jnp.float32).astype(jnp.bfloat16)
        for step in range(steps):
            total = refs[step * (received + 1)][:, columns]
            for value_ref in refs[step * (received + 1) + 1:(step + 1) * (received + 1)]:
                total = total + value_ref[:, columns].astype(jnp.float32)
            value = total + ADAPTER_SCALE * lifted[step * rows:(step + 1) * rows].astype(jnp.float32)
            done_ref[step, :, columns] = value.astype(done_ref.dtype)
        lifted_ref[:, columns] = lifted[steps * rows:]
    copy = pltpu.make_async_copy(done_ref, out_ref.at[pl.ds(0, steps)], sem)
    copy.start()
    copy.wait()


def finish_steps(totals, chosen, slots, order, panels):
    steps, width = len(totals), panels[0].shape[1]
    rows = chosen.shape[0] // (steps + 1)
    vmem_spec = pl.BlockSpec(memory_space=pltpu.VMEM)
    arrays = [value for total in totals for value in total]
    return pl.pallas_call(
        functools.partial(finish_body, len(totals[0]) - 1, len(panels)),
        in_specs=[vmem_spec, vmem_spec, pl.BlockSpec(memory_space=pltpu.SMEM)] + [vmem_spec] * (len(panels) + len(arrays)),
        out_specs=[pl.BlockSpec(memory_space=pl.ANY), vmem_spec],
        out_shape=[
            jax.ShapeDtypeStruct((steps + 1, rows, width), jnp.bfloat16),
            jax.ShapeDtypeStruct((rows, width), jnp.bfloat16),
        ],
        scratch_shapes=[pltpu.VMEM((steps, rows, width), jnp.bfloat16), pltpu.SemaphoreType.DMA],
        compiler_params=pltpu.CompilerParams(vmem_limit_bytes=VMEM_BYTES),
        cost_estimate=pl.CostEstimate(flops=0, bytes_accessed=0, transcendentals=0),
        name="finish_steps",
    )(chosen, slots, order, *panels, *arrays)


def last_body(partial_ref, lifted_ref, *refs):
    out_ref, done_ref, sem = refs[-3:]
    total = refs[0][...]
    for value_ref in refs[1:-3]:
        total = total + value_ref[...].astype(jnp.float32)
    value = total + ADAPTER_SCALE * lifted_ref[...].astype(jnp.float32)
    done_ref[0] = value.astype(done_ref.dtype)
    copy = pltpu.make_async_copy(done_ref, out_ref.at[pl.ds(out_ref.shape[0] - 1, 1)], sem)
    copy.start()
    copy.wait()


def finish_last(partial, lifted, arrays):
    vmem_spec = pl.BlockSpec(memory_space=pltpu.VMEM)
    any_spec = pl.BlockSpec(memory_space=pl.ANY)
    return pl.pallas_call(
        last_body,
        in_specs=[any_spec] + [vmem_spec] * (1 + len(arrays)),
        out_specs=any_spec,
        out_shape=jax.ShapeDtypeStruct(partial.shape, partial.dtype),
        input_output_aliases={0: 0},
        scratch_shapes=[pltpu.VMEM((1,) + partial.shape[1:], partial.dtype), pltpu.SemaphoreType.DMA],
        compiler_params=pltpu.CompilerParams(vmem_limit_bytes=VMEM_BYTES),
        cost_estimate=pl.CostEstimate(flops=0, bytes_accessed=0, transcendentals=0),
        name="finish_last",
    )(partial, lifted, *arrays)


def per_device(hidden, base_weight, down_a, up_b, adapter_ids, owner_map):
    step_count, per_block, _ = hidden.shape
    n_tensor = lax.axis_size("tp")
    n_rep = lax.axis_size("rep")
    n_sub = lax.axis_size("sub")
    n_owners = n_rep * n_sub
    tensor_index = lax.axis_index("tp")
    rep_index = lax.axis_index("rep")
    sub_index = lax.axis_index("sub")
    owner_index = lax.axis_index(("rep", "sub"))
    requests = per_block * n_owners
    rows_mine = requests // n_tensor
    group = n_tensor // n_rep
    group_index = tensor_index // group
    owned_slots, _, rank_size = down_a.shape
    slot_count = owned_slots * n_owners
    width = base_weight.shape[1]

    def after(value, *done):
        return lax.optimization_barrier((value, *done))[0]

    def swap_cores(value):
        return lax.ppermute(value, "sub", [(i, i ^ 1) for i in range(n_sub)])

    def from_rep(value, shift):
        return lax.ppermute(value, "rep", [((i + shift) % n_rep, i) for i in range(n_rep)])

    def swap_tensor(value, bit):
        return lax.ppermute(value, "tp", [(i, i ^ bit) for i in range(n_tensor)])

    def to_group(value, hop):
        moved = group * hop
        return lax.ppermute(value, "tp", [(i, (i + moved) % n_tensor) for i in range(n_tensor)])

    def pick(values, index):
        value = values[0]
        for at in range(1, len(values)):
            value = jnp.where(index == at, values[at], value)
        return value

    keeps = (tensor_index // (group // 2)) % 2
    pos = (sub_index == keeps).astype(jnp.int32).reshape(1)

    siblings = swap_cores(hidden)
    pieces = [(step, shift) for step in range(step_count) for shift in range(1, n_rep)]
    source = pltpu.with_memory_space_constraint(hidden, pltpu.HBM)
    weight = pltpu.with_memory_space_constraint(base_weight, pltpu.HBM)
    remote = {(0, shift): from_rep(hidden[:1], shift) for shift in range(1, n_rep)}

    def spread_panels(panels, order, bits):
        for bit in bits:
            panels = panels + [swap_tensor(panel, bit) for panel in panels]
            order = order + [at ^ bit for at in order]
        return panels, order

    bits = [n_tensor >> at for at in range(1, n_tensor.bit_length())]
    order = [0, bits[0], bits[1]]
    panels = [up_b] + [swap_tensor(up_b, at) for at in order[1:]]

    my_ids = lax.dynamic_slice_in_dim(adapter_ids, tensor_index * rows_mine, rows_mine)
    iota = lax.broadcasted_iota(jnp.int32, (rows_mine, slot_count), 1)
    my_slot = jnp.sum((my_ids == iota).astype(jnp.int32) * owner_map[None, :], axis=1)
    owned_hot = my_slot[:, None] == (
        owner_index * owned_slots + lax.broadcasted_iota(jnp.int32, (rows_mine, owned_slots), 1)
    )

    first_leg, halved, begun, second_leg, ended = [], {}, set(), [], {}

    def second_half(total, received, steps, kind):
        total = total + received.astype(jnp.float32)
        rows, columns = total.shape
        extent, bit = rows // steps, group // 4
        while bit:
            extent //= 2
            halves = total.reshape(steps, 2, extent, columns)
            mine = (tensor_index // bit) % 2
            kept = lax.dynamic_index_in_dim(halves, mine, 1, keepdims=False)
            sent = lax.dynamic_index_in_dim(halves, 1 - mine, 1, keepdims=False)
            total = kept + swap_tensor(sent.astype(kind), bit).astype(jnp.float32)
            bit //= 2
        return total.reshape(steps, extent, columns)

    def gap(token, jobs, short=False):
        nonlocal first_leg, second_leg
        due, kept_back = (first_leg[:1], first_leg[1:]) if short else (first_leg, [])
        for parts, received, keep, kind in due:
            steps = sum(length for _, length in parts)
            total, begin = second_half(after(keep, token), received, steps, kind), 0
            for key, length in parts:
                for at in range(begin, begin + length):
                    halved[key[0] + at - begin, key[1]] = total[at]
                    if (key[0] + at - begin, key[1]) == (step_count - 1, 0):
                        halved[RANK_NAME, 0] = total[at][:, width:]
                begin += length
        waiting = second_leg if short else []
        closed = {name: (after(kept, token), *received) for name, kept, received in ([] if short else second_leg)}
        started, sends = [], []
        for name in sorted({name for name, _ in halved}):
            if name in begun or name == RANK_NAME or any((name, at) not in halved for at in range(n_rep)):
                continue
            begun.add(name)
            values = [halved[name, at] for at in range(n_rep)]
            columns = min(value.shape[1] for value in values)
            values = [value[:, :columns] for value in values]
            kept = pick(values, (group_index - rep_index) % n_rep)
            sends.append([
                pick(values, (group_index + hop - rep_index) % n_rep).astype(jnp.bfloat16) for hop in range(1, n_rep)
            ])
            started.append((name, kept))
        sends, token = lax.optimization_barrier((sends, token))
        first_sends, closed = lax.optimization_barrier(([job[1] for job in jobs], closed))
        ended.update(closed)
        first_leg = kept_back + [
            (parts, swap_tensor(send, group // 2), keep, kind) for (parts, _, keep, kind), send in zip(jobs, first_sends)
        ]
        second_leg = waiting + [
            (name, kept, [to_group(value, hop + 1) for hop, value in enumerate(sent)])
            for (name, kept), sent in zip(started, sends)
        ]
        return sends

    factors = jnp.swapaxes(down_a, 1, 2)

    lead = step_count // 2
    last_ranks, next_local = {}, lead
    send, keep, *slices = partial_products(
        pos, [(source, siblings, 0, lead)], weight, factors, staged=step_count - 1
    )
    for step, rows in enumerate(slices, 1):
        remote.update({(step, shift): from_rep(rows, shift) for shift in range(1, n_rep)})
    jobs = [([((0, 0), lead)], send, keep, jnp.bfloat16)]
    for piece, (step, shift) in enumerate(pieces):
        arrived = [received for _, received, _, _ in first_leg] if piece > 0 else []
        sends = gap(send, jobs)
        own, panels, *_ = lax.optimization_barrier((remote[step, shift], panels, arrived, send))
        if piece == 0:
            panels, order = panels + [swap_tensor(panels[1], bits[1])], order + [bits[0] ^ bits[1]]
            panels, order = spread_panels(panels, order, bits[2:])
        sib = swap_cores(own)
        if piece > 0:
            sends = sends + gap(send, [], short=True)
        own, sib, siblings, _ = lax.optimization_barrier((own, sib, siblings, sends))
        last, chunks, keys = step == step_count - 1, [(own, sib, 0, 1)], [(step, shift)]
        if next_local < step_count:
            chunks.append((source, siblings, next_local, 1))
            keys.append((next_local, 0))
            next_local += 1
        outs = partial_products(pos, chunks, weight, factors, last)
        send, count = outs[0], len(chunks)
        jobs = [([(key, 1)], outs[at], outs[count + at], jnp.bfloat16) for at, key in enumerate(keys)]
        if last:
            last_ranks[shift] = outs[2 * count:]
    gap(send, jobs)
    for shift, ranks in last_ranks.items():
        halved[RANK_NAME, shift] = second_half(ranks[1], swap_tensor(ranks[0], group // 2), 1, jnp.float32)[0]
    values = [halved[RANK_NAME, at] for at in range(n_rep)]
    ended[RANK_NAME] = (pick(values, (group_index - rep_index) % n_rep), *[
        to_group(pick(values, (group_index + hop - rep_index) % n_rep), hop) for hop in range(1, n_rep)
    ])
    rounded = gap(send, [])

    def rank_sum(name):
        kept, *received = [value[:, -rank_columns(factors):] for value in ended[name]]
        for value in received:
            kept = kept + value.astype(jnp.float32)
        return kept[:, :owned_slots * rank_size]

    finished = jnp.stack([rank_sum(step) for step in range(step_count - 1)] + [rank_sum(RANK_NAME)])
    finished = finished.astype(jnp.bfloat16).reshape(step_count, rows_mine, owned_slots, rank_size)
    finished = lax.optimization_barrier((finished, rounded))[0]
    ended.update((name, (kept, *received)) for name, kept, received in second_leg)
    masked = jnp.sum(
        jnp.where(owned_hot[None, :, :, None], finished, 0), axis=2, dtype=jnp.float32
    ).astype(jnp.bfloat16)
    chosen = masked
    for turn in range(1, n_owners):
        chosen = chosen + lax.ppermute(
            masked, ("rep", "sub"), [(i, (i + turn) % n_owners) for i in range(n_owners)]
        )
    panel_slots = jnp.stack([
        (tensor_index ^ at) * up_b.shape[0] + each for at in order for each in range(up_b.shape[0])
    ]).astype(jnp.int32)

    panels = [panel.reshape(-1, width) for panel in panels]
    partial, lifted = finish_steps(
        [ended[step] for step in range(step_count - 1)],
        chosen.reshape(step_count * rows_mine, rank_size),
        jnp.broadcast_to(my_slot, (step_count, rows_mine)).reshape(step_count * rows_mine, 1),
        panel_slots,
        panels,
    )
    return finish_last(partial, lifted, ended[step_count - 1])


def solution(mesh):
    return jax.shard_map(
        per_device,
        mesh=mesh,
        in_specs=(
            P(None, ("groups", "rep", "sub"), "tp"),
            P("tp", ("rep", "sub")),
            P(("rep", "sub"), "tp", None),
            P("tp", None, ("rep", "sub")),
            P("groups", None),
            P(),
        ),
        out_specs=P(None, ("groups", "tp"), ("rep", "sub")),
        check_vma=False,
    )
```

```python
import functools

import jax
import jax.numpy as jnp
from jax import lax
from jax.experimental import pallas as pl
from jax.experimental.pallas import tpu as pltpu
from jax.sharding import PartitionSpec as P

ADAPTER_SCALE = 0.5
BLOCK_N = 256
BLOCK = 1024
BUFFERS = 4
RANK_NAME = 1000
VMEM_BYTES = 20 * 1024 * 1024


def block_shape(depth, width):
    columns = BLOCK if width % BLOCK == 0 else width
    for size in (BLOCK, BLOCK // 2, BLOCK // 4):
        if depth % size == 0:
            return size, columns
    return depth, columns


def rank_columns(factors):
    slots, rank, _ = factors.shape
    return -(-slots * rank // 128) * 128


def matmul_body(spans, staged, apart, pos_ref, *refs):
    sources = refs[:2 * len(spans)]
    w_ref, a_ref = refs[2 * len(spans):2 * len(spans) + 2]
    outs = refs[2 * len(spans) + 2:]
    send_refs, keep_refs, outs = outs[:len(spans)], outs[len(spans):2 * len(spans)], outs[2 * len(spans):]
    outs, refs = (outs[:-7], outs[-7:]) if staged else (outs[:-5], outs[-5:])
    x_ref, w_buf, total_ref, x_sems, w_sems = refs[:5]
    rows = total_ref.shape[0]
    edges = [0]
    for ref in send_refs:
        edges.append(edges[-1] + ref.shape[0])
    depth, width = w_ref.shape
    slots, rank, _ = a_ref.shape
    buffers, block_k, block_w = w_buf.shape
    block_n = min(BLOCK_N, block_w)
    depths, count = depth // block_k, (depth // block_k) * (width // block_w)

    def fetch(block, slot):
        begin = pl.multiple_of(lax.rem(block, depths) * block_k, block_k)
        left = pl.multiple_of(lax.div(block, depths) * block_w, block_w)
        return pltpu.make_async_copy(
            w_ref.at[pl.ds(begin, block_k), pl.ds(left, block_w)], w_buf.at[slot], w_sems.at[slot]
        )

    own_at = pos_ref[0]
    copies, begin = [], 0
    for index, (first, steps) in enumerate(spans):
        for core, at in enumerate((own_at, 1 - own_at)):
            source = sources[2 * index + core]
            copies.append(pltpu.make_async_copy(
                source.at[pl.ds(first, steps)], x_ref.at[at, pl.ds(begin, steps)], x_sems.at[2 * index + core]
            ))
        begin += steps
    for copy in copies:
        copy.start()
    if staged:
        stage_ref, stage_sems = refs[5:]
        stage_in = pltpu.make_async_copy(sources[0].at[pl.ds(1, staged)], stage_ref, stage_sems.at[staged])
        stage_in.start()
        stage_out = [
            pltpu.make_async_copy(stage_ref.at[pl.ds(index, 1)], out_ref, stage_sems.at[index])
            for index, out_ref in enumerate(outs)
        ]
    for block in range(buffers):
        fetch(jnp.int32(block), block).start()
    for ref in keep_refs:
        ref[...] = jnp.zeros_like(ref)
    total_ref[...] = jnp.zeros_like(total_ref)
    send_rank, keep_ranks = (outs[0], outs[1:2]) if apart else (total_ref, keep_refs)
    if apart:
        for ref in outs[:2]:
            ref[...] = jnp.zeros_like(ref)
    for copy in copies:
        copy.wait()
    if staged:
        stage_in.wait()
        for copy in stage_out:
            copy.start()
    for slot in range(slots):
        x = x_ref[...].reshape(2 * rows, depth)
        part = lax.dot_general(
            x, a_ref[slot], (((1,), (1,)), ((), ())), preferred_element_type=jnp.float32
        )
        begin = slot * rank + (0 if apart else width)
        send_rank[:, begin:begin + rank] = part[:rows]
        for index, ref in enumerate(keep_ranks):
            ref[:, begin:begin + rank] = part[rows + edges[index]:rows + edges[index + 1]]

    @pl.loop(0, count)
    def _(block):
        slot = lax.rem(block, buffers)
        fetch(block, slot).wait()
        inner = pl.ds(pl.multiple_of(lax.rem(block, depths) * block_k, block_k), block_k)
        left = pl.multiple_of(lax.div(block, depths) * block_w, block_w)
        x = x_ref[:, :, :, inner].reshape(2 * rows, block_k)
        for place in range(block_w // block_n):
            columns = pl.ds(left + place * block_n, block_n)
            term = jnp.dot(
                x, w_buf[slot, :, place * block_n:(place + 1) * block_n], preferred_element_type=jnp.float32
            )
            total_ref[:, columns] += term[:rows]
            for index, ref in enumerate(keep_refs):
                ref[:, columns] += term[rows + edges[index]:rows + edges[index + 1]]

        @pl.when(block + buffers < count)
        def _():
            fetch(block + buffers, slot).start()

    for index, ref in enumerate(send_refs):
        ref[...] = total_ref[edges[index]:edges[index + 1]].astype(ref.dtype)
    if staged:
        for copy in stage_out:
            copy.wait()


def partial_products(pos, chunks, weight, factors, apart=False, staged=0):
    _, per_block, depth = chunks[0][0].shape
    width = weight.shape[1]
    spans = tuple((first, steps) for _, _, first, steps in chunks)
    steps = sum(length for _, length in spans)
    rows = steps * per_block
    block_k, block_w = block_shape(depth, width)
    buffers = min(BUFFERS, (depth // block_k) * (width // block_w))
    any_spec = pl.BlockSpec(memory_space=pl.ANY)
    vmem_spec = pl.BlockSpec(memory_space=pltpu.VMEM)
    extra = rank_columns(factors)
    columns = width + (0 if apart else extra)
    out_shape = [
        jax.ShapeDtypeStruct((length * per_block, columns), kind)
        for kind in (jnp.bfloat16, jnp.float32) for _, length in spans
    ] + [jax.ShapeDtypeStruct((rows, extra), jnp.float32)] * (2 if apart else 0)
    out_specs = [vmem_spec] * len(out_shape)
    out_shape += [pltpu.HBM((1, per_block, depth), jnp.bfloat16)] * staged
    out_specs += [any_spec] * staged
    return pl.pallas_call(
        functools.partial(matmul_body, spans, staged, apart),
        in_specs=[pl.BlockSpec(memory_space=pltpu.SMEM)] + [any_spec] * (2 * len(chunks) + 1) + [vmem_spec],
        out_specs=out_specs,
        out_shape=out_shape,
        scratch_shapes=[
            pltpu.VMEM((2, steps, per_block, depth), jnp.bfloat16),
            pltpu.VMEM((buffers, block_k, block_w), jnp.bfloat16),
            pltpu.VMEM((rows, columns), jnp.float32),
            pltpu.SemaphoreType.DMA((2 * len(chunks),)),
            pltpu.SemaphoreType.DMA((buffers,)),
        ] + ([
            pltpu.VMEM((staged, per_block, depth), jnp.bfloat16),
            pltpu.SemaphoreType.DMA((staged + 1,)),
        ] if staged else []),
        compiler_params=pltpu.CompilerParams(vmem_limit_bytes=VMEM_BYTES),
        cost_estimate=pl.CostEstimate(flops=0, bytes_accessed=0, transcendentals=0),
        name="partial_products",
    )(pos, *[source for own, sib, _, _ in chunks for source in (own, sib)], weight, factors)


def finish_body(received, panels, chosen_ref, slot_ref, order_ref, *refs):
    panel_refs, refs = refs[:panels], refs[panels:]
    per_panel = panel_refs[0].shape[0]
    out_ref, lifted_ref, done_ref, sem = refs[-4:]
    steps, rows, width = done_ref.shape
    rank = chosen_ref.shape[1]
    chosen = chosen_ref[...]
    slot = slot_ref[...]
    spread = jnp.concatenate(
        [
            jnp.where(slot == order_ref[place], chosen, jnp.zeros_like(chosen))
            for place in range(panels * per_panel // rank)
        ],
        axis=1,
    )
    block_n = min(BLOCK_N, width)
    for place in range(width // block_n):
        columns = slice(place * block_n, (place + 1) * block_n)
        panel = jnp.concatenate([panel_ref[:, columns] for panel_ref in panel_refs], axis=0)
        lifted = jnp.dot(spread, panel, preferred_element_type=jnp.float32).astype(jnp.bfloat16)
        for step in range(steps):
            total = refs[step * (received + 1)][:, columns]
            for value_ref in refs[step * (received + 1) + 1:(step + 1) * (received + 1)]:
                total = total + value_ref[:, columns].astype(jnp.float32)
            value = total + ADAPTER_SCALE * lifted[step * rows:(step + 1) * rows].astype(jnp.float32)
            done_ref[step, :, columns] = value.astype(done_ref.dtype)
        lifted_ref[:, columns] = lifted[steps * rows:]
    copy = pltpu.make_async_copy(done_ref, out_ref.at[pl.ds(0, steps)], sem)
    copy.start()
    copy.wait()


def finish_steps(totals, chosen, slots, order, panels):
    steps, width = len(totals), panels[0].shape[1]
    rows = chosen.shape[0] // (steps + 1)
    vmem_spec = pl.BlockSpec(memory_space=pltpu.VMEM)
    arrays = [value for total in totals for value in total]
    return pl.pallas_call(
        functools.partial(finish_body, len(totals[0]) - 1, len(panels)),
        in_specs=[vmem_spec, vmem_spec, pl.BlockSpec(memory_space=pltpu.SMEM)] + [vmem_spec] * (len(panels) + len(arrays)),
        out_specs=[pl.BlockSpec(memory_space=pl.ANY), vmem_spec],
        out_shape=[
            jax.ShapeDtypeStruct((steps + 1, rows, width), jnp.bfloat16),
            jax.ShapeDtypeStruct((rows, width), jnp.bfloat16),
        ],
        scratch_shapes=[pltpu.VMEM((steps, rows, width), jnp.bfloat16), pltpu.SemaphoreType.DMA],
        compiler_params=pltpu.CompilerParams(vmem_limit_bytes=VMEM_BYTES),
        cost_estimate=pl.CostEstimate(flops=0, bytes_accessed=0, transcendentals=0),
        name="finish_steps",
    )(chosen, slots, order, *panels, *arrays)


def last_body(partial_ref, lifted_ref, *refs):
    out_ref, done_ref, sem = refs[-3:]
    total = refs[0][...]
    for value_ref in refs[1:-3]:
        total = total + value_ref[...].astype(jnp.float32)
    value = total + ADAPTER_SCALE * lifted_ref[...].astype(jnp.float32)
    done_ref[0] = value.astype(done_ref.dtype)
    copy = pltpu.make_async_copy(done_ref, out_ref.at[pl.ds(out_ref.shape[0] - 1, 1)], sem)
    copy.start()
    copy.wait()


def finish_last(partial, lifted, arrays):
    vmem_spec = pl.BlockSpec(memory_space=pltpu.VMEM)
    any_spec = pl.BlockSpec(memory_space=pl.ANY)
    return pl.pallas_call(
        last_body,
        in_specs=[any_spec] + [vmem_spec] * (1 + len(arrays)),
        out_specs=any_spec,
        out_shape=jax.ShapeDtypeStruct(partial.shape, partial.dtype),
        input_output_aliases={0: 0},
        scratch_shapes=[pltpu.VMEM((1,) + partial.shape[1:], partial.dtype), pltpu.SemaphoreType.DMA],
        compiler_params=pltpu.CompilerParams(vmem_limit_bytes=VMEM_BYTES),
        cost_estimate=pl.CostEstimate(flops=0, bytes_accessed=0, transcendentals=0),
        name="finish_last",
    )(partial, lifted, *arrays)


def per_device(hidden, base_weight, down_a, up_b, adapter_ids, owner_map):
    step_count, per_block, _ = hidden.shape
    n_tensor = lax.axis_size("tp")
    n_rep = lax.axis_size("rep")
    n_sub = lax.axis_size("sub")
    n_owners = n_rep * n_sub
    tensor_index = lax.axis_index("tp")
    rep_index = lax.axis_index("rep")
    sub_index = lax.axis_index("sub")
    owner_index = lax.axis_index(("rep", "sub"))
    requests = per_block * n_owners
    rows_mine = requests // n_tensor
    group = n_tensor // n_rep
    group_index = tensor_index // group
    owned_slots, _, rank_size = down_a.shape
    slot_count = owned_slots * n_owners
    width = base_weight.shape[1]

    def after(value, *done):
        return lax.optimization_barrier((value, *done))[0]

    def swap_cores(value):
        return lax.ppermute(value, "sub", [(i, i ^ 1) for i in range(n_sub)])

    def from_rep(value, shift):
        return lax.ppermute(value, "rep", [((i + shift) % n_rep, i) for i in range(n_rep)])

    def swap_tensor(value, bit):
        return lax.ppermute(value, "tp", [(i, i ^ bit) for i in range(n_tensor)])

    def to_group(value, hop):
        moved = group * hop
        return lax.ppermute(value, "tp", [(i, (i + moved) % n_tensor) for i in range(n_tensor)])

    def pick(values, index):
        value = values[0]
        for at in range(1, len(values)):
            value = jnp.where(index == at, values[at], value)
        return value

    keeps = (tensor_index // (group // 2)) % 2
    pos = (sub_index == keeps).astype(jnp.int32).reshape(1)

    siblings = swap_cores(hidden)
    pieces = [(step, shift) for step in range(step_count) for shift in range(1, n_rep)]
    source = pltpu.with_memory_space_constraint(hidden, pltpu.HBM)
    weight = pltpu.with_memory_space_constraint(base_weight, pltpu.HBM)
    remote = {(0, shift): from_rep(hidden[:1], shift) for shift in range(1, n_rep)}

    def spread_panels(panels, order, bits):
        for bit in bits:
            panels = panels + [swap_tensor(panel, bit) for panel in panels]
            order = order + [at ^ bit for at in order]
        return panels, order

    bits = [n_tensor >> at for at in range(1, n_tensor.bit_length())]
    order = [0, bits[0], bits[1]]
    panels = [up_b] + [swap_tensor(up_b, at) for at in order[1:]]

    my_ids = lax.dynamic_slice_in_dim(adapter_ids, tensor_index * rows_mine, rows_mine)
    iota = lax.broadcasted_iota(jnp.int32, (rows_mine, slot_count), 1)
    my_slot = jnp.sum((my_ids == iota).astype(jnp.int32) * owner_map[None, :], axis=1)
    owned_hot = my_slot[:, None] == (
        owner_index * owned_slots + lax.broadcasted_iota(jnp.int32, (rows_mine, owned_slots), 1)
    )

    first_leg, halved, begun, second_leg, ended = [], {}, set(), [], {}

    def second_half(total, received, steps, kind):
        total = total + received.astype(jnp.float32)
        rows, columns = total.shape
        extent, bit = rows // steps, group // 4
        while bit:
            extent //= 2
            halves = total.reshape(steps, 2, extent, columns)
            mine = (tensor_index // bit) % 2
            kept = lax.dynamic_index_in_dim(halves, mine, 1, keepdims=False)
            sent = lax.dynamic_index_in_dim(halves, 1 - mine, 1, keepdims=False)
            total = kept + swap_tensor(sent.astype(kind), bit).astype(jnp.float32)
            bit //= 2
        return total.reshape(steps, extent, columns)

    def gap(token, jobs):
        nonlocal first_leg, second_leg
        for parts, received, keep, kind in first_leg:
            steps = sum(length for _, length in parts)
            total, begin = second_half(after(keep, token), received, steps, kind), 0
            for key, length in parts:
                for at in range(begin, begin + length):
                    halved[key[0] + at - begin, key[1]] = total[at]
                    if (key[0] + at - begin, key[1]) == (step_count - 1, 0):
                        halved[RANK_NAME, 0] = total[at][:, width:]
                begin += length
        closed = {name: (after(kept, token), *received) for name, kept, received in second_leg}
        started, sends = [], []
        for name in sorted({name for name, _ in halved}):
            if name in begun or name == RANK_NAME or any((name, at) not in halved for at in range(n_rep)):
                continue
            begun.add(name)
            values = [halved[name, at] for at in range(n_rep)]
            columns = min(value.shape[1] for value in values)
            values = [value[:, :columns] for value in values]
            kept = pick(values, (group_index - rep_index) % n_rep)
            sends.append([
                pick(values, (group_index + hop - rep_index) % n_rep).astype(jnp.bfloat16) for hop in range(1, n_rep)
            ])
            started.append((name, kept))
        sends, token = lax.optimization_barrier((sends, token))
        first_sends, closed = lax.optimization_barrier(([job[1] for job in jobs], closed))
        ended.update(closed)
        first_leg = [
            (parts, swap_tensor(send, group // 2), keep, kind) for (parts, _, keep, kind), send in zip(jobs, first_sends)
        ]
        second_leg = [
            (name, kept, [to_group(value, hop + 1) for hop, value in enumerate(sent)])
            for (name, kept), sent in zip(started, sends)
        ]
        return sends

    factors = jnp.swapaxes(down_a, 1, 2)

    lead = step_count // 2
    last_ranks, next_local = {}, lead
    send, keep, *slices = partial_products(
        pos, [(source, siblings, 0, lead)], weight, factors, staged=step_count - 1
    )
    for step, rows in enumerate(slices, 1):
        remote.update({(step, shift): from_rep(rows, shift) for shift in range(1, n_rep)})
    jobs = [([((0, 0), lead)], send, keep, jnp.bfloat16)]
    for piece, (step, shift) in enumerate(pieces):
        arrived = [received for _, received, _, _ in first_leg] if piece == 1 else []
        sends = gap(send, jobs)
        own, panels, *_ = lax.optimization_barrier((remote[step, shift], panels, arrived, send))
        if piece == 0:
            panels, order = panels + [swap_tensor(panels[1], bits[1])], order + [bits[0] ^ bits[1]]
            panels, order = spread_panels(panels, order, bits[2:])
        sib = swap_cores(own)
        own, sib, siblings, _ = lax.optimization_barrier((own, sib, siblings, sends))
        last, chunks, keys = step == step_count - 1, [(own, sib, 0, 1)], [(step, shift)]
        if next_local < step_count:
            chunks.append((source, siblings, next_local, 1))
            keys.append((next_local, 0))
            next_local += 1
        outs = partial_products(pos, chunks, weight, factors, last)
        send, count = outs[0], len(chunks)
        jobs = [([(key, 1)], outs[at], outs[count + at], jnp.bfloat16) for at, key in enumerate(keys)]
        if last:
            last_ranks[shift] = outs[2 * count:]
    gap(send, jobs)
    for shift, ranks in last_ranks.items():
        halved[RANK_NAME, shift] = second_half(ranks[1], swap_tensor(ranks[0], group // 2), 1, jnp.float32)[0]
    values = [halved[RANK_NAME, at] for at in range(n_rep)]
    ended[RANK_NAME] = (pick(values, (group_index - rep_index) % n_rep), *[
        to_group(pick(values, (group_index + hop - rep_index) % n_rep), hop) for hop in range(1, n_rep)
    ])
    rounded = gap(send, [])

    def rank_sum(name):
        kept, *received = [value[:, -rank_columns(factors):] for value in ended[name]]
        for value in received:
            kept = kept + value.astype(jnp.float32)
        return kept[:, :owned_slots * rank_size]

    finished = jnp.stack([rank_sum(step) for step in range(step_count - 1)] + [rank_sum(RANK_NAME)])
    finished = finished.astype(jnp.bfloat16).reshape(step_count, rows_mine, owned_slots, rank_size)
    finished = lax.optimization_barrier((finished, rounded))[0]
    ended.update((name, (kept, *received)) for name, kept, received in second_leg)
    masked = jnp.sum(
        jnp.where(owned_hot[None, :, :, None], finished, 0), axis=2, dtype=jnp.float32
    ).astype(jnp.bfloat16)
    chosen = masked
    for turn in range(1, n_owners):
        chosen = chosen + lax.ppermute(
            masked, ("rep", "sub"), [(i, (i + turn) % n_owners) for i in range(n_owners)]
        )
    panel_slots = jnp.stack([
        (tensor_index ^ at) * up_b.shape[0] + each for at in order for each in range(up_b.shape[0])
    ]).astype(jnp.int32)

    panels = [panel.reshape(-1, width) for panel in panels]
    partial, lifted = finish_steps(
        [ended[step] for step in range(step_count - 1)],
        chosen.reshape(step_count * rows_mine, rank_size),
        jnp.broadcast_to(my_slot, (step_count, rows_mine)).reshape(step_count * rows_mine, 1),
        panel_slots,
        panels,
    )
    return finish_last(partial, lifted, ended[step_count - 1])


def solution(mesh):
    return jax.shard_map(
        per_device,
        mesh=mesh,
        in_specs=(
            P(None, ("groups", "rep", "sub"), "tp"),
            P("tp", ("rep", "sub")),
            P(("rep", "sub"), "tp", None),
            P("tp", None, ("rep", "sub")),
            P("groups", None),
            P(),
        ),
        out_specs=P(None, ("groups", "tp"), ("rep", "sub")),
        check_vma=False,
    )
```

```python
import functools

import jax
import jax.numpy as jnp
from jax import lax
from jax.experimental import pallas as pl
from jax.experimental.pallas import tpu as pltpu
from jax.sharding import PartitionSpec as P

ADAPTER_SCALE = 0.5
BLOCK_N = 256
BLOCK = 1024
BUFFERS = 4
RANK_NAME = 1000
VMEM_BYTES = 20 * 1024 * 1024


def block_shape(depth, width):
    columns = BLOCK if width % BLOCK == 0 else width
    for size in (BLOCK, BLOCK // 2, BLOCK // 4):
        if depth % size == 0:
            return size, columns
    return depth, columns


def rank_columns(factors):
    slots, rank, _ = factors.shape
    return -(-slots * rank // 128) * 128


def matmul_body(spans, staged, apart, pos_ref, *refs):
    sources = refs[:2 * len(spans)]
    w_ref, a_ref = refs[2 * len(spans):2 * len(spans) + 2]
    outs = refs[2 * len(spans) + 2:]
    send_refs, keep_refs, outs = outs[:len(spans)], outs[len(spans):2 * len(spans)], outs[2 * len(spans):]
    outs, refs = (outs[:-7], outs[-7:]) if staged else (outs[:-5], outs[-5:])
    x_ref, w_buf, total_ref, x_sems, w_sems = refs[:5]
    rows = total_ref.shape[0]
    edges = [0]
    for ref in send_refs:
        edges.append(edges[-1] + ref.shape[0])
    depth, width = w_ref.shape
    slots, rank, _ = a_ref.shape
    buffers, block_k, block_w = w_buf.shape
    block_n = min(BLOCK_N, block_w)
    depths, count = depth // block_k, (depth // block_k) * (width // block_w)

    def fetch(block, slot):
        begin = pl.multiple_of(lax.rem(block, depths) * block_k, block_k)
        left = pl.multiple_of(lax.div(block, depths) * block_w, block_w)
        return pltpu.make_async_copy(
            w_ref.at[pl.ds(begin, block_k), pl.ds(left, block_w)], w_buf.at[slot], w_sems.at[slot]
        )

    own_at = pos_ref[0]
    copies, begin = [], 0
    for index, (first, steps) in enumerate(spans):
        for core, at in enumerate((own_at, 1 - own_at)):
            source = sources[2 * index + core]
            copies.append(pltpu.make_async_copy(
                source.at[pl.ds(first, steps)], x_ref.at[at, pl.ds(begin, steps)], x_sems.at[2 * index + core]
            ))
        begin += steps
    for copy in copies:
        copy.start()
    if staged:
        stage_ref, stage_sems = refs[5:]
        stage_in = pltpu.make_async_copy(sources[0].at[pl.ds(1, staged)], stage_ref, stage_sems.at[staged])
        stage_in.start()
        stage_out = [
            pltpu.make_async_copy(stage_ref.at[pl.ds(index, 1)], out_ref, stage_sems.at[index])
            for index, out_ref in enumerate(outs)
        ]
    for block in range(buffers):
        fetch(jnp.int32(block), block).start()
    for ref in keep_refs:
        ref[...] = jnp.zeros_like(ref)
    total_ref[...] = jnp.zeros_like(total_ref)
    send_rank, keep_ranks = (outs[0], outs[1:2]) if apart else (total_ref, keep_refs)
    if apart:
        for ref in outs[:2]:
            ref[...] = jnp.zeros_like(ref)
    for copy in copies:
        copy.wait()
    if staged:
        stage_in.wait()
        for copy in stage_out:
            copy.start()
    for slot in range(slots):
        x = x_ref[...].reshape(2 * rows, depth)
        part = lax.dot_general(
            x, a_ref[slot], (((1,), (1,)), ((), ())), preferred_element_type=jnp.float32
        )
        begin = slot * rank + (0 if apart else width)
        send_rank[:, begin:begin + rank] = part[:rows]
        for index, ref in enumerate(keep_ranks):
            ref[:, begin:begin + rank] = part[rows + edges[index]:rows + edges[index + 1]]

    @pl.loop(0, count)
    def _(block):
        slot = lax.rem(block, buffers)
        fetch(block, slot).wait()
        inner = pl.ds(pl.multiple_of(lax.rem(block, depths) * block_k, block_k), block_k)
        left = pl.multiple_of(lax.div(block, depths) * block_w, block_w)
        x = x_ref[:, :, :, inner].reshape(2 * rows, block_k)
        for place in range(block_w // block_n):
            columns = pl.ds(left + place * block_n, block_n)
            term = jnp.dot(
                x, w_buf[slot, :, place * block_n:(place + 1) * block_n], preferred_element_type=jnp.float32
            )
            total_ref[:, columns] += term[:rows]
            for index, ref in enumerate(keep_refs):
                ref[:, columns] += term[rows + edges[index]:rows + edges[index + 1]]

        @pl.when(block + buffers < count)
        def _():
            fetch(block + buffers, slot).start()

    for index, ref in enumerate(send_refs):
        ref[...] = total_ref[edges[index]:edges[index + 1]].astype(ref.dtype)
    if staged:
        for copy in stage_out:
            copy.wait()


def partial_products(pos, chunks, weight, factors, apart=False, staged=0):
    _, per_block, depth = chunks[0][0].shape
    width = weight.shape[1]
    spans = tuple((first, steps) for _, _, first, steps in chunks)
    steps = sum(length for _, length in spans)
    rows = steps * per_block
    block_k, block_w = block_shape(depth, width)
    buffers = min(BUFFERS, (depth // block_k) * (width // block_w))
    any_spec = pl.BlockSpec(memory_space=pl.ANY)
    vmem_spec = pl.BlockSpec(memory_space=pltpu.VMEM)
    extra = rank_columns(factors)
    columns = width + (0 if apart else extra)
    out_shape = [
        jax.ShapeDtypeStruct((length * per_block, columns), kind)
        for kind in (jnp.bfloat16, jnp.float32) for _, length in spans
    ] + [jax.ShapeDtypeStruct((rows, extra), jnp.float32)] * (2 if apart else 0)
    out_specs = [vmem_spec] * len(out_shape)
    out_shape += [pltpu.HBM((1, per_block, depth), jnp.bfloat16)] * staged
    out_specs += [any_spec] * staged
    return pl.pallas_call(
        functools.partial(matmul_body, spans, staged, apart),
        in_specs=[pl.BlockSpec(memory_space=pltpu.SMEM)] + [any_spec] * (2 * len(chunks) + 1) + [vmem_spec],
        out_specs=out_specs,
        out_shape=out_shape,
        scratch_shapes=[
            pltpu.VMEM((2, steps, per_block, depth), jnp.bfloat16),
            pltpu.VMEM((buffers, block_k, block_w), jnp.bfloat16),
            pltpu.VMEM((rows, columns), jnp.float32),
            pltpu.SemaphoreType.DMA((2 * len(chunks),)),
            pltpu.SemaphoreType.DMA((buffers,)),
        ] + ([
            pltpu.VMEM((staged, per_block, depth), jnp.bfloat16),
            pltpu.SemaphoreType.DMA((staged + 1,)),
        ] if staged else []),
        compiler_params=pltpu.CompilerParams(vmem_limit_bytes=VMEM_BYTES),
        cost_estimate=pl.CostEstimate(flops=0, bytes_accessed=0, transcendentals=0),
        name="partial_products",
    )(pos, *[source for own, sib, _, _ in chunks for source in (own, sib)], weight, factors)


def finish_body(received, panels, chosen_ref, slot_ref, order_ref, *refs):
    panel_refs, refs = refs[:panels], refs[panels:]
    per_panel = panel_refs[0].shape[0]
    out_ref, lifted_ref, done_ref, sem = refs[-4:]
    steps, rows, width = done_ref.shape
    rank = chosen_ref.shape[1]
    chosen = chosen_ref[...]
    slot = slot_ref[...]
    spread = jnp.concatenate(
        [
            jnp.where(slot == order_ref[place], chosen, jnp.zeros_like(chosen))
            for place in range(panels * per_panel // rank)
        ],
        axis=1,
    )
    block_n = min(BLOCK_N, width)
    for place in range(width // block_n):
        columns = slice(place * block_n, (place + 1) * block_n)
        panel = jnp.concatenate([panel_ref[:, columns] for panel_ref in panel_refs], axis=0)
        lifted = jnp.dot(spread, panel, preferred_element_type=jnp.float32).astype(jnp.bfloat16)
        for step in range(steps):
            total = refs[step * (received + 1)][:, columns]
            for value_ref in refs[step * (received + 1) + 1:(step + 1) * (received + 1)]:
                total = total + value_ref[:, columns].astype(jnp.float32)
            value = total + ADAPTER_SCALE * lifted[step * rows:(step + 1) * rows].astype(jnp.float32)
            done_ref[step, :, columns] = value.astype(done_ref.dtype)
        lifted_ref[:, columns] = lifted[steps * rows:]
    copy = pltpu.make_async_copy(done_ref, out_ref.at[pl.ds(0, steps)], sem)
    copy.start()
    copy.wait()


def finish_steps(totals, chosen, slots, order, panels):
    steps, width = len(totals), panels[0].shape[1]
    rows = chosen.shape[0] // (steps + 1)
    vmem_spec = pl.BlockSpec(memory_space=pltpu.VMEM)
    arrays = [value for total in totals for value in total]
    return pl.pallas_call(
        functools.partial(finish_body, len(totals[0]) - 1, len(panels)),
        in_specs=[vmem_spec, vmem_spec, pl.BlockSpec(memory_space=pltpu.SMEM)] + [vmem_spec] * (len(panels) + len(arrays)),
        out_specs=[pl.BlockSpec(memory_space=pl.ANY), vmem_spec],
        out_shape=[
            jax.ShapeDtypeStruct((steps + 1, rows, width), jnp.bfloat16),
            jax.ShapeDtypeStruct((rows, width), jnp.bfloat16),
        ],
        scratch_shapes=[pltpu.VMEM((steps, rows, width), jnp.bfloat16), pltpu.SemaphoreType.DMA],
        compiler_params=pltpu.CompilerParams(vmem_limit_bytes=VMEM_BYTES),
        cost_estimate=pl.CostEstimate(flops=0, bytes_accessed=0, transcendentals=0),
        name="finish_steps",
    )(chosen, slots, order, *panels, *arrays)


def last_body(partial_ref, lifted_ref, *refs):
    out_ref, done_ref, sem = refs[-3:]
    total = refs[0][...]
    for value_ref in refs[1:-3]:
        total = total + value_ref[...].astype(jnp.float32)
    value = total + ADAPTER_SCALE * lifted_ref[...].astype(jnp.float32)
    done_ref[0] = value.astype(done_ref.dtype)
    copy = pltpu.make_async_copy(done_ref, out_ref.at[pl.ds(out_ref.shape[0] - 1, 1)], sem)
    copy.start()
    copy.wait()


def finish_last(partial, lifted, arrays):
    vmem_spec = pl.BlockSpec(memory_space=pltpu.VMEM)
    any_spec = pl.BlockSpec(memory_space=pl.ANY)
    return pl.pallas_call(
        last_body,
        in_specs=[any_spec] + [vmem_spec] * (1 + len(arrays)),
        out_specs=any_spec,
        out_shape=jax.ShapeDtypeStruct(partial.shape, partial.dtype),
        input_output_aliases={0: 0},
        scratch_shapes=[pltpu.VMEM((1,) + partial.shape[1:], partial.dtype), pltpu.SemaphoreType.DMA],
        compiler_params=pltpu.CompilerParams(vmem_limit_bytes=VMEM_BYTES),
        cost_estimate=pl.CostEstimate(flops=0, bytes_accessed=0, transcendentals=0),
        name="finish_last",
    )(partial, lifted, *arrays)


def per_device(hidden, base_weight, down_a, up_b, adapter_ids, owner_map):
    step_count, per_block, _ = hidden.shape
    n_tensor = lax.axis_size("tp")
    n_rep = lax.axis_size("rep")
    n_sub = lax.axis_size("sub")
    n_owners = n_rep * n_sub
    tensor_index = lax.axis_index("tp")
    rep_index = lax.axis_index("rep")
    sub_index = lax.axis_index("sub")
    owner_index = lax.axis_index(("rep", "sub"))
    requests = per_block * n_owners
    rows_mine = requests // n_tensor
    group = n_tensor // n_rep
    group_index = tensor_index // group
    owned_slots, _, rank_size = down_a.shape
    slot_count = owned_slots * n_owners
    width = base_weight.shape[1]

    def after(value, *done):
        return lax.optimization_barrier((value, *done))[0]

    def swap_cores(value):
        return lax.ppermute(value, "sub", [(i, i ^ 1) for i in range(n_sub)])

    def from_rep(value, shift):
        return lax.ppermute(value, "rep", [((i + shift) % n_rep, i) for i in range(n_rep)])

    def swap_tensor(value, bit):
        return lax.ppermute(value, "tp", [(i, i ^ bit) for i in range(n_tensor)])

    def to_group(value, hop):
        moved = group * hop
        return lax.ppermute(value, "tp", [(i, (i + moved) % n_tensor) for i in range(n_tensor)])

    def pick(values, index):
        value = values[0]
        for at in range(1, len(values)):
            value = jnp.where(index == at, values[at], value)
        return value

    keeps = (tensor_index // (group // 2)) % 2
    pos = (sub_index == keeps).astype(jnp.int32).reshape(1)

    siblings = swap_cores(hidden)
    pieces = [(step, shift) for step in range(step_count) for shift in range(1, n_rep)]
    source = pltpu.with_memory_space_constraint(hidden, pltpu.HBM)
    weight = pltpu.with_memory_space_constraint(base_weight, pltpu.HBM)
    remote = {(0, shift): from_rep(hidden[:1], shift) for shift in range(1, n_rep)}

    def spread_panels(panels, order, bits):
        for bit in bits:
            panels = panels + [swap_tensor(panel, bit) for panel in panels]
            order = order + [at ^ bit for at in order]
        return panels, order

    bits = [n_tensor >> at for at in range(1, n_tensor.bit_length())]
    order = [0, bits[0], bits[1]]
    panels = [up_b] + [swap_tensor(up_b, at) for at in order[1:]]

    my_ids = lax.dynamic_slice_in_dim(adapter_ids, tensor_index * rows_mine, rows_mine)
    iota = lax.broadcasted_iota(jnp.int32, (rows_mine, slot_count), 1)
    my_slot = jnp.sum((my_ids == iota).astype(jnp.int32) * owner_map[None, :], axis=1)
    owned_hot = my_slot[:, None] == (
        owner_index * owned_slots + lax.broadcasted_iota(jnp.int32, (rows_mine, owned_slots), 1)
    )

    first_leg, halved, begun, second_leg, ended = [], {}, set(), [], {}

    def second_half(total, received, steps, kind):
        total = total + received.astype(jnp.float32)
        rows, columns = total.shape
        extent, bit = rows // steps, group // 4
        while bit:
            extent //= 2
            halves = total.reshape(steps, 2, extent, columns)
            mine = (tensor_index // bit) % 2
            kept = lax.dynamic_index_in_dim(halves, mine, 1, keepdims=False)
            sent = lax.dynamic_index_in_dim(halves, 1 - mine, 1, keepdims=False)
            total = kept + swap_tensor(sent.astype(kind), bit).astype(jnp.float32)
            bit //= 2
        return total.reshape(steps, extent, columns)

    def gap(token, jobs, ahead=()):
        nonlocal first_leg, second_leg
        for parts, received, keep, kind in first_leg:
            steps = sum(length for _, length in parts)
            total, begin = second_half(after(keep, token), received, steps, kind), 0
            for key, length in parts:
                for at in range(begin, begin + length):
                    halved[key[0] + at - begin, key[1]] = total[at]
                    if (key[0] + at - begin, key[1]) == (step_count - 1, 0):
                        halved[RANK_NAME, 0] = total[at][:, width:]
                begin += length
        closed = {name: (after(kept, token), *received) for name, kept, received in second_leg}
        started, sends = [], []
        for name in sorted({name for name, _ in halved}):
            if name in begun or name == RANK_NAME or any((name, at) not in halved for at in range(n_rep)):
                continue
            begun.add(name)
            values = [halved[name, at] for at in range(n_rep)]
            columns = min(value.shape[1] for value in values)
            values = [value[:, :columns] for value in values]
            kept = pick(values, (group_index - rep_index) % n_rep)
            sends.append([
                pick(values, (group_index + hop - rep_index) % n_rep).astype(jnp.bfloat16) for hop in range(1, n_rep)
            ])
            started.append((name, kept))
        sends, token, ahead = lax.optimization_barrier((sends, token, ahead))
        first_sends, closed = lax.optimization_barrier(([job[1] for job in jobs], closed))
        ended.update(closed)
        first_leg = [
            (parts, swap_tensor(send, group // 2), keep, kind) for (parts, _, keep, kind), send in zip(jobs, first_sends)
        ]
        second_leg = [
            (name, kept, [to_group(value, hop + 1) for hop, value in enumerate(sent)])
            for (name, kept), sent in zip(started, sends)
        ]
        return sends, ahead

    factors = jnp.swapaxes(down_a, 1, 2)

    lead = step_count // 2
    last_ranks, next_local = {}, lead
    send, keep, *slices = partial_products(
        pos, [(source, siblings, 0, lead)], weight, factors, staged=step_count - 1
    )
    for step, rows in enumerate(slices, 1):
        remote.update({(step, shift): from_rep(rows, shift) for shift in range(1, n_rep)})
    jobs = [([((0, 0), lead)], send, keep, jnp.bfloat16)]
    for piece, (step, shift) in enumerate(pieces):
        arrived = [received for _, received, _, _ in first_leg] if piece == 1 else []
        sends, _ = gap(send, jobs)
        own, panels, *_ = lax.optimization_barrier((remote[step, shift], panels, arrived, send))
        if piece == 0:
            panels, order = panels + [swap_tensor(panels[1], bits[1])], order + [bits[0] ^ bits[1]]
            panels, order = spread_panels(panels, order, bits[2:])
        sib = swap_cores(own)
        own, sib, siblings, _ = lax.optimization_barrier((own, sib, siblings, sends))
        last, chunks, keys = step == step_count - 1, [(own, sib, 0, 1)], [(step, shift)]
        if next_local < step_count:
            chunks.append((source, siblings, next_local, 1))
            keys.append((next_local, 0))
            next_local += 1
        outs = partial_products(pos, chunks, weight, factors, last)
        send, count = outs[0], len(chunks)
        jobs = [([(key, 1)], outs[at], outs[count + at], jnp.bfloat16) for at, key in enumerate(keys)]
        if last:
            last_ranks[shift] = outs[2 * count:]
    for shift, ranks in last_ranks.items():
        halved[RANK_NAME, shift] = second_half(ranks[1], swap_tensor(ranks[0], group // 2), 1, jnp.float32)[0]
    values = [halved[RANK_NAME, at] for at in range(n_rep)]
    ahead = [pick(values, (group_index + hop - rep_index) % n_rep) for hop in range(1, n_rep)]
    _, ahead = gap(send, jobs, ahead)
    ended[RANK_NAME] = (
        pick(values, (group_index - rep_index) % n_rep),
        *[to_group(value, hop + 1) for hop, value in enumerate(ahead)],
    )
    rounded, _ = gap(send, [])

    def rank_sum(name):
        kept, *received = [value[:, -rank_columns(factors):] for value in ended[name]]
        for value in received:
            kept = kept + value.astype(jnp.float32)
        return kept[:, :owned_slots * rank_size]

    finished = jnp.stack([rank_sum(step) for step in range(step_count - 1)] + [rank_sum(RANK_NAME)])
    finished = finished.astype(jnp.bfloat16).reshape(step_count, rows_mine, owned_slots, rank_size)
    finished = lax.optimization_barrier((finished, rounded))[0]
    ended.update((name, (kept, *received)) for name, kept, received in second_leg)
    masked = jnp.sum(
        jnp.where(owned_hot[None, :, :, None], finished, 0), axis=2, dtype=jnp.float32
    ).astype(jnp.bfloat16)
    chosen = masked
    for turn in range(1, n_owners):
        chosen = chosen + lax.ppermute(
            masked, ("rep", "sub"), [(i, (i + turn) % n_owners) for i in range(n_owners)]
        )
    panel_slots = jnp.stack([
        (tensor_index ^ at) * up_b.shape[0] + each for at in order for each in range(up_b.shape[0])
    ]).astype(jnp.int32)

    panels = [panel.reshape(-1, width) for panel in panels]
    partial, lifted = finish_steps(
        [ended[step] for step in range(step_count - 1)],
        chosen.reshape(step_count * rows_mine, rank_size),
        jnp.broadcast_to(my_slot, (step_count, rows_mine)).reshape(step_count * rows_mine, 1),
        panel_slots,
        panels,
    )
    return finish_last(partial, lifted, ended[step_count - 1])


def solution(mesh):
    return jax.shard_map(
        per_device,
        mesh=mesh,
        in_specs=(
            P(None, ("groups", "rep", "sub"), "tp"),
            P("tp", ("rep", "sub")),
            P(("rep", "sub"), "tp", None),
            P("tp", None, ("rep", "sub")),
            P("groups", None),
            P(),
        ),
        out_specs=P(None, ("groups", "tp"), ("rep", "sub")),
        check_vma=False,
    )
```

```python
import functools

import jax
import jax.numpy as jnp
from jax import lax
from jax.experimental import pallas as pl
from jax.experimental.pallas import tpu as pltpu
from jax.sharding import PartitionSpec as P

ADAPTER_SCALE = 0.5
BLOCK_N = 256
BLOCK = 1024
BUFFERS = 4
RANK_NAME = 1000
VMEM_BYTES = 20 * 1024 * 1024


def block_shape(depth, width):
    columns = BLOCK if width % BLOCK == 0 else width
    for size in (BLOCK, BLOCK // 2, BLOCK // 4):
        if depth % size == 0:
            return size, columns
    return depth, columns


def rank_columns(factors):
    slots, rank, _ = factors.shape
    return -(-slots * rank // 128) * 128


def matmul_body(spans, staged, apart, pos_ref, *refs):
    sources = refs[:2 * len(spans)]
    w_ref, a_ref = refs[2 * len(spans):2 * len(spans) + 2]
    outs = refs[2 * len(spans) + 2:]
    send_refs, keep_refs, outs = outs[:len(spans)], outs[len(spans):2 * len(spans)], outs[2 * len(spans):]
    outs, refs = (outs[:-7], outs[-7:]) if staged else (outs[:-5], outs[-5:])
    x_ref, w_buf, total_ref, x_sems, w_sems = refs[:5]
    rows = total_ref.shape[0]
    edges = [0]
    for ref in send_refs:
        edges.append(edges[-1] + ref.shape[0])
    depth, width = w_ref.shape
    slots, rank, _ = a_ref.shape
    buffers, block_k, block_w = w_buf.shape
    block_n = min(BLOCK_N, block_w)
    depths, count = depth // block_k, (depth // block_k) * (width // block_w)

    def fetch(block, slot):
        begin = pl.multiple_of(lax.rem(block, depths) * block_k, block_k)
        left = pl.multiple_of(lax.div(block, depths) * block_w, block_w)
        return pltpu.make_async_copy(
            w_ref.at[pl.ds(begin, block_k), pl.ds(left, block_w)], w_buf.at[slot], w_sems.at[slot]
        )

    own_at = pos_ref[0]
    copies, begin = [], 0
    for index, (first, steps) in enumerate(spans):
        for core, at in enumerate((own_at, 1 - own_at)):
            source = sources[2 * index + core]
            copies.append(pltpu.make_async_copy(
                source.at[pl.ds(first, steps)], x_ref.at[at, pl.ds(begin, steps)], x_sems.at[2 * index + core]
            ))
        begin += steps
    for copy in copies:
        copy.start()
    if staged:
        stage_ref, stage_sems = refs[5:]
        stage_in = pltpu.make_async_copy(sources[0].at[pl.ds(1, staged)], stage_ref, stage_sems.at[staged])
        stage_in.start()
        stage_out = [
            pltpu.make_async_copy(stage_ref.at[pl.ds(index, 1)], out_ref, stage_sems.at[index])
            for index, out_ref in enumerate(outs)
        ]
    for block in range(buffers):
        fetch(jnp.int32(block), block).start()
    for ref in keep_refs:
        ref[...] = jnp.zeros_like(ref)
    total_ref[...] = jnp.zeros_like(total_ref)
    send_rank, keep_ranks = (outs[0], outs[1:2]) if apart else (total_ref, keep_refs)
    if apart:
        for ref in outs[:2]:
            ref[...] = jnp.zeros_like(ref)
    for copy in copies:
        copy.wait()
    if staged:
        stage_in.wait()
        for copy in stage_out:
            copy.start()
    for slot in range(slots):
        x = x_ref[...].reshape(2 * rows, depth)
        part = lax.dot_general(
            x, a_ref[slot], (((1,), (1,)), ((), ())), preferred_element_type=jnp.float32
        )
        begin = slot * rank + (0 if apart else width)
        send_rank[:, begin:begin + rank] = part[:rows]
        for index, ref in enumerate(keep_ranks):
            ref[:, begin:begin + rank] = part[rows + edges[index]:rows + edges[index + 1]]

    @pl.loop(0, count)
    def _(block):
        slot = lax.rem(block, buffers)
        fetch(block, slot).wait()
        inner = pl.ds(pl.multiple_of(lax.rem(block, depths) * block_k, block_k), block_k)
        left = pl.multiple_of(lax.div(block, depths) * block_w, block_w)
        x = x_ref[:, :, :, inner].reshape(2 * rows, block_k)
        for place in range(block_w // block_n):
            columns = pl.ds(left + place * block_n, block_n)
            term = jnp.dot(
                x, w_buf[slot, :, place * block_n:(place + 1) * block_n], preferred_element_type=jnp.float32
            )
            total_ref[:, columns] += term[:rows]
            for index, ref in enumerate(keep_refs):
                ref[:, columns] += term[rows + edges[index]:rows + edges[index + 1]]

        @pl.when(block + buffers < count)
        def _():
            fetch(block + buffers, slot).start()

    for index, ref in enumerate(send_refs):
        ref[...] = total_ref[edges[index]:edges[index + 1]].astype(ref.dtype)
    if staged:
        for copy in stage_out:
            copy.wait()


def partial_products(pos, chunks, weight, factors, apart=False, staged=0):
    _, per_block, depth = chunks[0][0].shape
    width = weight.shape[1]
    spans = tuple((first, steps) for _, _, first, steps in chunks)
    steps = sum(length for _, length in spans)
    rows = steps * per_block
    block_k, block_w = block_shape(depth, width)
    buffers = min(BUFFERS, (depth // block_k) * (width // block_w))
    any_spec = pl.BlockSpec(memory_space=pl.ANY)
    vmem_spec = pl.BlockSpec(memory_space=pltpu.VMEM)
    extra = rank_columns(factors)
    columns = width + (0 if apart else extra)
    out_shape = [
        jax.ShapeDtypeStruct((length * per_block, columns), kind)
        for kind in (jnp.bfloat16, jnp.float32) for _, length in spans
    ] + [jax.ShapeDtypeStruct((rows, extra), jnp.float32)] * (2 if apart else 0)
    out_specs = [vmem_spec] * len(out_shape)
    out_shape += [pltpu.HBM((1, per_block, depth), jnp.bfloat16)] * staged
    out_specs += [any_spec] * staged
    return pl.pallas_call(
        functools.partial(matmul_body, spans, staged, apart),
        in_specs=[pl.BlockSpec(memory_space=pltpu.SMEM)] + [any_spec] * (2 * len(chunks) + 1) + [vmem_spec],
        out_specs=out_specs,
        out_shape=out_shape,
        scratch_shapes=[
            pltpu.VMEM((2, steps, per_block, depth), jnp.bfloat16),
            pltpu.VMEM((buffers, block_k, block_w), jnp.bfloat16),
            pltpu.VMEM((rows, columns), jnp.float32),
            pltpu.SemaphoreType.DMA((2 * len(chunks),)),
            pltpu.SemaphoreType.DMA((buffers,)),
        ] + ([
            pltpu.VMEM((staged, per_block, depth), jnp.bfloat16),
            pltpu.SemaphoreType.DMA((staged + 1,)),
        ] if staged else []),
        compiler_params=pltpu.CompilerParams(vmem_limit_bytes=VMEM_BYTES),
        cost_estimate=pl.CostEstimate(flops=0, bytes_accessed=0, transcendentals=0),
        name="partial_products",
    )(pos, *[source for own, sib, _, _ in chunks for source in (own, sib)], weight, factors)


def finish_body(received, panels, chosen_ref, slot_ref, order_ref, *refs):
    panel_refs, refs = refs[:panels], refs[panels:]
    per_panel = panel_refs[0].shape[0]
    out_ref, lifted_ref, done_ref, sem = refs[-4:]
    steps, rows, width = done_ref.shape
    rank = chosen_ref.shape[1]
    chosen = chosen_ref[...]
    slot = slot_ref[...]
    spread = jnp.concatenate(
        [
            jnp.where(slot == order_ref[place], chosen, jnp.zeros_like(chosen))
            for place in range(panels * per_panel // rank)
        ],
        axis=1,
    )
    block_n = min(BLOCK_N, width)
    for place in range(width // block_n):
        columns = slice(place * block_n, (place + 1) * block_n)
        panel = jnp.concatenate([panel_ref[:, columns] for panel_ref in panel_refs], axis=0)
        lifted = jnp.dot(spread, panel, preferred_element_type=jnp.float32).astype(jnp.bfloat16)
        for step in range(steps):
            total = refs[step * (received + 1)][:, columns]
            for value_ref in refs[step * (received + 1) + 1:(step + 1) * (received + 1)]:
                total = total + value_ref[:, columns].astype(jnp.float32)
            value = total + ADAPTER_SCALE * lifted[step * rows:(step + 1) * rows].astype(jnp.float32)
            done_ref[step, :, columns] = value.astype(done_ref.dtype)
        lifted_ref[:, columns] = lifted[steps * rows:]
    copy = pltpu.make_async_copy(done_ref, out_ref.at[pl.ds(0, steps)], sem)
    copy.start()
    copy.wait()


def finish_steps(totals, chosen, slots, order, panels):
    steps, width = len(totals), panels[0].shape[1]
    rows = chosen.shape[0] // (steps + 1)
    vmem_spec = pl.BlockSpec(memory_space=pltpu.VMEM)
    arrays = [value for total in totals for value in total]
    return pl.pallas_call(
        functools.partial(finish_body, len(totals[0]) - 1, len(panels)),
        in_specs=[vmem_spec, vmem_spec, pl.BlockSpec(memory_space=pltpu.SMEM)] + [vmem_spec] * (len(panels) + len(arrays)),
        out_specs=[pl.BlockSpec(memory_space=pl.ANY), vmem_spec],
        out_shape=[
            jax.ShapeDtypeStruct((steps + 1, rows, width), jnp.bfloat16),
            jax.ShapeDtypeStruct((rows, width), jnp.bfloat16),
        ],
        scratch_shapes=[pltpu.VMEM((steps, rows, width), jnp.bfloat16), pltpu.SemaphoreType.DMA],
        compiler_params=pltpu.CompilerParams(vmem_limit_bytes=VMEM_BYTES),
        cost_estimate=pl.CostEstimate(flops=0, bytes_accessed=0, transcendentals=0),
        name="finish_steps",
    )(chosen, slots, order, *panels, *arrays)


def last_body(partial_ref, lifted_ref, *refs):
    out_ref, done_ref, sem = refs[-3:]
    total = refs[0][...]
    for value_ref in refs[1:-3]:
        total = total + value_ref[...].astype(jnp.float32)
    value = total + ADAPTER_SCALE * lifted_ref[...].astype(jnp.float32)
    done_ref[0] = value.astype(done_ref.dtype)
    copy = pltpu.make_async_copy(done_ref, out_ref.at[pl.ds(out_ref.shape[0] - 1, 1)], sem)
    copy.start()
    copy.wait()


def finish_last(partial, lifted, arrays):
    vmem_spec = pl.BlockSpec(memory_space=pltpu.VMEM)
    any_spec = pl.BlockSpec(memory_space=pl.ANY)
    return pl.pallas_call(
        last_body,
        in_specs=[any_spec] + [vmem_spec] * (1 + len(arrays)),
        out_specs=any_spec,
        out_shape=jax.ShapeDtypeStruct(partial.shape, partial.dtype),
        input_output_aliases={0: 0},
        scratch_shapes=[pltpu.VMEM((1,) + partial.shape[1:], partial.dtype), pltpu.SemaphoreType.DMA],
        compiler_params=pltpu.CompilerParams(vmem_limit_bytes=VMEM_BYTES),
        cost_estimate=pl.CostEstimate(flops=0, bytes_accessed=0, transcendentals=0),
        name="finish_last",
    )(partial, lifted, *arrays)


def per_device(hidden, base_weight, down_a, up_b, adapter_ids, owner_map):
    step_count, per_block, _ = hidden.shape
    n_tensor = lax.axis_size("tp")
    n_rep = lax.axis_size("rep")
    n_sub = lax.axis_size("sub")
    n_owners = n_rep * n_sub
    tensor_index = lax.axis_index("tp")
    rep_index = lax.axis_index("rep")
    sub_index = lax.axis_index("sub")
    owner_index = lax.axis_index(("rep", "sub"))
    requests = per_block * n_owners
    rows_mine = requests // n_tensor
    group = n_tensor // n_rep
    group_index = tensor_index // group
    owned_slots, _, rank_size = down_a.shape
    slot_count = owned_slots * n_owners
    width = base_weight.shape[1]

    def after(value, *done):
        return lax.optimization_barrier((value, *done))[0]

    def swap_cores(value):
        return lax.ppermute(value, "sub", [(i, i ^ 1) for i in range(n_sub)])

    def from_rep(value, shift):
        return lax.ppermute(value, "rep", [((i + shift) % n_rep, i) for i in range(n_rep)])

    def swap_tensor(value, bit):
        return lax.ppermute(value, "tp", [(i, i ^ bit) for i in range(n_tensor)])

    def to_group(value, hop):
        moved = group * hop
        return lax.ppermute(value, "tp", [(i, (i + moved) % n_tensor) for i in range(n_tensor)])

    def pick(values, index):
        value = values[0]
        for at in range(1, len(values)):
            value = jnp.where(index == at, values[at], value)
        return value

    keeps = (tensor_index // (group // 2)) % 2
    pos = (sub_index == keeps).astype(jnp.int32).reshape(1)

    siblings = swap_cores(hidden)
    pieces = [(step, shift) for step in range(step_count) for shift in range(1, n_rep)]
    source = pltpu.with_memory_space_constraint(hidden, pltpu.HBM)
    weight = pltpu.with_memory_space_constraint(base_weight, pltpu.HBM)
    remote = {(0, shift): from_rep(hidden[:1], shift) for shift in range(1, n_rep)}

    def spread_panels(panels, order, bits):
        for bit in bits:
            panels = panels + [swap_tensor(panel, bit) for panel in panels]
            order = order + [at ^ bit for at in order]
        return panels, order

    bits = [n_tensor >> at for at in range(1, n_tensor.bit_length())]
    order = [0, bits[0], bits[1]]
    panels = [up_b] + [swap_tensor(up_b, at) for at in order[1:]]

    my_ids = lax.dynamic_slice_in_dim(adapter_ids, tensor_index * rows_mine, rows_mine)
    iota = lax.broadcasted_iota(jnp.int32, (rows_mine, slot_count), 1)
    my_slot = jnp.sum((my_ids == iota).astype(jnp.int32) * owner_map[None, :], axis=1)
    owned_hot = my_slot[:, None] == (
        owner_index * owned_slots + lax.broadcasted_iota(jnp.int32, (rows_mine, owned_slots), 1)
    )

    first_leg, halved, begun, second_leg, ended = [], {}, set(), [], {}

    def second_half(total, received, steps, kind):
        total = total + received.astype(jnp.float32)
        rows, columns = total.shape
        extent, bit = rows // steps, group // 4
        while bit:
            extent //= 2
            halves = total.reshape(steps, 2, extent, columns)
            mine = (tensor_index // bit) % 2
            kept = lax.dynamic_index_in_dim(halves, mine, 1, keepdims=False)
            sent = lax.dynamic_index_in_dim(halves, 1 - mine, 1, keepdims=False)
            total = kept + swap_tensor(sent.astype(kind), bit).astype(jnp.float32)
            bit //= 2
        return total.reshape(steps, extent, columns)

    def gap(token, jobs, ahead=()):
        nonlocal first_leg, second_leg
        for parts, received, keep, kind in first_leg:
            steps = sum(length for _, length in parts)
            total, begin = second_half(after(keep, token), received, steps, kind), 0
            for key, length in parts:
                for at in range(begin, begin + length):
                    halved[key[0] + at - begin, key[1]] = total[at]
                    if (key[0] + at - begin, key[1]) == (step_count - 1, 0):
                        halved[RANK_NAME, 0] = total[at][:, width:]
                begin += length
        closed = {name: (after(kept, token), *received) for name, kept, received in second_leg}
        started, sends = [], []
        for name in sorted({name for name, _ in halved}):
            if name in begun or name == RANK_NAME or any((name, at) not in halved for at in range(n_rep)):
                continue
            begun.add(name)
            values = [halved[name, at] for at in range(n_rep)]
            columns = min(value.shape[1] for value in values)
            values = [value[:, :columns] for value in values]
            kept = pick(values, (group_index - rep_index) % n_rep)
            sends.append([
                pick(values, (group_index + hop - rep_index) % n_rep).astype(jnp.bfloat16) for hop in range(1, n_rep)
            ])
            started.append((name, kept))
        sends, token, ahead = lax.optimization_barrier((sends, token, ahead))
        first_sends, closed = lax.optimization_barrier(([job[1] for job in jobs], closed))
        ended.update(closed)
        first_leg = [
            (parts, swap_tensor(send, group // 2), keep, kind) for (parts, _, keep, kind), send in zip(jobs, first_sends)
        ]
        second_leg = [
            (name, kept, [to_group(value, hop + 1) for hop, value in enumerate(sent)])
            for (name, kept), sent in zip(started, sends)
        ]
        return sends, ahead

    factors = jnp.swapaxes(down_a, 1, 2)

    lead = step_count // 2
    last_ranks, next_local = {}, lead
    send, keep, *slices = partial_products(
        pos, [(source, siblings, 0, lead)], weight, factors, staged=step_count - 1
    )
    for step, rows in enumerate(slices, 1):
        remote.update({(step, shift): from_rep(rows, shift) for shift in range(1, n_rep)})
    jobs = [([((0, 0), lead)], send, keep, jnp.bfloat16)]
    for piece, (step, shift) in enumerate(pieces):
        arrived = [received for _, received, _, _ in first_leg] if piece == 1 else []
        sends, _ = gap(send, jobs)
        own, panels, *_ = lax.optimization_barrier((remote[step, shift], panels, arrived, send))
        if piece == 0:
            panels, order = panels + [swap_tensor(panels[1], bits[1])], order + [bits[0] ^ bits[1]]
            panels, order = spread_panels(panels, order, bits[2:])
        sib = swap_cores(own)
        own, sib, siblings, _ = lax.optimization_barrier((own, sib, siblings, sends))
        last, chunks, keys = step == step_count - 1, [(own, sib, 0, 1)], [(step, shift)]
        if next_local < step_count:
            chunks.append((source, siblings, next_local, 1))
            keys.append((next_local, 0))
            next_local += 1
        outs = partial_products(pos, chunks, weight, factors, last)
        send, count = outs[0], len(chunks)
        jobs = [([(key, 1)], outs[at], outs[count + at], jnp.bfloat16) for at, key in enumerate(keys)]
        if last:
            last_ranks[shift] = outs[2 * count:]
    for shift, ranks in last_ranks.items():
        halved[RANK_NAME, shift] = second_half(ranks[1], swap_tensor(ranks[0], group // 2), 1, jnp.float32)[0]
    values = [halved[RANK_NAME, at] for at in range(n_rep)]
    ahead = [pick(values, (group_index + hop - rep_index) % n_rep) for hop in range(1, n_rep)]
    _, ahead = gap(send, jobs, ahead)
    ended[RANK_NAME] = (
        pick(values, (group_index - rep_index) % n_rep),
        *[to_group(value, hop + 1) for hop, value in enumerate(ahead)],
    )
    rounded, pending = gap(send, [], {name: received for name, _, received in second_leg})
    for name, received in pending.items():
        ended[name] = (ended[name][0], *received)

    def rank_sum(name):
        kept, *received = [value[:, -rank_columns(factors):] for value in ended[name]]
        for value in received:
            kept = kept + value.astype(jnp.float32)
        return kept[:, :owned_slots * rank_size]

    finished = jnp.stack([rank_sum(step) for step in range(step_count - 1)] + [rank_sum(RANK_NAME)])
    finished = finished.astype(jnp.bfloat16).reshape(step_count, rows_mine, owned_slots, rank_size)
    finished = lax.optimization_barrier((finished, rounded))[0]
    ended.update((name, (kept, *received)) for name, kept, received in second_leg)
    masked = jnp.sum(
        jnp.where(owned_hot[None, :, :, None], finished, 0), axis=2, dtype=jnp.float32
    ).astype(jnp.bfloat16)
    chosen = masked
    for turn in range(1, n_owners):
        chosen = chosen + lax.ppermute(
            masked, ("rep", "sub"), [(i, (i + turn) % n_owners) for i in range(n_owners)]
        )
    panel_slots = jnp.stack([
        (tensor_index ^ at) * up_b.shape[0] + each for at in order for each in range(up_b.shape[0])
    ]).astype(jnp.int32)

    panels = [panel.reshape(-1, width) for panel in panels]
    partial, lifted = finish_steps(
        [ended[step] for step in range(step_count - 1)],
        chosen.reshape(step_count * rows_mine, rank_size),
        jnp.broadcast_to(my_slot, (step_count, rows_mine)).reshape(step_count * rows_mine, 1),
        panel_slots,
        panels,
    )
    return finish_last(partial, lifted, ended[step_count - 1])


def solution(mesh):
    return jax.shard_map(
        per_device,
        mesh=mesh,
        in_specs=(
            P(None, ("groups", "rep", "sub"), "tp"),
            P("tp", ("rep", "sub")),
            P(("rep", "sub"), "tp", None),
            P("tp", None, ("rep", "sub")),
            P("groups", None),
            P(),
        ),
        out_specs=P(None, ("groups", "tp"), ("rep", "sub")),
        check_vma=False,
    )
```

```python
import functools

import jax
import jax.numpy as jnp
from jax import lax
from jax.experimental import pallas as pl
from jax.experimental.pallas import tpu as pltpu
from jax.sharding import PartitionSpec as P

ADAPTER_SCALE = 0.5
BLOCK_N = 256
BLOCK = 1024
BUFFERS = 5
RANK_NAME = 1000
VMEM_BYTES = 20 * 1024 * 1024


def block_shape(depth, width):
    columns = BLOCK if width % BLOCK == 0 else width
    for size in (BLOCK, BLOCK // 2, BLOCK // 4):
        if depth % size == 0:
            return size, columns
    return depth, columns


def rank_columns(factors):
    slots, rank, _ = factors.shape
    return -(-slots * rank // 128) * 128


def matmul_body(spans, staged, apart, pos_ref, *refs):
    sources = refs[:2 * len(spans)]
    w_ref, a_ref = refs[2 * len(spans):2 * len(spans) + 2]
    outs = refs[2 * len(spans) + 2:]
    send_refs, keep_refs, outs = outs[:len(spans)], outs[len(spans):2 * len(spans)], outs[2 * len(spans):]
    outs, refs = (outs[:-7], outs[-7:]) if staged else (outs[:-5], outs[-5:])
    x_ref, w_buf, total_ref, x_sems, w_sems = refs[:5]
    rows = total_ref.shape[0]
    edges = [0]
    for ref in send_refs:
        edges.append(edges[-1] + ref.shape[0])
    depth, width = w_ref.shape
    slots, rank, _ = a_ref.shape
    buffers, block_k, block_w = w_buf.shape
    block_n = min(BLOCK_N, block_w)
    depths, count = depth // block_k, (depth // block_k) * (width // block_w)

    def fetch(block, slot):
        begin = pl.multiple_of(lax.rem(block, depths) * block_k, block_k)
        left = pl.multiple_of(lax.div(block, depths) * block_w, block_w)
        return pltpu.make_async_copy(
            w_ref.at[pl.ds(begin, block_k), pl.ds(left, block_w)], w_buf.at[slot], w_sems.at[slot]
        )

    own_at = pos_ref[0]
    copies, begin = [], 0
    for index, (first, steps) in enumerate(spans):
        for core, at in enumerate((own_at, 1 - own_at)):
            source = sources[2 * index + core]
            copies.append(pltpu.make_async_copy(
                source.at[pl.ds(first, steps)], x_ref.at[at, pl.ds(begin, steps)], x_sems.at[2 * index + core]
            ))
        begin += steps
    for copy in copies:
        copy.start()
    if staged:
        stage_ref, stage_sems = refs[5:]
        stage_in = pltpu.make_async_copy(sources[0].at[pl.ds(1, staged)], stage_ref, stage_sems.at[staged])
        stage_in.start()
        stage_out = [
            pltpu.make_async_copy(stage_ref.at[pl.ds(index, 1)], out_ref, stage_sems.at[index])
            for index, out_ref in enumerate(outs)
        ]
    for block in range(buffers):
        fetch(jnp.int32(block), block).start()
    for ref in keep_refs:
        ref[...] = jnp.zeros_like(ref)
    total_ref[...] = jnp.zeros_like(total_ref)
    send_rank, keep_ranks = (outs[0], outs[1:2]) if apart else (total_ref, keep_refs)
    if apart:
        for ref in outs[:2]:
            ref[...] = jnp.zeros_like(ref)
    for copy in copies:
        copy.wait()
    if staged:
        stage_in.wait()
        for copy in stage_out:
            copy.start()
    for slot in range(slots):
        x = x_ref[...].reshape(2 * rows, depth)
        part = lax.dot_general(
            x, a_ref[slot], (((1,), (1,)), ((), ())), preferred_element_type=jnp.float32
        )
        begin = slot * rank + (0 if apart else width)
        send_rank[:, begin:begin + rank] = part[:rows]
        for index, ref in enumerate(keep_ranks):
            ref[:, begin:begin + rank] = part[rows + edges[index]:rows + edges[index + 1]]

    @pl.loop(0, count)
    def _(block):
        slot = lax.rem(block, buffers)
        fetch(block, slot).wait()
        inner = pl.ds(pl.multiple_of(lax.rem(block, depths) * block_k, block_k), block_k)
        left = pl.multiple_of(lax.div(block, depths) * block_w, block_w)
        x = x_ref[:, :, :, inner].reshape(2 * rows, block_k)
        for place in range(block_w // block_n):
            columns = pl.ds(left + place * block_n, block_n)
            term = jnp.dot(
                x, w_buf[slot, :, place * block_n:(place + 1) * block_n], preferred_element_type=jnp.float32
            )
            total_ref[:, columns] += term[:rows]
            for index, ref in enumerate(keep_refs):
                ref[:, columns] += term[rows + edges[index]:rows + edges[index + 1]]

        @pl.when(block + buffers < count)
        def _():
            fetch(block + buffers, slot).start()

    for index, ref in enumerate(send_refs):
        ref[...] = total_ref[edges[index]:edges[index + 1]].astype(ref.dtype)
    if staged:
        for copy in stage_out:
            copy.wait()


def partial_products(pos, chunks, weight, factors, apart=False, staged=0):
    _, per_block, depth = chunks[0][0].shape
    width = weight.shape[1]
    spans = tuple((first, steps) for _, _, first, steps in chunks)
    steps = sum(length for _, length in spans)
    rows = steps * per_block
    block_k, block_w = block_shape(depth, width)
    buffers = min(BUFFERS, (depth // block_k) * (width // block_w))
    any_spec = pl.BlockSpec(memory_space=pl.ANY)
    vmem_spec = pl.BlockSpec(memory_space=pltpu.VMEM)
    extra = rank_columns(factors)
    columns = width + (0 if apart else extra)
    out_shape = [
        jax.ShapeDtypeStruct((length * per_block, columns), kind)
        for kind in (jnp.bfloat16, jnp.float32) for _, length in spans
    ] + [jax.ShapeDtypeStruct((rows, extra), jnp.float32)] * (2 if apart else 0)
    out_specs = [vmem_spec] * len(out_shape)
    out_shape += [pltpu.HBM((1, per_block, depth), jnp.bfloat16)] * staged
    out_specs += [any_spec] * staged
    return pl.pallas_call(
        functools.partial(matmul_body, spans, staged, apart),
        in_specs=[pl.BlockSpec(memory_space=pltpu.SMEM)] + [any_spec] * (2 * len(chunks) + 1) + [vmem_spec],
        out_specs=out_specs,
        out_shape=out_shape,
        scratch_shapes=[
            pltpu.VMEM((2, steps, per_block, depth), jnp.bfloat16),
            pltpu.VMEM((buffers, block_k, block_w), jnp.bfloat16),
            pltpu.VMEM((rows, columns), jnp.float32),
            pltpu.SemaphoreType.DMA((2 * len(chunks),)),
            pltpu.SemaphoreType.DMA((buffers,)),
        ] + ([
            pltpu.VMEM((staged, per_block, depth), jnp.bfloat16),
            pltpu.SemaphoreType.DMA((staged + 1,)),
        ] if staged else []),
        compiler_params=pltpu.CompilerParams(vmem_limit_bytes=VMEM_BYTES),
        cost_estimate=pl.CostEstimate(flops=0, bytes_accessed=0, transcendentals=0),
        name="partial_products",
    )(pos, *[source for own, sib, _, _ in chunks for source in (own, sib)], weight, factors)


def finish_body(received, panels, chosen_ref, slot_ref, order_ref, *refs):
    panel_refs, refs = refs[:panels], refs[panels:]
    per_panel = panel_refs[0].shape[0]
    out_ref, lifted_ref, done_ref, sem = refs[-4:]
    steps, rows, width = done_ref.shape
    rank = chosen_ref.shape[1]
    chosen = chosen_ref[...]
    slot = slot_ref[...]
    spread = jnp.concatenate(
        [
            jnp.where(slot == order_ref[place], chosen, jnp.zeros_like(chosen))
            for place in range(panels * per_panel // rank)
        ],
        axis=1,
    )
    block_n = min(BLOCK_N, width)
    for place in range(width // block_n):
        columns = slice(place * block_n, (place + 1) * block_n)
        panel = jnp.concatenate([panel_ref[:, columns] for panel_ref in panel_refs], axis=0)
        lifted = jnp.dot(spread, panel, preferred_element_type=jnp.float32).astype(jnp.bfloat16)
        for step in range(steps):
            total = refs[step * (received + 1)][:, columns]
            for value_ref in refs[step * (received + 1) + 1:(step + 1) * (received + 1)]:
                total = total + value_ref[:, columns].astype(jnp.float32)
            value = total + ADAPTER_SCALE * lifted[step * rows:(step + 1) * rows].astype(jnp.float32)
            done_ref[step, :, columns] = value.astype(done_ref.dtype)
        lifted_ref[:, columns] = lifted[steps * rows:]
    copy = pltpu.make_async_copy(done_ref, out_ref.at[pl.ds(0, steps)], sem)
    copy.start()
    copy.wait()


def finish_steps(totals, chosen, slots, order, panels):
    steps, width = len(totals), panels[0].shape[1]
    rows = chosen.shape[0] // (steps + 1)
    vmem_spec = pl.BlockSpec(memory_space=pltpu.VMEM)
    arrays = [value for total in totals for value in total]
    return pl.pallas_call(
        functools.partial(finish_body, len(totals[0]) - 1, len(panels)),
        in_specs=[vmem_spec, vmem_spec, pl.BlockSpec(memory_space=pltpu.SMEM)] + [vmem_spec] * (len(panels) + len(arrays)),
        out_specs=[pl.BlockSpec(memory_space=pl.ANY), vmem_spec],
        out_shape=[
            jax.ShapeDtypeStruct((steps + 1, rows, width), jnp.bfloat16),
            jax.ShapeDtypeStruct((rows, width), jnp.bfloat16),
        ],
        scratch_shapes=[pltpu.VMEM((steps, rows, width), jnp.bfloat16), pltpu.SemaphoreType.DMA],
        compiler_params=pltpu.CompilerParams(vmem_limit_bytes=VMEM_BYTES),
        cost_estimate=pl.CostEstimate(flops=0, bytes_accessed=0, transcendentals=0),
        name="finish_steps",
    )(chosen, slots, order, *panels, *arrays)


def last_body(partial_ref, lifted_ref, *refs):
    out_ref, done_ref, sem = refs[-3:]
    total = refs[0][...]
    for value_ref in refs[1:-3]:
        total = total + value_ref[...].astype(jnp.float32)
    value = total + ADAPTER_SCALE * lifted_ref[...].astype(jnp.float32)
    done_ref[0] = value.astype(done_ref.dtype)
    copy = pltpu.make_async_copy(done_ref, out_ref.at[pl.ds(out_ref.shape[0] - 1, 1)], sem)
    copy.start()
    copy.wait()


def finish_last(partial, lifted, arrays):
    vmem_spec = pl.BlockSpec(memory_space=pltpu.VMEM)
    any_spec = pl.BlockSpec(memory_space=pl.ANY)
    return pl.pallas_call(
        last_body,
        in_specs=[any_spec] + [vmem_spec] * (1 + len(arrays)),
        out_specs=any_spec,
        out_shape=jax.ShapeDtypeStruct(partial.shape, partial.dtype),
        input_output_aliases={0: 0},
        scratch_shapes=[pltpu.VMEM((1,) + partial.shape[1:], partial.dtype), pltpu.SemaphoreType.DMA],
        compiler_params=pltpu.CompilerParams(vmem_limit_bytes=VMEM_BYTES),
        cost_estimate=pl.CostEstimate(flops=0, bytes_accessed=0, transcendentals=0),
        name="finish_last",
    )(partial, lifted, *arrays)


def per_device(hidden, base_weight, down_a, up_b, adapter_ids, owner_map):
    step_count, per_block, _ = hidden.shape
    n_tensor = lax.axis_size("tp")
    n_rep = lax.axis_size("rep")
    n_sub = lax.axis_size("sub")
    n_owners = n_rep * n_sub
    tensor_index = lax.axis_index("tp")
    rep_index = lax.axis_index("rep")
    sub_index = lax.axis_index("sub")
    owner_index = lax.axis_index(("rep", "sub"))
    requests = per_block * n_owners
    rows_mine = requests // n_tensor
    group = n_tensor // n_rep
    group_index = tensor_index // group
    owned_slots, _, rank_size = down_a.shape
    slot_count = owned_slots * n_owners
    width = base_weight.shape[1]

    def after(value, *done):
        return lax.optimization_barrier((value, *done))[0]

    def swap_cores(value):
        return lax.ppermute(value, "sub", [(i, i ^ 1) for i in range(n_sub)])

    def from_rep(value, shift):
        return lax.ppermute(value, "rep", [((i + shift) % n_rep, i) for i in range(n_rep)])

    def swap_tensor(value, bit):
        return lax.ppermute(value, "tp", [(i, i ^ bit) for i in range(n_tensor)])

    def to_group(value, hop):
        moved = group * hop
        return lax.ppermute(value, "tp", [(i, (i + moved) % n_tensor) for i in range(n_tensor)])

    def pick(values, index):
        value = values[0]
        for at in range(1, len(values)):
            value = jnp.where(index == at, values[at], value)
        return value

    keeps = (tensor_index // (group // 2)) % 2
    pos = (sub_index == keeps).astype(jnp.int32).reshape(1)

    siblings = swap_cores(hidden)
    pieces = [(step, shift) for step in range(step_count) for shift in range(1, n_rep)]
    source = pltpu.with_memory_space_constraint(hidden, pltpu.HBM)
    weight = pltpu.with_memory_space_constraint(base_weight, pltpu.HBM)
    remote = {(0, shift): from_rep(hidden[:1], shift) for shift in range(1, n_rep)}

    def spread_panels(panels, order, bits):
        for bit in bits:
            panels = panels + [swap_tensor(panel, bit) for panel in panels]
            order = order + [at ^ bit for at in order]
        return panels, order

    bits = [n_tensor >> at for at in range(1, n_tensor.bit_length())]
    order = [0, bits[0], bits[1]]
    panels = [up_b] + [swap_tensor(up_b, at) for at in order[1:]]

    my_ids = lax.dynamic_slice_in_dim(adapter_ids, tensor_index * rows_mine, rows_mine)
    iota = lax.broadcasted_iota(jnp.int32, (rows_mine, slot_count), 1)
    my_slot = jnp.sum((my_ids == iota).astype(jnp.int32) * owner_map[None, :], axis=1)
    owned_hot = my_slot[:, None] == (
        owner_index * owned_slots + lax.broadcasted_iota(jnp.int32, (rows_mine, owned_slots), 1)
    )

    first_leg, halved, begun, second_leg, ended = [], {}, set(), [], {}

    def second_half(total, received, steps, kind):
        total = total + received.astype(jnp.float32)
        rows, columns = total.shape
        extent, bit = rows // steps, group // 4
        while bit:
            extent //= 2
            halves = total.reshape(steps, 2, extent, columns)
            mine = (tensor_index // bit) % 2
            kept = lax.dynamic_index_in_dim(halves, mine, 1, keepdims=False)
            sent = lax.dynamic_index_in_dim(halves, 1 - mine, 1, keepdims=False)
            total = kept + swap_tensor(sent.astype(kind), bit).astype(jnp.float32)
            bit //= 2
        return total.reshape(steps, extent, columns)

    def gap(token, jobs):
        nonlocal first_leg, second_leg
        for parts, received, keep, kind in first_leg:
            steps = sum(length for _, length in parts)
            total, begin = second_half(after(keep, token), received, steps, kind), 0
            for key, length in parts:
                for at in range(begin, begin + length):
                    halved[key[0] + at - begin, key[1]] = total[at]
                    if (key[0] + at - begin, key[1]) == (step_count - 1, 0):
                        halved[RANK_NAME, 0] = total[at][:, width:]
                begin += length
        closed = {name: (after(kept, token), *received) for name, kept, received in second_leg}
        started, sends = [], []
        for name in sorted({name for name, _ in halved}):
            if name in begun or name == RANK_NAME or any((name, at) not in halved for at in range(n_rep)):
                continue
            begun.add(name)
            values = [halved[name, at] for at in range(n_rep)]
            columns = min(value.shape[1] for value in values)
            values = [value[:, :columns] for value in values]
            kept = pick(values, (group_index - rep_index) % n_rep)
            sends.append([
                pick(values, (group_index + hop - rep_index) % n_rep).astype(jnp.bfloat16) for hop in range(1, n_rep)
            ])
            started.append((name, kept))
        sends, token = lax.optimization_barrier((sends, token))
        first_sends, closed = lax.optimization_barrier(([job[1] for job in jobs], closed))
        ended.update(closed)
        first_leg = [
            (parts, swap_tensor(send, group // 2), keep, kind) for (parts, _, keep, kind), send in zip(jobs, first_sends)
        ]
        second_leg = [
            (name, kept, [to_group(value, hop + 1) for hop, value in enumerate(sent)])
            for (name, kept), sent in zip(started, sends)
        ]
        return sends

    factors = jnp.swapaxes(down_a, 1, 2)

    lead = step_count // 2
    last_ranks, next_local = {}, lead
    send, keep, *slices = partial_products(
        pos, [(source, siblings, 0, lead)], weight, factors, staged=step_count - 1
    )
    for step, rows in enumerate(slices, 1):
        remote.update({(step, shift): from_rep(rows, shift) for shift in range(1, n_rep)})
    jobs = [([((0, 0), lead)], send, keep, jnp.bfloat16)]
    for piece, (step, shift) in enumerate(pieces):
        sends = gap(send, jobs)
        own, panels, _ = lax.optimization_barrier((remote[step, shift], panels, send))
        if piece == 0:
            panels, order = panels + [swap_tensor(panels[1], bits[1])], order + [bits[0] ^ bits[1]]
            panels, order = spread_panels(panels, order, bits[2:])
        sib = swap_cores(own)
        own, sib, siblings, _ = lax.optimization_barrier((own, sib, siblings, sends))
        last, chunks, keys = step == step_count - 1, [(own, sib, 0, 1)], [(step, shift)]
        if next_local < step_count:
            chunks.append((source, siblings, next_local, 1))
            keys.append((next_local, 0))
            next_local += 1
        outs = partial_products(pos, chunks, weight, factors, last)
        send, count = outs[0], len(chunks)
        jobs = [([(key, 1)], outs[at], outs[count + at], jnp.bfloat16) for at, key in enumerate(keys)]
        if last:
            last_ranks[shift] = outs[2 * count:]
    gap(send, jobs)
    for shift, ranks in last_ranks.items():
        halved[RANK_NAME, shift] = second_half(ranks[1], swap_tensor(ranks[0], group // 2), 1, jnp.float32)[0]
    values = [halved[RANK_NAME, at] for at in range(n_rep)]
    ended[RANK_NAME] = (pick(values, (group_index - rep_index) % n_rep), *[
        to_group(pick(values, (group_index + hop - rep_index) % n_rep), hop) for hop in range(1, n_rep)
    ])
    rounded = gap(send, [])

    def rank_sum(name):
        kept, *received = [value[:, -rank_columns(factors):] for value in ended[name]]
        for value in received:
            kept = kept + value.astype(jnp.float32)
        return kept[:, :owned_slots * rank_size]

    finished = jnp.stack([rank_sum(step) for step in range(step_count - 1)] + [rank_sum(RANK_NAME)])
    finished = finished.astype(jnp.bfloat16).reshape(step_count, rows_mine, owned_slots, rank_size)
    finished = lax.optimization_barrier((finished, rounded))[0]
    ended.update((name, (kept, *received)) for name, kept, received in second_leg)
    masked = jnp.sum(
        jnp.where(owned_hot[None, :, :, None], finished, 0), axis=2, dtype=jnp.float32
    ).astype(jnp.bfloat16)
    chosen = masked
    for turn in range(1, n_owners):
        chosen = chosen + lax.ppermute(
            masked, ("rep", "sub"), [(i, (i + turn) % n_owners) for i in range(n_owners)]
        )
    panel_slots = jnp.stack([
        (tensor_index ^ at) * up_b.shape[0] + each for at in order for each in range(up_b.shape[0])
    ]).astype(jnp.int32)

    panels = [panel.reshape(-1, width) for panel in panels]
    partial, lifted = finish_steps(
        [ended[step] for step in range(step_count - 1)],
        chosen.reshape(step_count * rows_mine, rank_size),
        jnp.broadcast_to(my_slot, (step_count, rows_mine)).reshape(step_count * rows_mine, 1),
        panel_slots,
        panels,
    )
    return finish_last(partial, lifted, ended[step_count - 1])


def solution(mesh):
    return jax.shard_map(
        per_device,
        mesh=mesh,
        in_specs=(
            P(None, ("groups", "rep", "sub"), "tp"),
            P("tp", ("rep", "sub")),
            P(("rep", "sub"), "tp", None),
            P("tp", None, ("rep", "sub")),
            P("groups", None),
            P(),
        ),
        out_specs=P(None, ("groups", "tp"), ("rep", "sub")),
        check_vma=False,
    )
```
